32 devices in a mesh: dp: 2 (over x), row: 4 (over z), col: 4 (over y, core).
Axes of the slice: x: 2, y: 2, z: 4, core: 2. Of those that a mesh axis runs over, the one named last changes fastest.
Arguments:
- tokens: bfloat16 [4, 8, 1024, 768], P(None, None, 'col', ('dp', 'row')), may hold values from -6 to 6
- cotangent: bfloat16 [4, 8, 1024, 768], P(None, ('dp', 'row'), 'col'), may hold values from -6 to 6
- lengths: int32 [4, 8], replicated, may hold values from 1 to 1024, 5120 in all within a row
- seq_order: int32 [4, 8], replicated, may hold values from 0 to 7, each once within a row
- w_qkv: bfloat16 [768, 2304], P(('dp', 'row'), 'col'), may hold values from -0.21875 to 0.21875
- w_out: bfloat16 [768, 768], P(('dp', 'row'), 'col'), may hold values from -2 to 2
- w_up: bfloat16 [768, 3072], P(('dp', 'row'), 'col'), may hold values from -0.21875 to 0.21875
- w_down: bfloat16 [3072, 768], P(('dp', 'row'), 'col'), may hold values from -0.109375 to 0.109375
- gain_one: bfloat16 [768], P(('dp', 'row', 'col')), may hold values from 0.5 to 1.5
- shift_one: bfloat16 [768], P(('dp', 'row', 'col')), may hold values from -1 to 1
- gain_two: bfloat16 [768], P(('dp', 'row', 'col')), may hold values from 0.5 to 1.5
- shift_two: bfloat16 [768], P(('dp', 'row', 'col')), may hold values from -1 to 1
Outputs:
- output: bfloat16 [4, 8, 1024, 768], P(None, ('dp', 'row'), 'col')
- tokens_grad: bfloat16 [4, 8, 1024, 768], P(None, None, 'col', ('dp', 'row'))
- w_qkv_grad: float32 [768, 2304], P(('dp', 'row'), 'col')
- w_out_grad: float32 [768, 768], P(('dp', 'row'), 'col')
- w_up_grad: float32 [768, 3072], P(('dp', 'row'), 'col')
- w_down_grad: float32 [3072, 768], P(('dp', 'row'), 'col')
- gain_one_grad: float32 [768], P(('dp', 'row', 'col'))
- shift_one_grad: float32 [768], P(('dp', 'row', 'col'))
- gain_two_grad: float32 [768], P(('dp', 'row', 'col'))
- shift_two_grad: float32 [768], P(('dp', 'row', 'col'))
The draws below stay inside these ranges and needn't reach their ends.
Inputs may be any that keep to these rules, and one draw needn't show every extreme that they name: `seq_order`: each row is a permutation of the micro-batch's 8 sequences. In every micro-batch the lengths add up to 5120, and the longest is 1024.
All inputs are finite; a program needn't handle non-finite values.
Results may differ from the reference program's by a relative error of at most 0.017.
Values may be sent and summed in bfloat16 or wider, within the bound.
A program may use at most 256 MiB of HBM per device.

```python
import math
import jax
import jax.numpy as jnp
import numpy as np
from jax import lax

D = 768
HEADS = 12
HEAD = 64
FF = 3072
LEN = 1024
MICRO = 4
NSEQ = 8


def spiked(entries, own_key, source, target, blocks, factor):
    def block_of(dim):
        return (jnp.arange(entries.shape[dim]) // (entries.shape[dim] // blocks)).reshape((-1,) + (1,) * (entries.ndim - 1 - dim))

    one_side = jax.random.permutation(own_key, blocks)[block_of(target)]
    second = (block_of(target) + blocks // 2) % blocks
    return jnp.where((block_of(source) == one_side) | (block_of(source) == second), factor * entries, entries)


def steps_of(own_key, dims, split, least, high):
    gain, own = 1.0, jax.random.fold_in(own_key, 6)
    for position, parts in split:
        steps = jnp.exp(jax.random.uniform(jax.random.fold_in(own, position), (parts,), jnp.float32, least / len(split), high / len(split)))
        gain = gain * jnp.repeat(steps, dims[position] // parts).reshape([-1 if axis == position else 1 for axis in range(len(dims))])
    return gain


def split_up(amount, total, bound, skew):
    loads = [(1 << 20) // math.isqrt(grade ** skew) + 1 for grade in range(2, amount + 1)]
    spare, given = total - bound - (amount - 1), [1] * (amount - 1)
    while spare > 0:
        candidates = [i for i in range(amount - 1) if given[i] < bound]
        whole, left = sum([loads[i] for i in candidates]), spare
        for i in candidates:
            extra = min(bound - given[i], max(1, left * loads[i] // whole), spare)
            given[i] = given[i] + extra
            spare = spare - extra
    return np.array([bound] + given)


def uneven_parts(stream_key, count, total, reach, lean):
    if count == 2:
        one = jax.random.randint(stream_key, (), max(1, total - reach), min(reach, total - 1) + 1)
        return jnp.stack([one, total - one])
    sizes = jnp.asarray(split_up(count, total, reach, lean), jnp.int32)
    twos = (count - 1) // 2
    source_of, taker = sizes[1:1 + 2 * twos:2], sizes[2:2 + 2 * twos:2]
    margin = jnp.minimum(source_of - 1, reach - taker)
    shifted = jax.random.randint(jax.random.fold_in(stream_key, 1), (twos,), 0, 1 << 20) % (margin + 1)
    sizes = sizes.at[1:1 + 2 * twos:2].set(source_of - shifted).at[2:2 + 2 * twos:2].set(taker + shifted)
    return sizes[jax.random.permutation(jax.random.fold_in(stream_key, 2), count)]


def normal_values(own_key, dims, spread, reach, shards=(), kind=jnp.bfloat16):
    level = steps_of(own_key, dims, shards, -0.22, 0.18) if shards else 1.0
    values = jax.random.normal(own_key, dims, jnp.float32) * spread * level
    return jnp.minimum(jnp.maximum(values, -reach), reach).astype(kind)


def gaussian_with(key, extent, deviation, reach, shards, heavy, kind=jnp.bfloat16):
    values = deviation * jax.random.normal(key, extent, jnp.float32)
    if shards:
        values = values * steps_of(key, extent, shards, -0.22, 0.18)
    return jnp.clip(spiked(values, jax.random.fold_in(key, 3), *heavy), -reach, reach).astype(kind)


def setup_inputs(seed: int = 0) -> dict:
    streams_of = jax.random.split(jax.random.key(seed), 13)
    return {
        "tokens": normal_values(streams_of[0], (MICRO, NSEQ, LEN, D), 1.0, 6.0, ((2, 4), (3, 8))),
        "cotangent": gaussian_with(streams_of[1], (MICRO, NSEQ, LEN, D), 1.0, 6.0, ((1, 8), (2, 4)), (1, 3, 8, 2.0)),
        "lengths": jax.vmap(lambda own: uneven_parts(own, NSEQ, NSEQ * LEN * 5 // 8, LEN, 2))(jax.random.split(streams_of[2], MICRO)).reshape((MICRO, NSEQ)).astype(jnp.int32),
        "seq_order": jax.vmap(lambda own: jax.random.permutation(own, NSEQ))(jax.random.split(streams_of[3], MICRO)).reshape((MICRO, NSEQ)).astype(jnp.int32),
        "w_qkv": normal_values(streams_of[4], (D, 3 * D), D ** -0.5, 0.21875, ((0, 8), (1, 4))),
        "w_out": normal_values(streams_of[5], (D, D), 8 ** -0.5, 2.0, ((0, 8), (1, 4))),
        "w_up": normal_values(streams_of[6], (D, FF), D ** -0.5, 0.21875, ((0, 8), (1, 4))),
        "w_down": normal_values(streams_of[7], (FF, D), FF ** -0.5, 0.109375, ((0, 8), (1, 4))),
        "gain_one": jnp.clip(1.0 + 0.1 * jax.random.normal(streams_of[8], (D,), jnp.float32), 0.5, 1.5).astype(jnp.bfloat16),
        "shift_one": normal_values(streams_of[9], (D,), 0.2, 1.0, ((0, 32),)),
        "gain_two": jnp.clip(1.0 + 0.1 * jax.random.normal(streams_of[10], (D,), jnp.float32), 0.5, 1.5).astype(jnp.bfloat16),
        "shift_two": normal_values(streams_of[11], (D,), 0.2, 1.0, ((0, 32),)),
    }


NEGATIVE = -1000000000.0
EPSILON = 1e-12
ROOT_HALF = 0.7071067811865476

@jax.custom_vjp
def low(v):
    return lax.optimization_barrier(v.astype(jnp.bfloat16)).astype(jnp.float32)

@jax.custom_vjp
def low_back(v):
    return v

def low_keep(v):
    return (low(v), None)

def low_pass(kept, grad):
    return (grad,)

def back_keep(v):
    return (v, None)

def back_low(kept, grad):
    return (low(grad),)
low.defvjp(low_keep, low_pass)
low_back.defvjp(back_keep, back_low)

def layer_norm(values, factor, offset):
    average = lax.optimization_barrier(jnp.mean(values, axis=-1, keepdims=True))
    centered = values - average
    variance = lax.optimization_barrier(jnp.mean(centered * centered, axis=-1, keepdims=True))
    return centered * lax.rsqrt(variance + EPSILON) * factor + offset

def gelu_act(values):
    return 0.5 * values * (1.0 + lax.erf(values * ROOT_HALF))

def matmul(left, right):
    return jnp.dot(left, right, precision=lax.Precision.HIGHEST, preferred_element_type=jnp.float32)

def encode(seq_in, valid_keys, p_qkv, p_out, p_up, p_down, p_gain_one, p_shift_one, p_gain_two, p_shift_two):
    qkv = low_back(low(matmul(seq_in, p_qkv)))
    query_heads = qkv[:, :D].reshape(LEN, HEADS, HEAD)
    key_heads = qkv[:, D:2 * D].reshape(LEN, HEADS, HEAD)
    value_heads = qkv[:, 2 * D:].reshape(LEN, HEADS, HEAD)
    scores = jnp.einsum('qhe,khe->hqk', query_heads, key_heads, precision=lax.Precision.HIGHEST) * 0.125
    scores = low_back(scores)
    scores = jnp.where(valid_keys[None, None, :], scores, NEGATIVE)
    row_top = lax.optimization_barrier(jnp.max(scores, axis=-1, keepdims=True))
    exp_scores = jnp.exp(scores - row_top)
    attn_probs = low(exp_scores / lax.optimization_barrier(jnp.sum(exp_scores, axis=-1, keepdims=True)))
    context = jnp.einsum('hqk,khe->qhe', attn_probs, value_heads, precision=lax.Precision.HIGHEST)
    context = low_back(low(context.reshape(LEN, D)))
    attn_out = low_back(matmul(context, p_out))
    hidden = layer_norm(seq_in + attn_out, p_gain_one, p_shift_one)
    pre_act = low_back(matmul(low(hidden), p_up))
    act_low = low(gelu_act(pre_act))
    down_out = low_back(matmul(act_low, p_down))
    return layer_norm(hidden + down_out, p_gain_two, p_shift_two)

def reference(tokens, cotangent, lengths, seq_order, w_qkv, w_out, w_up, w_down, gain_one, shift_one, gain_two, shift_two):
    params = (w_qkv.astype(jnp.float32), w_out.astype(jnp.float32), w_up.astype(jnp.float32), w_down.astype(jnp.float32), gain_one.astype(jnp.float32), shift_one.astype(jnp.float32), gain_two.astype(jnp.float32), shift_two.astype(jnp.float32))
    key_pos = jnp.arange(LEN, dtype=jnp.int32)

    def one_slot(totals, slot_idx):
        micro_idx = slot_idx // NSEQ
        place = slot_idx % NSEQ
        source = seq_order[micro_idx, place]
        seq_in = tokens[micro_idx, source].astype(jnp.float32)
        valid_keys = key_pos < lengths[micro_idx, source]

        def forward(seq_rows, p_qkv, p_out, p_up, p_down, p_gain_one, p_shift_one, p_gain_two, p_shift_two):
            return encode(seq_rows, valid_keys, p_qkv, p_out, p_up, p_down, p_gain_one, p_shift_one, p_gain_two, p_shift_two)
        result, pullback = jax.vjp(forward, seq_in, params[0], params[1], params[2], params[3], params[4], params[5], params[6], params[7])
        grad_terms = pullback(cotangent[micro_idx, place].astype(jnp.float32))
        new_totals = tuple((total + term for total, term in zip(totals, grad_terms[1:])))
        return (new_totals, (result.astype(jnp.bfloat16), grad_terms[0]))
    start = tuple((jnp.zeros(p.shape, jnp.float32) for p in params))
    totals, (outputs, seq_grads) = lax.scan(one_slot, start, jnp.arange(MICRO * NSEQ, dtype=jnp.int32))
    output = outputs.reshape(MICRO, NSEQ, LEN, D)
    seq_grads = seq_grads.reshape(MICRO, NSEQ, LEN, D)
    inverse = jnp.argsort(seq_order, axis=1).astype(jnp.int32)
    tokens_grad = jnp.take_along_axis(seq_grads, inverse[:, :, None, None], axis=1).astype(jnp.bfloat16)
    return (output, tokens_grad, totals[0], totals[1], totals[2], totals[3], totals[4], totals[5], totals[6], totals[7])
```

```python
import functools

import jax
import jax.numpy as jnp
from jax import lax
from jax.experimental import pallas as pl
from jax.experimental.pallas import tpu as pltpu
from jax.sharding import PartitionSpec as P

HEAD = 64
NEGATIVE = -1000000000.0
EPSILON = 1e-12
ROOT_HALF = 0.7071067811865476
MESH = pl.DeviceIdType.MESH
BF = jnp.bfloat16
F32 = jnp.float32


def aligned(value, step):
    return pl.multiple_of(value, step)


class Place:
    def __init__(self, n_dp, n_row, n_col):
        self.n_dp, self.n_row, self.n_col = n_dp, n_row, n_col
        self.n = n_dp * n_row * n_col
        self.x = lax.axis_index("dp")
        self.z = lax.axis_index("row")
        self.c = lax.axis_index("col")
        self.y, self.k = self.c // 2, self.c % 2
        self.g = self.x * n_row + self.z
        self.flat = self.g * n_col + self.c

    def of_flat(self, flat):
        group = flat // self.n_col
        return (group // self.n_row, group % self.n_row, flat % self.n_col)

    def dev(self, x=None, z=None, y=None, k=None):
        x = self.x if x is None else x
        z = self.z if z is None else z
        y = self.y if y is None else y
        k = self.k if k is None else k
        return (x, z, y * 2 + k)

    def barrier(self):
        sem = pltpu.get_barrier_semaphore()

        def greet(i, carry):
            pl.semaphore_signal(
                sem, inc=1, device_id=self.of_flat((self.flat + i) % self.n), device_id_type=MESH
            )
            return carry

        lax.fori_loop(1, self.n, greet, 0)
        pl.semaphore_wait(sem, self.n - 1)


class Lanes:
    def __init__(self, send_sems, recv_sems):
        self.send_sems, self.recv_sems, self.used, self.sent = send_sems, recv_sems, 0, []

    def slot(self):
        self.used += 1
        return self.used - 1

    def copy(self, src, dst, device, slot):
        return pltpu.make_async_remote_copy(
            src_ref=src, dst_ref=dst, send_sem=self.send_sems.at[slot],
            recv_sem=self.recv_sems.at[slot], device_id=device, device_id_type=MESH,
        )

    def send(self, src, dst, device):
        slot = self.slot()
        made = self.copy(src, dst, device, slot)
        made.start()
        self.sent.append(made)
        return slot

    def arrived(self, landing, slot, device):
        self.copy(landing, landing, device, slot).wait_recv()

    def finish(self):
        for made in self.sent:
            made.wait_send()
        self.sent = []


class Gather:
    def __init__(self, place, lanes, region, first):
        self.place, self.lanes, self.region, self.first = place, lanes, region, first
        self.slots = {}

    def start(self, own):
        p, lanes = self.place, self.lanes
        mine = self.region(p.x, p.z, 1, p.y, p.k, 1)
        for i in range(1, p.n_row):
            self.slots["z", i] = lanes.send(own, mine, p.dev(z=(p.z + i) % p.n_row))

    def hop(self):
        p, lanes = self.place, self.lanes
        for i in range(1, p.n_row):
            source = (p.z + p.n_row - i) % p.n_row
            lanes.arrived(self.region(p.x, source, 1, p.y, p.k, 1), self.slots["z", i], p.dev(z=source))
        line = self.region(p.x, 0, p.n_row, p.y, p.k, 1)
        if self.first == "x":
            self.slots["one"] = lanes.send(line, line, p.dev(x=1 - p.x))
            self.slots["two"] = lanes.send(line, line, p.dev(y=1 - p.y))
        else:
            self.slots["one"] = lanes.send(line, line, p.dev(y=1 - p.y))
            self.slots["two"] = lanes.send(line, line, p.dev(x=1 - p.x))
        self.slots["core"] = lanes.send(line, line, p.dev(k=1 - p.k))

    def turn(self):
        p, lanes = self.place, self.lanes
        if self.first == "x":
            peer, after = p.dev(x=1 - p.x), p.dev(y=1 - p.y)
            line = self.region(1 - p.x, 0, p.n_row, p.y, p.k, 1)
        else:
            peer, after = p.dev(y=1 - p.y), p.dev(x=1 - p.x)
            line = self.region(p.x, 0, p.n_row, 1 - p.y, p.k, 1)
        lanes.arrived(line, self.slots["one"], peer)
        self.slots["three"] = lanes.send(line, line, after)
        self.slots["core_one"] = lanes.send(line, line, p.dev(k=1 - p.k))

    def last(self):
        p, lanes = self.place, self.lanes
        if self.first == "x":
            peer = p.dev(y=1 - p.y)
            parts = (self.region(p.x, 0, p.n_row, 1 - p.y, p.k, 1), self.region(1 - p.x, 0, p.n_row, 1 - p.y, p.k, 1))
        else:
            peer = p.dev(x=1 - p.x)
            parts = (self.region(1 - p.x, 0, p.n_row, p.y, p.k, 1), self.region(1 - p.x, 0, p.n_row, 1 - p.y, p.k, 1))
        for name, part in zip(("two", "three"), parts):
            lanes.arrived(part, self.slots[name], peer)
            self.slots["core_" + name] = lanes.send(part, part, p.dev(k=1 - p.k))

    def end(self):
        p, lanes = self.place, self.lanes
        other, peer = 1 - p.k, p.dev(k=1 - p.k)
        lanes.arrived(self.region(p.x, 0, p.n_row, p.y, other, 1), self.slots["core"], peer)
        if self.first == "x":
            parts = ((1 - p.x, p.y), (p.x, 1 - p.y), (1 - p.x, 1 - p.y))
        else:
            parts = ((p.x, 1 - p.y), (1 - p.x, p.y), (1 - p.x, 1 - p.y))
        for name, (x, y) in zip(("core_one", "core_two", "core_three"), parts):
            lanes.arrived(self.region(x, 0, p.n_row, y, other, 1), self.slots[name], peer)


def rows_region(ref, n_row):
    width = ref.shape[3] // 2

    def region(x, z, nz, y, k, ny):
        if nz == 1:
            return ref.at[x * n_row + z, k, :, pl.ds(aligned(y * width, 128), width)]
        return ref.at[pl.ds(x * n_row + z, nz), k, :, pl.ds(aligned(y * width, 128), width)]

    return region


def lanes_region(ref, n_dp, n_row):
    width = ref.shape[3] // (n_dp * n_row)

    def region(x, z, nz, y, k, ny):
        return ref.at[y, k, :, pl.ds(aligned((x * n_row + z) * width, 128), nz * width)]

    return region


def gather_kernel(
    dims, seq_ref, tok_ref, cot_ref, qkv_ref, out_ref, up_ref, down_ref, norm_ref,
    xt_ref, cotf_ref, gqkv_ref, gout_ref, gup_ref, gdown_ref, gnorm_ref,
    tsend, half_qkv, half_out, half_up, pair_qkv, pair_out, pair_up,
    tok_send, tok_recv, cot_send, cot_recv, w_send, w_recv, local_sem,
):
    n_dp, n_row, n_col = dims
    p = Place(n_dp, n_row, n_col)
    micro, slots = tok_ref.shape[0], tok_ref.shape[1]
    span = tok_ref.shape[3]
    p.barrier()
    lanes = Lanes(w_send, w_recv)
    partner = p.dev(k=1 - p.k)
    halves = []
    for block, landing in ((qkv_ref, half_qkv), (out_ref, half_out), (up_ref, half_up)):
        rows = landing.shape[0]
        slot = lanes.send(block.at[pl.ds(aligned((1 - p.k) * rows, 16), rows), :], landing, partner)
        halves.append((block, landing, slot, rows))
    for m in range(micro):
        for j in range(slots):
            tsend[m * slots + j] = tok_ref[m, seq_ref[m, j]]

    def tok_copy(i):
        target = (p.flat + i) % p.n
        return pltpu.make_async_remote_copy(
            src_ref=tsend.at[(target % n_col) * slots + target // n_col],
            dst_ref=xt_ref.at[p.g, :, pl.ds(aligned(p.c * span, 128), span)],
            send_sem=tok_send.at[i], recv_sem=tok_recv.at[i],
            device_id=p.of_flat(target), device_id_type=MESH,
        )

    def tok_start(i, carry):
        tok_copy(i).start()
        return carry

    lax.fori_loop(1, p.n, tok_start, 0)
    own_tok = pltpu.make_async_copy(
        tsend.at[p.c * slots + p.g], xt_ref.at[p.g, :, pl.ds(aligned(p.c * span, 128), span)], local_sem.at[0]
    )
    own_tok.start()
    gathers = []
    locals_ = []
    specs = (
        (halves[0], pair_qkv, rows_region(gqkv_ref, n_row), "x"),
        (halves[1], pair_out, rows_region(gout_ref, n_row), "y"),
        (halves[2], pair_up, rows_region(gup_ref, n_row), "x"),
    )
    for index, ((block, landing, slot, rows), pair, region, first) in enumerate(specs):
        lanes.arrived(landing, slot, partner)
        mine = block[pl.ds(aligned(p.k * rows, 16), rows), :]
        theirs = landing[...]
        width = mine.shape[1]
        pair[:, :width] = jnp.where(p.k == 0, mine, theirs)
        pair[:, width:] = jnp.where(p.k == 0, theirs, mine)
        local = pltpu.make_async_copy(pair, region(p.x, p.z, 1, p.y, p.k, 1), local_sem.at[1 + index])
        local.start()
        locals_.append(local)
        gather = Gather(p, lanes, region, first)
        gather.start(pair)
        gathers.append(gather)
    for block, region, first in (
        (down_ref, lanes_region(gdown_ref, n_dp, n_row), "y"),
        (norm_ref, rows_region(gnorm_ref, n_row), "y"),
    ):
        local = pltpu.make_async_copy(block, region(p.x, p.z, 1, p.y, p.k, 1), local_sem.at[1 + len(gathers)])
        local.start()
        locals_.append(local)
        gather = Gather(p, lanes, region, first)
        gather.start(block)
        gathers.append(gather)

    rows = cot_ref.shape[1]

    def cot_copy(i):
        target = (p.c + i) % n_col
        return pltpu.make_async_remote_copy(
            src_ref=cot_ref.at[target], dst_ref=cotf_ref.at[p.c],
            send_sem=cot_send.at[i], recv_sem=cot_recv.at[i],
            device_id=(p.x, p.z, target), device_id_type=MESH,
        )

    for i in range(1, n_col):
        cot_copy(i).start()
    own_cot = pltpu.make_async_copy(cot_ref.at[p.c], cotf_ref.at[p.c], local_sem.at[6])
    own_cot.start()
    for local in locals_:
        local.wait()
    order = (gathers[0], gathers[3], gathers[2], gathers[1], gathers[4])
    for gather in order:
        gather.hop()
    for gather in order:
        gather.turn()
    for gather in order:
        gather.last()
    for gather in order:
        gather.end()
    own_tok.wait()
    own_cot.wait()

    def tok_wait(i, carry):
        source = (p.flat + p.n - i) % p.n
        landing = xt_ref.at[source // n_col, :, pl.ds(aligned((source % n_col) * span, 128), span)]
        pltpu.make_async_remote_copy(
            src_ref=landing, dst_ref=landing, send_sem=tok_send.at[i], recv_sem=tok_recv.at[i],
            device_id=p.of_flat(source), device_id_type=MESH,
        ).wait_recv()
        tok_copy(i).wait_send()
        return carry

    lax.fori_loop(1, p.n, tok_wait, 0)
    for i in range(1, n_col):
        source = (p.c + n_col - i) % n_col
        pltpu.make_async_remote_copy(
            src_ref=cotf_ref.at[source], dst_ref=cotf_ref.at[source],
            send_sem=cot_send.at[i], recv_sem=cot_recv.at[i],
            device_id=(p.x, p.z, source), device_id_type=MESH,
        ).wait_recv()
        cot_copy(i).wait_send()
    lanes.finish()


ANY = pl.BlockSpec(memory_space=pl.ANY)
VM = pl.BlockSpec(memory_space=pltpu.VMEM)
SM = pl.BlockSpec(memory_space=pltpu.SMEM)


def gather_all(dims, seq_order, tok_t, cot, w_qkv, w_out, w_up, w_down_t, norms):
    n_dp, n_row, n_col = dims
    groups = n_dp * n_row
    micro, slots, feats, span = tok_t.shape
    qr, qc = w_qkv.shape
    orow, oc = w_out.shape
    ur, uc = w_up.shape
    dr, dc = w_down_t.shape
    shape = jax.ShapeDtypeStruct
    outs = (
        shape((groups, feats, n_col * span), BF),
        shape((n_col,) + cot.shape[1:], BF),
        shape((groups, 2, qr // 2, qc * n_col), BF),
        shape((groups, 2, orow // 2, oc * n_col), BF),
        shape((groups, 2, ur // 2, uc * n_col), BF),
        shape((2, 2, dr, dc * groups), BF),
        shape((groups, 2, 16, 256), BF),
    )
    dma = pltpu.SemaphoreType.DMA
    return pl.pallas_call(
        functools.partial(gather_kernel, dims),
        out_shape=outs,
        in_specs=[SM, VM, ANY, VM, VM, VM, VM, VM],
        out_specs=[ANY] * 7,
        scratch_shapes=[
            pltpu.VMEM((micro * slots, feats, span), BF),
            pltpu.VMEM((qr // 2, qc), BF),
            pltpu.VMEM((orow // 2, oc), BF),
            pltpu.VMEM((ur // 2, uc), BF),
            pltpu.VMEM((qr // 2, qc * 2), BF),
            pltpu.VMEM((orow // 2, oc * 2), BF),
            pltpu.VMEM((ur // 2, uc * 2), BF),
            dma((n_dp * n_row * n_col,)), dma((n_dp * n_row * n_col,)),
            dma((n_col,)), dma((n_col,)),
            dma((80,)), dma((80,)), dma((8,)),
        ],
        compiler_params=pltpu.CompilerParams(
            collective_id=0, has_side_effects=True, vmem_limit_bytes=48 * 2**20
        ),
        name="gather_all",
    )(seq_order, tok_t, cot, w_qkv, w_out, w_up, w_down_t, norms)


class Reduce:
    def __init__(self, place, lanes, grad, b0, b1, b2, b3, kind, first):
        self.p, self.lanes, self.grad, self.b = place, lanes, grad, (b0, b1, b2, b3)
        self.kind, self.first, self.slots = kind, first, {}

    def start(self):
        p = self.p
        self.slots[0] = self.lanes.send(self.grad.at[:, 1 - p.k], self.b[0], p.dev(k=1 - p.k))

    def half(self, ref, axis, side):
        if self.kind == "rows" and axis == "x" or self.kind == "lanes" and axis == "y":
            if self.kind == "lanes":
                return ref.at[side]
            count = ref.shape[0] // 2
            return ref.at[pl.ds(side * count, count)]
        width = ref.shape[-1] // 2
        lead = (slice(None),) * (len(ref.shape) - 1)
        return ref.at[lead + (pl.ds(aligned(side * width, 128), width),)]

    def axes(self):
        return ("x", "y") if self.first == "x" else ("y", "x")

    def send_half(self, stage, axis):
        p = self.p
        side = p.x if axis == "x" else p.y
        peer = p.dev(x=1 - p.x) if axis == "x" else p.dev(y=1 - p.y)
        self.slots[stage] = self.lanes.send(self.half(self.b[stage - 1], axis, 1 - side), self.b[stage], peer)

    def add_half(self, stage, axis):
        p = self.p
        side = p.x if axis == "x" else p.y
        peer = p.dev(x=1 - p.x) if axis == "x" else p.dev(y=1 - p.y)
        self.lanes.arrived(self.b[stage], self.slots[stage], peer)
        add_into(self.b[stage], self.half(self.b[stage - 1], axis, side))

    def one(self):
        p = self.p
        self.lanes.arrived(self.b[0], self.slots[0], p.dev(k=1 - p.k))
        add_into(self.b[0], self.grad.at[:, p.k])
        self.send_half(1, self.axes()[0])

    def two(self):
        self.add_half(1, self.axes()[0])
        self.send_half(2, self.axes()[1])

    def part(self, z):
        ref = self.b[2]
        if self.kind == "rows":
            return ref.at[z]
        width = self.b[3].shape[-1]
        return ref.at[:, pl.ds(aligned(z * width, 128), width)]

    def three(self):
        p = self.p
        self.add_half(2, self.axes()[1])
        for i in range(1, p.n_row):
            target = (p.z + i) % p.n_row
            self.slots["z", i] = self.lanes.send(self.part(target), self.b[3].at[i - 1], p.dev(z=target))

    def four(self):
        p = self.p
        total = self.part(p.z)[...].astype(F32)
        for i in range(1, p.n_row):
            source = (p.z + p.n_row - i) % p.n_row
            self.lanes.arrived(self.b[3].at[i - 1], self.slots["z", i], p.dev(z=source))
            total = total + self.b[3][i - 1].astype(F32)
        return total


def add_into(target, term):
    shape = target.shape
    if len(shape) == 2:
        target[...] = (target[...].astype(F32) + term[...].astype(F32)).astype(BF)
        return

    def body(i, carry):
        target[i] = (target[i].astype(F32) + term[i].astype(F32)).astype(BF)
        return carry

    lax.fori_loop(0, shape[0], body, 0)


def reduce_kernel(
    dims, seq_ref, dxt_ref, outf_ref, gqkv_ref, gout_ref, gup_ref, gdown_ref,
    output_ref, tgrad_ref, rqkv_ref, rout_ref, rup_ref, rdown_ref,
    trecv, q0, q1, q2, q3, o0, o1, o2, o3, u0, u1, u2, u3, d0, d1, d2, d3,
    fq, fo, fu, tok_send, tok_recv, out_send, out_recv, w_send, w_recv, local_sem,
):
    n_dp, n_row, n_col = dims
    p = Place(n_dp, n_row, n_col)
    micro, slots = tgrad_ref.shape[0], tgrad_ref.shape[1]
    span = tgrad_ref.shape[3]
    p.barrier()
    lanes = Lanes(w_send, w_recv)
    partner = p.dev(k=1 - p.k)
    down = Reduce(p, lanes, gdown_ref, d0, d1, d2, d3, "lanes", "x")
    up = Reduce(p, lanes, gup_ref, u0, u1, u2, u3, "rows", "y")
    out = Reduce(p, lanes, gout_ref, o0, o1, o2, o3, "rows", "x")
    qkv = Reduce(p, lanes, gqkv_ref, q0, q1, q2, q3, "rows", "y")
    order = (down, up, out, qkv)
    for r in order:
        r.start()

    def tok_copy(i):
        target = (p.flat + i) % p.n
        return pltpu.make_async_remote_copy(
            src_ref=dxt_ref.at[target // n_col, :, pl.ds(aligned((target % n_col) * span, 128), span)],
            dst_ref=trecv.at[p.c * slots + p.g],
            send_sem=tok_send.at[i], recv_sem=tok_recv.at[i],
            device_id=p.of_flat(target), device_id_type=MESH,
        )

    def tok_start(i, carry):
        tok_copy(i).start()
        return carry

    lax.fori_loop(1, p.n, tok_start, 0)
    own_tok = pltpu.make_async_copy(
        dxt_ref.at[p.g, :, pl.ds(aligned(p.c * span, 128), span)], trecv.at[p.c * slots + p.g], local_sem.at[0]
    )
    own_tok.start()

    def out_copy(i):
        target = (p.c + i) % n_col
        return pltpu.make_async_remote_copy(
            src_ref=outf_ref.at[target], dst_ref=output_ref.at[p.c],
            send_sem=out_send.at[i], recv_sem=out_recv.at[i],
            device_id=(p.x, p.z, target), device_id_type=MESH,
        )

    for i in range(1, n_col):
        out_copy(i).start()
    own_out = pltpu.make_async_copy(outf_ref.at[p.c], output_ref.at[p.c], local_sem.at[1])
    own_out.start()
    for r in order:
        r.one()
    for r in order:
        r.two()
    for r in order:
        r.three()
    rdown_ref[...] = down.four()
    ends = []
    for r, temp, result in ((up, fu, rup_ref), (out, fo, rout_ref), (qkv, fq, rqkv_ref)):
        total = r.four()
        rows, width = total.shape[0], total.shape[1] // 2
        temp[...] = jnp.where(p.k == 0, total[:, width:], total[:, :width])
        where_ = result.at[pl.ds(aligned(p.k * rows, 16), rows), :]
        result[pl.ds(aligned(p.k * rows, 16), rows), :] = jnp.where(p.k == 0, total[:, :width], total[:, width:])
        slot = lanes.send(temp, where_, partner)
        ends.append((result, rows, slot))
    own_tok.wait()
    own_out.wait()

    def tok_wait(i, carry):
        source = (p.flat + p.n - i) % p.n
        landing = trecv.at[(source % n_col) * slots + source // n_col]
        pltpu.make_async_remote_copy(
            src_ref=landing, dst_ref=landing, send_sem=tok_send.at[i], recv_sem=tok_recv.at[i],
            device_id=p.of_flat(source), device_id_type=MESH,
        ).wait_recv()
        tok_copy(i).wait_send()
        return carry

    lax.fori_loop(1, p.n, tok_wait, 0)
    for m in range(micro):
        for s in range(slots):
            place = jnp.int32(0)
            for j in range(slots):
                place = jnp.where(seq_ref[m, j] == s, jnp.int32(j), place)
            tgrad_ref[m, s] = trecv[m * slots + place]
    for result, rows, slot in ends:
        lanes.arrived(result.at[pl.ds(aligned((1 - p.k) * rows, 16), rows), :], slot, partner)
    for i in range(1, n_col):
        source = (p.c + n_col - i) % n_col
        pltpu.make_async_remote_copy(
            src_ref=output_ref.at[source], dst_ref=output_ref.at[source],
            send_sem=out_send.at[i], recv_sem=out_recv.at[i],
            device_id=(p.x, p.z, source), device_id_type=MESH,
        ).wait_recv()
        out_copy(i).wait_send()
    lanes.finish()


def reduce_all(dims, seq_order, dxt, outf, g_qkv, g_out, g_up, g_down_t):
    n_dp, n_row, n_col = dims
    groups = n_dp * n_row
    micro, slots = seq_order.shape
    feats, span = dxt.shape[1], dxt.shape[2] // n_col
    shape = jax.ShapeDtypeStruct
    buffers = []
    for g in (g_qkv, g_out, g_up):
        r, _, h, c = g.shape
        buffers += [
            pltpu.VMEM((r, h, c), BF),
        ]
        if g is g_out:
            buffers += [pltpu.VMEM((r // 2, h, c), BF)]
        else:
            buffers += [pltpu.VMEM((r, h, c // 2), BF)]
        buffers += [pltpu.VMEM((r // 2, h, c // 2), BF), pltpu.VMEM((n_row - 1, h, c // 2), BF)]
    _, _, h, c = g_down_t.shape
    buffers += [
        pltpu.VMEM((2, h, c), BF), pltpu.VMEM((2, h, c // 2), BF), pltpu.VMEM((h, c // 2), BF),
        pltpu.VMEM((n_row - 1, h, c // groups), BF),
    ]
    outs = (
        shape((n_col,) + outf.shape[1:], BF),
        shape((micro, slots, feats, span), BF),
        shape((g_qkv.shape[2] * 2, g_qkv.shape[3] // n_col), F32),
        shape((g_out.shape[2] * 2, g_out.shape[3] // n_col), F32),
        shape((g_up.shape[2] * 2, g_up.shape[3] // n_col), F32),
        shape((h, c // groups), F32),
    )
    temps = [pltpu.VMEM((g.shape[2], g.shape[3] // n_col), F32) for g in (g_qkv, g_out, g_up)]
    dma = pltpu.SemaphoreType.DMA
    return pl.pallas_call(
        functools.partial(reduce_kernel, dims),
        out_shape=outs,
        in_specs=[SM, VM, ANY, VM, VM, VM, VM],
        out_specs=[ANY, VM, VM, VM, VM, VM],
        scratch_shapes=[pltpu.VMEM((micro * slots, feats, span), BF)] + buffers + temps + [
            dma((n_dp * n_row * n_col,)), dma((n_dp * n_row * n_col,)),
            dma((n_col,)), dma((n_col,)),
            dma((40,)), dma((40,)), dma((8,)),
        ],
        compiler_params=pltpu.CompilerParams(
            collective_id=1, has_side_effects=True, vmem_limit_bytes=56 * 2**20
        ),
        name="reduce_all",
    )(seq_order, dxt, outf, g_qkv, g_out, g_up, g_down_t)


def layer_norm(values, factor, offset):
    average = jnp.mean(values, axis=-1, keepdims=True)
    centered = values - average
    variance = jnp.mean(centered * centered, axis=-1, keepdims=True)
    return centered * lax.rsqrt(variance + EPSILON) * factor + offset


def gelu_act(values):
    return 0.5 * values * (1.0 + lax.erf(values * ROOT_HALF))


def product(left, right):
    return jnp.dot(left, right, preferred_element_type=F32)


def product_tn(left, right):
    return lax.dot_general(left, right, (((0,), (0,)), ((), ())), preferred_element_type=F32)


def product_nt(left, right):
    return lax.dot_general(left, right, (((1,), (1,)), ((), ())), preferred_element_type=F32)


def attention(qkv, length):
    rows, width = qkv.shape[0], qkv.shape[1] // 3
    heads = width // HEAD
    q, k, v = (qkv[:, i * width:(i + 1) * width].reshape(rows, heads, HEAD) for i in range(3))
    scores = jnp.einsum("qhe,khe->hqk", q, k, preferred_element_type=F32) * 0.125
    valid = jnp.arange(rows, dtype=jnp.int32) < length
    scores = jnp.where(valid[None, None, :], scores, NEGATIVE)
    top = jnp.max(scores, axis=-1, keepdims=True)
    exps = jnp.exp(scores - top)
    total = jnp.sum(exps, axis=-1, keepdims=True)
    probs = (exps / total).astype(BF)
    context = jnp.einsum("hqk,khe->qhe", probs, v, preferred_element_type=F32)
    return context.astype(BF).reshape(rows, width), top + jnp.log(total)


def attention_back(qkv, length, stats, d_context):
    rows, width = qkv.shape[0], qkv.shape[1] // 3
    heads = width // HEAD
    q, k, v = (qkv[:, i * width:(i + 1) * width].reshape(rows, heads, HEAD) for i in range(3))
    dc = d_context.reshape(rows, heads, HEAD)
    scores = jnp.einsum("qhe,khe->hqk", q, k, preferred_element_type=F32) * 0.125
    valid = jnp.arange(rows, dtype=jnp.int32) < length
    scores = jnp.where(valid[None, None, :], scores, NEGATIVE)
    soft = jnp.exp(scores - stats)
    d_probs = jnp.einsum("qhe,khe->hqk", dc, v, preferred_element_type=F32)
    delta = jnp.sum(soft * d_probs, axis=-1, keepdims=True)
    d_scores = (soft * (d_probs - delta)).astype(BF)
    dq = jnp.einsum("hqk,khe->qhe", d_scores, k, preferred_element_type=F32) * 0.125
    dk = jnp.einsum("hqk,qhe->khe", d_scores, q, preferred_element_type=F32) * 0.125
    dv = jnp.einsum("hqk,qhe->khe", soft.astype(BF), dc, preferred_element_type=F32)
    return jnp.concatenate([a.astype(BF).reshape(rows, width) for a in (dq, dk, dv)], axis=-1)


def middle(x, context, cot, w_out, w_up, w_down_t, gain_one, shift_one, gain_two, shift_two):
    mixed = x.astype(F32) + product(context, w_out)
    hidden = layer_norm(mixed, gain_one, shift_one)
    hidden_low = hidden.astype(BF)
    pre_act = product(hidden_low, w_up)
    act_low = gelu_act(pre_act).astype(BF)
    summed = hidden + product_nt(act_low, w_down_t)
    output = layer_norm(summed, gain_two, shift_two).astype(BF)
    _, norm_two_back = jax.vjp(layer_norm, summed, gain_two, shift_two)
    g_summed, g_gain_two, g_shift_two = norm_two_back(cot.astype(F32))
    d_down = g_summed.astype(BF)
    g_down_t = product_tn(d_down, act_low).astype(BF)
    d_act = product(d_down, w_down_t)
    _, gelu_back = jax.vjp(gelu_act, pre_act)
    d_pre = gelu_back(d_act)[0].astype(BF)
    g_up = product_tn(hidden_low, d_pre).astype(BF)
    g_hidden = g_summed + product_nt(d_pre, w_up)
    _, norm_one_back = jax.vjp(layer_norm, mixed, gain_one, shift_one)
    g_mixed, g_gain_one, g_shift_one = norm_one_back(g_hidden)
    d_attn = g_mixed.astype(BF)
    g_out = product_tn(context, d_attn).astype(BF)
    d_context = product_nt(d_attn, w_out).astype(BF)
    return output, g_mixed, d_context, g_down_t, g_up, g_out, (g_gain_one, g_shift_one, g_gain_two, g_shift_two)


def take_blocks(blocks, places):
    def body(place_ref, in_ref, out_ref):
        def step(i, carry):
            out_ref[i] = in_ref[place_ref[i]]
            return carry

        lax.fori_loop(0, blocks.shape[0], step, 0)

    return pl.pallas_call(
        body, out_shape=jax.ShapeDtypeStruct(blocks.shape, blocks.dtype), in_specs=[SM, VM], out_specs=VM,
        compiler_params=pltpu.CompilerParams(vmem_limit_bytes=48 * 2**20), name="take_blocks",
    )(places, blocks)


def own_length(lengths, seq_order):
    n_row = lax.axis_size("row")
    slot = lax.axis_index("dp") * n_row + lax.axis_index("row")
    micro = lax.axis_index("col")
    index = jnp.arange(seq_order.shape[1], dtype=jnp.int32)
    order = jnp.sum(jnp.where(jnp.arange(seq_order.shape[0])[:, None] == micro, seq_order, 0), axis=0)
    source = jnp.sum(jnp.where(index == slot, order, 0))
    mine = jnp.sum(jnp.where(jnp.arange(seq_order.shape[0])[:, None] == micro, lengths, 0), axis=0)
    return jnp.sum(jnp.where(index == source, mine, 0))


def local(
    tokens, cotangent, lengths, seq_order, w_qkv, w_out, w_up, w_down, gain_one, shift_one, gain_two, shift_two,
):
    dims = tuple(lax.axis_size(a) for a in ("dp", "row", "col"))
    n_dp, n_row, n_col = dims
    groups = n_dp * n_row
    micro, slots, span, feats = tokens.shape
    width = cotangent.shape[3]
    rows = span * n_col
    direct = n_dp == 2 and n_col == 4 and feats % 32 == 0 and w_qkv.shape[0] % 32 == 0
    tok_t = jnp.swapaxes(tokens, 2, 3)
    w_down_t = w_down.T
    norms = jnp.stack([gain_one, shift_one, gain_two, shift_two])
    length = own_length(lengths, seq_order)
    everyone = ("dp", "row", "col")
    if direct:
        packed = jnp.pad(norms, ((0, 12), (0, 128 - norms.shape[1])))
        xt, cot, f_qkv, f_out, f_up, f_down_t, f_norms = gather_all(
            dims, seq_order, tok_t, cotangent[:, 0], w_qkv, w_out, w_up, w_down_t, packed
        )
        xt = xt.reshape(width, rows)
        cot = cot.reshape(rows, width)
        f_qkv, f_out, f_up, f_down_t = (
            f_qkv.reshape(width, -1), f_out.reshape(width, -1), f_up.reshape(width, -1), f_down_t.reshape(width, -1)
        )
        f_norms = f_norms.reshape(groups, 2, 16, 2, 128)[:, :, :4, :, : norms.shape[1]]
        f_norms = f_norms.transpose(2, 0, 3, 1, 4).reshape(4, width)
    else:
        offset = jnp.arange(micro, dtype=jnp.int32)[:, None] * slots
        sent = take_blocks(tok_t.reshape(micro * slots, feats, span), (seq_order + offset).reshape(-1))
        sent = jnp.swapaxes(sent.reshape(micro, slots, feats, span), 0, 1).reshape(micro * slots, feats, span)
        got = lax.all_to_all(sent, everyone, split_axis=0, concat_axis=0, tiled=True)
        xt = got.reshape(groups, n_col, feats, span).transpose(0, 2, 1, 3).reshape(width, rows)
        cot = lax.all_to_all(cotangent[:, 0], "col", split_axis=0, concat_axis=0, tiled=True).reshape(rows, width)

        def whole(w, row_axes, col_axes):
            w = lax.all_gather(w, col_axes, axis=1, tiled=True)
            return lax.all_gather(w, row_axes, axis=0, tiled=True)

        f_qkv, f_out, f_up = (whole(w, ("dp", "row"), "col") for w in (w_qkv, w_out, w_up))
        f_down_t = whole(w_down_t, "col", ("dp", "row"))
        f_norms = lax.all_gather(norms, everyone, axis=1, tiled=True)
    gains = [f_norms[i].astype(F32) for i in range(4)]
    x = xt.T
    qkv = product(x, f_qkv).astype(BF)
    context, stats = attention(qkv, length)
    output, g_mixed, d_context, g_down_t, g_up, g_out, norm_grads = middle(
        x, context, cot, f_out, f_up, f_down_t, *gains
    )
    d_qkv = attention_back(qkv, length, stats, d_context)
    g_qkv = product(xt, d_qkv).astype(BF)
    dxt = (g_mixed + product_nt(d_qkv, f_qkv)).astype(BF).T
    n_sum = lax.psum_scatter(
        jnp.stack(norm_grads), everyone, scatter_dimension=1, tiled=True
    )
    if direct:
        output, tgrad, r_qkv, r_out, r_up, r_down_t = reduce_all(
            dims, seq_order, dxt.reshape(groups, feats, rows), output.reshape(n_col, span, width),
            g_qkv.reshape(groups, 2, -1, g_qkv.shape[1]), g_out.reshape(groups, 2, -1, g_out.shape[1]),
            g_up.reshape(groups, 2, -1, g_up.shape[1]), g_down_t.reshape(2, 2, -1, g_down_t.shape[1]),
        )
    else:
        output = lax.all_to_all(output.reshape(n_col, span, width), "col", split_axis=0, concat_axis=0, tiled=True)
        sent = dxt.reshape(groups, feats, n_col, span).transpose(0, 2, 1, 3).reshape(micro * slots, feats, span)
        got = lax.all_to_all(sent, everyone, split_axis=0, concat_axis=0, tiled=True)
        got = jnp.swapaxes(got.reshape(slots, micro, feats, span), 0, 1).reshape(micro * slots, feats, span)
        index = jnp.arange(slots, dtype=jnp.int32)
        inverse = jnp.sum(jnp.where(seq_order[:, :, None] == index, index[None, :, None], 0), axis=1)
        offset = jnp.arange(micro, dtype=jnp.int32)[:, None] * slots
        tgrad = take_blocks(got, (inverse + offset).reshape(-1)).reshape(micro, slots, feats, span)

        def parts(g, row_axes, col_axes):
            g = lax.psum_scatter(g, col_axes, scatter_dimension=1, tiled=True)
            return lax.psum_scatter(g, row_axes, scatter_dimension=0, tiled=True).astype(F32)

        r_qkv, r_out, r_up = (parts(g, ("dp", "row"), "col") for g in (g_qkv, g_out, g_up))
        r_down_t = parts(g_down_t, "col", ("dp", "row"))
    return (
        output[:, None], jnp.swapaxes(tgrad, 2, 3), r_qkv, r_out, r_up, r_down_t.T,
        n_sum[0], n_sum[1], n_sum[2], n_sum[3],
    )


def solution(mesh):
    rows = ("dp", "row")
    every = ("dp", "row", "col")
    in_specs = (
        P(None, None, "col", rows), P(None, rows, "col", None), P(), P(),
        P(rows, "col"), P(rows, "col"), P(rows, "col"), P(rows, "col"),
        P(every), P(every), P(every), P(every),
    )
    out_specs = (
        P(None, rows, "col", None), P(None, None, "col", rows),
        P(rows, "col"), P(rows, "col"), P(rows, "col"), P(rows, "col"),
        P(every), P(every), P(every), P(every),
    )
    return jax.shard_map(local, mesh=mesh, in_specs=in_specs, out_specs=out_specs, check_vma=False)
```

```python
import functools

import jax
import jax.numpy as jnp
from jax import lax
from jax.experimental import pallas as pl
from jax.experimental.pallas import tpu as pltpu
from jax.sharding import PartitionSpec as P

HEAD = 64
NEGATIVE = -1000000000.0
EPSILON = 1e-12
ROOT_HALF = 0.7071067811865476
MESH = pl.DeviceIdType.MESH
BF = jnp.bfloat16
F32 = jnp.float32
ANY = pl.BlockSpec(memory_space=pl.ANY)
VM = pl.BlockSpec(memory_space=pltpu.VMEM)
SM = pl.BlockSpec(memory_space=pltpu.SMEM)
DMA = pltpu.SemaphoreType.DMA


def aligned(value, step):
    return pl.multiple_of(value, step)


def product(left, right):
    return jnp.dot(left, right, preferred_element_type=F32)


def product_tn(left, right):
    return lax.dot_general(left, right, (((0,), (0,)), ((), ())), preferred_element_type=F32)


def product_nt(left, right):
    return lax.dot_general(left, right, (((1,), (1,)), ((), ())), preferred_element_type=F32)


class Place:
    def __init__(self, n_dp, n_row, n_col):
        self.n_dp, self.n_row, self.n_col = n_dp, n_row, n_col
        self.n = n_dp * n_row * n_col
        self.x = lax.axis_index("dp")
        self.z = lax.axis_index("row")
        self.c = lax.axis_index("col")
        self.y, self.k = self.c // 2, self.c % 2
        self.g = self.x * n_row + self.z
        self.flat = self.g * n_col + self.c

    def of_flat(self, flat):
        group = flat // self.n_col
        return (group // self.n_row, group % self.n_row, flat % self.n_col)

    def dev(self, x=None, z=None, y=None, k=None):
        x = self.x if x is None else x
        z = self.z if z is None else z
        y = self.y if y is None else y
        k = self.k if k is None else k
        return (x, z, y * 2 + k)

    def greet(self):
        sem = pltpu.get_barrier_semaphore()

        def one(i, carry):
            pl.semaphore_signal(
                sem, inc=1, device_id=self.of_flat((self.flat + i) % self.n), device_id_type=MESH
            )
            return carry

        lax.fori_loop(1, self.n, one, 0)

    def met(self):
        pl.semaphore_wait(pltpu.get_barrier_semaphore(), self.n - 1)


class Lanes:
    def __init__(self, send_sems, recv_sems):
        self.send_sems, self.recv_sems, self.sent = send_sems, recv_sems, []
        self.used = [0, 0]

    def take(self, which, count):
        first = self.used[which]
        self.used[which] += count
        return first

    def copy(self, src, dst, device, s, r):
        return pltpu.make_async_remote_copy(
            src_ref=src, dst_ref=dst, send_sem=self.send_sems.at[s],
            recv_sem=self.recv_sems.at[r], device_id=device, device_id_type=MESH,
        )

    def send(self, make, held=None):
        self.copy(*make()).start()
        self.sent.append((make, held))

    def arrived(self, landing, device, r):
        self.copy(landing, landing, device, 0, r).wait_recv()

    def finish(self):
        for make, held in self.sent:
            if held is None:
                self.copy(*make()).wait_send()
            else:
                pl.when(held())(lambda make=make: self.copy(*make()).wait_send())
        self.sent = []


class Gather:
    def __init__(self, place, lanes, region, first):
        self.p, self.lanes, self.region, self.first = p, lanes, region, first = place, lanes, region, first
        self.to_x, self.to_y, self.to_core = p.dev(x=1 - p.x), p.dev(y=1 - p.y), p.dev(k=1 - p.k)
        self.one, self.two = (self.to_x, self.to_y) if first == "x" else (self.to_y, self.to_x)
        n = p.n_row
        self.s = {name: lanes.take(0, n) for name in ("up", "down", 1, 2, 3, "core")}
        self.r = {name: lanes.take(1, n) for name in ("z", 1, 2, 3, "core")}

    def side(self, hop):
        p = self.p
        x_side = hop in ((1, 3) if self.first == "x" else (2, 3))
        y_side = hop in ((2, 3) if self.first == "x" else (1, 3))
        return (1 - p.x if x_side else p.x), (1 - p.y if y_side else p.y)

    def at(self, hop, z, k):
        x, y = self.side(hop)
        return self.region(x, z, 1, y, k)

    def line(self, hop, k):
        x, y = self.side(hop)
        return self.region(x, 0, self.p.n_row, y, k)

    def start(self, own):
        p = self.p

        def to(hop, device):
            return lambda: (own, self.at(0, p.z, p.k), device, self.s[hop] + p.z, self.r[hop] + p.z)

        self.lanes.send(to(1, self.one))
        self.lanes.send(to(2, self.two))
        self.own = own

    def z_start(self):
        p, own = self.p, self.own
        for name, step in (("up", 1), ("down", -1)):
            def held(step=step):
                return p.z + 1 < p.n_row if step == 1 else p.z >= 1

            def make(name=name, step=step):
                return (own, self.at(0, p.z, p.k), p.dev(z=p.z + step), self.s[name] + p.z, self.r["z"] + p.z)

            pl.when(held())(lambda make=make, held=held: self.lanes.send(make, held))

    def z_step(self, distance):
        p = self.p
        for name, step in (("up", 1), ("down", -1)):
            source = (lambda step=step: p.z - step * distance)

            def here(step=step):
                return p.z >= distance if step == 1 else p.z + distance < p.n_row

            def further(step=step):
                if step == 1:
                    return (p.z >= distance) & (p.z + 1 < p.n_row)
                return (p.z + distance < p.n_row) & (p.z >= 1)

            def arrive(name=name, step=step, source=source):
                ref = self.at(0, source(), p.k)
                self.lanes.arrived(ref, p.dev(z=p.z - step), self.r["z"] + source())

            def onward(name=name, step=step, source=source):
                ref = self.at(0, source(), p.k)
                return (ref, ref, p.dev(z=p.z + step), self.s[name] + source(), self.r["z"] + source())

            def over(hop, device, source=source):
                def make():
                    ref = self.at(0, source(), p.k)
                    return (ref, ref, device, self.s[hop] + source(), self.r[hop] + source())
                return make

            def body():
                arrive()
                if distance < p.n_row - 1:
                    pl.when(further())(lambda: self.lanes.send(onward, further))
                self.lanes.send(over(1, self.one), here)
                self.lanes.send(over(2, self.two), here)

            pl.when(here())(body)

    def z_steps(self):
        for distance in range(1, self.p.n_row):
            self.z_step(distance)
        self.local.wait()
        self.to_other_core(0)

    def to_other_core(self, hop):
        def make():
            line = self.line(hop, self.p.k)
            return (line, line, self.to_core, self.s["core"] + hop, self.r["core"] + hop)
        self.lanes.send(make)

    def first_steps(self):
        p = self.p
        n = p.n_row
        order = (lambda: p.z, lambda: p.z + 1 - 2 * (p.z % 2), lambda: n - 1 - p.z, lambda: (p.z + n // 2) % n)
        for source in order:
            self.lanes.arrived(self.at(1, source(), p.k), self.one, self.r[1] + source())

            def make(source=source):
                ref = self.at(1, source(), p.k)
                return (ref, ref, self.two, self.s[3] + source(), self.r[3] + source())

            self.lanes.send(make)
        self.to_other_core(1)

    def second_steps(self):
        p = self.p
        for hop in (2, 3):
            for i in range(p.n_row):
                self.lanes.arrived(self.at(hop, i, p.k), self.two, self.r[hop] + i)
            self.to_other_core(hop)

    def end(self):
        for hop in range(4):
            self.lanes.arrived(self.line(hop, 1 - self.p.k), self.to_core, self.r["core"] + hop)


def rows_region(ref, n_row, low=0, high=None):
    width = ref.shape[3] // 2
    high = width if high is None else high

    def region(x, z, nz, y, k):
        columns = pl.ds(aligned(y * width + low, 128), high - low)
        if nz == 1:
            return ref.at[x * n_row + z, k, :, columns]
        return ref.at[pl.ds(x * n_row + z, nz), k, :, columns]

    return region


def lanes_region(ref, n_dp, n_row, low=0, high=None):
    width = ref.shape[3] // (n_dp * n_row)
    high = ref.shape[2] if high is None else high

    def region(x, z, nz, y, k):
        return ref.at[y, k, pl.ds(low, high - low), pl.ds(aligned((x * n_row + z) * width, 128), nz * width)]

    return region


CHUNK = 512


def forward_kernel(
    dims, seq_ref, len_ref, tok_ref, cot_ref, qkv_ref, out_ref, up_ref, down_ref, norm_ref,
    x_out, xt_out, cot_out, wqkv_out, wout_out, wup_out, wdown_out, norm_out, qkv_out, ctx_out, lse_out,
    tsend, half_qkv, half_out, half_up, pair_qkv, pair_out, pair_up,
    xt_v, x_v, w_v, qkv_v, ctx_v, lse_v,
    tok_send, tok_recv, norm_send, norm_recv, cot_send, cot_recv, w_send, w_recv, half_send, half_recv, local_sem,
):
    n_dp, n_row, n_col = dims
    p = Place(n_dp, n_row, n_col)
    micro, slots, _, span = tok_ref.shape
    rows, width = x_v.shape
    p.greet()
    for m in range(micro):
        for j in range(slots):
            tsend[m * slots + j] = tok_ref[m, seq_ref[m, j]]
    p.met()
    halves = Lanes(half_send, half_recv)
    lanes = Lanes(w_send, w_recv)
    partner = p.dev(k=1 - p.k)
    for i, (block, landing) in enumerate(((qkv_ref, half_qkv), (out_ref, half_out), (up_ref, half_up))):
        def make(i=i, block=block, landing=landing):
            count = landing.shape[0]
            return (block.at[pl.ds(aligned((1 - p.k) * count, 16), count), :], landing, partner, i, i)
        halves.send(make)

    def join(i, block, landing, pair):
        halves.arrived(landing, partner, i)
        count, across = landing.shape
        mine = block[pl.ds(aligned(p.k * count, 16), count), :]
        theirs = landing[...]
        pair[:, :across] = jnp.where(p.k == 0, mine, theirs)
        pair[:, across:] = jnp.where(p.k == 0, theirs, mine)

    local = []

    def keep(src, dst):
        made = pltpu.make_async_copy(src, dst, local_sem.at[len(local)])
        made.start()
        local.append(made)
        return made

    region_qkv = rows_region(w_v, n_row)
    join(0, qkv_ref, half_qkv, pair_qkv)
    own_w = keep(pair_qkv, region_qkv(p.x, p.z, 1, p.y, p.k))
    g_qkv = Gather(p, lanes, region_qkv, "x")
    g_qkv.local = own_w
    g_qkv.start(pair_qkv)
    g_qkv.z_start()

    def tok_copy(i):
        target = (p.flat + i) % p.n
        return pltpu.make_async_remote_copy(
            src_ref=tsend.at[(target % n_col) * slots + target // n_col],
            dst_ref=xt_v.at[p.g, :, pl.ds(aligned(p.c * span, 128), span)],
            send_sem=tok_send.at[i], recv_sem=tok_recv.at[i],
            device_id=p.of_flat(target), device_id_type=MESH,
        )

    def norm_copy(i):
        return pltpu.make_async_remote_copy(
            src_ref=norm_ref, dst_ref=norm_out.at[p.flat],
            send_sem=norm_send.at[i], recv_sem=norm_recv.at[i],
            device_id=p.of_flat((p.flat + i) % p.n), device_id_type=MESH,
        )

    def tok_start(i, carry):
        tok_copy(i).start()
        return carry

    def norm_start(i, carry):
        norm_copy(i).start()
        return carry

    lax.fori_loop(1, p.n, tok_start, 0)
    own_tok = keep(tsend.at[p.c * slots + p.g], xt_v.at[p.g, :, pl.ds(aligned(p.c * span, 128), span)])

    waves = []

    def wave(own, region, first):
        gather = Gather(p, lanes, region, first)
        gather.local = keep(own, region(p.x, p.z, 1, p.y, p.k))
        gather.start(own)
        waves.append(gather)

    join(1, out_ref, half_out, pair_out)
    wave(pair_out, rows_region(wout_out, n_row), "y")
    join(2, up_ref, half_up, pair_up)
    cut = pair_up.shape[1] // 2
    wave(pair_up.at[:, pl.ds(0, cut)], rows_region(wup_out, n_row, 0, cut), "y")
    wave(pair_up.at[:, pl.ds(cut, cut)], rows_region(wup_out, n_row, cut, 2 * cut), "y")
    cut = down_ref.shape[0] // 2
    wave(down_ref.at[pl.ds(0, cut), :], lanes_region(wdown_out, n_dp, n_row, 0, cut), "y")
    wave(down_ref.at[pl.ds(cut, cut), :], lanes_region(wdown_out, n_dp, n_row, cut, 2 * cut), "y")
    lax.fori_loop(1, p.n, norm_start, 0)
    own_norm = keep(norm_ref, norm_out.at[p.flat])

    def cot_copy(i):
        target = (p.c + i) % n_col
        return pltpu.make_async_remote_copy(
            src_ref=cot_ref.at[target], dst_ref=cot_out.at[p.c],
            send_sem=cot_send.at[i], recv_sem=cot_recv.at[i],
            device_id=(p.x, p.z, target), device_id_type=MESH,
        )

    own_cot = keep(cot_ref.at[p.c], cot_out.at[p.c])
    g_qkv.z_steps()
    waves[0].z_start()
    waves[1].z_start()
    g_qkv.first_steps()
    g_qkv.second_steps()
    own_tok.wait()

    def tok_wait(i, carry):
        source = (p.flat + p.n - i) % p.n
        landing = xt_v.at[source // n_col, :, pl.ds(aligned((source % n_col) * span, 128), span)]
        pltpu.make_async_remote_copy(
            src_ref=landing, dst_ref=landing, send_sem=tok_send.at[i], recv_sem=tok_recv.at[i],
            device_id=p.of_flat(source), device_id_type=MESH,
        ).wait_recv()
        return carry

    lax.fori_loop(1, p.n, tok_wait, 0)
    keep(xt_v, xt_out)

    def turn(i, carry):
        at = pl.ds(aligned(i * 256, 256), 256)
        x_v[at, :] = xt_v[:, :, at].reshape(width, 256).T
        return carry

    lax.fori_loop(0, rows // 256, turn, 0)
    keep(x_v, x_out)
    g_qkv.end()
    keep(w_v, wqkv_out)

    def project(i, carry):
        at = pl.ds(aligned(i * 256, 256), 256)
        qkv_v[:, at] = product(x_v[...], w_v[:, :, :, at].reshape(width, 256)).astype(BF)
        return carry

    lax.fori_loop(0, 3 * width // 256, project, 0)
    keep(qkv_v, qkv_out)
    out, up_a, up_b, down_a, down_b = waves

    def begin_cot():
        for i in range(1, n_col):
            cot_copy(i).start()

    events = {
        0: (out.z_steps, up_b.z_start),
        1: (up_a.z_steps, down_a.z_start, out.first_steps),
        2: (up_a.first_steps,),
        3: (up_b.z_steps, down_b.z_start, out.second_steps),
        4: (up_b.first_steps,),
        5: (down_a.z_steps, begin_cot),
        6: (down_a.first_steps, up_a.second_steps),
        7: (down_b.z_steps,),
        8: (down_b.first_steps,),
        9: (up_b.second_steps,),
    }
    length = len_ref[p.c, seq_ref[p.c, p.g]]
    bias = jnp.where(lax.broadcasted_iota(jnp.int32, (rows, 1), 0) < length, 0.0, NEGATIVE)
    chunks = rows // CHUNK

    def attend(step, carry):
        for when_, acts in events.items():
            def act(acts=acts):
                for a in acts:
                    a()
            pl.when(step == when_)(act)
        pair, at_row = step // chunks, step % chunks
        columns = [pl.ds(aligned(i * width + pair * 128, 128), 128) for i in range(3)]
        keys = qkv_v[:, columns[1]]
        values_t = qkv_v[:, columns[2]].T
        lane = lax.broadcasted_iota(jnp.int32, (rows, 128), 1)
        own_rows = pl.ds(aligned(at_row * CHUNK, CHUNK), CHUNK)
        queries = qkv_v[own_rows, columns[0]] * jnp.asarray(0.125, BF)
        for h in range(2):
            mine = jnp.where((lane < HEAD) == (h == 0), keys, jnp.zeros_like(keys))
            scores = product_nt(mine, queries) + bias
            top = jnp.max(scores, axis=0, keepdims=True)
            exps = jnp.exp(scores - top)
            total = jnp.sum(exps, axis=0, keepdims=True)
            context = product(values_t[h * HEAD:(h + 1) * HEAD], exps.astype(BF))
            head_rows = pl.ds(aligned(pair * 128 + h * HEAD, HEAD), HEAD)
            ctx_v[head_rows, own_rows] = (context * (1.0 / total)).astype(BF)
            lse_v[2 * pair + h, :, own_rows] = top + jnp.log(total)
        return carry

    lax.fori_loop(0, width // 128 * chunks, attend, 0)
    keep(ctx_v, ctx_out)
    keep(lse_v, lse_out)
    down_a.second_steps()
    down_b.second_steps()
    for gather in waves:
        gather.end()
    own_norm.wait()

    def small_wait(i, carry):
        source = (p.flat + p.n - i) % p.n
        pltpu.make_async_remote_copy(
            src_ref=norm_ref, dst_ref=norm_out.at[source], send_sem=norm_send.at[i], recv_sem=norm_recv.at[i],
            device_id=p.of_flat(source), device_id_type=MESH,
        ).wait_recv()
        norm_copy(i).wait_send()
        tok_copy(i).wait_send()
        return carry

    lax.fori_loop(1, p.n, small_wait, 0)
    for i in range(1, n_col):
        source = (p.c + n_col - i) % n_col
        pltpu.make_async_remote_copy(
            src_ref=cot_out.at[source], dst_ref=cot_out.at[source],
            send_sem=cot_send.at[i], recv_sem=cot_recv.at[i],
            device_id=(p.x, p.z, source), device_id_type=MESH,
        ).wait_recv()
        cot_copy(i).wait_send()
    waited = [own_tok, own_norm, own_w] + [gather.local for gather in waves]
    for made in local:
        if not any(made is w for w in waited):
            made.wait()
    halves.finish()
    lanes.finish()


def forward(dims, seq_order, lengths, tok_t, cot, w_qkv, w_out, w_up, w_down_t, norms):
    n_dp, n_row, n_col = dims
    groups, n = n_dp * n_row, n_dp * n_row * n_col
    micro, slots, feats, span = tok_t.shape
    rows, width = n_col * span, groups * feats
    heads = width // HEAD
    qr, qc = w_qkv.shape
    orow, oc = w_out.shape
    ur, uc = w_up.shape
    dr, dc = w_down_t.shape
    shape = jax.ShapeDtypeStruct
    outs = (
        shape((rows, width), BF),
        shape((groups, feats, rows), BF),
        shape((n_col,) + cot.shape[1:], BF),
        shape((groups, 2, qr // 2, qc * n_col), BF),
        shape((groups, 2, orow // 2, oc * n_col), BF),
        shape((groups, 2, ur // 2, uc * n_col), BF),
        shape((2, 2, dr, dc * groups), BF),
        shape((n,) + norms.shape, BF),
        shape((rows, 3 * width), BF),
        shape((width, rows), BF),
        shape((heads, 1, rows), F32),
    )
    return pl.pallas_call(
        functools.partial(forward_kernel, dims),
        out_shape=outs,
        in_specs=[SM, SM, VM, ANY, VM, VM, VM, VM, VM],
        out_specs=[ANY] * len(outs),
        scratch_shapes=[
            pltpu.VMEM((micro * slots, feats, span), BF),
            pltpu.VMEM((qr // 2, qc), BF),
            pltpu.VMEM((orow // 2, oc), BF),
            pltpu.VMEM((ur // 2, uc), BF),
            pltpu.VMEM((qr // 2, qc * 2), BF),
            pltpu.VMEM((orow // 2, oc * 2), BF),
            pltpu.VMEM((ur // 2, uc * 2), BF),
            pltpu.VMEM((groups, feats, rows), BF),
            pltpu.VMEM((rows, width), BF),
            pltpu.VMEM((groups, 2, qr // 2, qc * n_col), BF),
            pltpu.VMEM((rows, 3 * width), BF),
            pltpu.VMEM((width, rows), BF),
            pltpu.VMEM((heads, 1, rows), F32),
            DMA((n,)), DMA((n,)), DMA((n,)), DMA((n,)), DMA((n_col,)), DMA((n_col,)),
            DMA((6 * 6 * n_row,)), DMA((6 * 5 * n_row,)), DMA((3,)), DMA((3,)), DMA((24,)),
        ],
        compiler_params=pltpu.CompilerParams(
            collective_id=0, has_side_effects=True, vmem_limit_bytes=58 * 2**20
        ),
        name="forward_part",
    )(seq_order, lengths, tok_t, cot, w_qkv, w_out, w_up, w_down_t, norms)


BACK_CHUNK = 256


def add_into(target, term):
    shape = target.shape
    if len(shape) == 2:
        target[...] = (target[...].astype(F32) + term[...].astype(F32)).astype(BF)
        return

    def body(i, carry):
        target[i] = (target[i].astype(F32) + term[i].astype(F32)).astype(BF)
        return carry

    lax.fori_loop(0, shape[0], body, 0)


class Reduce:
    def __init__(self, place, lanes, theirs, mine, buffers, kind, first):
        self.p, self.lanes, self.theirs, self.mine, self.b = place, lanes, theirs, mine, buffers
        self.kind, self.axes = kind, ("x", "y") if first == "x" else ("y", "x")
        self.s = [lanes.take(0, 1) for _ in range(3)] + [lanes.take(0, place.n_row - 1)]
        self.r = [lanes.take(1, 1) for _ in range(3)] + [lanes.take(1, place.n_row - 1)]

    def start(self):
        p = self.p
        self.lanes.send(lambda: (self.theirs, self.b[0], p.dev(k=1 - p.k), self.s[0], self.r[0]))

    def half(self, ref, axis, side):
        if self.kind == "lanes" and axis == "y":
            return ref.at[side]
        if self.kind == "rows" and axis == "x":
            count = ref.shape[0] // 2
            return ref.at[pl.ds(side * count, count)]
        width = ref.shape[-1] // 2
        lead = (slice(None),) * (len(ref.shape) - 1)
        return ref.at[lead + (pl.ds(aligned(side * width, 128), width),)]

    def where(self, axis):
        p = self.p
        return (p.x, p.dev(x=1 - p.x)) if axis == "x" else (p.y, p.dev(y=1 - p.y))

    def send_half(self, stage):
        def make():
            side, peer = self.where(self.axes[stage - 1])
            return (self.half(self.b[stage - 1], self.axes[stage - 1], 1 - side), self.b[stage], peer, self.s[stage], self.r[stage])

        self.lanes.send(make)

    def add_half(self, stage):
        side, peer = self.where(self.axes[stage - 1])
        self.lanes.arrived(self.b[stage], peer, self.r[stage])
        add_into(self.b[stage], self.half(self.b[stage - 1], self.axes[stage - 1], side))

    def one(self):
        p = self.p
        self.lanes.arrived(self.b[0], p.dev(k=1 - p.k), self.r[0])
        add_into(self.b[0], self.mine)
        self.send_half(1)

    def two(self):
        self.add_half(1)
        self.send_half(2)

    def part(self, z):
        ref = self.b[2]
        if self.kind == "rows":
            return ref.at[z]
        width = self.b[3].shape[-1]
        return ref.at[:, pl.ds(aligned(z * width, 128), width)]

    def three(self):
        p = self.p
        self.add_half(2)
        for i in range(1, p.n_row):
            def make(i=i):
                target = (p.z + i) % p.n_row
                return (self.part(target), self.b[3].at[i - 1], p.dev(z=target), self.s[3] + i - 1, self.r[3] + i - 1)
            self.lanes.send(make)

    def four(self):
        p = self.p
        total = self.part(p.z)[...].astype(F32)
        for i in range(1, p.n_row):
            source = (p.z + p.n_row - i) % p.n_row
            self.lanes.arrived(self.b[3].at[i - 1], p.dev(z=source), self.r[3] + i - 1)
            total = total + self.b[3][i - 1].astype(F32)
        return total


def piece_buffers(kind, first, lead, rows, columns, n_row, groups):
    if kind == "lanes":
        one = (2, rows, columns // 2) if first == "x" else (rows, columns)
        return [(2, rows, columns), one, (rows, columns // 2), (n_row - 1, rows, columns // groups)]
    one = (lead // 2, rows, columns) if first == "x" else (lead, rows, columns // 2)
    return [(lead, rows, columns), one, (lead // 2, rows, columns // 2), (n_row - 1, rows, columns // 2)]


def backward_kernel(
    dims, plan, seq_ref, qkv_ref, ctx_ref, lse_ref, dctx_ref, xt_ref, w_ref, gm_ref, outf_ref, gout_ref, gup_ref, gdown_ref,
    ngrad_ref, output_ref, tgrad_ref, rqkv_ref, rout_ref, rup_ref, rdown_ref, nsum_ref, *scratch,
):
    n_dp, n_row, n_col = dims
    p = Place(n_dp, n_row, n_col)
    groups = n_dp * n_row
    (
        qkv_v, ctx_v, lse_v, dctx_v, xt_v, w_v, gm_v, m_out, m_up, m_down, grad_v, dqt_v, dk_v, dv_v, acc_k, acc_v, dxt_v, trecv,
        nrecv, fq, fo, fu, tok_send, tok_recv, norm_send, norm_recv, out_send, out_recv, w_send, w_recv, local_sem,
    ) = scratch[:31]
    pieces = scratch[31:]
    micro, slots, _, span = tgrad_ref.shape
    width, rows = ctx_ref.shape
    p.greet()
    local = []

    def keep(src, dst):
        made = pltpu.make_async_copy(src, dst, local_sem.at[len(local)])
        made.start()
        local.append(made)
        return made

    needed = [keep(qkv_ref, qkv_v), keep(dctx_ref, dctx_v), keep(ctx_ref, ctx_v), keep(lse_ref, lse_v)]
    mine_down = keep(gdown_ref.at[:, p.k], m_down)
    mine_up = keep(gup_ref.at[:, p.k], m_up)
    mine_out = keep(gout_ref.at[:, p.k], m_out)
    later = [keep(w_ref, w_v), keep(gm_ref, gm_v), keep(xt_ref, xt_v)]
    own_out = keep(outf_ref.at[p.c], output_ref.at[p.c])
    p.met()
    lanes = Lanes(w_send, w_recv)
    partner = p.dev(k=1 - p.k)
    waves = {"down": [], "up": [], "out": [], "qkv": []}
    whole = {"down": gdown_ref, "up": gup_ref, "out": gout_ref, "qkv": grad_v}
    carried = {"down": m_down, "up": m_up, "out": m_out}
    for index, (name, kind, first, low, count) in enumerate(plan):
        at = pl.ds(low, count)
        theirs = whole[name].at[:, 1 - p.k, at]
        mine = carried[name].at[:, at] if name != "qkv" else grad_v.at[:, p.k, at]
        waves[name].append(Reduce(p, lanes, theirs, mine, pieces[4 * index:4 * index + 4], kind, first))
    d, u, o, q = waves["down"], waves["up"], waves["out"], waves["qkv"]

    def norm_copy(i):
        target = (p.flat + i) % p.n
        return pltpu.make_async_remote_copy(
            src_ref=ngrad_ref.at[target], dst_ref=nrecv.at[p.flat],
            send_sem=norm_send.at[i], recv_sem=norm_recv.at[i],
            device_id=p.of_flat(target), device_id_type=MESH,
        )

    def norm_start(i, carry):
        norm_copy(i).start()
        return carry

    def out_copy(i):
        target = (p.c + i) % n_col
        return pltpu.make_async_remote_copy(
            src_ref=outf_ref.at[target], dst_ref=output_ref.at[p.c],
            send_sem=out_send.at[i], recv_sem=out_recv.at[i],
            device_id=(p.x, p.z, target), device_id_type=MESH,
        )

    def begin_out():
        for i in range(1, n_col):
            out_copy(i).start()

    d[0].start()
    u[0].start()
    lax.fori_loop(1, p.n, norm_start, 0)
    nrecv[p.flat] = ngrad_ref[p.flat]
    for made in needed:
        made.wait()
    mine_down.wait()
    mine_up.wait()
    mine_out.wait()

    def finish_rows(piece, temp, result, low):
        total = piece.four()
        count, across = total.shape[0], total.shape[1] // 2
        half_rows = result.shape[0] // 2
        temp[pl.ds(low, count), :] = jnp.where(p.k == 0, total[:, across:], total[:, :across])
        result[pl.ds(aligned(p.k * half_rows + low, 16), count), :] = jnp.where(p.k == 0, total[:, :across], total[:, across:])
        s, r = lanes.take(0, 1), lanes.take(1, 1)
        place = lambda k: result.at[pl.ds(aligned(k * half_rows + low, 16), count), :]
        lanes.send(lambda: (temp.at[pl.ds(low, count), :], place(p.k), partner, s, r))
        ends.append(lambda: lanes.arrived(place(1 - p.k), partner, r))

    ends = []

    def finish_down(piece, low):
        total = piece.four()
        rdown_ref[pl.ds(low, total.shape[0]), :] = total

    lows = {name: [low for other, _, _, low, _ in plan if other == name] for name in waves}
    down_end = [functools.partial(finish_down, piece, low) for piece, low in zip(d, lows["down"])]
    up_end = [functools.partial(finish_rows, piece, fu, rup_ref, low) for piece, low in zip(u, lows["up"])]
    out_end = [functools.partial(finish_rows, piece, fo, rout_ref, low) for piece, low in zip(o, lows["out"])]
    qkv_end = [functools.partial(finish_rows, piece, fq, rqkv_ref, low) for piece, low in zip(q, lows["qkv"])]
    events = {
        0: (d[1].start, u[1].start),
        1: (d[0].one, u[0].one),
        2: (d[2].start, u[2].start, o[0].start),
        4: (d[1].one,),
        5: (u[1].one,),
        6: (d[0].two,),
        7: (u[0].two,),
        9: (d[2].one,),
        10: (u[2].one,),
        11: (d[1].two,),
        12: (u[1].two, d[0].three),
        13: (u[0].three, o[0].one),
        15: (d[2].two,),
        16: (u[2].two, d[1].three),
        17: (u[1].three,),
        18: (o[0].two, down_end[0], begin_out),
        19: (up_end[0],),
        20: (d[2].three,),
        21: (u[2].three, o[0].three),
        22: (down_end[1],),
        23: (up_end[1],),
    }
    length_bias = jnp.where(lax.broadcasted_iota(jnp.int32, (rows, 1), 0) < seq_ref[1, p.c, seq_ref[0, p.c, p.g]], 0.0, NEGATIVE)
    chunks = rows // BACK_CHUNK

    def attend(step, carry):
        for when_, acts in events.items():
            def act(acts=acts):
                for a in acts:
                    a()
            pl.when(step == when_)(act)
        pair, at_row = step // chunks, step % chunks
        columns = [pl.ds(aligned(i * width + pair * 128, 128), 128) for i in range(3)]
        keys, values = qkv_v[:, columns[1]], qkv_v[:, columns[2]]
        keys_t = keys.T
        lane = lax.broadcasted_iota(jnp.int32, (rows, 128), 1)
        short = lax.broadcasted_iota(jnp.int32, (BACK_CHUNK, 128), 1)
        own_rows = pl.ds(aligned(at_row * BACK_CHUNK, BACK_CHUNK), BACK_CHUNK)
        queries = qkv_v[own_rows, columns[0]] * jnp.asarray(0.125, BF)
        back = dctx_v[own_rows, columns[0]]
        back_t = back.T.astype(F32)
        forth_t = ctx_v[pl.ds(aligned(pair * 128, 128), 128), own_rows].astype(F32)
        both = back_t * forth_t
        d_keys = d_values = None
        for h in range(2):
            def own(block, index):
                return jnp.where((index < HEAD) == (h == 0), block, jnp.zeros_like(block))
            delta = jnp.sum(both[h * HEAD:(h + 1) * HEAD], axis=0, keepdims=True)
            scores = product_nt(own(keys, lane), queries) + length_bias
            soft = jnp.exp(scores - lse_v[2 * pair + h, :, own_rows])
            d_probs = product_nt(own(values, lane), back)
            d_scores = (soft * (d_probs - delta)).astype(BF)
            head_rows = pl.ds(aligned(pair * 128 + h * HEAD, HEAD), HEAD)
            dqt_v[head_rows, own_rows] = (product(keys_t[h * HEAD:(h + 1) * HEAD], d_scores) * 0.125).astype(BF)
            to_values = product(soft.astype(BF), own(back, short))
            to_keys = product(d_scores, own(queries, short))
            d_values = to_values if d_values is None else d_values + to_values
            d_keys = to_keys if d_keys is None else d_keys + to_keys

        @pl.when(at_row == 0)
        def _():
            acc_k[...] = d_keys
            acc_v[...] = d_values

        @pl.when(at_row > 0)
        def _():
            acc_k[...] += d_keys
            acc_v[...] += d_values

        @pl.when(at_row == chunks - 1)
        def _():
            dk_v[:, columns[0]] = acc_k[...].astype(BF)
            dv_v[:, columns[0]] = acc_v[...].astype(BF)
        return carry

    lax.fori_loop(0, width // 128 * chunks, attend, 0)
    for made in later:
        made.wait()

    def tok_copy(target):
        return pltpu.make_async_remote_copy(
            src_ref=dxt_v.at[target // n_col, :, pl.ds(aligned((target % n_col) * span, 128), span)],
            dst_ref=trecv.at[p.c * slots + p.g],
            send_sem=tok_send.at[target], recv_sem=tok_recv.at[p.flat],
            device_id=p.of_flat(target), device_id_type=MESH,
        )

    half_groups = groups // 2
    half_width = width // 2
    for part in range(2):
        near = pl.ds(part * half_groups, half_groups)
        w_rows = lambda i: w_v[near, :, :, i * width:(i + 1) * width].reshape(half_width, width)
        total = gm_v[:, part * half_width:(part + 1) * half_width].T
        total = total + product(w_rows(0), dqt_v[...])
        total = total + product_nt(w_rows(1), dk_v[...])
        total = total + product_nt(w_rows(2), dv_v[...])
        dxt_v[near] = total.astype(BF).reshape(half_groups, width // groups, rows)

        def tok_start(i, carry, part=part):
            base = part * half_groups * n_col
            target = base + (p.flat + i) % (half_groups * n_col)

            @pl.when(target != p.flat)
            def _():
                tok_copy(target).start()
            return carry

        lax.fori_loop(0, half_groups * n_col, tok_start, 0)
    own_tok = keep(dxt_v.at[p.g, :, pl.ds(aligned(p.c * span, 128), span)], trecv.at[p.c * slots + p.g])

    def grad_q(i, carry):
        at = pl.ds(aligned(i * 256, 256), 256)
        grad_v[:, :, :, at] = product_nt(xt_v[...].reshape(width, rows), dqt_v[at, :]).astype(BF).reshape(groups, 2, -1, 256)
        return carry

    def grad_k(i, carry):
        at = pl.ds(aligned(i * 256, 256), 256)
        to = lambda j: pl.ds(aligned(j * width + i * 256, 256), 256)
        xt = xt_v[...].reshape(width, rows)
        grad_v[:, :, :, to(1)] = product(xt, dk_v[:, at]).astype(BF).reshape(groups, 2, -1, 256)
        grad_v[:, :, :, to(2)] = product(xt, dv_v[:, at]).astype(BF).reshape(groups, 2, -1, 256)
        return carry

    lax.fori_loop(0, width // 256, grad_q, 0)
    lax.fori_loop(0, width // 256, grad_k, 0)
    for piece in q:
        piece.start()
    for piece in q:
        piece.one()
    down_end[2]()
    up_end[2]()
    out_end[0]()
    for piece in q:
        piece.two()
    for piece in q:
        piece.three()

    def norm_wait(i, carry):
        source = (p.flat + p.n - i) % p.n
        pltpu.make_async_remote_copy(
            src_ref=nrecv.at[source], dst_ref=nrecv.at[source], send_sem=norm_send.at[i], recv_sem=norm_recv.at[i],
            device_id=p.of_flat(source), device_id_type=MESH,
        ).wait_recv()
        norm_copy(i).wait_send()
        return carry

    lax.fori_loop(1, p.n, norm_wait, 0)
    nsum_ref[...] = jnp.sum(nrecv[...], axis=0)
    for end in qkv_end:
        end()
    own_tok.wait()

    def tok_wait(i, carry):
        source = (p.flat + p.n - i) % p.n
        landing = trecv.at[(source % n_col) * slots + source // n_col]
        pltpu.make_async_remote_copy(
            src_ref=landing, dst_ref=landing, send_sem=tok_send.at[source], recv_sem=tok_recv.at[source],
            device_id=p.of_flat(source), device_id_type=MESH,
        ).wait_recv()
        tok_copy((p.flat + i) % p.n).wait_send()
        return carry

    lax.fori_loop(1, p.n, tok_wait, 0)
    for m in range(micro):
        for s in range(slots):
            place = jnp.int32(0)
            for j in range(slots):
                place = jnp.where(seq_ref[0, m, j] == s, jnp.int32(j), place)
            tgrad_ref[m, s] = trecv[m * slots + place]
    for end in ends:
        end()
    for i in range(1, n_col):
        source = (p.c + n_col - i) % n_col
        pltpu.make_async_remote_copy(
            src_ref=output_ref.at[source], dst_ref=output_ref.at[source],
            send_sem=out_send.at[i], recv_sem=out_recv.at[i],
            device_id=(p.x, p.z, source), device_id_type=MESH,
        ).wait_recv()
        out_copy(i).wait_send()
    own_out.wait()
    lanes.finish()


def backward(dims, seq_order, lengths, qkv, ctx_t, lse, d_context, xt, w_qkv, g_mixed, outf, g_out, g_up, g_down_t, n_grads):
    n_dp, n_row, n_col = dims
    groups, n = n_dp * n_row, n_dp * n_row * n_col
    micro, slots = seq_order.shape
    width, rows = ctx_t.shape
    feats, span = width // groups, rows // n_col
    shape = jax.ShapeDtypeStruct
    plan, buffers = [], []
    for name, grad, kind, first, count in (
        ("down", g_down_t, "lanes", "x", 3), ("up", g_up, "rows", "y", 3), ("out", g_out, "rows", "x", 1),
        ("qkv", w_qkv, "rows", "y", 3),
    ):
        lead, _, across, columns = grad.shape
        each = across // count
        for i in range(count):
            plan.append((name, kind, first, i * each, each))
            buffers += [pltpu.VMEM(b, BF) for b in piece_buffers(kind, first, lead, each, columns, n_row, groups)]
    outs = (
        shape((n_col,) + outf.shape[1:], BF),
        shape((micro, slots, feats, span), BF),
        shape((w_qkv.shape[2] * 2, w_qkv.shape[3] // n_col), F32),
        shape((g_out.shape[2] * 2, g_out.shape[3] // n_col), F32),
        shape((g_up.shape[2] * 2, g_up.shape[3] // n_col), F32),
        shape((g_down_t.shape[2], g_down_t.shape[3] // groups), F32),
        shape(n_grads.shape[1:], F32),
    )
    vm = lambda like, kind=BF: pltpu.VMEM(like.shape, kind)
    temps = [pltpu.VMEM((g.shape[2], g.shape[3] // n_col), F32) for g in (w_qkv, g_out, g_up)]
    carried = [pltpu.VMEM((g.shape[0],) + g.shape[2:], BF) for g in (g_out, g_up, g_down_t)]
    return pl.pallas_call(
        functools.partial(backward_kernel, dims, plan),
        out_shape=outs,
        in_specs=[SM, ANY, ANY, ANY, ANY, ANY, ANY, ANY, ANY, ANY, ANY, ANY, VM],
        out_specs=[ANY, VM, VM, VM, VM, VM, VM],
        scratch_shapes=[
            vm(qkv), vm(ctx_t), vm(lse, F32), vm(d_context), vm(xt), vm(w_qkv), vm(g_mixed, F32), *carried, vm(w_qkv),
            pltpu.VMEM((width, rows), BF), pltpu.VMEM((rows, width), BF), pltpu.VMEM((rows, width), BF),
            pltpu.VMEM((rows, 128), F32), pltpu.VMEM((rows, 128), F32),
            pltpu.VMEM((groups, feats, rows), BF), pltpu.VMEM((micro * slots, feats, span), BF),
            vm(n_grads, F32), *temps,
            DMA((n,)), DMA((n,)), DMA((n,)), DMA((n,)), DMA((n_col,)), DMA((n_col,)),
            DMA((80,)), DMA((80,)), DMA((16,)), *buffers,
        ],
        compiler_params=pltpu.CompilerParams(
            collective_id=1, has_side_effects=True, vmem_limit_bytes=62 * 2**20
        ),
        name="backward_part",
    )(jnp.stack([seq_order, lengths]), qkv, ctx_t, lse, d_context, xt, w_qkv, g_mixed, outf, g_out, g_up, g_down_t, n_grads)
def layer_norm(values, factor, offset):
    average = jnp.mean(values, axis=-1, keepdims=True)
    centered = values - average
    variance = jnp.mean(centered * centered, axis=-1, keepdims=True)
    return centered * lax.rsqrt(variance + EPSILON) * factor + offset


def gelu_act(values):
    return 0.5 * values * (1.0 + lax.erf(values * ROOT_HALF))


def attention(qkv, length):
    rows, width = qkv.shape[0], qkv.shape[1] // 3
    heads = width // HEAD
    q, k, v = (qkv[:, i * width:(i + 1) * width].reshape(rows, heads, HEAD) for i in range(3))
    scores = jnp.einsum("qhe,khe->hqk", q, k, preferred_element_type=F32) * 0.125
    valid = jnp.arange(rows, dtype=jnp.int32) < length
    scores = jnp.where(valid[None, None, :], scores, NEGATIVE)
    top = jnp.max(scores, axis=-1, keepdims=True)
    exps = jnp.exp(scores - top)
    total = jnp.sum(exps, axis=-1, keepdims=True)
    probs = (exps / total).astype(BF)
    context = jnp.einsum("hqk,khe->qhe", probs, v, preferred_element_type=F32)
    return context.astype(BF).reshape(rows, width), top + jnp.log(total)


def attention_back(qkv, length, stats, d_context):
    rows, width = qkv.shape[0], qkv.shape[1] // 3
    heads = width // HEAD
    q, k, v = (qkv[:, i * width:(i + 1) * width].reshape(rows, heads, HEAD) for i in range(3))
    dc = d_context.reshape(rows, heads, HEAD)
    scores = jnp.einsum("qhe,khe->hqk", q, k, preferred_element_type=F32) * 0.125
    valid = jnp.arange(rows, dtype=jnp.int32) < length
    scores = jnp.where(valid[None, None, :], scores, NEGATIVE)
    soft = jnp.exp(scores - stats)
    d_probs = jnp.einsum("qhe,khe->hqk", dc, v, preferred_element_type=F32)
    delta = jnp.sum(soft * d_probs, axis=-1, keepdims=True)
    d_scores = (soft * (d_probs - delta)).astype(BF)
    dq = jnp.einsum("hqk,khe->qhe", d_scores, k, preferred_element_type=F32) * 0.125
    dk = jnp.einsum("hqk,qhe->khe", d_scores, q, preferred_element_type=F32) * 0.125
    dv = jnp.einsum("hqk,qhe->khe", soft.astype(BF), dc, preferred_element_type=F32)
    return jnp.concatenate([a.astype(BF).reshape(rows, width) for a in (dq, dk, dv)], axis=-1)


def middle(x, context, context_t, cot, w_out, w_up, w_down_t, gain_one, shift_one, gain_two, shift_two):
    mixed = x.astype(F32) + product(context, w_out)
    hidden = layer_norm(mixed, gain_one, shift_one)
    hidden_low = hidden.astype(BF)
    pre_act = product(hidden_low, w_up)
    act_low = gelu_act(pre_act).astype(BF)
    summed = hidden + product_nt(act_low, w_down_t)
    output = layer_norm(summed, gain_two, shift_two).astype(BF)
    _, norm_two_back = jax.vjp(layer_norm, summed, gain_two, shift_two)
    g_summed, g_gain_two, g_shift_two = norm_two_back(cot.astype(F32))
    d_down = g_summed.astype(BF)
    g_down_t = product_tn(d_down, act_low).astype(BF)
    d_act = product(d_down, w_down_t)
    _, gelu_back = jax.vjp(gelu_act, pre_act)
    d_pre = gelu_back(d_act)[0].astype(BF)
    g_up = product_tn(hidden_low, d_pre).astype(BF)
    g_hidden = g_summed + product_nt(d_pre, w_up)
    _, norm_one_back = jax.vjp(layer_norm, mixed, gain_one, shift_one)
    g_mixed, g_gain_one, g_shift_one = norm_one_back(g_hidden)
    d_attn = g_mixed.astype(BF)
    g_out = product(context_t, d_attn).astype(BF)
    d_context = product_nt(d_attn, w_out).astype(BF)
    return output, g_mixed, d_context, g_down_t, g_up, g_out, (g_gain_one, g_shift_one, g_gain_two, g_shift_two)


def take_blocks(blocks, places):
    def body(place_ref, in_ref, out_ref):
        def step(i, carry):
            out_ref[i] = in_ref[place_ref[i]]
            return carry

        lax.fori_loop(0, blocks.shape[0], step, 0)

    return pl.pallas_call(
        body, out_shape=jax.ShapeDtypeStruct(blocks.shape, blocks.dtype), in_specs=[SM, VM], out_specs=VM,
        compiler_params=pltpu.CompilerParams(vmem_limit_bytes=48 * 2**20), name="take_blocks",
    )(places, blocks)


def own_length(lengths, seq_order):
    n_row = lax.axis_size("row")
    slot = lax.axis_index("dp") * n_row + lax.axis_index("row")
    micro = lax.axis_index("col")
    index = jnp.arange(seq_order.shape[1], dtype=jnp.int32)
    order = jnp.sum(jnp.where(jnp.arange(seq_order.shape[0])[:, None] == micro, seq_order, 0), axis=0)
    source = jnp.sum(jnp.where(index == slot, order, 0))
    mine = jnp.sum(jnp.where(jnp.arange(seq_order.shape[0])[:, None] == micro, lengths, 0), axis=0)
    return jnp.sum(jnp.where(index == source, mine, 0))


def local(
    tokens, cotangent, lengths, seq_order, w_qkv, w_out, w_up, w_down, gain_one, shift_one, gain_two, shift_two,
):
    dims = tuple(lax.axis_size(a) for a in ("dp", "row", "col"))
    n_dp, n_row, n_col = dims
    groups = n_dp * n_row
    micro, slots, span, feats = tokens.shape
    width = cotangent.shape[3]
    rows = span * n_col
    direct = n_dp == 2 and n_col == 4 and feats % 32 == 0 and w_qkv.shape[0] % 32 == 0
    tok_t = jnp.swapaxes(tokens, 2, 3)
    w_down_t = w_down.T
    norms = jnp.stack([gain_one, shift_one, gain_two, shift_two])
    length = own_length(lengths, seq_order)
    everyone = ("dp", "row", "col")
    if direct:
        packed = jnp.pad(norms, ((0, 12), (0, 128 - norms.shape[1])))
        x, xt, cot, w_joined, f_out, f_up, f_down_t, f_norms, qkv, context_t, lse = forward(
            dims, seq_order, lengths, tok_t, cotangent[:, 0], w_qkv, w_out, w_up, w_down_t, packed
        )
        cot = cot.reshape(rows, width)
        f_out, f_up, f_down_t = f_out.reshape(width, -1), f_up.reshape(width, -1), f_down_t.reshape(width, -1)
        f_norms = jnp.swapaxes(f_norms[:, :4, : norms.shape[1]], 0, 1).reshape(4, width)
    else:
        offset = jnp.arange(micro, dtype=jnp.int32)[:, None] * slots
        sent = take_blocks(tok_t.reshape(micro * slots, feats, span), (seq_order + offset).reshape(-1))
        sent = jnp.swapaxes(sent.reshape(micro, slots, feats, span), 0, 1).reshape(micro * slots, feats, span)
        got = lax.all_to_all(sent, everyone, split_axis=0, concat_axis=0, tiled=True)
        xt = got.reshape(groups, n_col, feats, span).transpose(0, 2, 1, 3).reshape(width, rows)
        cot = lax.all_to_all(cotangent[:, 0], "col", split_axis=0, concat_axis=0, tiled=True).reshape(rows, width)

        def whole(w, row_axes, col_axes):
            w = lax.all_gather(w, col_axes, axis=1, tiled=True)
            return lax.all_gather(w, row_axes, axis=0, tiled=True)

        f_qkv, f_out, f_up = (whole(w, ("dp", "row"), "col") for w in (w_qkv, w_out, w_up))
        f_down_t = whole(w_down_t, "col", ("dp", "row"))
        f_norms = lax.all_gather(norms, everyone, axis=1, tiled=True)
    gains = [f_norms[i].astype(F32) for i in range(4)]
    if not direct:
        x = xt.T
        qkv = product(x, f_qkv).astype(BF)
        context, stats = attention(qkv, length)
        context_t = context.T
    output, g_mixed, d_context, g_down_t, g_up, g_out, norm_grads = middle(
        x, context_t.T, context_t, cot, f_out, f_up, f_down_t, *gains
    )
    norm_grads = jnp.stack(norm_grads)
    if direct:
        each = norms.shape[1]
        n_grads = jnp.swapaxes(norm_grads.reshape(4, width // each, each), 0, 1)
        n_grads = jnp.pad(n_grads, ((0, 0), (0, 4), (0, 128 - each)))
        output, tgrad, r_qkv, r_out, r_up, r_down_t, n_sum = backward(
            dims, seq_order, lengths, qkv, context_t, lse, d_context, xt, w_joined, g_mixed,
            output.reshape(n_col, span, width), g_out.reshape(groups, 2, -1, g_out.shape[1]),
            g_up.reshape(groups, 2, -1, g_up.shape[1]), g_down_t.reshape(2, 2, -1, g_down_t.shape[1]), n_grads,
        )
        n_sum = n_sum[:4, :each]
    else:
        d_qkv = attention_back(qkv, length, stats, d_context)
        g_qkv = product(xt, d_qkv).astype(BF)
        dxt = (g_mixed + product_nt(d_qkv, f_qkv)).astype(BF).T
        n_sum = lax.psum_scatter(norm_grads, everyone, scatter_dimension=1, tiled=True)
        output = lax.all_to_all(output.reshape(n_col, span, width), "col", split_axis=0, concat_axis=0, tiled=True)
        sent = dxt.reshape(groups, feats, n_col, span).transpose(0, 2, 1, 3).reshape(micro * slots, feats, span)
        got = lax.all_to_all(sent, everyone, split_axis=0, concat_axis=0, tiled=True)
        got = jnp.swapaxes(got.reshape(slots, micro, feats, span), 0, 1).reshape(micro * slots, feats, span)
        index = jnp.arange(slots, dtype=jnp.int32)
        inverse = jnp.sum(jnp.where(seq_order[:, :, None] == index, index[None, :, None], 0), axis=1)
        offset = jnp.arange(micro, dtype=jnp.int32)[:, None] * slots
        tgrad = take_blocks(got, (inverse + offset).reshape(-1)).reshape(micro, slots, feats, span)

        def parts(g, row_axes, col_axes):
            g = lax.psum_scatter(g, col_axes, scatter_dimension=1, tiled=True)
            return lax.psum_scatter(g, row_axes, scatter_dimension=0, tiled=True).astype(F32)

        r_qkv, r_out, r_up = (parts(g, ("dp", "row"), "col") for g in (g_qkv, g_out, g_up))
        r_down_t = parts(g_down_t, "col", ("dp", "row"))
    return (
        output[:, None], jnp.swapaxes(tgrad, 2, 3), r_qkv, r_out, r_up, r_down_t.T,
        n_sum[0], n_sum[1], n_sum[2], n_sum[3],
    )


def solution(mesh):
    rows = ("dp", "row")
    every = ("dp", "row", "col")
    in_specs = (
        P(None, None, "col", rows), P(None, rows, "col", None), P(), P(),
        P(rows, "col"), P(rows, "col"), P(rows, "col"), P(rows, "col"),
        P(every), P(every), P(every), P(every),
    )
    out_specs = (
        P(None, rows, "col", None), P(None, None, "col", rows),
        P(rows, "col"), P(rows, "col"), P(rows, "col"), P(rows, "col"),
        P(every), P(every), P(every), P(every),
    )
    return jax.shard_map(local, mesh=mesh, in_specs=in_specs, out_specs=out_specs, check_vma=False)
```

```python
import functools

import jax
import jax.numpy as jnp
from jax import lax
from jax.experimental import pallas as pl
from jax.experimental.pallas import tpu as pltpu
from jax.sharding import PartitionSpec as P

HEAD = 64
NEGATIVE = -1000000000.0
EPSILON = 1e-12
ROOT_HALF = 0.7071067811865476
ROOT_TWO_PI = 0.3989422804014327
MESH = pl.DeviceIdType.MESH
BF = jnp.bfloat16
F32 = jnp.float32
ANY = pl.BlockSpec(memory_space=pl.ANY)
VM = pl.BlockSpec(memory_space=pltpu.VMEM)
SM = pl.BlockSpec(memory_space=pltpu.SMEM)
DMA = pltpu.SemaphoreType.DMA


def aligned(value, step):
    return pl.multiple_of(value, step)


def product(left, right):
    return jnp.dot(left, right, preferred_element_type=F32)


def product_tn(left, right):
    return lax.dot_general(left, right, (((0,), (0,)), ((), ())), preferred_element_type=F32)


def product_nt(left, right):
    return lax.dot_general(left, right, (((1,), (1,)), ((), ())), preferred_element_type=F32)


class Place:
    def __init__(self, n_dp, n_row, n_col):
        self.n_dp, self.n_row, self.n_col = n_dp, n_row, n_col
        self.n = n_dp * n_row * n_col
        self.x = lax.axis_index("dp")
        self.z = lax.axis_index("row")
        self.c = lax.axis_index("col")
        self.y, self.k = self.c // 2, self.c % 2
        self.g = self.x * n_row + self.z
        self.flat = self.g * n_col + self.c

    def of_flat(self, flat):
        group = flat // self.n_col
        return (group // self.n_row, group % self.n_row, flat % self.n_col)

    def dev(self, x=None, z=None, y=None, k=None):
        x = self.x if x is None else x
        z = self.z if z is None else z
        y = self.y if y is None else y
        k = self.k if k is None else k
        return (x, z, y * 2 + k)

    def greet(self):
        sem = pltpu.get_barrier_semaphore()

        def one(i, carry):
            pl.semaphore_signal(
                sem, inc=1, device_id=self.of_flat((self.flat + i) % self.n), device_id_type=MESH
            )
            return carry

        lax.fori_loop(1, self.n, one, 0)

    def met(self):
        pl.semaphore_wait(pltpu.get_barrier_semaphore(), self.n - 1)


class Lanes:
    def __init__(self, send_sems, recv_sems):
        self.send_sems, self.recv_sems, self.sent = send_sems, recv_sems, []
        self.used = [0, 0]

    def take(self, which, count):
        first = self.used[which]
        self.used[which] += count
        return first

    def copy(self, src, dst, device, s, r):
        return pltpu.make_async_remote_copy(
            src_ref=src, dst_ref=dst, send_sem=self.send_sems.at[s],
            recv_sem=self.recv_sems.at[r], device_id=device, device_id_type=MESH,
        )

    def send(self, make, held=None):
        self.copy(*make()).start()
        self.sent.append((make, held))

    def arrived(self, landing, device, r):
        self.copy(landing, landing, device, 0, r).wait_recv()

    def finish(self):
        for make, held in self.sent:
            if held is None:
                self.copy(*make()).wait_send()
            else:
                pl.when(held())(lambda make=make: self.copy(*make()).wait_send())
        self.sent = []


class Gather:
    def __init__(self, place, lanes, region, first):
        self.p, self.lanes, self.region, self.first = p, lanes, region, first = place, lanes, region, first
        self.to_x, self.to_y, self.to_core = p.dev(x=1 - p.x), p.dev(y=1 - p.y), p.dev(k=1 - p.k)
        self.one, self.two = (self.to_x, self.to_y) if first == "x" else (self.to_y, self.to_x)
        n = p.n_row
        self.s = {name: lanes.take(0, n) for name in ("up", "down", 1, 2, 3, "core")}
        self.r = {name: lanes.take(1, n) for name in ("z", 1, 2, 3, "core")}

    def side(self, hop):
        p = self.p
        x_side = hop in ((1, 3) if self.first == "x" else (2, 3))
        y_side = hop in ((2, 3) if self.first == "x" else (1, 3))
        return (1 - p.x if x_side else p.x), (1 - p.y if y_side else p.y)

    def at(self, hop, z, k):
        x, y = self.side(hop)
        return self.region(x, z, 1, y, k)

    def line(self, hop, k):
        x, y = self.side(hop)
        return self.region(x, 0, self.p.n_row, y, k)

    def start(self, own):
        p = self.p

        def to(hop, device):
            return lambda: (own, self.at(0, p.z, p.k), device, self.s[hop] + p.z, self.r[hop] + p.z)

        self.lanes.send(to(1, self.one))
        self.lanes.send(to(2, self.two))
        self.own = own

    def z_start(self):
        p, own = self.p, self.own
        for name, step in (("up", 1), ("down", -1)):
            def held(step=step):
                return p.z + 1 < p.n_row if step == 1 else p.z >= 1

            def make(name=name, step=step):
                return (own, self.at(0, p.z, p.k), p.dev(z=p.z + step), self.s[name] + p.z, self.r["z"] + p.z)

            pl.when(held())(lambda make=make, held=held: self.lanes.send(make, held))

    def z_step(self, distance):
        p = self.p
        for name, step in (("up", 1), ("down", -1)):
            source = (lambda step=step: p.z - step * distance)

            def here(step=step):
                return p.z >= distance if step == 1 else p.z + distance < p.n_row

            def further(step=step):
                if step == 1:
                    return (p.z >= distance) & (p.z + 1 < p.n_row)
                return (p.z + distance < p.n_row) & (p.z >= 1)

            def arrive(name=name, step=step, source=source):
                ref = self.at(0, source(), p.k)
                self.lanes.arrived(ref, p.dev(z=p.z - step), self.r["z"] + source())

            def onward(name=name, step=step, source=source):
                ref = self.at(0, source(), p.k)
                return (ref, ref, p.dev(z=p.z + step), self.s[name] + source(), self.r["z"] + source())

            def over(hop, device, source=source):
                def make():
                    ref = self.at(0, source(), p.k)
                    return (ref, ref, device, self.s[hop] + source(), self.r[hop] + source())
                return make

            def body():
                arrive()
                if distance < p.n_row - 1:
                    pl.when(further())(lambda: self.lanes.send(onward, further))
                self.lanes.send(over(1, self.one), here)
                self.lanes.send(over(2, self.two), here)

            pl.when(here())(body)

    def z_steps(self):
        for distance in range(1, self.p.n_row):
            self.z_step(distance)
        self.z_done()

    def z_done(self):
        self.local.wait()
        self.to_other_core(0)

    def to_other_core(self, hop):
        def make():
            line = self.line(hop, self.p.k)
            return (line, line, self.to_core, self.s["core"] + hop, self.r["core"] + hop)
        self.lanes.send(make)

    def first_steps(self):
        p = self.p
        n = p.n_row
        order = (lambda: p.z, lambda: p.z + 1 - 2 * (p.z % 2), lambda: n - 1 - p.z, lambda: (p.z + n // 2) % n)
        for source in order:
            self.lanes.arrived(self.at(1, source(), p.k), self.one, self.r[1] + source())

            def make(source=source):
                ref = self.at(1, source(), p.k)
                return (ref, ref, self.two, self.s[3] + source(), self.r[3] + source())

            self.lanes.send(make)
        self.to_other_core(1)

    def second_steps(self, hops=(2, 3)):
        p = self.p
        for hop in hops:
            for i in range(p.n_row):
                self.lanes.arrived(self.at(hop, i, p.k), self.two, self.r[hop] + i)
            self.to_other_core(hop)

    def stage(self, name):
        if name == "z":
            self.z_start()
        elif name == "f":
            self.first_steps()
        elif name == "s":
            self.second_steps((2,))
        elif name == "t":
            self.second_steps((3,))
        else:
            self.z_step(int(name))
            if int(name) == self.p.n_row - 1:
                self.z_done()

    def end(self):
        for hop in range(4):
            self.lanes.arrived(self.line(hop, 1 - self.p.k), self.to_core, self.r["core"] + hop)


def rows_region(ref, n_row, low=0, high=None):
    width = ref.shape[3] // 2
    high = width if high is None else high

    def region(x, z, nz, y, k):
        columns = pl.ds(aligned(y * width + low, 128), high - low)
        if nz == 1:
            return ref.at[x * n_row + z, k, :, columns]
        return ref.at[pl.ds(x * n_row + z, nz), k, :, columns]

    return region


def lanes_region(ref, n_dp, n_row, low=0, high=None):
    width = ref.shape[3] // (n_dp * n_row)
    high = ref.shape[2] if high is None else high

    def region(x, z, nz, y, k):
        return ref.at[y, k, pl.ds(low, high - low), pl.ds(aligned((x * n_row + z) * width, 128), nz * width)]

    return region


CHUNK = 512
ROWS = 256
BATCH = (6, 6, 6, 6, 7)
SCHEDULE = {
    "first": {4: "oz uz", 5: "o1 u1 vz"},
    "turn": {0: "o2 u2 v1 dz", 2: "o3 u3 v2 d1"},
    "project": {0: "of v3 d2", 3: "uf d3", 6: "vf ez"},
    "attend": {0: "df os e1", 1: "e2", 2: "us e3", 3: "ot ut", 4: "ef", 5: "vs", 6: "vt", 8: "cot", 9: "ds", 11: "dt"},
    "mix": {1: "es"},
    "rise": {0: "et"},
}


def forward_kernel(
    dims, seq_ref, len_ref, tok_ref, cot_ref, qkv_ref, out_ref, up_ref, down_ref, norm_ref,
    xt_out, wqkv_out, qkv_out, ctx_out, lse_out, output_out, gm_out, dctx_out, gout_out, gup_out, gdown_out, nsum_out,
    tsend, half_qkv, half_out, half_up, pair_qkv, pair_out, pair_up,
    xt_v, x_v, w_v, wide_v, ctx_v, lse_v, wout_v, wup_v, wdown_v, norm_v, gains_v, cot_v, act_v, mixed_v, gsum_v, hl_v,
    output_v, down_v, attn_v, dctx_v, turn_v, nsum_v,
    tok_send, tok_recv, norm_send, norm_recv, cot_send, cot_recv, w_send, w_recv, half_send, half_recv, local_sem, out_send, out_recv,
):
    n_dp, n_row, n_col = dims
    p = Place(n_dp, n_row, n_col)
    micro, slots, _, span = tok_ref.shape
    rows, width = x_v.shape
    qkv_v = wide_v.at[:, pl.ds(0, 3 * width)]
    p.greet()
    for m in range(micro):
        for j in range(slots):
            tsend[m * slots + j] = tok_ref[m, seq_ref[m, j]]
    p.met()
    halves = Lanes(half_send, half_recv)
    lanes = Lanes(w_send, w_recv)
    partner = p.dev(k=1 - p.k)
    for i, (block, landing) in enumerate(((qkv_ref, half_qkv), (out_ref, half_out), (up_ref, half_up))):
        def make(i=i, block=block, landing=landing):
            count = landing.shape[0]
            return (block.at[pl.ds(aligned((1 - p.k) * count, 16), count), :], landing, partner, i, i)
        halves.send(make)

    def join(i, block, landing, pair):
        halves.arrived(landing, partner, i)
        count, across = landing.shape
        mine = block[pl.ds(aligned(p.k * count, 16), count), :]
        theirs = landing[...]
        pair[:, :across] = jnp.where(p.k == 0, mine, theirs)
        pair[:, across:] = jnp.where(p.k == 0, theirs, mine)

    local = []

    def keep(src, dst):
        made = pltpu.make_async_copy(src, dst, local_sem.at[len(local)])
        made.start()
        local.append(made)
        return made

    region_qkv = rows_region(w_v, n_row)
    join(0, qkv_ref, half_qkv, pair_qkv)
    own_w = keep(pair_qkv, region_qkv(p.x, p.z, 1, p.y, p.k))
    g_qkv = Gather(p, lanes, region_qkv, "x")
    g_qkv.local = own_w
    g_qkv.start(pair_qkv)
    g_qkv.z_start()

    def tok_copy(i):
        target = (p.flat + i) % p.n
        return pltpu.make_async_remote_copy(
            src_ref=tsend.at[(target % n_col) * slots + target // n_col],
            dst_ref=xt_v.at[p.g, :, pl.ds(aligned(p.c * span, 128), span)],
            send_sem=tok_send.at[i], recv_sem=tok_recv.at[i],
            device_id=p.of_flat(target), device_id_type=MESH,
        )

    def norm_copy(i):
        return pltpu.make_async_remote_copy(
            src_ref=norm_ref, dst_ref=norm_v.at[p.flat],
            send_sem=norm_send.at[i], recv_sem=norm_recv.at[i],
            device_id=p.of_flat((p.flat + i) % p.n), device_id_type=MESH,
        )

    sent = [1]

    def tok_batch(count):
        def one(j, carry):
            tok_copy((j * 13) % p.n).start()
            return carry

        lax.fori_loop(sent[0], min(sent[0] + count, p.n), one, 0)
        sent[0] = min(sent[0] + count, p.n)

    def norm_start(i, carry):
        norm_copy(i).start()
        return carry

    tok_batch(BATCH[0])
    own_tok = keep(tsend.at[p.c * slots + p.g], xt_v.at[p.g, :, pl.ds(aligned(p.c * span, 128), span)])

    waves = []

    def wave(own, region, first):
        gather = Gather(p, lanes, region, first)
        gather.local = keep(own, region(p.x, p.z, 1, p.y, p.k))
        gather.start(own)
        waves.append(gather)

    join(1, out_ref, half_out, pair_out)
    wave(pair_out, rows_region(wout_v, n_row), "y")
    join(2, up_ref, half_up, pair_up)
    cut = pair_up.shape[1] // 2
    wave(pair_up.at[:, pl.ds(0, cut)], rows_region(wup_v, n_row, 0, cut), "y")
    wave(pair_up.at[:, pl.ds(cut, cut)], rows_region(wup_v, n_row, cut, 2 * cut), "y")
    cut = down_ref.shape[0] // 2
    wave(down_ref.at[pl.ds(0, cut), :], lanes_region(wdown_v, n_dp, n_row, 0, cut), "y")
    wave(down_ref.at[pl.ds(cut, cut), :], lanes_region(wdown_v, n_dp, n_row, cut, 2 * cut), "y")
    lax.fori_loop(1, p.n, norm_start, 0)
    own_norm = keep(norm_ref, norm_v.at[p.flat])

    def cot_copy(i):
        target = (p.c + i) % n_col
        return pltpu.make_async_remote_copy(
            src_ref=cot_ref.at[target], dst_ref=cot_v.at[p.c],
            send_sem=cot_send.at[i], recv_sem=cot_recv.at[i],
            device_id=(p.x, p.z, target), device_id_type=MESH,
        )

    own_cot = keep(cot_ref.at[p.c], cot_v.at[p.c])
    names = dict(zip("ouvde", waves))

    def begin_cot():
        for i in range(1, n_col):
            cot_copy(i).start()

    def agenda(phase):
        table = {}
        for turn, steps in SCHEDULE.get(phase, {}).items():
            table[turn] = [begin_cot if step == "cot" else functools.partial(names[step[0]].stage, step[1:]) for step in steps.split()]
        return table

    first = agenda("first")

    def now(turn):
        for act in first.get(turn, ()):
            act()

    now(0)
    for distance in range(1, n_row):
        g_qkv.z_step(distance)
        tok_batch(BATCH[distance])
        now(distance)
    g_qkv.z_done()
    g_qkv.first_steps()
    tok_batch(BATCH[4])
    now(4)
    g_qkv.second_steps()
    tok_batch(p.n)
    now(5)
    own_tok.wait()

    def tok_wait(i, carry):
        source = (p.flat + p.n - i) % p.n
        landing = xt_v.at[source // n_col, :, pl.ds(aligned((source % n_col) * span, 128), span)]
        pltpu.make_async_remote_copy(
            src_ref=landing, dst_ref=landing, send_sem=tok_send.at[i], recv_sem=tok_recv.at[i],
            device_id=p.of_flat(source), device_id_type=MESH,
        ).wait_recv()
        return carry

    lax.fori_loop(1, p.n, tok_wait, 0)
    keep(xt_v, xt_out)

    def turn(i, carry):
        run_events(i, agenda("turn"))
        at = pl.ds(aligned(i * 256, 256), 256)
        x_v[at, :] = xt_v[:, :, at].reshape(width, 256).T
        return carry

    lax.fori_loop(0, rows // 256, turn, 0)
    g_qkv.end()
    keep(w_v, wqkv_out)

    def project(i, carry):
        run_events(i, agenda("project"))
        at = pl.ds(aligned(i * 256, 256), 256)
        wide_v[:, at] = product(x_v[...], w_v[:, :, :, at].reshape(width, 256)).astype(BF)
        return carry

    lax.fori_loop(0, 3 * width // 256, project, 0)
    kept_qkv = keep(qkv_v, qkv_out)
    out, up_a, up_b, down_a, down_b = waves
    length = len_ref[p.c, seq_ref[p.c, p.g]]
    bias = jnp.where(lax.broadcasted_iota(jnp.int32, (rows, 1), 0) < length, 0.0, NEGATIVE)
    chunks = rows // CHUNK

    def attend(step, carry):
        run_events(step, agenda("attend"))
        pair, at_row = step // chunks, step % chunks
        columns = [pl.ds(aligned(i * width + pair * 128, 128), 128) for i in range(3)]
        keys = wide_v[:, columns[1]]
        values_t = wide_v[:, columns[2]].T
        lane = lax.broadcasted_iota(jnp.int32, (rows, 128), 1)
        own_rows = pl.ds(aligned(at_row * CHUNK, CHUNK), CHUNK)
        queries = wide_v[own_rows, columns[0]] * jnp.asarray(0.125, BF)
        for h in range(2):
            mine = jnp.where((lane < HEAD) == (h == 0), keys, jnp.zeros_like(keys))
            scores = product_nt(mine, queries) + bias
            top = jnp.max(scores, axis=0, keepdims=True)
            exps = jnp.exp(scores - top)
            total = jnp.sum(exps, axis=0, keepdims=True)
            context = product(values_t[h * HEAD:(h + 1) * HEAD], exps.astype(BF))
            head_rows = pl.ds(aligned(pair * 128 + h * HEAD, HEAD), HEAD)
            ctx_v[head_rows, own_rows] = (context * (1.0 / total)).astype(BF)
            lse_v[2 * pair + h, :, own_rows] = top + jnp.log(total)
        return carry

    lax.fori_loop(0, width // 128 * chunks, attend, 0)
    keep(ctx_v, ctx_out)
    keep(lse_v, lse_out)

    own_norm.wait()

    def norm_wait(i, carry):
        source = (p.flat + p.n - i) % p.n
        pltpu.make_async_remote_copy(
            src_ref=norm_ref, dst_ref=norm_v.at[source], send_sem=norm_send.at[i], recv_sem=norm_recv.at[i],
            device_id=p.of_flat(source), device_id_type=MESH,
        ).wait_recv()
        return carry

    lax.fori_loop(1, p.n, norm_wait, 0)
    each = width // p.n
    gains_v[...] = jnp.zeros_like(gains_v)
    for source in range(p.n):
        low = source * each // 128 * 128
        gains_v[:, low:low + 256] += norm_v[source].astype(F32)
    gain_one, shift_one, gain_two, shift_two = (gains_v[i:i + 1, :width] for i in range(4))

    def normal(values):
        centered = values - jnp.mean(values, axis=-1, keepdims=True)
        scale = lax.rsqrt(jnp.mean(centered * centered, axis=-1, keepdims=True) + EPSILON)
        return centered * scale, scale

    def normal_back(grad, unit, scale, gain):
        grad = grad * gain
        return scale * (grad - jnp.mean(grad, axis=-1, keepdims=True) - unit * jnp.mean(grad * unit, axis=-1, keepdims=True))

    nsum_v[...] = jnp.zeros_like(nsum_v)
    whole = lambda ref: ref[...].reshape(width, -1)
    out.end()

    def mix(step, carry):
        run_events(step, agenda("mix"))
        at = pl.ds(aligned(step * ROWS, ROWS), ROWS)
        mixed = x_v[at, :].astype(F32) + product_tn(ctx_v[:, at], whole(wout_v))
        mixed_v[at, :] = mixed
        unit, _ = normal(mixed)
        hl_v[at, :] = (unit * gain_one + shift_one).astype(BF)
        return carry

    lax.fori_loop(0, rows // ROWS, mix, 0)
    up_a.end()
    up_b.end()
    kept_qkv.wait()

    def rise(step, carry):
        run_events(step, agenda("rise"))
        at = pl.ds(aligned(step * 256, 256), 256)
        pre = product(hl_v[...], wup_v[:, :, :, at].reshape(width, 256))
        half = 0.5 * (1.0 + lax.erf(pre * ROOT_HALF))
        act_v[:, at] = (pre * half).astype(BF)
        wide_v[:, at] = (half + pre * jnp.exp(pre * pre * -0.5) * ROOT_TWO_PI).astype(BF)
        return carry

    lax.fori_loop(0, 4 * width // 256, rise, 0)
    down_a.end()
    down_b.end()
    for i in range(1, n_col):
        source = (p.c + n_col - i) % n_col
        pltpu.make_async_remote_copy(
            src_ref=cot_v.at[source], dst_ref=cot_v.at[source],
            send_sem=cot_send.at[i], recv_sem=cot_recv.at[i],
            device_id=(p.x, p.z, source), device_id_type=MESH,
        ).wait_recv()
    own_cot.wait()

    def out_copy(target):
        return pltpu.make_async_remote_copy(
            src_ref=output_v.at[pl.ds(aligned(target * span, 16), span), :], dst_ref=output_out.at[p.c],
            send_sem=out_send.at[target], recv_sem=out_recv.at[p.c],
            device_id=(p.x, p.z, target), device_id_type=MESH,
        )

    def fall(step, carry):
        at = pl.ds(aligned(step * ROWS, ROWS), ROWS)
        unit_one, _ = normal(mixed_v[at, :])
        summed = unit_one * gain_one + shift_one + product_nt(act_v[at, :], whole(wdown_v))
        unit, scale = normal(summed)
        output_v[at, :] = (unit * gain_two + shift_two).astype(BF)
        per = span // ROWS
        cot = cot_v[step // per, pl.ds(aligned(step % per * ROWS, ROWS), ROWS), :].astype(F32)
        nsum_v[2:3, :] += jnp.sum(cot * unit, axis=0, keepdims=True)
        nsum_v[3:4, :] += jnp.sum(cot, axis=0, keepdims=True)
        grad = normal_back(cot, unit, scale, gain_two)
        gsum_v[at, :] = grad
        down_v[at, :] = grad.astype(BF)
        turn_v[:, at] = grad.T.astype(BF)
        target = step // per

        @pl.when((step % per == per - 1) & (target != p.c))
        def _():
            out_copy(target).start()
        return carry

    lax.fori_loop(0, rows // ROWS, fall, 0)
    keep(output_v.at[pl.ds(aligned(p.c * span, 16), span), :], output_out.at[p.c])

    def rise_back(step, carry):
        at = pl.ds(aligned(step * 256, 256), 256)
        back = product(down_v[...], wdown_v[:, :, :, at].reshape(width, 256))
        wide_v[:, at] = (back * wide_v[:, at].astype(F32)).astype(BF)
        return carry

    lax.fori_loop(0, 4 * width // 256, rise_back, 0)
    lanes.finish()

    def grad_down(step, carry):
        at = pl.ds(aligned(step * 256, 256), 256)
        wdown_v[:, :, :, at] = product(turn_v[...], act_v[:, at]).astype(BF).reshape(wdown_v.shape[:3] + (256,))
        return carry

    lax.fori_loop(0, 4 * width // 256, grad_down, 0)
    keep(wdown_v, gdown_out)

    def mix_back(step, carry):
        at = pl.ds(aligned(step * ROWS, ROWS), ROWS)
        grad = gsum_v[at, :] + product_nt(wide_v[at, :], whole(wup_v))
        unit, scale = normal(mixed_v[at, :])
        nsum_v[0:1, :] += jnp.sum(grad * unit, axis=0, keepdims=True)
        nsum_v[1:2, :] += jnp.sum(grad, axis=0, keepdims=True)
        grad = normal_back(grad, unit, scale, gain_one)
        gsum_v[at, :] = grad
        low = grad.astype(BF)
        attn_v[at, :] = low
        dctx_v[at, :] = product_nt(low, whole(wout_v)).astype(BF)
        turn_v[:, at] = hl_v[at, :].T
        return carry

    lax.fori_loop(0, rows // ROWS, mix_back, 0)
    keep(gsum_v, gm_out)
    keep(dctx_v, dctx_out)
    keep(nsum_v, nsum_out)

    def grad_up(step, carry):
        at = pl.ds(aligned(step * 256, 256), 256)
        wup_v[:, :, :, at] = product(turn_v[...], wide_v[:, at]).astype(BF).reshape(wup_v.shape[:3] + (256,))
        return carry

    lax.fori_loop(0, 4 * width // 256, grad_up, 0)
    keep(wup_v, gup_out)

    def grad_out(step, carry):
        at = pl.ds(aligned(step * 256, 256), 256)
        wout_v[:, :, :, at] = product(ctx_v[...], attn_v[:, at]).astype(BF).reshape(wout_v.shape[:3] + (256,))
        return carry

    lax.fori_loop(0, width // 256, grad_out, 0)
    keep(wout_v, gout_out)

    def small_wait(i, carry):
        norm_copy(i).wait_send()
        tok_copy(i).wait_send()
        return carry

    lax.fori_loop(1, p.n, small_wait, 0)
    for i in range(1, n_col):
        cot_copy(i).wait_send()
        source = (p.c + n_col - i) % n_col
        pltpu.make_async_remote_copy(
            src_ref=output_out.at[source], dst_ref=output_out.at[source],
            send_sem=out_send.at[source], recv_sem=out_recv.at[source],
            device_id=(p.x, p.z, source), device_id_type=MESH,
        ).wait_recv()
        out_copy((p.c + i) % n_col).wait_send()
    waited = [own_tok, own_norm, own_w, own_cot, kept_qkv] + [gather.local for gather in waves]
    for made in local:
        if not any(made is w for w in waited):
            made.wait()
    halves.finish()


def run_events(step, events):
    for when_, acts in events.items():
        def act(acts=acts):
            for a in acts:
                a()
        pl.when(step == when_)(act)


def forward(dims, seq_order, lengths, tok_t, cot, w_qkv, w_out, w_up, w_down_t, norms):
    n_dp, n_row, n_col = dims
    groups, n = n_dp * n_row, n_dp * n_row * n_col
    micro, slots, feats, span = tok_t.shape
    rows, width = n_col * span, groups * feats
    heads = width // HEAD
    qr, qc = w_qkv.shape
    orow, oc = w_out.shape
    ur, uc = w_up.shape
    dr, dc = w_down_t.shape
    shape = jax.ShapeDtypeStruct
    joined = (groups, 2, qr // 2, qc * n_col)
    out_all = (groups, 2, orow // 2, oc * n_col)
    up_all = (groups, 2, ur // 2, uc * n_col)
    down_all = (2, 2, dr, dc * groups)
    outs = (
        shape((groups, feats, rows), BF),
        shape(joined, BF),
        shape((rows, 3 * width), BF),
        shape((width, rows), BF),
        shape((heads, 1, rows), F32),
        shape((n_col, span, width), BF),
        shape((rows, width), F32),
        shape((rows, width), BF),
        shape(out_all, BF),
        shape(up_all, BF),
        shape(down_all, BF),
        shape((8, width), F32),
    )
    vm = pltpu.VMEM
    return pl.pallas_call(
        functools.partial(forward_kernel, dims),
        out_shape=outs,
        in_specs=[SM, SM, VM, ANY, VM, VM, VM, VM, VM],
        out_specs=[ANY] * len(outs),
        scratch_shapes=[
            vm((micro * slots, feats, span), BF),
            vm((qr // 2, qc), BF), vm((orow // 2, oc), BF), vm((ur // 2, uc), BF),
            vm((qr // 2, qc * 2), BF), vm((orow // 2, oc * 2), BF), vm((ur // 2, uc * 2), BF),
            vm((groups, feats, rows), BF),
            vm((rows, width), BF),
            vm(joined, BF),
            vm((rows, 4 * width), BF),
            vm((width, rows), BF),
            vm((heads, 1, rows), F32),
            vm(out_all, BF), vm(up_all, BF), vm(down_all, BF),
            vm((n,) + norms.shape, BF),
            vm((norms.shape[0], width + 256), F32),
            vm(cot.shape, BF),
            vm((rows, 4 * width), BF),
            vm((rows, width), F32), vm((rows, width), F32),
            vm((rows, width), BF), vm((rows, width), BF), vm((rows, width), BF), vm((rows, width), BF), vm((rows, width), BF),
            vm((width, rows), BF),
            vm((8, width), F32),
            DMA((n,)), DMA((n,)), DMA((n,)), DMA((n,)), DMA((n_col,)), DMA((n_col,)),
            DMA((6 * 6 * n_row,)), DMA((6 * 5 * n_row,)), DMA((3,)), DMA((3,)), DMA((24,)), DMA((n_col,)), DMA((n_col,)),
        ],
        compiler_params=pltpu.CompilerParams(
            collective_id=0, has_side_effects=True, vmem_limit_bytes=63 * 2**20
        ),
        name="forward_part",
    )(seq_order, lengths, tok_t, cot, w_qkv, w_out, w_up, w_down_t, norms)


BACK_CHUNK = 256


def add_into(target, term):
    shape = target.shape
    if len(shape) == 2:
        target[...] = (target[...].astype(F32) + term[...].astype(F32)).astype(BF)
        return

    def body(i, carry):
        target[i] = (target[i].astype(F32) + term[i].astype(F32)).astype(BF)
        return carry

    lax.fori_loop(0, shape[0], body, 0)


class Reduce:
    def __init__(self, place, lanes, theirs, mine, buffers, kind, first):
        self.p, self.lanes, self.theirs, self.mine, self.b = place, lanes, theirs, mine, buffers
        self.kind, self.axes = kind, ("x", "y") if first == "x" else ("y", "x")
        self.s = [lanes.take(0, 1) for _ in range(3)] + [lanes.take(0, place.n_row - 1)]
        self.r = [lanes.take(1, 1) for _ in range(3)] + [lanes.take(1, place.n_row - 1)]

    def start(self):
        p = self.p
        self.lanes.send(lambda: (self.theirs, self.b[0], p.dev(k=1 - p.k), self.s[0], self.r[0]))

    def half(self, ref, axis, side):
        if self.kind == "lanes" and axis == "y":
            return ref.at[side]
        if self.kind == "rows" and axis == "x":
            count = ref.shape[0] // 2
            return ref.at[pl.ds(side * count, count)]
        width = ref.shape[-1] // 2
        lead = (slice(None),) * (len(ref.shape) - 1)
        return ref.at[lead + (pl.ds(aligned(side * width, 128), width),)]

    def where(self, axis):
        p = self.p
        return (p.x, p.dev(x=1 - p.x)) if axis == "x" else (p.y, p.dev(y=1 - p.y))

    def send_half(self, stage):
        def make():
            side, peer = self.where(self.axes[stage - 1])
            return (self.half(self.b[stage - 1], self.axes[stage - 1], 1 - side), self.b[stage], peer, self.s[stage], self.r[stage])

        self.lanes.send(make)

    def add_half(self, stage):
        side, peer = self.where(self.axes[stage - 1])
        self.lanes.arrived(self.b[stage], peer, self.r[stage])
        add_into(self.b[stage], self.half(self.b[stage - 1], self.axes[stage - 1], side))

    def one(self):
        p = self.p
        self.lanes.arrived(self.b[0], p.dev(k=1 - p.k), self.r[0])
        add_into(self.b[0], self.mine)
        self.send_half(1)

    def two(self):
        self.add_half(1)
        self.send_half(2)

    def part(self, z):
        ref = self.b[2]
        if self.kind == "rows":
            return ref.at[z]
        width = self.b[3].shape[-1]
        return ref.at[:, pl.ds(aligned(z * width, 128), width)]

    def three(self):
        p = self.p
        self.add_half(2)
        for i in range(1, p.n_row):
            def make(i=i):
                target = (p.z + i) % p.n_row
                return (self.part(target), self.b[3].at[i - 1], p.dev(z=target), self.s[3] + i - 1, self.r[3] + i - 1)
            self.lanes.send(make)

    def four(self):
        p = self.p
        total = self.part(p.z)[...].astype(F32)
        for i in range(1, p.n_row):
            source = (p.z + p.n_row - i) % p.n_row
            self.lanes.arrived(self.b[3].at[i - 1], p.dev(z=source), self.r[3] + i - 1)
            total = total + self.b[3][i - 1].astype(F32)
        return total


def piece_buffers(kind, first, lead, rows, columns, n_row, groups):
    if kind == "lanes":
        one = (2, rows, columns // 2) if first == "x" else (rows, columns)
        return [(2, rows, columns), one, (rows, columns // 2), (n_row - 1, rows, columns // groups)]
    one = (lead // 2, rows, columns) if first == "x" else (lead, rows, columns // 2)
    return [(lead, rows, columns), one, (lead // 2, rows, columns // 2), (n_row - 1, rows, columns // 2)]


def backward_kernel(
    dims, plan, seq_ref, qkv_ref, ctx_ref, lse_ref, dctx_ref, xt_ref, w_ref, gm_ref, gout_ref, gup_ref, gdown_ref,
    ngrad_ref, tgrad_ref, rqkv_ref, rout_ref, rup_ref, rdown_ref, nsum_ref, *scratch,
):
    n_dp, n_row, n_col = dims
    p = Place(n_dp, n_row, n_col)
    groups = n_dp * n_row
    (
        qkv_v, ctx_v, lse_v, dctx_v, xt_v, w_v, gm_v, m_out, m_up, m_down, grad_v, dqt_v, dk_v, dv_v, acc_k, acc_v, dxt_v, trecv,
        nrecv, fq, fo, fu, tok_send, tok_recv, norm_send, norm_recv, w_send, w_recv, local_sem,
    ) = scratch[:29]
    pieces = scratch[29:]
    micro, slots, _, span = tgrad_ref.shape
    width, rows = ctx_ref.shape
    p.greet()
    local = []

    def keep(src, dst):
        made = pltpu.make_async_copy(src, dst, local_sem.at[len(local)])
        made.start()
        local.append(made)
        return made

    needed = [keep(qkv_ref, qkv_v), keep(dctx_ref, dctx_v), keep(ctx_ref, ctx_v), keep(lse_ref, lse_v)]
    mine_down = keep(gdown_ref.at[:, p.k], m_down)
    mine_up = keep(gup_ref.at[:, p.k], m_up)
    mine_out = keep(gout_ref.at[:, p.k], m_out)
    later = [keep(w_ref, w_v), keep(gm_ref, gm_v), keep(xt_ref, xt_v)]
    p.met()
    lanes = Lanes(w_send, w_recv)
    partner = p.dev(k=1 - p.k)
    waves = {"down": [], "up": [], "out": [], "qkv": []}
    whole = {"down": gdown_ref, "up": gup_ref, "out": gout_ref, "qkv": grad_v}
    carried = {"down": m_down, "up": m_up, "out": m_out}
    for index, (name, kind, first, low, count) in enumerate(plan):
        at = pl.ds(low, count)
        theirs = whole[name].at[:, 1 - p.k, at]
        mine = carried[name].at[:, at] if name != "qkv" else grad_v.at[:, p.k, at]
        waves[name].append(Reduce(p, lanes, theirs, mine, pieces[4 * index:4 * index + 4], kind, first))
    d, u, o, q = waves["down"], waves["up"], waves["out"], waves["qkv"]

    def norm_copy(i):
        target = (p.flat + i) % p.n
        return pltpu.make_async_remote_copy(
            src_ref=ngrad_ref.at[target], dst_ref=nrecv.at[p.flat],
            send_sem=norm_send.at[i], recv_sem=norm_recv.at[i],
            device_id=p.of_flat(target), device_id_type=MESH,
        )

    def norm_start(i, carry):
        norm_copy(i).start()
        return carry

    d[0].start()
    u[0].start()
    lax.fori_loop(1, p.n, norm_start, 0)
    nrecv[p.flat] = ngrad_ref[p.flat]
    for made in needed:
        made.wait()
    mine_down.wait()
    mine_up.wait()
    mine_out.wait()

    def finish_rows(piece, temp, result, low):
        total = piece.four()
        count, across = total.shape[0], total.shape[1] // 2
        half_rows = result.shape[0] // 2
        temp[pl.ds(low, count), :] = jnp.where(p.k == 0, total[:, across:], total[:, :across])
        result[pl.ds(aligned(p.k * half_rows + low, 16), count), :] = jnp.where(p.k == 0, total[:, :across], total[:, across:])
        s, r = lanes.take(0, 1), lanes.take(1, 1)
        place = lambda k: result.at[pl.ds(aligned(k * half_rows + low, 16), count), :]
        lanes.send(lambda: (temp.at[pl.ds(low, count), :], place(p.k), partner, s, r))
        ends.append(lambda: lanes.arrived(place(1 - p.k), partner, r))

    ends = []

    def finish_down(piece, low):
        total = piece.four()
        rdown_ref[pl.ds(low, total.shape[0]), :] = total

    lows = {name: [low for other, _, _, low, _ in plan if other == name] for name in waves}
    down_end = [functools.partial(finish_down, piece, low) for piece, low in zip(d, lows["down"])]
    up_end = [functools.partial(finish_rows, piece, fu, rup_ref, low) for piece, low in zip(u, lows["up"])]
    out_end = [functools.partial(finish_rows, piece, fo, rout_ref, low) for piece, low in zip(o, lows["out"])]
    qkv_end = [functools.partial(finish_rows, piece, fq, rqkv_ref, low) for piece, low in zip(q, lows["qkv"])]
    events = {
        0: (d[1].start, u[1].start),
        1: (d[0].one, u[0].one),
        2: (d[2].start, u[2].start, o[0].start),
        4: (d[1].one,),
        5: (u[1].one,),
        6: (d[0].two,),
        7: (u[0].two,),
        9: (d[2].one,),
        10: (u[2].one,),
        11: (d[1].two,),
        12: (u[1].two, d[0].three),
        13: (u[0].three, o[0].one),
        15: (d[2].two,),
        16: (u[2].two, d[1].three),
        17: (u[1].three,),
        18: (o[0].two, down_end[0]),
        19: (up_end[0],),
        20: (d[2].three,),
        21: (u[2].three, o[0].three),
        22: (down_end[1],),
        23: (up_end[1],),
    }
    length_bias = jnp.where(lax.broadcasted_iota(jnp.int32, (rows, 1), 0) < seq_ref[1, p.c, seq_ref[0, p.c, p.g]], 0.0, NEGATIVE)
    chunks = rows // BACK_CHUNK

    def attend(step, carry):
        for when_, acts in events.items():
            def act(acts=acts):
                for a in acts:
                    a()
            pl.when(step == when_)(act)
        pair, at_row = step // chunks, step % chunks
        columns = [pl.ds(aligned(i * width + pair * 128, 128), 128) for i in range(3)]
        keys, values = qkv_v[:, columns[1]], qkv_v[:, columns[2]]
        keys_t = keys.T
        lane = lax.broadcasted_iota(jnp.int32, (rows, 128), 1)
        short = lax.broadcasted_iota(jnp.int32, (BACK_CHUNK, 128), 1)
        own_rows = pl.ds(aligned(at_row * BACK_CHUNK, BACK_CHUNK), BACK_CHUNK)
        queries = qkv_v[own_rows, columns[0]] * jnp.asarray(0.125, BF)
        back = dctx_v[own_rows, columns[0]]
        back_t = back.T.astype(F32)
        forth_t = ctx_v[pl.ds(aligned(pair * 128, 128), 128), own_rows].astype(F32)
        both = back_t * forth_t
        d_keys = d_values = None
        for h in range(2):
            def own(block, index):
                return jnp.where((index < HEAD) == (h == 0), block, jnp.zeros_like(block))
            delta = jnp.sum(both[h * HEAD:(h + 1) * HEAD], axis=0, keepdims=True)
            scores = product_nt(own(keys, lane), queries) + length_bias
            soft = jnp.exp(scores - lse_v[2 * pair + h, :, own_rows])
            d_probs = product_nt(own(values, lane), back)
            d_scores = (soft * (d_probs - delta)).astype(BF)
            head_rows = pl.ds(aligned(pair * 128 + h * HEAD, HEAD), HEAD)
            dqt_v[head_rows, own_rows] = (product(keys_t[h * HEAD:(h + 1) * HEAD], d_scores) * 0.125).astype(BF)
            to_values = product(soft.astype(BF), own(back, short))
            to_keys = product(d_scores, own(queries, short))
            d_values = to_values if d_values is None else d_values + to_values
            d_keys = to_keys if d_keys is None else d_keys + to_keys

        @pl.when(at_row == 0)
        def _():
            acc_k[...] = d_keys
            acc_v[...] = d_values

        @pl.when(at_row > 0)
        def _():
            acc_k[...] += d_keys
            acc_v[...] += d_values

        @pl.when(at_row == chunks - 1)
        def _():
            dk_v[:, columns[0]] = acc_k[...].astype(BF)
            dv_v[:, columns[0]] = acc_v[...].astype(BF)
        return carry

    lax.fori_loop(0, width // 128 * chunks, attend, 0)
    for made in later:
        made.wait()

    def tok_copy(target):
        return pltpu.make_async_remote_copy(
            src_ref=dxt_v.at[target // n_col, :, pl.ds(aligned((target % n_col) * span, 128), span)],
            dst_ref=trecv.at[p.c * slots + p.g],
            send_sem=tok_send.at[target], recv_sem=tok_recv.at[p.flat],
            device_id=p.of_flat(target), device_id_type=MESH,
        )

    half_groups = groups // 2
    half_width = width // 2
    for part in range(2):
        near = pl.ds(part * half_groups, half_groups)
        w_rows = lambda i: w_v[near, :, :, i * width:(i + 1) * width].reshape(half_width, width)
        total = gm_v[:, part * half_width:(part + 1) * half_width].T
        total = total + product(w_rows(0), dqt_v[...])
        total = total + product_nt(w_rows(1), dk_v[...])
        total = total + product_nt(w_rows(2), dv_v[...])
        dxt_v[near] = total.astype(BF).reshape(half_groups, width // groups, rows)

        def tok_start(i, carry, part=part):
            base = part * half_groups * n_col
            target = base + (p.flat + i) % (half_groups * n_col)

            @pl.when(target != p.flat)
            def _():
                tok_copy(target).start()
            return carry

        lax.fori_loop(0, half_groups * n_col, tok_start, 0)
    own_tok = keep(dxt_v.at[p.g, :, pl.ds(aligned(p.c * span, 128), span)], trecv.at[p.c * slots + p.g])

    def grad_q(i, carry):
        at = pl.ds(aligned(i * 256, 256), 256)
        grad_v[:, :, :, at] = product_nt(xt_v[...].reshape(width, rows), dqt_v[at, :]).astype(BF).reshape(groups, 2, -1, 256)
        return carry

    def grad_k(i, carry):
        at = pl.ds(aligned(i * 256, 256), 256)
        to = lambda j: pl.ds(aligned(j * width + i * 256, 256), 256)
        xt = xt_v[...].reshape(width, rows)
        grad_v[:, :, :, to(1)] = product(xt, dk_v[:, at]).astype(BF).reshape(groups, 2, -1, 256)
        grad_v[:, :, :, to(2)] = product(xt, dv_v[:, at]).astype(BF).reshape(groups, 2, -1, 256)
        return carry

    lax.fori_loop(0, width // 256, grad_q, 0)
    lax.fori_loop(0, width // 256, grad_k, 0)
    for piece in q:
        piece.start()
    for piece in q:
        piece.one()
    down_end[2]()
    up_end[2]()
    out_end[0]()
    for piece in q:
        piece.two()
    for piece in q:
        piece.three()

    def norm_wait(i, carry):
        source = (p.flat + p.n - i) % p.n
        pltpu.make_async_remote_copy(
            src_ref=nrecv.at[source], dst_ref=nrecv.at[source], send_sem=norm_send.at[i], recv_sem=norm_recv.at[i],
            device_id=p.of_flat(source), device_id_type=MESH,
        ).wait_recv()
        norm_copy(i).wait_send()
        return carry

    lax.fori_loop(1, p.n, norm_wait, 0)
    nsum_ref[...] = jnp.sum(nrecv[...], axis=0)
    for end in qkv_end:
        end()
    own_tok.wait()

    def tok_wait(i, carry):
        source = (p.flat + p.n - i) % p.n
        landing = trecv.at[(source % n_col) * slots + source // n_col]
        pltpu.make_async_remote_copy(
            src_ref=landing, dst_ref=landing, send_sem=tok_send.at[source], recv_sem=tok_recv.at[source],
            device_id=p.of_flat(source), device_id_type=MESH,
        ).wait_recv()
        tok_copy((p.flat + i) % p.n).wait_send()
        return carry

    lax.fori_loop(1, p.n, tok_wait, 0)
    for m in range(micro):
        for s in range(slots):
            place = jnp.int32(0)
            for j in range(slots):
                place = jnp.where(seq_ref[0, m, j] == s, jnp.int32(j), place)
            tgrad_ref[m, s] = trecv[m * slots + place]
    for end in ends:
        end()
    lanes.finish()


def backward(dims, seq_order, lengths, qkv, ctx_t, lse, d_context, xt, w_qkv, g_mixed, g_out, g_up, g_down_t, n_grads):
    n_dp, n_row, n_col = dims
    groups, n = n_dp * n_row, n_dp * n_row * n_col
    micro, slots = seq_order.shape
    width, rows = ctx_t.shape
    feats, span = width // groups, rows // n_col
    shape = jax.ShapeDtypeStruct
    plan, buffers = [], []
    for name, grad, kind, first, count in (
        ("down", g_down_t, "lanes", "x", 3), ("up", g_up, "rows", "y", 3), ("out", g_out, "rows", "x", 1),
        ("qkv", w_qkv, "rows", "y", 3),
    ):
        lead, _, across, columns = grad.shape
        each = across // count
        for i in range(count):
            plan.append((name, kind, first, i * each, each))
            buffers += [pltpu.VMEM(b, BF) for b in piece_buffers(kind, first, lead, each, columns, n_row, groups)]
    outs = (
        shape((micro, slots, feats, span), BF),
        shape((w_qkv.shape[2] * 2, w_qkv.shape[3] // n_col), F32),
        shape((g_out.shape[2] * 2, g_out.shape[3] // n_col), F32),
        shape((g_up.shape[2] * 2, g_up.shape[3] // n_col), F32),
        shape((g_down_t.shape[2], g_down_t.shape[3] // groups), F32),
        shape(n_grads.shape[1:], F32),
    )
    vm = lambda like, kind=BF: pltpu.VMEM(like.shape, kind)
    temps = [pltpu.VMEM((g.shape[2], g.shape[3] // n_col), F32) for g in (w_qkv, g_out, g_up)]
    carried = [pltpu.VMEM((g.shape[0],) + g.shape[2:], BF) for g in (g_out, g_up, g_down_t)]
    return pl.pallas_call(
        functools.partial(backward_kernel, dims, plan),
        out_shape=outs,
        in_specs=[SM, ANY, ANY, ANY, ANY, ANY, ANY, ANY, ANY, ANY, ANY, VM],
        out_specs=[VM, VM, VM, VM, VM, VM],
        scratch_shapes=[
            vm(qkv), vm(ctx_t), vm(lse, F32), vm(d_context), vm(xt), vm(w_qkv), vm(g_mixed, F32), *carried, vm(w_qkv),
            pltpu.VMEM((width, rows), BF), pltpu.VMEM((rows, width), BF), pltpu.VMEM((rows, width), BF),
            pltpu.VMEM((rows, 128), F32), pltpu.VMEM((rows, 128), F32),
            pltpu.VMEM((groups, feats, rows), BF), pltpu.VMEM((micro * slots, feats, span), BF),
            vm(n_grads, F32), *temps,
            DMA((n,)), DMA((n,)), DMA((n,)), DMA((n,)),
            DMA((80,)), DMA((80,)), DMA((16,)), *buffers,
        ],
        compiler_params=pltpu.CompilerParams(
            collective_id=1, has_side_effects=True, vmem_limit_bytes=62 * 2**20
        ),
        name="backward_part",
    )(jnp.stack([seq_order, lengths]), qkv, ctx_t, lse, d_context, xt, w_qkv, g_mixed, g_out, g_up, g_down_t, n_grads)
def layer_norm(values, factor, offset):
    average = jnp.mean(values, axis=-1, keepdims=True)
    centered = values - average
    variance = jnp.mean(centered * centered, axis=-1, keepdims=True)
    return centered * lax.rsqrt(variance + EPSILON) * factor + offset


def gelu_act(values):
    return 0.5 * values * (1.0 + lax.erf(values * ROOT_HALF))


def attention(qkv, length):
    rows, width = qkv.shape[0], qkv.shape[1] // 3
    heads = width // HEAD
    q, k, v = (qkv[:, i * width:(i + 1) * width].reshape(rows, heads, HEAD) for i in range(3))
    scores = jnp.einsum("qhe,khe->hqk", q, k, preferred_element_type=F32) * 0.125
    valid = jnp.arange(rows, dtype=jnp.int32) < length
    scores = jnp.where(valid[None, None, :], scores, NEGATIVE)
    top = jnp.max(scores, axis=-1, keepdims=True)
    exps = jnp.exp(scores - top)
    total = jnp.sum(exps, axis=-1, keepdims=True)
    probs = (exps / total).astype(BF)
    context = jnp.einsum("hqk,khe->qhe", probs, v, preferred_element_type=F32)
    return context.astype(BF).reshape(rows, width), top + jnp.log(total)


def attention_back(qkv, length, stats, d_context):
    rows, width = qkv.shape[0], qkv.shape[1] // 3
    heads = width // HEAD
    q, k, v = (qkv[:, i * width:(i + 1) * width].reshape(rows, heads, HEAD) for i in range(3))
    dc = d_context.reshape(rows, heads, HEAD)
    scores = jnp.einsum("qhe,khe->hqk", q, k, preferred_element_type=F32) * 0.125
    valid = jnp.arange(rows, dtype=jnp.int32) < length
    scores = jnp.where(valid[None, None, :], scores, NEGATIVE)
    soft = jnp.exp(scores - stats)
    d_probs = jnp.einsum("qhe,khe->hqk", dc, v, preferred_element_type=F32)
    delta = jnp.sum(soft * d_probs, axis=-1, keepdims=True)
    d_scores = (soft * (d_probs - delta)).astype(BF)
    dq = jnp.einsum("hqk,khe->qhe", d_scores, k, preferred_element_type=F32) * 0.125
    dk = jnp.einsum("hqk,qhe->khe", d_scores, q, preferred_element_type=F32) * 0.125
    dv = jnp.einsum("hqk,qhe->khe", soft.astype(BF), dc, preferred_element_type=F32)
    return jnp.concatenate([a.astype(BF).reshape(rows, width) for a in (dq, dk, dv)], axis=-1)


def middle(x, context, context_t, cot, w_out, w_up, w_down_t, gain_one, shift_one, gain_two, shift_two):
    mixed = x.astype(F32) + product(context, w_out)
    hidden = layer_norm(mixed, gain_one, shift_one)
    hidden_low = hidden.astype(BF)
    pre_act = product(hidden_low, w_up)
    act_low = gelu_act(pre_act).astype(BF)
    summed = hidden + product_nt(act_low, w_down_t)
    output = layer_norm(summed, gain_two, shift_two).astype(BF)
    _, norm_two_back = jax.vjp(layer_norm, summed, gain_two, shift_two)
    g_summed, g_gain_two, g_shift_two = norm_two_back(cot.astype(F32))
    d_down = g_summed.astype(BF)
    g_down_t = product_tn(d_down, act_low).astype(BF)
    d_act = product(d_down, w_down_t)
    _, gelu_back = jax.vjp(gelu_act, pre_act)
    d_pre = gelu_back(d_act)[0].astype(BF)
    g_up = product_tn(hidden_low, d_pre).astype(BF)
    g_hidden = g_summed + product_nt(d_pre, w_up)
    _, norm_one_back = jax.vjp(layer_norm, mixed, gain_one, shift_one)
    g_mixed, g_gain_one, g_shift_one = norm_one_back(g_hidden)
    d_attn = g_mixed.astype(BF)
    g_out = product(context_t, d_attn).astype(BF)
    d_context = product_nt(d_attn, w_out).astype(BF)
    return output, g_mixed, d_context, g_down_t, g_up, g_out, (g_gain_one, g_shift_one, g_gain_two, g_shift_two)


def take_blocks(blocks, places):
    def body(place_ref, in_ref, out_ref):
        def step(i, carry):
            out_ref[i] = in_ref[place_ref[i]]
            return carry

        lax.fori_loop(0, blocks.shape[0], step, 0)

    return pl.pallas_call(
        body, out_shape=jax.ShapeDtypeStruct(blocks.shape, blocks.dtype), in_specs=[SM, VM], out_specs=VM,
        compiler_params=pltpu.CompilerParams(vmem_limit_bytes=48 * 2**20), name="take_blocks",
    )(places, blocks)


def own_length(lengths, seq_order):
    n_row = lax.axis_size("row")
    slot = lax.axis_index("dp") * n_row + lax.axis_index("row")
    micro = lax.axis_index("col")
    index = jnp.arange(seq_order.shape[1], dtype=jnp.int32)
    order = jnp.sum(jnp.where(jnp.arange(seq_order.shape[0])[:, None] == micro, seq_order, 0), axis=0)
    source = jnp.sum(jnp.where(index == slot, order, 0))
    mine = jnp.sum(jnp.where(jnp.arange(seq_order.shape[0])[:, None] == micro, lengths, 0), axis=0)
    return jnp.sum(jnp.where(index == source, mine, 0))


def local(
    tokens, cotangent, lengths, seq_order, w_qkv, w_out, w_up, w_down, gain_one, shift_one, gain_two, shift_two,
):
    dims = tuple(lax.axis_size(a) for a in ("dp", "row", "col"))
    n_dp, n_row, n_col = dims
    groups = n_dp * n_row
    micro, slots, span, feats = tokens.shape
    width = cotangent.shape[3]
    rows = span * n_col
    direct = n_dp == 2 and n_col == 4 and feats % 32 == 0 and w_qkv.shape[0] % 32 == 0
    tok_t = jnp.swapaxes(tokens, 2, 3)
    w_down_t = w_down.T
    norms = jnp.stack([gain_one, shift_one, gain_two, shift_two])
    length = own_length(lengths, seq_order)
    everyone = ("dp", "row", "col")
    if direct:
        each = norms.shape[1]
        place = (lax.axis_index("dp") * n_row + lax.axis_index("row")) * n_col + lax.axis_index("col")
        lane = jnp.arange(256, dtype=jnp.int32)
        here = lane[None, :] == (place * each) % 128 + jnp.arange(each, dtype=jnp.int32)[:, None]
        packed = jnp.sum(jnp.where(here[None], norms[:, :, None].astype(F32), 0.0), axis=1).astype(BF)
        packed = jnp.pad(packed, ((0, 12), (0, 0)))
        xt, w_joined, qkv, context_t, lse, output, g_mixed, d_context, g_out, g_up, g_down_t, norm_grads = forward(
            dims, seq_order, lengths, tok_t, cotangent[:, 0], w_qkv, w_out, w_up, w_down_t, packed
        )
        norm_grads = norm_grads[:4]
    else:
        offset = jnp.arange(micro, dtype=jnp.int32)[:, None] * slots
        sent = take_blocks(tok_t.reshape(micro * slots, feats, span), (seq_order + offset).reshape(-1))
        sent = jnp.swapaxes(sent.reshape(micro, slots, feats, span), 0, 1).reshape(micro * slots, feats, span)
        got = lax.all_to_all(sent, everyone, split_axis=0, concat_axis=0, tiled=True)
        xt = got.reshape(groups, n_col, feats, span).transpose(0, 2, 1, 3).reshape(width, rows)
        cot = lax.all_to_all(cotangent[:, 0], "col", split_axis=0, concat_axis=0, tiled=True).reshape(rows, width)

        def whole(w, row_axes, col_axes):
            w = lax.all_gather(w, col_axes, axis=1, tiled=True)
            return lax.all_gather(w, row_axes, axis=0, tiled=True)

        f_qkv, f_out, f_up = (whole(w, ("dp", "row"), "col") for w in (w_qkv, w_out, w_up))
        f_down_t = whole(w_down_t, "col", ("dp", "row"))
        f_norms = lax.all_gather(norms, everyone, axis=1, tiled=True)
    if direct:
        n_grads = jnp.swapaxes(norm_grads.reshape(4, width // each, each), 0, 1)
        n_grads = jnp.pad(n_grads, ((0, 0), (0, 4), (0, 128 - each)))
        tgrad, r_qkv, r_out, r_up, r_down_t, n_sum = backward(
            dims, seq_order, lengths, qkv, context_t, lse, d_context, xt, w_joined, g_mixed,
            g_out, g_up, g_down_t, n_grads,
        )
        n_sum = n_sum[:4, :each]
    else:
        gains = [f_norms[i].astype(F32) for i in range(4)]
        x = xt.T
        qkv = product(x, f_qkv).astype(BF)
        context, stats = attention(qkv, length)
        output, g_mixed, d_context, g_down_t, g_up, g_out, norm_grads = middle(
            x, context, context.T, cot, f_out, f_up, f_down_t, *gains
        )
        norm_grads = jnp.stack(norm_grads)
        d_qkv = attention_back(qkv, length, stats, d_context)
        g_qkv = product(xt, d_qkv).astype(BF)
        dxt = (g_mixed + product_nt(d_qkv, f_qkv)).astype(BF).T
        n_sum = lax.psum_scatter(norm_grads, everyone, scatter_dimension=1, tiled=True)
        output = lax.all_to_all(output.reshape(n_col, span, width), "col", split_axis=0, concat_axis=0, tiled=True)
        sent = dxt.reshape(groups, feats, n_col, span).transpose(0, 2, 1, 3).reshape(micro * slots, feats, span)
        got = lax.all_to_all(sent, everyone, split_axis=0, concat_axis=0, tiled=True)
        got = jnp.swapaxes(got.reshape(slots, micro, feats, span), 0, 1).reshape(micro * slots, feats, span)
        index = jnp.arange(slots, dtype=jnp.int32)
        inverse = jnp.sum(jnp.where(seq_order[:, :, None] == index, index[None, :, None], 0), axis=1)
        offset = jnp.arange(micro, dtype=jnp.int32)[:, None] * slots
        tgrad = take_blocks(got, (inverse + offset).reshape(-1)).reshape(micro, slots, feats, span)

        def parts(g, row_axes, col_axes):
            g = lax.psum_scatter(g, col_axes, scatter_dimension=1, tiled=True)
            return lax.psum_scatter(g, row_axes, scatter_dimension=0, tiled=True).astype(F32)

        r_qkv, r_out, r_up = (parts(g, ("dp", "row"), "col") for g in (g_qkv, g_out, g_up))
        r_down_t = parts(g_down_t, "col", ("dp", "row"))
    return (
        output[:, None], jnp.swapaxes(tgrad, 2, 3), r_qkv, r_out, r_up, r_down_t.T,
        n_sum[0], n_sum[1], n_sum[2], n_sum[3],
    )


def solution(mesh):
    rows = ("dp", "row")
    every = ("dp", "row", "col")
    in_specs = (
        P(None, None, "col", rows), P(None, rows, "col", None), P(), P(),
        P(rows, "col"), P(rows, "col"), P(rows, "col"), P(rows, "col"),
        P(every), P(every), P(every), P(every),
    )
    out_specs = (
        P(None, rows, "col", None), P(None, None, "col", rows),
        P(rows, "col"), P(rows, "col"), P(rows, "col"), P(rows, "col"),
        P(every), P(every), P(every), P(every),
    )
    return jax.shard_map(local, mesh=mesh, in_specs=in_specs, out_specs=out_specs, check_vma=False)
```

```python
import functools

import jax
import jax.numpy as jnp
from jax import lax
from jax.experimental import pallas as pl
from jax.experimental.pallas import tpu as pltpu
from jax.sharding import PartitionSpec as P

HEAD = 64
NEGATIVE = -1000000000.0
EPSILON = 1e-12
ROOT_HALF = 0.7071067811865476
ROOT_TWO_PI = 0.3989422804014327
MESH = pl.DeviceIdType.MESH
BF = jnp.bfloat16
F32 = jnp.float32
ANY = pl.BlockSpec(memory_space=pl.ANY)
VM = pl.BlockSpec(memory_space=pltpu.VMEM)
SM = pl.BlockSpec(memory_space=pltpu.SMEM)
DMA = pltpu.SemaphoreType.DMA


def aligned(value, step):
    return pl.multiple_of(value, step)


def product(left, right):
    return jnp.dot(left, right, preferred_element_type=F32)


def product_tn(left, right):
    return lax.dot_general(left, right, (((0,), (0,)), ((), ())), preferred_element_type=F32)


def product_nt(left, right):
    return lax.dot_general(left, right, (((1,), (1,)), ((), ())), preferred_element_type=F32)


class Place:
    def __init__(self, n_dp, n_row, n_col):
        self.n_dp, self.n_row, self.n_col = n_dp, n_row, n_col
        self.n = n_dp * n_row * n_col
        self.x = lax.axis_index("dp")
        self.z = lax.axis_index("row")
        self.c = lax.axis_index("col")
        self.y, self.k = self.c // 2, self.c % 2
        self.g = self.x * n_row + self.z
        self.flat = self.g * n_col + self.c

    def of_flat(self, flat):
        group = flat // self.n_col
        return (group // self.n_row, group % self.n_row, flat % self.n_col)

    def dev(self, x=None, z=None, y=None, k=None):
        x = self.x if x is None else x
        z = self.z if z is None else z
        y = self.y if y is None else y
        k = self.k if k is None else k
        return (x, z, y * 2 + k)

    def greet(self):
        sem = pltpu.get_barrier_semaphore()

        def one(i, carry):
            pl.semaphore_signal(
                sem, inc=1, device_id=self.of_flat((self.flat + i) % self.n), device_id_type=MESH
            )
            return carry

        lax.fori_loop(1, self.n, one, 0)

    def met(self):
        pl.semaphore_wait(pltpu.get_barrier_semaphore(), self.n - 1)


class Lanes:
    def __init__(self, send_sems, recv_sems):
        self.send_sems, self.recv_sems, self.sent = send_sems, recv_sems, []
        self.used = [0, 0]

    def take(self, which, count):
        first = self.used[which]
        self.used[which] += count
        return first

    def copy(self, src, dst, device, s, r):
        return pltpu.make_async_remote_copy(
            src_ref=src, dst_ref=dst, send_sem=self.send_sems.at[s],
            recv_sem=self.recv_sems.at[r], device_id=device, device_id_type=MESH,
        )

    def send(self, make):
        self.copy(*make()).start()
        self.sent.append(make)

    def arrived(self, landing, device, r):
        self.copy(landing, landing, device, 0, r).wait_recv()

    def finish(self):
        for make in self.sent:
            self.copy(*make()).wait_send()
        self.sent = []


class Gather:
    def __init__(self, place, lanes, region, first):
        self.p, self.lanes, self.region, self.first = p, lanes, region, first = place, lanes, region, first
        self.to_x, self.to_y, self.to_core = p.dev(x=1 - p.x), p.dev(y=1 - p.y), p.dev(k=1 - p.k)
        self.one, self.two = (self.to_x, self.to_y) if first == "x" else (self.to_y, self.to_x)
        n = p.n_row
        self.s = {name: lanes.take(0, n) for name in ("z", 1, 2, 3, "core")}
        self.r = {name: lanes.take(1, n) for name in ("z", 1, 2, 3, "core")}
        self.far = (p.z + n // 2) % n
        self.near = p.z + 1 - 2 * (p.z % 2)
        self.cross = (self.near + n // 2) % n
        self.to_near = p.dev(z=self.near)

    def side(self, hop):
        p = self.p
        x_side = hop in ((1, 3) if self.first == "x" else (2, 3))
        y_side = hop in ((2, 3) if self.first == "x" else (1, 3))
        return (1 - p.x if x_side else p.x), (1 - p.y if y_side else p.y)

    def at(self, hop, z, k):
        x, y = self.side(hop)
        return self.region(x, z, 1, y, k)

    def line(self, hop, k):
        x, y = self.side(hop)
        return self.region(x, 0, self.p.n_row, y, k)

    def start(self, own):
        p = self.p

        def to(hop, device):
            return lambda: (own, self.at(0, p.z, p.k), device, self.s[hop] + p.z, self.r[hop] + p.z)

        self.lanes.send(to(1, self.one))
        self.lanes.send(to(2, self.two))
        self.own = own

    def z_start(self):
        p, own = self.p, self.own
        self.lanes.send(lambda: (own, self.at(0, p.z, p.k), p.dev(z=self.far), self.s["z"], self.r["z"]))
        self.lanes.send(lambda: (own, self.at(0, p.z, p.k), p.dev(z=self.near), self.s["z"] + 1, self.r["z"] + 1))

    def z_step(self, number):
        p = self.p
        source = (self.far, self.near, self.cross)[number - 1]
        peer = self.far if number == 1 else self.near
        self.lanes.arrived(self.at(0, source, p.k), p.dev(z=peer), self.r["z"] + number - 1)

        def to(device, hop, index):
            def make():
                ref = self.at(0, source, p.k)
                return (ref, ref, device, self.s[hop] + index, self.r[hop] + index)
            return make

        if number == 1:
            self.lanes.send(to(self.to_near, "z", 2))
        self.lanes.send(to(self.one, 1, source))
        self.lanes.send(to(self.two, 2, source))

    def z_steps(self):
        for distance in range(1, self.p.n_row):
            self.z_step(distance)
        self.z_done()

    def z_done(self):
        self.local.wait()
        self.to_other_core(0)

    def to_other_core(self, hop):
        def make():
            line = self.line(hop, self.p.k)
            return (line, line, self.to_core, self.s["core"] + hop, self.r["core"] + hop)
        self.lanes.send(make)

    def first_steps(self):
        p = self.p
        for source in (p.z, self.far, self.near, self.cross):
            self.lanes.arrived(self.at(1, source, p.k), self.one, self.r[1] + source)

            def make(source=source):
                ref = self.at(1, source, p.k)
                return (ref, ref, self.two, self.s[3] + source, self.r[3] + source)

            self.lanes.send(make)
        self.to_other_core(1)

    def second_steps(self, hops=(2, 3)):
        p = self.p
        for hop in hops:
            for i in range(p.n_row):
                self.lanes.arrived(self.at(hop, i, p.k), self.two, self.r[hop] + i)
            self.to_other_core(hop)

    def stage(self, name):
        if name == "z":
            self.z_start()
        elif name == "f":
            self.first_steps()
        elif name == "s":
            self.second_steps((2,))
        elif name == "t":
            self.second_steps((3,))
        else:
            self.z_step(int(name))
            if name == "3":
                self.z_done()

    def end(self):
        for hop in range(4):
            self.lanes.arrived(self.line(hop, 1 - self.p.k), self.to_core, self.r["core"] + hop)


def rows_region(ref, n_row, low=0, high=None):
    width = ref.shape[3] // 2
    high = width if high is None else high

    def region(x, z, nz, y, k):
        columns = pl.ds(aligned(y * width + low, 128), high - low)
        if nz == 1:
            return ref.at[x * n_row + z, k, :, columns]
        return ref.at[pl.ds(x * n_row + z, nz), k, :, columns]

    return region


def lanes_region(ref, n_dp, n_row, low=0, high=None):
    width = ref.shape[3] // (n_dp * n_row)
    high = ref.shape[2] if high is None else high

    def region(x, z, nz, y, k):
        return ref.at[y, k, pl.ds(low, high - low), pl.ds(aligned((x * n_row + z) * width, 128), nz * width)]

    return region


CHUNK = 512
ROWS = 256
BATCH = (6, 6, 6, 6, 7)
FIRST = {"q": "x", "o": "y", "u": "y", "v": "y", "d": "y", "e": "y"}
DOWN, UP, OUT, JOINED = "xyx", "xyx", "y", "xyx"
SCHEDULE = {
    "first": {4: "oz uz", 5: "o1 u1 vz"},
    "turn": {0: "o2 u2 v1 dz", 2: "o3 u3 v2 d1"},
    "project": {0: "of v3 d2", 3: "uf d3", 6: "vf ez"},
    "attend": {0: "df os e1", 1: "e2", 2: "us e3", 3: "ot ut", 4: "ef", 5: "vs", 6: "vt", 7: "c1", 8: "c2 c3", 9: "ds", 11: "dt"},
    "mix": {1: "es"},
    "rise": {0: "et"},
}


def forward_kernel(
    dims, seq_ref, len_ref, tok_ref, cot_ref, qkv_ref, out_ref, up_ref, down_ref, norm_ref,
    xt_out, wqkv_out, qkv_out, ctx_out, lse_out, output_out, gm_out, dctx_out, gout_out, gup_out, part_x_out, part_y_out, nsum_out,
    tsend, half_qkv, half_out, half_up, pair_qkv, pair_out, pair_up,
    xt_v, x_v, w_v, wide_v, ctx_v, lse_v, wout_v, wup_v, wdown_v, norm_v, gains_v, cot_v, act_v, mixed_v, gsum_v, hl_v,
    output_v, down_v, attn_v, dctx_v, turn_v, nsum_v,
    tok_send, tok_recv, norm_send, norm_recv, cot_send, cot_recv, w_send, w_recv, half_send, half_recv, local_sem, out_send, out_recv, r_send, r_recv,
    *pieces,
):
    n_dp, n_row, n_col = dims
    p = Place(n_dp, n_row, n_col)
    micro, slots, _, span = tok_ref.shape
    rows, width = x_v.shape
    qkv_v = wide_v.at[:, pl.ds(0, 3 * width)]
    p.greet()
    for m in range(micro):
        for j in range(slots):
            tsend[m * slots + j] = tok_ref[m, seq_ref[m, j]]
    p.met()
    halves = Lanes(half_send, half_recv)
    lanes = Lanes(w_send, w_recv)
    partner = p.dev(k=1 - p.k)
    for i, (block, landing) in enumerate(((qkv_ref, half_qkv), (out_ref, half_out), (up_ref, half_up))):
        def make(i=i, block=block, landing=landing):
            count = landing.shape[0]
            return (block.at[pl.ds(aligned((1 - p.k) * count, 16), count), :], landing, partner, i, i)
        halves.send(make)

    def join(i, block, landing, pair):
        halves.arrived(landing, partner, i)
        count, across = landing.shape
        mine = block[pl.ds(aligned(p.k * count, 16), count), :]
        theirs = landing[...]
        pair[:, :across] = jnp.where(p.k == 0, mine, theirs)
        pair[:, across:] = jnp.where(p.k == 0, theirs, mine)

    local = []

    def keep(src, dst):
        made = pltpu.make_async_copy(src, dst, local_sem.at[len(local)])
        made.start()
        local.append(made)
        return made

    region_qkv = rows_region(w_v, n_row)
    join(0, qkv_ref, half_qkv, pair_qkv)
    own_w = keep(pair_qkv, region_qkv(p.x, p.z, 1, p.y, p.k))
    g_qkv = Gather(p, lanes, region_qkv, FIRST["q"])
    g_qkv.local = own_w
    g_qkv.start(pair_qkv)
    g_qkv.z_start()

    def tok_copy(i):
        target = (p.flat + i) % p.n
        return pltpu.make_async_remote_copy(
            src_ref=tsend.at[(target % n_col) * slots + target // n_col],
            dst_ref=xt_v.at[p.g, :, pl.ds(aligned(p.c * span, 128), span)],
            send_sem=tok_send.at[i], recv_sem=tok_recv.at[i],
            device_id=p.of_flat(target), device_id_type=MESH,
        )

    def norm_copy(i):
        return pltpu.make_async_remote_copy(
            src_ref=norm_ref, dst_ref=norm_v.at[p.flat],
            send_sem=norm_send.at[i], recv_sem=norm_recv.at[i],
            device_id=p.of_flat((p.flat + i) % p.n), device_id_type=MESH,
        )

    sent = [1]

    def tok_batch(count):
        def one(j, carry):
            tok_copy((j * 13) % p.n).start()
            return carry

        lax.fori_loop(sent[0], min(sent[0] + count, p.n), one, 0)
        sent[0] = min(sent[0] + count, p.n)

    def norm_start(i, carry):
        norm_copy(i).start()
        return carry

    tok_batch(BATCH[0])
    own_tok = keep(tsend.at[p.c * slots + p.g], xt_v.at[p.g, :, pl.ds(aligned(p.c * span, 128), span)])

    waves = []

    def wave(own, region, first):
        gather = Gather(p, lanes, region, first)
        gather.local = keep(own, region(p.x, p.z, 1, p.y, p.k))
        gather.start(own)
        waves.append(gather)

    join(1, out_ref, half_out, pair_out)
    wave(pair_out, rows_region(wout_v, n_row), FIRST["o"])
    join(2, up_ref, half_up, pair_up)
    cut = pair_up.shape[1] // 2
    wave(pair_up.at[:, pl.ds(0, cut)], rows_region(wup_v, n_row, 0, cut), FIRST["u"])
    wave(pair_up.at[:, pl.ds(cut, cut)], rows_region(wup_v, n_row, cut, 2 * cut), FIRST["v"])
    cut = down_ref.shape[0] // 2
    wave(down_ref.at[pl.ds(0, cut), :], lanes_region(wdown_v, n_dp, n_row, 0, cut), FIRST["d"])
    wave(down_ref.at[pl.ds(cut, cut), :], lanes_region(wdown_v, n_dp, n_row, cut, 2 * cut), FIRST["e"])
    lax.fori_loop(1, p.n, norm_start, 0)
    own_norm = keep(norm_ref, norm_v.at[p.flat])

    def cot_copy(i):
        target = (p.c + i) % n_col
        return pltpu.make_async_remote_copy(
            src_ref=cot_ref.at[target], dst_ref=cot_v.at[p.c],
            send_sem=cot_send.at[i], recv_sem=cot_recv.at[i],
            device_id=(p.x, p.z, target), device_id_type=MESH,
        )

    own_cot = keep(cot_ref.at[p.c], cot_v.at[p.c])
    names = dict(zip("ouvde", waves))

    def begin_cot(i):
        cot_copy(i).start()

    def agenda(phase):
        table = {}
        for turn, steps in SCHEDULE.get(phase, {}).items():
            table[turn] = [functools.partial(begin_cot, int(step[1:])) if step[0] == "c" else functools.partial(names[step[0]].stage, step[1:]) for step in steps.split()]
        return table

    first = agenda("first")

    def now(turn):
        for act in first.get(turn, ()):
            act()

    now(0)
    for distance in range(1, n_row):
        g_qkv.z_step(distance)
        tok_batch(BATCH[distance])
        now(distance)
    g_qkv.z_done()
    g_qkv.first_steps()
    tok_batch(BATCH[4])
    now(4)
    g_qkv.second_steps()
    tok_batch(p.n)
    now(5)
    own_tok.wait()

    def tok_wait(i, carry):
        source = (p.flat + p.n - i) % p.n
        landing = xt_v.at[source // n_col, :, pl.ds(aligned((source % n_col) * span, 128), span)]
        pltpu.make_async_remote_copy(
            src_ref=landing, dst_ref=landing, send_sem=tok_send.at[i], recv_sem=tok_recv.at[i],
            device_id=p.of_flat(source), device_id_type=MESH,
        ).wait_recv()
        return carry

    lax.fori_loop(1, p.n, tok_wait, 0)
    keep(xt_v, xt_out)

    def turn(i, carry):
        run_events(i, agenda("turn"))
        at = pl.ds(aligned(i * 256, 256), 256)
        x_v[at, :] = xt_v[:, :, at].reshape(width, 256).T
        return carry

    lax.fori_loop(0, rows // 256, turn, 0)
    g_qkv.end()
    keep(w_v, wqkv_out)

    def project(i, carry):
        run_events(i, agenda("project"))
        at = pl.ds(aligned(i * 256, 256), 256)
        wide_v[:, at] = product(x_v[...], w_v[:, :, :, at].reshape(width, 256)).astype(BF)
        return carry

    lax.fori_loop(0, 3 * width // 256, project, 0)
    kept_qkv = keep(qkv_v, qkv_out)
    out, up_a, up_b, down_a, down_b = waves
    length = len_ref[p.c, seq_ref[p.c, p.g]]
    bias = jnp.where(lax.broadcasted_iota(jnp.int32, (rows, 1), 0) < length, 0.0, NEGATIVE)
    chunks = rows // CHUNK

    def attend(step, carry):
        run_events(step, agenda("attend"))
        pair, at_row = step // chunks, step % chunks
        columns = [pl.ds(aligned(i * width + pair * 128, 128), 128) for i in range(3)]
        keys = wide_v[:, columns[1]]
        values_t = wide_v[:, columns[2]].T
        lane = lax.broadcasted_iota(jnp.int32, (rows, 128), 1)
        own_rows = pl.ds(aligned(at_row * CHUNK, CHUNK), CHUNK)
        queries = wide_v[own_rows, columns[0]] * jnp.asarray(0.125, BF)
        for h in range(2):
            mine = jnp.where((lane < HEAD) == (h == 0), keys, jnp.zeros_like(keys))
            scores = product_nt(mine, queries) + bias
            top = jnp.max(scores, axis=0, keepdims=True)
            exps = jnp.exp(scores - top)
            total = jnp.sum(exps, axis=0, keepdims=True)
            context = product(values_t[h * HEAD:(h + 1) * HEAD], exps.astype(BF))
            head_rows = pl.ds(aligned(pair * 128 + h * HEAD, HEAD), HEAD)
            ctx_v[head_rows, own_rows] = (context * (1.0 / total)).astype(BF)
            lse_v[2 * pair + h, :, own_rows] = top + jnp.log(total)
        return carry

    lax.fori_loop(0, width // 128 * chunks, attend, 0)
    keep(ctx_v, ctx_out)
    keep(lse_v, lse_out)

    own_norm.wait()

    def norm_wait(i, carry):
        source = (p.flat + p.n - i) % p.n
        pltpu.make_async_remote_copy(
            src_ref=norm_ref, dst_ref=norm_v.at[source], send_sem=norm_send.at[i], recv_sem=norm_recv.at[i],
            device_id=p.of_flat(source), device_id_type=MESH,
        ).wait_recv()
        return carry

    lax.fori_loop(1, p.n, norm_wait, 0)
    each = width // p.n
    gains_v[...] = jnp.zeros_like(gains_v)
    for source in range(p.n):
        low = source * each // 128 * 128
        gains_v[:, low:low + 256] += norm_v[source].astype(F32)
    gain_one, shift_one, gain_two, shift_two = (gains_v[i:i + 1, :width] for i in range(4))

    def normal(values):
        centered = values - jnp.mean(values, axis=-1, keepdims=True)
        scale = lax.rsqrt(jnp.mean(centered * centered, axis=-1, keepdims=True) + EPSILON)
        return centered * scale, scale

    def normal_back(grad, unit, scale, gain):
        grad = grad * gain
        return scale * (grad - jnp.mean(grad, axis=-1, keepdims=True) - unit * jnp.mean(grad * unit, axis=-1, keepdims=True))

    nsum_v[...] = jnp.zeros_like(nsum_v)
    whole = lambda ref: ref[...].reshape(width, -1)
    out.end()

    def mix(step, carry):
        run_events(step, agenda("mix"))
        at = pl.ds(aligned(step * ROWS, ROWS), ROWS)
        mixed = x_v[at, :].astype(F32) + product_tn(ctx_v[:, at], whole(wout_v))
        mixed_v[at, :] = mixed
        unit, _ = normal(mixed)
        hl_v[at, :] = (unit * gain_one + shift_one).astype(BF)
        return carry

    lax.fori_loop(0, rows // ROWS, mix, 0)
    up_a.end()
    up_b.end()
    kept_qkv.wait()

    def rise(step, carry):
        run_events(step, agenda("rise"))
        at = pl.ds(aligned(step * 256, 256), 256)
        pre = product(hl_v[...], wup_v[:, :, :, at].reshape(width, 256))
        half = 0.5 * (1.0 + lax.erf(pre * ROOT_HALF))
        act_v[:, at] = (pre * half).astype(BF)
        wide_v[:, at] = (half + pre * jnp.exp(pre * pre * -0.5) * ROOT_TWO_PI).astype(BF)
        return carry

    lax.fori_loop(0, 4 * width // 256, rise, 0)
    down_a.end()
    down_b.end()
    for i in range(1, n_col):
        source = (p.c + n_col - i) % n_col
        pltpu.make_async_remote_copy(
            src_ref=cot_v.at[source], dst_ref=cot_v.at[source],
            send_sem=cot_send.at[i], recv_sem=cot_recv.at[i],
            device_id=(p.x, p.z, source), device_id_type=MESH,
        ).wait_recv()
    own_cot.wait()

    def out_copy(target):
        return pltpu.make_async_remote_copy(
            src_ref=output_v.at[pl.ds(aligned(target * span, 16), span), :], dst_ref=output_out.at[p.c],
            send_sem=out_send.at[target], recv_sem=out_recv.at[p.c],
            device_id=(p.x, p.z, target), device_id_type=MESH,
        )

    def fall(step, carry):
        at = pl.ds(aligned(step * ROWS, ROWS), ROWS)
        unit_one, _ = normal(mixed_v[at, :])
        summed = unit_one * gain_one + shift_one + product_nt(act_v[at, :], whole(wdown_v))
        unit, scale = normal(summed)
        output_v[at, :] = (unit * gain_two + shift_two).astype(BF)
        per = span // ROWS
        cot = cot_v[step // per, pl.ds(aligned(step % per * ROWS, ROWS), ROWS), :].astype(F32)
        nsum_v[2:3, :] += jnp.sum(cot * unit, axis=0, keepdims=True)
        nsum_v[3:4, :] += jnp.sum(cot, axis=0, keepdims=True)
        grad = normal_back(cot, unit, scale, gain_two)
        gsum_v[at, :] = grad
        down_v[at, :] = grad.astype(BF)
        turn_v[:, at] = grad.T.astype(BF)
        target = step // per

        @pl.when((step % per == per - 1) & (target != p.c))
        def _():
            out_copy(target).start()
        return carry

    lax.fori_loop(0, rows // ROWS, fall, 0)
    keep(output_v.at[pl.ds(aligned(p.c * span, 16), span), :], output_out.at[p.c])

    def rise_back(step, carry):
        at = pl.ds(aligned(step * 512, 512), 512)
        back = product(down_v[...], wdown_v[:, :, :, at].reshape(width, 512))
        wide_v[:, at] = (back * wide_v[:, at].astype(F32)).astype(BF)
        return carry

    lax.fori_loop(0, 4 * width // 512, rise_back, 0)
    lanes.finish()

    def grad_down(step, carry):
        at = pl.ds(aligned(step * 512, 512), 512)
        wdown_v[:, :, :, at] = product(turn_v[...], act_v[:, at]).astype(BF).reshape(wdown_v.shape[:3] + (512,))
        return carry

    lax.fori_loop(0, 4 * width // 512, grad_down, 0)

    rlanes = Lanes(r_send, r_recv)
    early = []
    piece_rows = wdown_v.shape[2] // len(DOWN)
    for i, axis in enumerate(DOWN):
        at = pl.ds(i * piece_rows, piece_rows)
        piece = Reduce(
            p, rlanes, wdown_v.at[:, 1 - p.k, at], wdown_v.at[:, p.k, at], pieces[2 * i:2 * i + 2] + (None, None, None), "lanes", axis
        )
        piece.start()
        early.append(piece)

    def mix_back(step, carry):
        run_events(step, {1: (early[0].one, early[1].one), 2: (early[2].one,)})
        at = pl.ds(aligned(step * ROWS, ROWS), ROWS)
        grad = gsum_v[at, :] + product_nt(wide_v[at, :], whole(wup_v))
        unit, scale = normal(mixed_v[at, :])
        nsum_v[0:1, :] += jnp.sum(grad * unit, axis=0, keepdims=True)
        nsum_v[1:2, :] += jnp.sum(grad, axis=0, keepdims=True)
        grad = normal_back(grad, unit, scale, gain_one)
        gsum_v[at, :] = grad
        low = grad.astype(BF)
        attn_v[at, :] = low
        dctx_v[at, :] = product_nt(low, whole(wout_v)).astype(BF)
        turn_v[:, at] = hl_v[at, :].T
        return carry

    lax.fori_loop(0, rows // ROWS, mix_back, 0)
    keep(gsum_v, gm_out)
    keep(dctx_v, dctx_out)
    keep(nsum_v, nsum_out)

    def grad_up(step, carry):
        at = pl.ds(aligned(step * 512, 512), 512)
        wup_v[:, :, :, at] = product(turn_v[...], wide_v[:, at]).astype(BF).reshape(wup_v.shape[:3] + (512,))
        return carry

    lax.fori_loop(0, 4 * width // 512, grad_up, 0)
    keep(wup_v, gup_out)

    def grad_out(step, carry):
        at = pl.ds(aligned(step * 256, 256), 256)
        wout_v[:, :, :, at] = product(ctx_v[...], attn_v[:, at]).astype(BF).reshape(wout_v.shape[:3] + (256,))
        return carry

    lax.fori_loop(0, width // 256, grad_out, 0)
    keep(wout_v, gout_out)
    outs = {"x": [part_x_out.at[i] for i in range(DOWN.count("x"))], "y": [part_y_out.at[i] for i in range(DOWN.count("y"))]}
    for piece, axis in zip(early, DOWN):
        piece.add_half(1)
        keep(piece.b[1], outs[axis].pop(0))

    def small_wait(i, carry):
        norm_copy(i).wait_send()
        tok_copy(i).wait_send()
        return carry

    lax.fori_loop(1, p.n, small_wait, 0)
    for i in range(1, n_col):
        cot_copy(i).wait_send()
        source = (p.c + n_col - i) % n_col
        pltpu.make_async_remote_copy(
            src_ref=output_out.at[source], dst_ref=output_out.at[source],
            send_sem=out_send.at[source], recv_sem=out_recv.at[source],
            device_id=(p.x, p.z, source), device_id_type=MESH,
        ).wait_recv()
        out_copy((p.c + i) % n_col).wait_send()
    waited = [own_tok, own_norm, own_w, own_cot, kept_qkv] + [gather.local for gather in waves]
    for made in local:
        if not any(made is w for w in waited):
            made.wait()
    halves.finish()
    rlanes.finish()


def run_events(step, events):
    for when_, acts in events.items():
        def act(acts=acts):
            for a in acts:
                a()
        pl.when(step == when_)(act)


def forward(dims, seq_order, lengths, tok_t, cot, w_qkv, w_out, w_up, w_down_t, norms):
    n_dp, n_row, n_col = dims
    groups, n = n_dp * n_row, n_dp * n_row * n_col
    micro, slots, feats, span = tok_t.shape
    rows, width = n_col * span, groups * feats
    heads = width // HEAD
    qr, qc = w_qkv.shape
    orow, oc = w_out.shape
    ur, uc = w_up.shape
    dr, dc = w_down_t.shape
    shape = jax.ShapeDtypeStruct
    joined = (groups, 2, qr // 2, qc * n_col)
    out_all = (groups, 2, orow // 2, oc * n_col)
    up_all = (groups, 2, ur // 2, uc * n_col)
    down_all = (2, 2, dr, dc * groups)
    outs = (
        shape((groups, feats, rows), BF),
        shape(joined, BF),
        shape((rows, 3 * width), BF),
        shape((width, rows), BF),
        shape((heads, 1, rows), F32),
        shape((n_col, span, width), BF),
        shape((rows, width), F32),
        shape((rows, width), BF),
        shape(out_all, BF),
        shape(up_all, BF),
        shape((DOWN.count("x"), 2, dr // len(DOWN), dc * groups // 2), BF),
        shape((DOWN.count("y"), dr // len(DOWN), dc * groups), BF),
        shape((8, width), F32),
    )
    vm = pltpu.VMEM
    early_buffers = [
        vm(size, BF) for axis in DOWN for size in piece_buffers("lanes", axis, 0, dr // len(DOWN), dc * groups, n_row, groups)[:2]
    ]
    return pl.pallas_call(
        functools.partial(forward_kernel, dims),
        out_shape=outs,
        in_specs=[SM, SM, VM, ANY, VM, VM, VM, VM, VM],
        out_specs=[ANY] * len(outs),
        scratch_shapes=[
            vm((micro * slots, feats, span), BF),
            vm((qr // 2, qc), BF), vm((orow // 2, oc), BF), vm((ur // 2, uc), BF),
            vm((qr // 2, qc * 2), BF), vm((orow // 2, oc * 2), BF), vm((ur // 2, uc * 2), BF),
            vm((groups, feats, rows), BF),
            vm((rows, width), BF),
            vm(joined, BF),
            vm((rows, 4 * width), BF),
            vm((width, rows), BF),
            vm((heads, 1, rows), F32),
            vm(out_all, BF), vm(up_all, BF), vm(down_all, BF),
            vm((n,) + norms.shape, BF),
            vm((norms.shape[0], width + 256), F32),
            vm(cot.shape, BF),
            vm((rows, 4 * width), BF),
            vm((rows, width), F32), vm((rows, width), F32),
            vm((rows, width), BF), vm((rows, width), BF), vm((rows, width), BF), vm((rows, width), BF), vm((rows, width), BF),
            vm((width, rows), BF),
            vm((8, width), F32),
            DMA((n,)), DMA((n,)), DMA((n,)), DMA((n,)), DMA((n_col,)), DMA((n_col,)),
            DMA((6 * 5 * n_row,)), DMA((6 * 5 * n_row,)), DMA((3,)), DMA((3,)), DMA((24,)), DMA((n_col,)), DMA((n_col,)),
            DMA((24,)), DMA((24,)), *early_buffers,
        ],
        compiler_params=pltpu.CompilerParams(
            collective_id=0, has_side_effects=True, vmem_limit_bytes=63 * 2**20
        ),
        name="forward_part",
    )(seq_order, lengths, tok_t, cot, w_qkv, w_out, w_up, w_down_t, norms)


BACK_CHUNK = 256
SUMS = {
    0: "u20 o00", 1: "u01 u11", 3: "u21 d13", 4: "d03", 6: "d23 d14", 7: "d04", 8: "a0 u02", 9: "o01 d24 d15", 10: "a1 d05",
    12: "u12 d25", 14: "u22 u03", 16: "b0", 17: "u13 u04", 18: "o02 b1", 20: "u14 u05", 21: "a2 u23", 22: "u15", 23: "o03",
}
PACE = "0-16 | c1 a3 b2 u24 o04 | 16-32 | c2 a4 b3 c3 b4 c4"
LATE = "o05 u25"


def add_into(target, term):
    shape = target.shape
    if len(shape) == 2:
        target[...] = (target[...].astype(F32) + term[...].astype(F32)).astype(BF)
        return

    def body(i, carry):
        target[i] = (target[i].astype(F32) + term[i].astype(F32)).astype(BF)
        return carry

    lax.fori_loop(0, shape[0], body, 0)


class Reduce:
    def __init__(self, place, lanes, theirs, mine, buffers, kind, first):
        self.p, self.lanes, self.theirs, self.mine, self.b = place, lanes, theirs, mine, buffers
        self.kind, self.axes = kind, ("x", "y") if first == "x" else ("y", "x")
        self.s = [lanes.take(0, 1) for _ in range(3)] + [lanes.take(0, 3)]
        self.r = [lanes.take(1, 1) for _ in range(3)] + [lanes.take(1, 3)]
        n = place.n_row
        self.far = (place.z + n // 2) % n
        self.near = place.z + 1 - 2 * (place.z % 2)
        self.cross = (self.near + n // 2) % n

    def start(self):
        p = self.p
        self.lanes.send(lambda: (self.theirs, self.b[0], p.dev(k=1 - p.k), self.s[0], self.r[0]))

    def half(self, ref, axis, side):
        if self.kind == "lanes" and axis == "y":
            return ref.at[side]
        if self.kind == "rows" and axis == "x":
            count = ref.shape[0] // 2
            return ref.at[pl.ds(side * count, count)]
        width = ref.shape[-1] // 2
        lead = (slice(None),) * (len(ref.shape) - 1)
        return ref.at[lead + (pl.ds(aligned(side * width, 128), width),)]

    def where(self, axis):
        p = self.p
        return (p.x, p.dev(x=1 - p.x)) if axis == "x" else (p.y, p.dev(y=1 - p.y))

    def send_half(self, stage):
        def make():
            side, peer = self.where(self.axes[stage - 1])
            return (self.half(self.b[stage - 1], self.axes[stage - 1], 1 - side), self.b[stage], peer, self.s[stage], self.r[stage])

        self.lanes.send(make)

    def add_half(self, stage):
        side, peer = self.where(self.axes[stage - 1])
        self.lanes.arrived(self.b[stage], peer, self.r[stage])
        add_into(self.b[stage], self.half(self.b[stage - 1], self.axes[stage - 1], side))

    def one(self):
        p = self.p
        self.lanes.arrived(self.b[0], p.dev(k=1 - p.k), self.r[0])
        add_into(self.b[0], self.mine)
        self.send_half(1)

    def two(self):
        self.add_half(1)
        self.send_half(2)

    def part(self, z):
        ref = self.b[2]
        if self.kind == "rows":
            return ref.at[z]
        width = self.b[3].shape[-1]
        return ref.at[:, pl.ds(aligned(z * width, 128), width)]

    def three(self):
        p = self.p
        self.add_half(2)
        for i, target in enumerate((self.cross, self.near)):
            def make(i=i, target=target):
                return (self.part(target), self.b[3].at[1 - i], p.dev(z=self.near), self.s[3] + i, self.r[3] + i)
            self.lanes.send(make)

    def four(self):
        p = self.p
        self.lanes.arrived(self.b[3].at[1], p.dev(z=self.near), self.r[3])
        add_into(self.b[3].at[1], self.part(self.far))
        self.lanes.send(lambda: (self.b[3].at[1], self.b[4], p.dev(z=self.far), self.s[3] + 2, self.r[3] + 2))

    def five(self):
        p = self.p
        self.lanes.arrived(self.b[3].at[0], p.dev(z=self.near), self.r[3] + 1)
        total = self.part(p.z)[...].astype(F32) + self.b[3][0].astype(F32)
        self.lanes.arrived(self.b[4], p.dev(z=self.far), self.r[3] + 2)
        return total + self.b[4][...].astype(F32)


def piece_buffers(kind, first, lead, rows, columns, n_row, groups):
    if kind == "lanes":
        one = (2, rows, columns // 2) if first == "x" else (rows, columns)
        return [(2, rows, columns), one, (rows, columns // 2), (2, rows, columns // groups), (rows, columns // groups)]
    one = (lead // 2, rows, columns) if first == "x" else (lead, rows, columns // 2)
    return [(lead, rows, columns), one, (lead // 2, rows, columns // 2), (2, rows, columns // 2), (rows, columns // 2)]


def backward_kernel(
    dims, plan, seq_ref, qkv_ref, ctx_ref, lse_ref, dctx_ref, xt_ref, w_ref, gm_ref, gout_ref, gup_ref, part_x_ref, part_y_ref,
    ngrad_ref, tgrad_ref, rqkv_ref, rout_ref, rup_ref, rdown_ref, nsum_ref, *scratch,
):
    n_dp, n_row, n_col = dims
    p = Place(n_dp, n_row, n_col)
    groups = n_dp * n_row
    (
        qkv_v, ctx_v, lse_v, dctx_v, xt_v, w_v, gm_v, m_out, m_up, ga_v, gb_v, gc_v, dqt_v, dk_v, dv_v, acc_k, acc_v, dxt_v, trecv,
        nrecv, fq, fo, fu, tok_send, tok_recv, norm_send, norm_recv, w_send, w_recv, local_sem,
    ) = scratch[:30]
    pieces = scratch[30:]
    micro, slots, _, span = tgrad_ref.shape
    width, rows = ctx_ref.shape
    p.greet()
    local = []

    def keep(src, dst):
        made = pltpu.make_async_copy(src, dst, local_sem.at[len(local)])
        made.start()
        local.append(made)
        return made

    needed = [keep(qkv_ref, qkv_v), keep(dctx_ref, dctx_v), keep(ctx_ref, ctx_v), keep(lse_ref, lse_v)]
    mine_up = keep(gup_ref.at[:, p.k], m_up)
    mine_out = keep(gout_ref.at[:, p.k], m_out)
    xt_load = keep(xt_ref, xt_v)
    later = [keep(w_ref, w_v), keep(gm_ref, gm_v)]
    p.met()
    lanes = Lanes(w_send, w_recv)
    partner = p.dev(k=1 - p.k)
    waves = {"down": [], "up": [], "out": [], "a": [], "b": [], "c": []}
    parts = []
    made_here = {"a": ga_v, "b": gb_v, "c": gc_v}
    whole = {"up": gup_ref, "out": gout_ref, **made_here}
    carried = {"up": m_up, "out": m_out}
    sources = {"x": [part_x_ref.at[i] for i in range(DOWN.count("x"))], "y": [part_y_ref.at[i] for i in range(DOWN.count("y"))]}
    for index, (name, kind, first, low, count) in enumerate(plan):
        if name == "down":
            piece = Reduce(p, lanes, None, None, pieces[5 * index:5 * index + 5], kind, first)
            parts.append(keep(sources[first].pop(0), piece.b[1]))
            waves["down"].append(piece)
            continue
        at = pl.ds(low, count)
        theirs = whole[name].at[:, 1 - p.k, at]
        mine = made_here[name].at[:, p.k, at] if name in made_here else carried[name].at[:, at]
        waves[name].append(Reduce(p, lanes, theirs, mine, pieces[5 * index:5 * index + 5], kind, first))
    d, u, o = waves["down"], waves["up"], waves["out"]
    joined = [waves[name][0] for name in "abc"]

    def norm_copy(i):
        target = (p.flat + i) % p.n
        return pltpu.make_async_remote_copy(
            src_ref=ngrad_ref.at[target], dst_ref=nrecv.at[p.flat],
            send_sem=norm_send.at[i], recv_sem=norm_recv.at[i],
            device_id=p.of_flat(target), device_id_type=MESH,
        )

    def norm_start(i, carry):
        norm_copy(i).start()
        return carry

    u[0].start()
    u[1].start()
    for made, piece in zip(parts, d):
        made.wait()
        piece.send_half(2)
    lax.fori_loop(1, p.n, norm_start, 0)
    nrecv[p.flat] = ngrad_ref[p.flat]
    for made in needed:
        made.wait()
    mine_up.wait()
    mine_out.wait()

    def finish_rows(piece, temp, result, low):
        total = piece()
        count, across = total.shape[0], total.shape[1] // 2
        half_rows = result.shape[0] // 2
        temp[pl.ds(low, count), :] = jnp.where(p.k == 0, total[:, across:], total[:, :across])
        result[pl.ds(aligned(p.k * half_rows + low, 16), count), :] = jnp.where(p.k == 0, total[:, :across], total[:, across:])
        s, r = lanes.take(0, 1), lanes.take(1, 1)
        place = lambda k: result.at[pl.ds(aligned(k * half_rows + low, 16), count), :]
        lanes.send(lambda: (temp.at[pl.ds(low, count), :], place(p.k), partner, s, r))
        ends.append(lambda: lanes.arrived(place(1 - p.k), partner, r))

    ends = []

    def finish_down(piece, low):
        total = piece.five()
        rdown_ref[pl.ds(low, total.shape[0]), :] = total

    lows = {name: [low for other, _, _, low, _ in plan if other == name] for name in waves}
    down_end = [functools.partial(finish_down, piece, low) for piece, low in zip(d, lows["down"])]
    up_end = [functools.partial(finish_rows, piece.five, fu, rup_ref, low) for piece, low in zip(u, lows["up"])]
    out_end = [functools.partial(finish_rows, piece.five, fo, rout_ref, low) for piece, low in zip(o, lows["out"])]

    def joined_total():
        blocks = [[total[:, i * 128:(i + 1) * 128] for i in range(3)] for total in (piece.five() for piece in joined)]
        middle = [piece[1] for piece in blocks]
        queries = [piece[0] for piece in blocks] + middle + [piece[2] for piece in blocks]
        return jnp.concatenate(queries, axis=1)

    def joined_end():
        finish_rows(joined_total, fq, rqkv_ref, 0)

    xt = lambda: xt_v[...].reshape(width, rows)
    pairs = width // 128

    def grad_part(grad, number):
        near, far = number, number + pairs // 2
        columns = lambda pair: slice(pair * 128, pair * 128 + 128)
        terms = (
            lambda: product_nt(xt(), dqt_v[columns(near), :]), lambda: product_nt(xt(), dqt_v[columns(far), :]),
            lambda: product(xt(), dk_v[:, columns(near)]), lambda: product(xt(), dk_v[:, columns(far)]),
            lambda: product(xt(), dv_v[:, columns(near)]), lambda: product(xt(), dv_v[:, columns(far)]),
        )
        for i, term in enumerate(terms):
            grad[:, :, :, columns(i)] = term().astype(BF).reshape(groups, 2, -1, 128)
        joined[number].start()

    def first_part():
        xt_load.wait()
        grad_part(ga_v, 0)

    table = {
        letter + str(i) + str(stage): act
        for letter, group, ends_ in (("d", d, down_end), ("u", u, up_end), ("o", o, out_end))
        for i, (piece, end) in enumerate(zip(group, ends_))
        for stage, act in enumerate((piece.start, piece.one, piece.two, piece.three, piece.four, end))
    }
    for letter, piece in zip("abc", joined):
        for stage, act in enumerate((piece.one, piece.two, piece.three, piece.four)):
            table[letter + str(stage + 1)] = act
    table.update({"a0": first_part, "b0": functools.partial(grad_part, gb_v, 1), "c0": functools.partial(grad_part, gc_v, 2)})
    events = {turn: [table[step] for step in steps.split()] for turn, steps in SUMS.items()}
    length_bias = jnp.where(lax.broadcasted_iota(jnp.int32, (rows, 1), 0) < seq_ref[1, p.c, seq_ref[0, p.c, p.g]], 0.0, NEGATIVE)
    chunks = rows // BACK_CHUNK

    def attend(step, carry):
        for when_, acts in events.items():
            def act(acts=acts):
                for a in acts:
                    a()
            pl.when(step == when_)(act)
        turn, at_row = step // chunks, step % chunks
        pair = turn % 2 * (pairs // 2) + turn // 2
        columns = [pl.ds(aligned(i * width + pair * 128, 128), 128) for i in range(3)]
        keys, values = qkv_v[:, columns[1]], qkv_v[:, columns[2]]
        keys_t = keys.T
        lane = lax.broadcasted_iota(jnp.int32, (rows, 128), 1)
        short = lax.broadcasted_iota(jnp.int32, (BACK_CHUNK, 128), 1)
        own_rows = pl.ds(aligned(at_row * BACK_CHUNK, BACK_CHUNK), BACK_CHUNK)
        queries = qkv_v[own_rows, columns[0]] * jnp.asarray(0.125, BF)
        back = dctx_v[own_rows, columns[0]]
        back_t = back.T.astype(F32)
        forth_t = ctx_v[pl.ds(aligned(pair * 128, 128), 128), own_rows].astype(F32)
        both = back_t * forth_t
        d_keys = d_values = None
        for h in range(2):
            def own(block, index):
                return jnp.where((index < HEAD) == (h == 0), block, jnp.zeros_like(block))
            delta = jnp.sum(both[h * HEAD:(h + 1) * HEAD], axis=0, keepdims=True)
            scores = product_nt(own(keys, lane), queries) + length_bias
            soft = jnp.exp(scores - lse_v[2 * pair + h, :, own_rows])
            d_probs = product_nt(own(values, lane), back)
            d_scores = (soft * (d_probs - delta)).astype(BF)
            head_rows = pl.ds(aligned(pair * 128 + h * HEAD, HEAD), HEAD)
            dqt_v[head_rows, own_rows] = (product(keys_t[h * HEAD:(h + 1) * HEAD], d_scores) * 0.125).astype(BF)
            to_values = product(soft.astype(BF), own(back, short))
            to_keys = product(d_scores, own(queries, short))
            d_values = to_values if d_values is None else d_values + to_values
            d_keys = to_keys if d_keys is None else d_keys + to_keys

        @pl.when(at_row == 0)
        def _():
            acc_k[...] = d_keys
            acc_v[...] = d_values

        @pl.when(at_row > 0)
        def _():
            acc_k[...] += d_keys
            acc_v[...] += d_values

        @pl.when(at_row == chunks - 1)
        def _():
            dk_v[:, columns[0]] = acc_k[...].astype(BF)
            dv_v[:, columns[0]] = acc_v[...].astype(BF)
        return carry

    lax.fori_loop(0, width // 128 * chunks, attend, 0)
    for made in later:
        made.wait()

    def tok_copy(target):
        return pltpu.make_async_remote_copy(
            src_ref=dxt_v.at[target // n_col, :, pl.ds(aligned((target % n_col) * span, 128), span)],
            dst_ref=trecv.at[p.c * slots + p.g],
            send_sem=tok_send.at[target], recv_sem=tok_recv.at[p.flat],
            device_id=p.of_flat(target), device_id_type=MESH,
        )

    half_groups = groups // 2
    half_width = width // 2

    def tok_batch(part, low, high):
        def one(i, carry):
            target = part * half_groups * n_col + (p.flat + i * 5) % (half_groups * n_col)

            @pl.when(target != p.flat)
            def _():
                tok_copy(target).start()
            return carry

        lax.fori_loop(low, high, one, 0)

    def grad_input(part):
        near = pl.ds(part * half_groups, half_groups)
        w_rows = lambda i: w_v[near, :, :, i * width:(i + 1) * width].reshape(half_width, width)
        total = gm_v[:, part * half_width:(part + 1) * half_width].T
        total = total + product(w_rows(0), dqt_v[...])
        total = total + product_nt(w_rows(1), dk_v[...])
        total = total + product_nt(w_rows(2), dv_v[...])
        dxt_v[near] = total.astype(BF).reshape(half_groups, width // groups, rows)

    count = half_groups * n_col
    table["c0"]()
    grad_input(0)
    made_parts = 1
    for step in PACE.replace("|", " ").split():
        if "-" not in step:
            table[step]()
            continue
        low, high = (int(number) for number in step.split("-"))
        if high > count and made_parts == 1:
            grad_input(1)
            made_parts = 2
            own_tok = keep(dxt_v.at[p.g, :, pl.ds(aligned(p.c * span, 128), span)], trecv.at[p.c * slots + p.g])
        for part in range(2):
            first, last = max(low, part * count) - part * count, min(high, part * count + count) - part * count
            if first < last:
                tok_batch(part, first, last)
    for step in LATE.split():
        table[step]()

    def norm_wait(i, carry):
        source = (p.flat + p.n - i) % p.n
        pltpu.make_async_remote_copy(
            src_ref=nrecv.at[source], dst_ref=nrecv.at[source], send_sem=norm_send.at[i], recv_sem=norm_recv.at[i],
            device_id=p.of_flat(source), device_id_type=MESH,
        ).wait_recv()
        norm_copy(i).wait_send()
        return carry

    lax.fori_loop(1, p.n, norm_wait, 0)
    nsum_ref[...] = jnp.sum(nrecv[...], axis=0)
    joined_end()
    own_tok.wait()

    def tok_wait(i, carry):
        source = (p.flat + p.n - i) % p.n
        landing = trecv.at[(source % n_col) * slots + source // n_col]
        pltpu.make_async_remote_copy(
            src_ref=landing, dst_ref=landing, send_sem=tok_send.at[source], recv_sem=tok_recv.at[source],
            device_id=p.of_flat(source), device_id_type=MESH,
        ).wait_recv()
        tok_copy((p.flat + i) % p.n).wait_send()
        return carry

    lax.fori_loop(1, p.n, tok_wait, 0)
    for m in range(micro):
        for s in range(slots):
            place = jnp.int32(0)
            for j in range(slots):
                place = jnp.where(seq_ref[0, m, j] == s, jnp.int32(j), place)
            tgrad_ref[m, s] = trecv[m * slots + place]
    for end in ends:
        end()
    lanes.finish()


def backward(dims, seq_order, lengths, qkv, ctx_t, lse, d_context, xt, w_qkv, g_mixed, g_out, g_up, part_x, part_y, n_grads):
    n_dp, n_row, n_col = dims
    groups, n = n_dp * n_row, n_dp * n_row * n_col
    micro, slots = seq_order.shape
    width, rows = ctx_t.shape
    feats, span = width // groups, rows // n_col
    shape = jax.ShapeDtypeStruct
    plan, buffers = [], []
    for name, grad, kind, axes in (
        ("down", part_y, "lanes", DOWN), ("up", g_up, "rows", UP), ("out", g_out, "rows", OUT),
        *((letter, g_out, "rows", axis) for letter, axis in zip("abc", JOINED)),
    ):
        if name == "down":
            lead, each, columns = 2, part_y.shape[1], part_y.shape[2]
        else:
            lead, _, across, columns = grad.shape
            each = across // len(axes)
        for i, axis in enumerate(axes):
            plan.append((name, kind, axis, i * each, each))
            sizes = piece_buffers(kind, axis, lead, each, columns, n_row, groups)
            if name == "down":
                sizes[0] = (16, 128)
            buffers += [pltpu.VMEM(size, BF) for size in sizes]
    outs = (
        shape((micro, slots, feats, span), BF),
        shape((w_qkv.shape[2] * 2, w_qkv.shape[3] // n_col), F32),
        shape((g_out.shape[2] * 2, g_out.shape[3] // n_col), F32),
        shape((g_up.shape[2] * 2, g_up.shape[3] // n_col), F32),
        shape((len(DOWN) * part_y.shape[1], part_y.shape[2] // groups), F32),
        shape(n_grads.shape[1:], F32),
    )
    vm = lambda like, kind=BF: pltpu.VMEM(like.shape, kind)
    temps = [pltpu.VMEM((g.shape[2], g.shape[3] // n_col), F32) for g in (w_qkv, g_out, g_up)]
    carried = [pltpu.VMEM((g.shape[0],) + g.shape[2:], BF) for g in (g_out, g_up)]
    return pl.pallas_call(
        functools.partial(backward_kernel, dims, plan),
        out_shape=outs,
        in_specs=[SM, ANY, ANY, ANY, ANY, ANY, ANY, ANY, ANY, ANY, ANY, ANY, VM],
        out_specs=[VM, VM, VM, VM, VM, VM],
        scratch_shapes=[
            vm(qkv), vm(ctx_t), vm(lse, F32), vm(d_context), vm(xt), vm(w_qkv), vm(g_mixed, F32), *carried, vm(g_out), vm(g_out), vm(g_out),
            pltpu.VMEM((width, rows), BF), pltpu.VMEM((rows, width), BF), pltpu.VMEM((rows, width), BF),
            pltpu.VMEM((rows, 128), F32), pltpu.VMEM((rows, 128), F32),
            pltpu.VMEM((groups, feats, rows), BF), pltpu.VMEM((micro * slots, feats, span), BF),
            vm(n_grads, F32), *temps,
            DMA((n,)), DMA((n,)), DMA((n,)), DMA((n,)),
            DMA((80,)), DMA((80,)), DMA((16,)), *buffers,
        ],
        compiler_params=pltpu.CompilerParams(
            collective_id=1, has_side_effects=True, vmem_limit_bytes=62 * 2**20
        ),
        name="backward_part",
    )(jnp.stack([seq_order, lengths]), qkv, ctx_t, lse, d_context, xt, w_qkv, g_mixed, g_out, g_up, part_x, part_y, n_grads)
def layer_norm(values, factor, offset):
    average = jnp.mean(values, axis=-1, keepdims=True)
    centered = values - average
    variance = jnp.mean(centered * centered, axis=-1, keepdims=True)
    return centered * lax.rsqrt(variance + EPSILON) * factor + offset


def gelu_act(values):
    return 0.5 * values * (1.0 + lax.erf(values * ROOT_HALF))


def attention(qkv, length):
    rows, width = qkv.shape[0], qkv.shape[1] // 3
    heads = width // HEAD
    q, k, v = (qkv[:, i * width:(i + 1) * width].reshape(rows, heads, HEAD) for i in range(3))
    scores = jnp.einsum("qhe,khe->hqk", q, k, preferred_element_type=F32) * 0.125
    valid = jnp.arange(rows, dtype=jnp.int32) < length
    scores = jnp.where(valid[None, None, :], scores, NEGATIVE)
    top = jnp.max(scores, axis=-1, keepdims=True)
    exps = jnp.exp(scores - top)
    total = jnp.sum(exps, axis=-1, keepdims=True)
    probs = (exps / total).astype(BF)
    context = jnp.einsum("hqk,khe->qhe", probs, v, preferred_element_type=F32)
    return context.astype(BF).reshape(rows, width), top + jnp.log(total)


def attention_back(qkv, length, stats, d_context):
    rows, width = qkv.shape[0], qkv.shape[1] // 3
    heads = width // HEAD
    q, k, v = (qkv[:, i * width:(i + 1) * width].reshape(rows, heads, HEAD) for i in range(3))
    dc = d_context.reshape(rows, heads, HEAD)
    scores = jnp.einsum("qhe,khe->hqk", q, k, preferred_element_type=F32) * 0.125
    valid = jnp.arange(rows, dtype=jnp.int32) < length
    scores = jnp.where(valid[None, None, :], scores, NEGATIVE)
    soft = jnp.exp(scores - stats)
    d_probs = jnp.einsum("qhe,khe->hqk", dc, v, preferred_element_type=F32)
    delta = jnp.sum(soft * d_probs, axis=-1, keepdims=True)
    d_scores = (soft * (d_probs - delta)).astype(BF)
    dq = jnp.einsum("hqk,khe->qhe", d_scores, k, preferred_element_type=F32) * 0.125
    dk = jnp.einsum("hqk,qhe->khe", d_scores, q, preferred_element_type=F32) * 0.125
    dv = jnp.einsum("hqk,qhe->khe", soft.astype(BF), dc, preferred_element_type=F32)
    return jnp.concatenate([a.astype(BF).reshape(rows, width) for a in (dq, dk, dv)], axis=-1)


def middle(x, context, context_t, cot, w_out, w_up, w_down_t, gain_one, shift_one, gain_two, shift_two):
    mixed = x.astype(F32) + product(context, w_out)
    hidden = layer_norm(mixed, gain_one, shift_one)
    hidden_low = hidden.astype(BF)
    pre_act = product(hidden_low, w_up)
    act_low = gelu_act(pre_act).astype(BF)
    summed = hidden + product_nt(act_low, w_down_t)
    output = layer_norm(summed, gain_two, shift_two).astype(BF)
    _, norm_two_back = jax.vjp(layer_norm, summed, gain_two, shift_two)
    g_summed, g_gain_two, g_shift_two = norm_two_back(cot.astype(F32))
    d_down = g_summed.astype(BF)
    g_down_t = product_tn(d_down, act_low).astype(BF)
    d_act = product(d_down, w_down_t)
    _, gelu_back = jax.vjp(gelu_act, pre_act)
    d_pre = gelu_back(d_act)[0].astype(BF)
    g_up = product_tn(hidden_low, d_pre).astype(BF)
    g_hidden = g_summed + product_nt(d_pre, w_up)
    _, norm_one_back = jax.vjp(layer_norm, mixed, gain_one, shift_one)
    g_mixed, g_gain_one, g_shift_one = norm_one_back(g_hidden)
    d_attn = g_mixed.astype(BF)
    g_out = product(context_t, d_attn).astype(BF)
    d_context = product_nt(d_attn, w_out).astype(BF)
    return output, g_mixed, d_context, g_down_t, g_up, g_out, (g_gain_one, g_shift_one, g_gain_two, g_shift_two)


def take_blocks(blocks, places):
    def body(place_ref, in_ref, out_ref):
        def step(i, carry):
            out_ref[i] = in_ref[place_ref[i]]
            return carry

        lax.fori_loop(0, blocks.shape[0], step, 0)

    return pl.pallas_call(
        body, out_shape=jax.ShapeDtypeStruct(blocks.shape, blocks.dtype), in_specs=[SM, VM], out_specs=VM,
        compiler_params=pltpu.CompilerParams(vmem_limit_bytes=48 * 2**20), name="take_blocks",
    )(places, blocks)


def own_length(lengths, seq_order):
    n_row = lax.axis_size("row")
    slot = lax.axis_index("dp") * n_row + lax.axis_index("row")
    micro = lax.axis_index("col")
    index = jnp.arange(seq_order.shape[1], dtype=jnp.int32)
    order = jnp.sum(jnp.where(jnp.arange(seq_order.shape[0])[:, None] == micro, seq_order, 0), axis=0)
    source = jnp.sum(jnp.where(index == slot, order, 0))
    mine = jnp.sum(jnp.where(jnp.arange(seq_order.shape[0])[:, None] == micro, lengths, 0), axis=0)
    return jnp.sum(jnp.where(index == source, mine, 0))


def local(
    tokens, cotangent, lengths, seq_order, w_qkv, w_out, w_up, w_down, gain_one, shift_one, gain_two, shift_two,
):
    dims = tuple(lax.axis_size(a) for a in ("dp", "row", "col"))
    n_dp, n_row, n_col = dims
    groups = n_dp * n_row
    micro, slots, span, feats = tokens.shape
    width = cotangent.shape[3]
    rows = span * n_col
    direct = n_dp == 2 and n_row == 4 and n_col == 4 and feats % 32 == 0 and w_qkv.shape[0] % 32 == 0
    tok_t = jnp.swapaxes(tokens, 2, 3)
    w_down_t = w_down.T
    norms = jnp.stack([gain_one, shift_one, gain_two, shift_two])
    length = own_length(lengths, seq_order)
    everyone = ("dp", "row", "col")
    if direct:
        each = norms.shape[1]
        place = (lax.axis_index("dp") * n_row + lax.axis_index("row")) * n_col + lax.axis_index("col")
        lane = jnp.arange(256, dtype=jnp.int32)
        here = lane[None, :] == (place * each) % 128 + jnp.arange(each, dtype=jnp.int32)[:, None]
        packed = jnp.sum(jnp.where(here[None], norms[:, :, None].astype(F32), 0.0), axis=1).astype(BF)
        packed = jnp.pad(packed, ((0, 12), (0, 0)))
        xt, w_joined, qkv, context_t, lse, output, g_mixed, d_context, g_out, g_up, part_x, part_y, norm_grads = forward(
            dims, seq_order, lengths, tok_t, cotangent[:, 0], w_qkv, w_out, w_up, w_down_t, packed
        )
        norm_grads = norm_grads[:4]
    else:
        offset = jnp.arange(micro, dtype=jnp.int32)[:, None] * slots
        sent = take_blocks(tok_t.reshape(micro * slots, feats, span), (seq_order + offset).reshape(-1))
        sent = jnp.swapaxes(sent.reshape(micro, slots, feats, span), 0, 1).reshape(micro * slots, feats, span)
        got = lax.all_to_all(sent, everyone, split_axis=0, concat_axis=0, tiled=True)
        xt = got.reshape(groups, n_col, feats, span).transpose(0, 2, 1, 3).reshape(width, rows)
        cot = lax.all_to_all(cotangent[:, 0], "col", split_axis=0, concat_axis=0, tiled=True).reshape(rows, width)

        def whole(w, row_axes, col_axes):
            w = lax.all_gather(w, col_axes, axis=1, tiled=True)
            return lax.all_gather(w, row_axes, axis=0, tiled=True)

        f_qkv, f_out, f_up = (whole(w, ("dp", "row"), "col") for w in (w_qkv, w_out, w_up))
        f_down_t = whole(w_down_t, "col", ("dp", "row"))
        f_norms = lax.all_gather(norms, everyone, axis=1, tiled=True)
    if direct:
        n_grads = jnp.swapaxes(norm_grads.reshape(4, width // each, each), 0, 1)
        n_grads = jnp.pad(n_grads, ((0, 0), (0, 4), (0, 128 - each)))
        tgrad, r_qkv, r_out, r_up, r_down_t, n_sum = backward(
            dims, seq_order, lengths, qkv, context_t, lse, d_context, xt, w_joined, g_mixed,
            g_out, g_up, part_x, part_y, n_grads,
        )
        n_sum = n_sum[:4, :each]
    else:
        gains = [f_norms[i].astype(F32) for i in range(4)]
        x = xt.T
        qkv = product(x, f_qkv).astype(BF)
        context, stats = attention(qkv, length)
        output, g_mixed, d_context, g_down_t, g_up, g_out, norm_grads = middle(
            x, context, context.T, cot, f_out, f_up, f_down_t, *gains
        )
        norm_grads = jnp.stack(norm_grads)
        d_qkv = attention_back(qkv, length, stats, d_context)
        g_qkv = product(xt, d_qkv).astype(BF)
        dxt = (g_mixed + product_nt(d_qkv, f_qkv)).astype(BF).T
        n_sum = lax.psum_scatter(norm_grads, everyone, scatter_dimension=1, tiled=True)
        output = lax.all_to_all(output.reshape(n_col, span, width), "col", split_axis=0, concat_axis=0, tiled=True)
        sent = dxt.reshape(groups, feats, n_col, span).transpose(0, 2, 1, 3).reshape(micro * slots, feats, span)
        got = lax.all_to_all(sent, everyone, split_axis=0, concat_axis=0, tiled=True)
        got = jnp.swapaxes(got.reshape(slots, micro, feats, span), 0, 1).reshape(micro * slots, feats, span)
        index = jnp.arange(slots, dtype=jnp.int32)
        inverse = jnp.sum(jnp.where(seq_order[:, :, None] == index, index[None, :, None], 0), axis=1)
        offset = jnp.arange(micro, dtype=jnp.int32)[:, None] * slots
        tgrad = take_blocks(got, (inverse + offset).reshape(-1)).reshape(micro, slots, feats, span)

        def parts(g, row_axes, col_axes):
            g = lax.psum_scatter(g, col_axes, scatter_dimension=1, tiled=True)
            return lax.psum_scatter(g, row_axes, scatter_dimension=0, tiled=True).astype(F32)

        r_qkv, r_out, r_up = (parts(g, ("dp", "row"), "col") for g in (g_qkv, g_out, g_up))
        r_down_t = parts(g_down_t, "col", ("dp", "row"))
    return (
        output[:, None], jnp.swapaxes(tgrad, 2, 3), r_qkv, r_out, r_up, r_down_t.T,
        n_sum[0], n_sum[1], n_sum[2], n_sum[3],
    )


def solution(mesh):
    rows = ("dp", "row")
    every = ("dp", "row", "col")
    in_specs = (
        P(None, None, "col", rows), P(None, rows, "col", None), P(), P(),
        P(rows, "col"), P(rows, "col"), P(rows, "col"), P(rows, "col"),
        P(every), P(every), P(every), P(every),
    )
    out_specs = (
        P(None, rows, "col", None), P(None, None, "col", rows),
        P(rows, "col"), P(rows, "col"), P(rows, "col"), P(rows, "col"),
        P(every), P(every), P(every), P(every),
    )
    return jax.shard_map(local, mesh=mesh, in_specs=in_specs, out_specs=out_specs, check_vma=False)
```

```python
import functools

import jax
import jax.numpy as jnp
from jax import lax
from jax.experimental import pallas as pl
from jax.experimental.pallas import tpu as pltpu
from jax.sharding import PartitionSpec as P

HEAD = 64
NEGATIVE = -1000000000.0
EPSILON = 1e-12
ROOT_HALF = 0.7071067811865476
ROOT_TWO_PI = 0.3989422804014327
MESH = pl.DeviceIdType.MESH
BF = jnp.bfloat16
F32 = jnp.float32
ANY = pl.BlockSpec(memory_space=pl.ANY)
VM = pl.BlockSpec(memory_space=pltpu.VMEM)
SM = pl.BlockSpec(memory_space=pltpu.SMEM)
DMA = pltpu.SemaphoreType.DMA


def aligned(value, step):
    return pl.multiple_of(value, step)


def product(left, right):
    return jnp.dot(left, right, preferred_element_type=F32)


def product_tn(left, right):
    return lax.dot_general(left, right, (((0,), (0,)), ((), ())), preferred_element_type=F32)


def product_nt(left, right):
    return lax.dot_general(left, right, (((1,), (1,)), ((), ())), preferred_element_type=F32)


class Place:
    def __init__(self, n_dp, n_row, n_col):
        self.n_dp, self.n_row, self.n_col = n_dp, n_row, n_col
        self.n = n_dp * n_row * n_col
        self.x = lax.axis_index("dp")
        self.z = lax.axis_index("row")
        self.c = lax.axis_index("col")
        self.y, self.k = self.c // 2, self.c % 2
        self.g = self.x * n_row + self.z
        self.flat = self.g * n_col + self.c

    def of_flat(self, flat):
        group = flat // self.n_col
        return (group // self.n_row, group % self.n_row, flat % self.n_col)

    def dev(self, x=None, z=None, y=None, k=None):
        x = self.x if x is None else x
        z = self.z if z is None else z
        y = self.y if y is None else y
        k = self.k if k is None else k
        return (x, z, y * 2 + k)

    def greet(self):
        sem = pltpu.get_barrier_semaphore()

        def one(i, carry):
            pl.semaphore_signal(
                sem, inc=1, device_id=self.of_flat((self.flat + i) % self.n), device_id_type=MESH
            )
            return carry

        lax.fori_loop(1, self.n, one, 0)

    def met(self):
        pl.semaphore_wait(pltpu.get_barrier_semaphore(), self.n - 1)


class Lanes:
    def __init__(self, send_sems, recv_sems):
        self.send_sems, self.recv_sems, self.sent = send_sems, recv_sems, []
        self.used = [0, 0]

    def take(self, which, count):
        first = self.used[which]
        self.used[which] += count
        return first

    def copy(self, src, dst, device, s, r):
        return pltpu.make_async_remote_copy(
            src_ref=src, dst_ref=dst, send_sem=self.send_sems.at[s],
            recv_sem=self.recv_sems.at[r], device_id=device, device_id_type=MESH,
        )

    def send(self, make):
        self.copy(*make()).start()
        self.sent.append(make)

    def arrived(self, landing, device, r):
        self.copy(landing, landing, device, 0, r).wait_recv()

    def finish(self):
        for make in self.sent:
            self.copy(*make()).wait_send()
        self.sent = []


class Gather:
    def __init__(self, place, lanes, region, first):
        self.p, self.lanes, self.region, self.first = p, lanes, region, first = place, lanes, region, first
        self.to_x, self.to_y, self.to_core = p.dev(x=1 - p.x), p.dev(y=1 - p.y), p.dev(k=1 - p.k)
        self.one, self.two = (self.to_x, self.to_y) if first == "x" else (self.to_y, self.to_x)
        n = p.n_row
        self.s = {name: lanes.take(0, n) for name in ("z", 1, 2, 3, "core")}
        self.r = {name: lanes.take(1, n) for name in ("z", 1, 2, 3, "core")}
        self.far = (p.z + n // 2) % n
        self.near = p.z + 1 - 2 * (p.z % 2)
        self.cross = (self.near + n // 2) % n
        self.to_near = p.dev(z=self.near)

    def side(self, hop):
        p = self.p
        x_side = hop in ((1, 3) if self.first == "x" else (2, 3))
        y_side = hop in ((2, 3) if self.first == "x" else (1, 3))
        return (1 - p.x if x_side else p.x), (1 - p.y if y_side else p.y)

    def at(self, hop, z, k):
        x, y = self.side(hop)
        return self.region(x, z, 1, y, k)

    def line(self, hop, k):
        x, y = self.side(hop)
        return self.region(x, 0, self.p.n_row, y, k)

    def start(self, own):
        p = self.p

        def to(hop, device):
            return lambda: (own, self.at(0, p.z, p.k), device, self.s[hop] + p.z, self.r[hop] + p.z)

        self.lanes.send(to(1, self.one))
        self.lanes.send(to(2, self.two))
        self.own = own

    def z_start(self):
        p, own = self.p, self.own
        self.lanes.send(lambda: (own, self.at(0, p.z, p.k), p.dev(z=self.far), self.s["z"], self.r["z"]))
        self.lanes.send(lambda: (own, self.at(0, p.z, p.k), p.dev(z=self.near), self.s["z"] + 1, self.r["z"] + 1))

    def z_step(self, number):
        p = self.p
        source = (self.far, self.near, self.cross)[number - 1]
        peer = self.far if number == 1 else self.near
        self.lanes.arrived(self.at(0, source, p.k), p.dev(z=peer), self.r["z"] + number - 1)

        def to(device, hop, index):
            def make():
                ref = self.at(0, source, p.k)
                return (ref, ref, device, self.s[hop] + index, self.r[hop] + index)
            return make

        if number == 1:
            self.lanes.send(to(self.to_near, "z", 2))
        self.lanes.send(to(self.one, 1, source))
        self.lanes.send(to(self.two, 2, source))

    def z_steps(self):
        for distance in range(1, self.p.n_row):
            self.z_step(distance)
        self.z_done()

    def z_done(self):
        self.local.wait()
        self.to_other_core(0)

    def to_other_core(self, hop):
        def make():
            line = self.line(hop, self.p.k)
            return (line, line, self.to_core, self.s["core"] + hop, self.r["core"] + hop)
        self.lanes.send(make)

    def first_steps(self):
        p = self.p
        for source in (p.z, self.far, self.near, self.cross):
            self.lanes.arrived(self.at(1, source, p.k), self.one, self.r[1] + source)

            def make(source=source):
                ref = self.at(1, source, p.k)
                return (ref, ref, self.two, self.s[3] + source, self.r[3] + source)

            self.lanes.send(make)
        self.to_other_core(1)

    def second_steps(self, hops=(2, 3)):
        p = self.p
        for hop in hops:
            for i in range(p.n_row):
                self.lanes.arrived(self.at(hop, i, p.k), self.two, self.r[hop] + i)
            self.to_other_core(hop)

    def stage(self, name):
        if name == "z":
            self.z_start()
        elif name == "f":
            self.first_steps()
        elif name == "s":
            self.second_steps((2,))
        elif name == "t":
            self.second_steps((3,))
        else:
            self.z_step(int(name))
            if name == "3":
                self.z_done()

    def end(self):
        for hop in range(4):
            self.lanes.arrived(self.line(hop, 1 - self.p.k), self.to_core, self.r["core"] + hop)


def rows_region(ref, n_row, low=0, high=None):
    width = ref.shape[3] // 2
    high = width if high is None else high

    def region(x, z, nz, y, k):
        columns = pl.ds(aligned(y * width + low, 128), high - low)
        if nz == 1:
            return ref.at[x * n_row + z, k, :, columns]
        return ref.at[pl.ds(x * n_row + z, nz), k, :, columns]

    return region


def lanes_region(ref, n_dp, n_row, low=0, high=None):
    width = ref.shape[3] // (n_dp * n_row)
    high = ref.shape[2] if high is None else high

    def region(x, z, nz, y, k):
        return ref.at[y, k, pl.ds(low, high - low), pl.ds(aligned((x * n_row + z) * width, 128), nz * width)]

    return region


CHUNK = 512
ROWS = 256
BATCH = (6, 6, 6, 6, 7)
FIRST = {"q": "x", "o": "y", "u": "y", "v": "y", "d": "y", "e": "y"}
DOWN, UP, OUT, JOINED = "xyx", "xyx", "y", "xyx"
SCHEDULE = {
    "first": {4: ("oz", "uz",), 5: ("o1", "u1", "vz",)},
    "turn": {0: ("o2", "u2", "v1", "dz",), 2: ("o3", "u3", "v2", "d1",)},
    "project": {0: ("of", "v3", "d2",), 3: ("uf", "d3",), 6: ("vf", "ez",)},
    "attend": {0: ("df", "os", "e1",), 1: ("e2",), 2: ("us", "e3",), 3: ("ot", "ut",), 4: ("ef",), 5: ("vs",), 6: ("vt",), 7: ("c1",), 8: ("c2", "c3",), 9: ("ds",), 11: ("dt",)},
    "mix": {1: ("es",)},
    "rise": {0: ("et",)},
}


def forward_kernel(
    dims, seq_ref, len_ref, tok_ref, cot_ref, qkv_ref, out_ref, up_ref, down_ref, norm_ref,
    xt_out, wqkv_out, qkv_out, ctx_out, lse_out, output_out, gm_out, dctx_out, gout_out, gup_out, part_x_out, part_y_out, nsum_out,
    tsend, half_qkv, half_out, half_up, pair_qkv, pair_out, pair_up,
    xt_v, x_v, w_v, wide_v, ctx_v, lse_v, wout_v, wup_v, wdown_v, norm_v, gains_v, cot_v, act_v, mixed_v, gsum_v, hl_v,
    output_v, down_v, attn_v, dctx_v, turn_v, nsum_v,
    tok_send, tok_recv, norm_send, norm_recv, cot_send, cot_recv, w_send, w_recv, half_send, half_recv, local_sem, out_send, out_recv, r_send, r_recv,
    *pieces,
):
    n_dp, n_row, n_col = dims
    p = Place(n_dp, n_row, n_col)
    micro, slots, _, span = tok_ref.shape
    rows, width = x_v.shape
    qkv_v = wide_v.at[:, pl.ds(0, 3 * width)]
    p.greet()
    for m in range(micro):
        for j in range(slots):
            tsend[m * slots + j] = tok_ref[m, seq_ref[m, j]]
    p.met()
    halves = Lanes(half_send, half_recv)
    lanes = Lanes(w_send, w_recv)
    partner = p.dev(k=1 - p.k)
    for i, (block, landing) in enumerate(((qkv_ref, half_qkv), (out_ref, half_out), (up_ref, half_up))):
        def make(i=i, block=block, landing=landing):
            count = landing.shape[0]
            return (block.at[pl.ds(aligned((1 - p.k) * count, 16), count), :], landing, partner, i, i)
        halves.send(make)

    def join(i, block, landing, pair):
        halves.arrived(landing, partner, i)
        count, across = landing.shape
        mine = block[pl.ds(aligned(p.k * count, 16), count), :]
        theirs = landing[...]
        pair[:, :across] = jnp.where(p.k == 0, mine, theirs)
        pair[:, across:] = jnp.where(p.k == 0, theirs, mine)

    local = []

    def keep(src, dst):
        made = pltpu.make_async_copy(src, dst, local_sem.at[len(local)])
        made.start()
        local.append(made)
        return made

    region_qkv = rows_region(w_v, n_row)
    join(0, qkv_ref, half_qkv, pair_qkv)
    own_w = keep(pair_qkv, region_qkv(p.x, p.z, 1, p.y, p.k))
    g_qkv = Gather(p, lanes, region_qkv, FIRST["q"])
    g_qkv.local = own_w
    g_qkv.start(pair_qkv)
    g_qkv.z_start()

    def tok_copy(i):
        target = (p.flat + i) % p.n
        return pltpu.make_async_remote_copy(
            src_ref=tsend.at[(target % n_col) * slots + target // n_col],
            dst_ref=xt_v.at[p.g, :, pl.ds(aligned(p.c * span, 128), span)],
            send_sem=tok_send.at[i], recv_sem=tok_recv.at[i],
            device_id=p.of_flat(target), device_id_type=MESH,
        )

    def norm_copy(i):
        return pltpu.make_async_remote_copy(
            src_ref=norm_ref, dst_ref=norm_v.at[p.flat],
            send_sem=norm_send.at[i], recv_sem=norm_recv.at[i],
            device_id=p.of_flat((p.flat + i) % p.n), device_id_type=MESH,
        )

    sent = [1]

    def tok_batch(count):
        def one(j, carry):
            tok_copy((j * 13) % p.n).start()
            return carry

        lax.fori_loop(sent[0], min(sent[0] + count, p.n), one, 0)
        sent[0] = min(sent[0] + count, p.n)

    def norm_start(i, carry):
        norm_copy(i).start()
        return carry

    tok_batch(BATCH[0])
    own_tok = keep(tsend.at[p.c * slots + p.g], xt_v.at[p.g, :, pl.ds(aligned(p.c * span, 128), span)])

    waves = []

    def wave(own, region, first):
        gather = Gather(p, lanes, region, first)
        gather.local = keep(own, region(p.x, p.z, 1, p.y, p.k))
        gather.start(own)
        waves.append(gather)

    join(1, out_ref, half_out, pair_out)
    wave(pair_out, rows_region(wout_v, n_row), FIRST["o"])
    join(2, up_ref, half_up, pair_up)
    cut = pair_up.shape[1] // 2
    wave(pair_up.at[:, pl.ds(0, cut)], rows_region(wup_v, n_row, 0, cut), FIRST["u"])
    wave(pair_up.at[:, pl.ds(cut, cut)], rows_region(wup_v, n_row, cut, 2 * cut), FIRST["v"])
    cut = down_ref.shape[0] // 2
    wave(down_ref.at[pl.ds(0, cut), :], lanes_region(wdown_v, n_dp, n_row, 0, cut), FIRST["d"])
    wave(down_ref.at[pl.ds(cut, cut), :], lanes_region(wdown_v, n_dp, n_row, cut, 2 * cut), FIRST["e"])
    lax.fori_loop(1, p.n, norm_start, 0)
    own_norm = keep(norm_ref, norm_v.at[p.flat])

    def cot_copy(i):
        target = (p.c + i) % n_col
        return pltpu.make_async_remote_copy(
            src_ref=cot_ref.at[target], dst_ref=cot_v.at[p.c],
            send_sem=cot_send.at[i], recv_sem=cot_recv.at[i],
            device_id=(p.x, p.z, target), device_id_type=MESH,
        )

    own_cot = keep(cot_ref.at[p.c], cot_v.at[p.c])
    names = dict(zip("ouvde", waves))

    def begin_cot(i):
        cot_copy(i).start()

    def agenda(phase):
        table = {}
        for turn, steps in SCHEDULE.get(phase, {}).items():
            table[turn] = [functools.partial(begin_cot, int(step[1:])) if step[0] == "c" else functools.partial(names[step[0]].stage, step[1:]) for step in steps]
        return table

    first = agenda("first")

    def now(turn):
        for act in first.get(turn, ()):
            act()

    now(0)
    for distance in range(1, n_row):
        g_qkv.z_step(distance)
        tok_batch(BATCH[distance])
        now(distance)
    g_qkv.z_done()
    g_qkv.first_steps()
    tok_batch(BATCH[4])
    now(4)
    g_qkv.second_steps()
    tok_batch(p.n)
    now(5)
    own_tok.wait()

    def tok_wait(i, carry):
        source = (p.flat + p.n - i) % p.n
        landing = xt_v.at[source // n_col, :, pl.ds(aligned((source % n_col) * span, 128), span)]
        pltpu.make_async_remote_copy(
            src_ref=landing, dst_ref=landing, send_sem=tok_send.at[i], recv_sem=tok_recv.at[i],
            device_id=p.of_flat(source), device_id_type=MESH,
        ).wait_recv()
        return carry

    lax.fori_loop(1, p.n, tok_wait, 0)
    keep(xt_v, xt_out)

    def turn(i, carry):
        run_events(i, agenda("turn"))
        at = pl.ds(aligned(i * 256, 256), 256)
        x_v[at, :] = xt_v[:, :, at].reshape(width, 256).T
        return carry

    lax.fori_loop(0, rows // 256, turn, 0)
    g_qkv.end()
    keep(w_v, wqkv_out)

    def project(i, carry):
        run_events(i, agenda("project"))
        at = pl.ds(aligned(i * 256, 256), 256)
        wide_v[:, at] = product(x_v[...], w_v[:, :, :, at].reshape(width, 256)).astype(BF)
        return carry

    lax.fori_loop(0, 3 * width // 256, project, 0)
    kept_qkv = keep(qkv_v, qkv_out)
    out, up_a, up_b, down_a, down_b = waves
    length = len_ref[p.c, seq_ref[p.c, p.g]]
    bias = jnp.where(lax.broadcasted_iota(jnp.int32, (rows, 1), 0) < length, 0.0, NEGATIVE)
    chunks = rows // CHUNK

    def attend(step, carry):
        run_events(step, agenda("attend"))
        pair, at_row = step // chunks, step % chunks
        columns = [pl.ds(aligned(i * width + pair * 128, 128), 128) for i in range(3)]
        keys = wide_v[:, columns[1]]
        values_t = wide_v[:, columns[2]].T
        lane = lax.broadcasted_iota(jnp.int32, (rows, 128), 1)
        own_rows = pl.ds(aligned(at_row * CHUNK, CHUNK), CHUNK)
        queries = wide_v[own_rows, columns[0]] * jnp.asarray(0.125, BF)
        for h in range(2):
            mine = jnp.where((lane < HEAD) == (h == 0), keys, jnp.zeros_like(keys))
            scores = product_nt(mine, queries) + bias
            top = jnp.max(scores, axis=0, keepdims=True)
            exps = jnp.exp(scores - top)
            total = jnp.sum(exps, axis=0, keepdims=True)
            context = product(values_t[h * HEAD:(h + 1) * HEAD], exps.astype(BF))
            head_rows = pl.ds(aligned(pair * 128 + h * HEAD, HEAD), HEAD)
            ctx_v[head_rows, own_rows] = (context * (1.0 / total)).astype(BF)
            lse_v[2 * pair + h, :, own_rows] = top + jnp.log(total)
        return carry

    lax.fori_loop(0, width // 128 * chunks, attend, 0)
    keep(ctx_v, ctx_out)
    keep(lse_v, lse_out)

    own_norm.wait()

    def norm_wait(i, carry):
        source = (p.flat + p.n - i) % p.n
        pltpu.make_async_remote_copy(
            src_ref=norm_ref, dst_ref=norm_v.at[source], send_sem=norm_send.at[i], recv_sem=norm_recv.at[i],
            device_id=p.of_flat(source), device_id_type=MESH,
        ).wait_recv()
        return carry

    lax.fori_loop(1, p.n, norm_wait, 0)
    each = width // p.n
    gains_v[...] = jnp.zeros_like(gains_v)
    for source in range(p.n):
        low = source * each // 128 * 128
        gains_v[:, low:low + 256] += norm_v[source].astype(F32)
    gain_one, shift_one, gain_two, shift_two = (gains_v[i:i + 1, :width] for i in range(4))

    def normal(values):
        centered = values - jnp.mean(values, axis=-1, keepdims=True)
        scale = lax.rsqrt(jnp.mean(centered * centered, axis=-1, keepdims=True) + EPSILON)
        return centered * scale, scale

    def normal_back(grad, unit, scale, gain):
        grad = grad * gain
        return scale * (grad - jnp.mean(grad, axis=-1, keepdims=True) - unit * jnp.mean(grad * unit, axis=-1, keepdims=True))

    nsum_v[...] = jnp.zeros_like(nsum_v)
    whole = lambda ref: ref[...].reshape(width, -1)
    out.end()

    def mix(step, carry):
        run_events(step, agenda("mix"))
        at = pl.ds(aligned(step * ROWS, ROWS), ROWS)
        mixed = x_v[at, :].astype(F32) + product_tn(ctx_v[:, at], whole(wout_v))
        mixed_v[at, :] = mixed
        unit, _ = normal(mixed)
        hl_v[at, :] = (unit * gain_one + shift_one).astype(BF)
        return carry

    lax.fori_loop(0, rows // ROWS, mix, 0)
    up_a.end()
    up_b.end()
    kept_qkv.wait()

    def rise(step, carry):
        run_events(step, agenda("rise"))
        at = pl.ds(aligned(step * 256, 256), 256)
        pre = product(hl_v[...], wup_v[:, :, :, at].reshape(width, 256))
        half = 0.5 * (1.0 + lax.erf(pre * ROOT_HALF))
        act_v[:, at] = (pre * half).astype(BF)
        wide_v[:, at] = (half + pre * jnp.exp(pre * pre * -0.5) * ROOT_TWO_PI).astype(BF)
        return carry

    lax.fori_loop(0, 4 * width // 256, rise, 0)
    down_a.end()
    down_b.end()
    for i in range(1, n_col):
        source = (p.c + n_col - i) % n_col
        pltpu.make_async_remote_copy(
            src_ref=cot_v.at[source], dst_ref=cot_v.at[source],
            send_sem=cot_send.at[i], recv_sem=cot_recv.at[i],
            device_id=(p.x, p.z, source), device_id_type=MESH,
        ).wait_recv()
    own_cot.wait()

    def out_copy(target):
        return pltpu.make_async_remote_copy(
            src_ref=output_v.at[pl.ds(aligned(target * span, 16), span), :], dst_ref=output_out.at[p.c],
            send_sem=out_send.at[target], recv_sem=out_recv.at[p.c],
            device_id=(p.x, p.z, target), device_id_type=MESH,
        )

    def fall(step, carry):
        at = pl.ds(aligned(step * ROWS, ROWS), ROWS)
        unit_one, _ = normal(mixed_v[at, :])
        summed = unit_one * gain_one + shift_one + product_nt(act_v[at, :], whole(wdown_v))
        unit, scale = normal(summed)
        output_v[at, :] = (unit * gain_two + shift_two).astype(BF)
        per = span // ROWS
        cot = cot_v[step // per, pl.ds(aligned(step % per * ROWS, ROWS), ROWS), :].astype(F32)
        nsum_v[2:3, :width] += jnp.sum(cot * unit, axis=0, keepdims=True)
        nsum_v[3:4, :width] += jnp.sum(cot, axis=0, keepdims=True)
        grad = normal_back(cot, unit, scale, gain_two)
        gsum_v[at, :] = grad
        down_v[at, :] = grad.astype(BF)
        turn_v[:, at] = grad.T.astype(BF)
        target = step // per

        @pl.when((step % per == per - 1) & (target != p.c))
        def _():
            out_copy(target).start()
        return carry

    lax.fori_loop(0, rows // ROWS, fall, 0)
    keep(output_v.at[pl.ds(aligned(p.c * span, 16), span), :], output_out.at[p.c])

    def rise_back(step, carry):
        at = pl.ds(aligned(step * 512, 512), 512)
        back = product(down_v[...], wdown_v[:, :, :, at].reshape(width, 512))
        wide_v[:, at] = (back * wide_v[:, at].astype(F32)).astype(BF)
        return carry

    lax.fori_loop(0, 4 * width // 512, rise_back, 0)
    lanes.finish()

    def grad_down(step, carry):
        at = pl.ds(aligned(step * 512, 512), 512)
        wdown_v[:, :, :, at] = product(turn_v[...], act_v[:, at]).astype(BF).reshape(wdown_v.shape[:3] + (512,))
        return carry

    lax.fori_loop(0, 4 * width // 512, grad_down, 0)

    rlanes = Lanes(r_send, r_recv)
    early = []
    piece_rows = wdown_v.shape[2] // len(DOWN)
    for i, axis in enumerate(DOWN):
        at = pl.ds(i * piece_rows, piece_rows)
        piece = Reduce(
            p, rlanes, wdown_v.at[:, 1 - p.k, at], wdown_v.at[:, p.k, at], pieces[2 * i:2 * i + 2] + (None, None, None), "lanes", axis
        )
        piece.start()
        early.append(piece)

    def mix_back(step, carry):
        run_events(step, {1: (early[0].one, early[1].one), 2: (early[2].one,)})
        at = pl.ds(aligned(step * ROWS, ROWS), ROWS)
        grad = gsum_v[at, :] + product_nt(wide_v[at, :], whole(wup_v))
        unit, scale = normal(mixed_v[at, :])
        nsum_v[0:1, :width] += jnp.sum(grad * unit, axis=0, keepdims=True)
        nsum_v[1:2, :width] += jnp.sum(grad, axis=0, keepdims=True)
        grad = normal_back(grad, unit, scale, gain_one)
        gsum_v[at, :] = grad
        low = grad.astype(BF)
        attn_v[at, :] = low
        dctx_v[at, :] = product_nt(low, whole(wout_v)).astype(BF)
        turn_v[:, at] = hl_v[at, :].T
        return carry

    lax.fori_loop(0, rows // ROWS, mix_back, 0)
    keep(gsum_v, gm_out)
    keep(dctx_v, dctx_out)
    keep(nsum_v, nsum_out)

    def grad_up(step, carry):
        at = pl.ds(aligned(step * 512, 512), 512)
        wup_v[:, :, :, at] = product(turn_v[...], wide_v[:, at]).astype(BF).reshape(wup_v.shape[:3] + (512,))
        return carry

    lax.fori_loop(0, 4 * width // 512, grad_up, 0)
    keep(wup_v, gup_out)

    def grad_out(step, carry):
        at = pl.ds(aligned(step * 256, 256), 256)
        wout_v[:, :, :, at] = product(ctx_v[...], attn_v[:, at]).astype(BF).reshape(wout_v.shape[:3] + (256,))
        return carry

    lax.fori_loop(0, width // 256, grad_out, 0)
    keep(wout_v, gout_out)
    outs = {"x": [part_x_out.at[i] for i in range(DOWN.count("x"))], "y": [part_y_out.at[i] for i in range(DOWN.count("y"))]}
    for piece, axis in zip(early, DOWN):
        piece.add_half(1)
        keep(piece.b[1], outs[axis].pop(0))

    def small_wait(i, carry):
        norm_copy(i).wait_send()
        tok_copy(i).wait_send()
        return carry

    lax.fori_loop(1, p.n, small_wait, 0)
    for i in range(1, n_col):
        cot_copy(i).wait_send()
        source = (p.c + n_col - i) % n_col
        pltpu.make_async_remote_copy(
            src_ref=output_out.at[source], dst_ref=output_out.at[source],
            send_sem=out_send.at[source], recv_sem=out_recv.at[source],
            device_id=(p.x, p.z, source), device_id_type=MESH,
        ).wait_recv()
        out_copy((p.c + i) % n_col).wait_send()
    waited = [own_tok, own_norm, own_w, own_cot, kept_qkv] + [gather.local for gather in waves]
    for made in local:
        if not any(made is w for w in waited):
            made.wait()
    halves.finish()
    rlanes.finish()


def run_events(step, events):
    for when_, acts in events.items():
        def act(acts=acts):
            for a in acts:
                a()
        pl.when(step == when_)(act)


def forward(dims, seq_order, lengths, tok_t, cot, w_qkv, w_out, w_up, w_down_t, norms):
    n_dp, n_row, n_col = dims
    groups, n = n_dp * n_row, n_dp * n_row * n_col
    micro, slots, feats, span = tok_t.shape
    rows, width = n_col * span, groups * feats
    heads = width // HEAD
    qr, qc = w_qkv.shape
    orow, oc = w_out.shape
    ur, uc = w_up.shape
    dr, dc = w_down_t.shape
    shape = jax.ShapeDtypeStruct
    joined = (groups, 2, qr // 2, qc * n_col)
    out_all = (groups, 2, orow // 2, oc * n_col)
    up_all = (groups, 2, ur // 2, uc * n_col)
    down_all = (2, 2, dr, dc * groups)
    outs = (
        shape((groups, feats, rows), BF),
        shape(joined, BF),
        shape((rows, 3 * width), BF),
        shape((width, rows), BF),
        shape((heads, 1, rows), F32),
        shape((n_col, span, width), BF),
        shape((rows, width), F32),
        shape((rows, width), BF),
        shape(out_all, BF),
        shape(up_all, BF),
        shape((DOWN.count("x"), 2, dr // len(DOWN), dc * groups // 2), BF),
        shape((DOWN.count("y"), dr // len(DOWN), dc * groups), BF),
        shape((8, width + 256), F32),
    )
    vm = pltpu.VMEM
    early_buffers = [
        vm(size, BF) for axis in DOWN for size in piece_buffers("lanes", axis, 0, dr // len(DOWN), dc * groups, n_row, groups)[:2]
    ]
    return pl.pallas_call(
        functools.partial(forward_kernel, dims),
        out_shape=outs,
        in_specs=[SM, SM, VM, ANY, VM, VM, VM, VM, VM],
        out_specs=[ANY] * len(outs),
        scratch_shapes=[
            vm((micro * slots, feats, span), BF),
            vm((qr // 2, qc), BF), vm((orow // 2, oc), BF), vm((ur // 2, uc), BF),
            vm((qr // 2, qc * 2), BF), vm((orow // 2, oc * 2), BF), vm((ur // 2, uc * 2), BF),
            vm((groups, feats, rows), BF),
            vm((rows, width), BF),
            vm(joined, BF),
            vm((rows, 4 * width), BF),
            vm((width, rows), BF),
            vm((heads, 1, rows), F32),
            vm(out_all, BF), vm(up_all, BF), vm(down_all, BF),
            vm((n,) + norms.shape, BF),
            vm((norms.shape[0], width + 256), F32),
            vm(cot.shape, BF),
            vm((rows, 4 * width), BF),
            vm((rows, width), F32), vm((rows, width), F32),
            vm((rows, width), BF), vm((rows, width), BF), vm((rows, width), BF), vm((rows, width), BF), vm((rows, width), BF),
            vm((width, rows), BF),
            vm((8, width + 256), F32),
            DMA((n,)), DMA((n,)), DMA((n,)), DMA((n,)), DMA((n_col,)), DMA((n_col,)),
            DMA((6 * 5 * n_row,)), DMA((6 * 5 * n_row,)), DMA((3,)), DMA((3,)), DMA((24,)), DMA((n_col,)), DMA((n_col,)),
            DMA((24,)), DMA((24,)), *early_buffers,
        ],
        compiler_params=pltpu.CompilerParams(
            collective_id=0, has_side_effects=True, vmem_limit_bytes=63 * 2**20
        ),
        name="forward_part",
    )(seq_order, lengths, tok_t, cot, w_qkv, w_out, w_up, w_down_t, norms)


BACK_CHUNK = 256
SUMS = {
    0: ("u20", "o00",), 1: ("u01", "u11",), 3: ("u21", "d13",), 4: ("d03",), 6: ("d23", "d14",), 7: ("d04",), 8: ("a0", "u02",), 9: ("o01", "d24", "d15",), 10: ("a1", "d05",),
    12: ("u12", "d25",), 14: ("u22", "u03",), 16: ("b0",), 17: ("u13", "u04",), 18: ("o02", "b1",), 20: ("u14", "u05",), 21: ("a2", "u23",), 22: ("u15",), 23: ("o03",),
}
PACE = ((0, 16), "c1", "a3", "b2", "u24", "o04", (16, 32), "c2", "a4", "b3", "c3", "b4", "c4")
LATE = ("o05", "u25")


def add_into(target, term):
    shape = target.shape
    if len(shape) == 2:
        target[...] = (target[...].astype(F32) + term[...].astype(F32)).astype(BF)
        return

    def body(i, carry):
        target[i] = (target[i].astype(F32) + term[i].astype(F32)).astype(BF)
        return carry

    lax.fori_loop(0, shape[0], body, 0)


class Reduce:
    def __init__(self, place, lanes, theirs, mine, buffers, kind, first):
        self.p, self.lanes, self.theirs, self.mine, self.b = place, lanes, theirs, mine, buffers
        self.kind, self.axes = kind, ("x", "y") if first == "x" else ("y", "x")
        self.s = [lanes.take(0, 1) for _ in range(3)] + [lanes.take(0, 3)]
        self.r = [lanes.take(1, 1) for _ in range(3)] + [lanes.take(1, 3)]
        n = place.n_row
        self.far = (place.z + n // 2) % n
        self.near = place.z + 1 - 2 * (place.z % 2)
        self.cross = (self.near + n // 2) % n

    def start(self):
        p = self.p
        self.lanes.send(lambda: (self.theirs, self.b[0], p.dev(k=1 - p.k), self.s[0], self.r[0]))

    def half(self, ref, axis, side):
        if self.kind == "lanes" and axis == "y":
            return ref.at[side]
        if self.kind == "rows" and axis == "x":
            count = ref.shape[0] // 2
            return ref.at[pl.ds(side * count, count)]
        width = ref.shape[-1] // 2
        lead = (slice(None),) * (len(ref.shape) - 1)
        return ref.at[lead + (pl.ds(aligned(side * width, 128), width),)]

    def where(self, axis):
        p = self.p
        return (p.x, p.dev(x=1 - p.x)) if axis == "x" else (p.y, p.dev(y=1 - p.y))

    def send_half(self, stage):
        def make():
            side, peer = self.where(self.axes[stage - 1])
            return (self.half(self.b[stage - 1], self.axes[stage - 1], 1 - side), self.b[stage], peer, self.s[stage], self.r[stage])

        self.lanes.send(make)

    def add_half(self, stage):
        side, peer = self.where(self.axes[stage - 1])
        self.lanes.arrived(self.b[stage], peer, self.r[stage])
        add_into(self.b[stage], self.half(self.b[stage - 1], self.axes[stage - 1], side))

    def one(self):
        p = self.p
        self.lanes.arrived(self.b[0], p.dev(k=1 - p.k), self.r[0])
        add_into(self.b[0], self.mine)
        self.send_half(1)

    def two(self):
        self.add_half(1)
        self.send_half(2)

    def part(self, z):
        ref = self.b[2]
        if self.kind == "rows":
            return ref.at[z]
        width = self.b[3].shape[-1]
        return ref.at[:, pl.ds(aligned(z * width, 128), width)]

    def three(self):
        p = self.p
        self.add_half(2)
        for i, target in enumerate((self.cross, self.near)):
            def make(i=i, target=target):
                return (self.part(target), self.b[3].at[1 - i], p.dev(z=self.near), self.s[3] + i, self.r[3] + i)
            self.lanes.send(make)

    def four(self):
        p = self.p
        self.lanes.arrived(self.b[3].at[1], p.dev(z=self.near), self.r[3])
        add_into(self.b[3].at[1], self.part(self.far))
        self.lanes.send(lambda: (self.b[3].at[1], self.b[4], p.dev(z=self.far), self.s[3] + 2, self.r[3] + 2))

    def five(self):
        p = self.p
        self.lanes.arrived(self.b[3].at[0], p.dev(z=self.near), self.r[3] + 1)
        total = self.part(p.z)[...].astype(F32) + self.b[3][0].astype(F32)
        self.lanes.arrived(self.b[4], p.dev(z=self.far), self.r[3] + 2)
        return total + self.b[4][...].astype(F32)


def piece_buffers(kind, first, lead, rows, columns, n_row, groups):
    if kind == "lanes":
        one = (2, rows, columns // 2) if first == "x" else (rows, columns)
        return [(2, rows, columns), one, (rows, columns // 2), (2, rows, columns // groups), (rows, columns // groups)]
    one = (lead // 2, rows, columns) if first == "x" else (lead, rows, columns // 2)
    return [(lead, rows, columns), one, (lead // 2, rows, columns // 2), (2, rows, columns // 2), (rows, columns // 2)]


def backward_kernel(
    dims, plan, seq_ref, len_ref, qkv_ref, ctx_ref, lse_ref, dctx_ref, xt_ref, w_ref, gm_ref, gout_ref, gup_ref, part_x_ref, part_y_ref,
    ngrad_ref, tgrad_ref, rqkv_ref, rout_ref, rup_ref, rdown_ref, nsum_ref, *scratch,
):
    n_dp, n_row, n_col = dims
    p = Place(n_dp, n_row, n_col)
    groups = n_dp * n_row
    (
        qkv_v, ctx_v, lse_v, dctx_v, xt_v, w_v, gm_v, m_out, m_up, ga_v, gb_v, gc_v, dqt_v, dk_v, dv_v, acc_k, acc_v, dxt_v, trecv,
        nrecv, fq, fo, fu, tok_send, tok_recv, norm_send, norm_recv, w_send, w_recv, local_sem,
    ) = scratch[:30]
    pieces = scratch[30:]
    micro, slots, _, span = tgrad_ref.shape
    width, rows = ctx_ref.shape
    p.greet()
    local = []

    def keep(src, dst):
        made = pltpu.make_async_copy(src, dst, local_sem.at[len(local)])
        made.start()
        local.append(made)
        return made

    needed = [keep(qkv_ref, qkv_v), keep(dctx_ref, dctx_v), keep(ctx_ref, ctx_v), keep(lse_ref, lse_v)]
    mine_up = keep(gup_ref.at[:, p.k], m_up)
    mine_out = keep(gout_ref.at[:, p.k], m_out)
    xt_load = keep(xt_ref, xt_v)
    later = [keep(w_ref, w_v), keep(gm_ref, gm_v)]
    p.met()
    lanes = Lanes(w_send, w_recv)
    partner = p.dev(k=1 - p.k)
    waves = {"down": [], "up": [], "out": [], "a": [], "b": [], "c": []}
    parts = []
    made_here = {"a": ga_v, "b": gb_v, "c": gc_v}
    whole = {"up": gup_ref, "out": gout_ref, **made_here}
    carried = {"up": m_up, "out": m_out}
    sources = {"x": [part_x_ref.at[i] for i in range(DOWN.count("x"))], "y": [part_y_ref.at[i] for i in range(DOWN.count("y"))]}
    for index, (name, kind, first, low, count) in enumerate(plan):
        if name == "down":
            piece = Reduce(p, lanes, None, None, pieces[5 * index:5 * index + 5], kind, first)
            parts.append(keep(sources[first].pop(0), piece.b[1]))
            waves["down"].append(piece)
            continue
        at = pl.ds(low, count)
        theirs = whole[name].at[:, 1 - p.k, at]
        mine = made_here[name].at[:, p.k, at] if name in made_here else carried[name].at[:, at]
        waves[name].append(Reduce(p, lanes, theirs, mine, pieces[5 * index:5 * index + 5], kind, first))
    d, u, o = waves["down"], waves["up"], waves["out"]
    joined = [waves[name][0] for name in "abc"]

    def window(device):
        return pl.ds(aligned(device * (width // p.n) // 128 * 128, 128), 256)

    def norm_copy(i):
        target = (p.flat + i) % p.n
        return pltpu.make_async_remote_copy(
            src_ref=ngrad_ref.at[:, window(target)], dst_ref=nrecv.at[p.flat],
            send_sem=norm_send.at[i], recv_sem=norm_recv.at[i],
            device_id=p.of_flat(target), device_id_type=MESH,
        )

    def norm_start(i, carry):
        norm_copy(i).start()
        return carry

    u[0].start()
    u[1].start()
    for made, piece in zip(parts, d):
        made.wait()
        piece.send_half(2)
    lax.fori_loop(1, p.n, norm_start, 0)
    nrecv[p.flat] = ngrad_ref[:, window(p.flat)]
    for made in needed:
        made.wait()
    mine_up.wait()
    mine_out.wait()

    def finish_rows(piece, temp, result, low):
        total = piece()
        count, across = total.shape[0], total.shape[1] // 2
        half_rows = result.shape[0] // 2
        temp[pl.ds(low, count), :] = jnp.where(p.k == 0, total[:, across:], total[:, :across])
        result[pl.ds(aligned(p.k * half_rows + low, 16), count), :] = jnp.where(p.k == 0, total[:, :across], total[:, across:])
        s, r = lanes.take(0, 1), lanes.take(1, 1)
        place = lambda k: result.at[pl.ds(aligned(k * half_rows + low, 16), count), :]
        lanes.send(lambda: (temp.at[pl.ds(low, count), :], place(p.k), partner, s, r))
        ends.append(lambda: lanes.arrived(place(1 - p.k), partner, r))

    ends = []

    def finish_down(piece, low):
        total = piece.five()
        rdown_ref[pl.ds(low, total.shape[0]), :] = total

    lows = {name: [low for other, _, _, low, _ in plan if other == name] for name in waves}
    down_end = [functools.partial(finish_down, piece, low) for piece, low in zip(d, lows["down"])]
    up_end = [functools.partial(finish_rows, piece.five, fu, rup_ref, low) for piece, low in zip(u, lows["up"])]
    out_end = [functools.partial(finish_rows, piece.five, fo, rout_ref, low) for piece, low in zip(o, lows["out"])]

    def joined_total():
        blocks = [[total[:, i * 128:(i + 1) * 128] for i in range(3)] for total in (piece.five() for piece in joined)]
        middle = [piece[1] for piece in blocks]
        queries = [piece[0] for piece in blocks] + middle + [piece[2] for piece in blocks]
        return jnp.concatenate(queries, axis=1)

    def joined_end():
        finish_rows(joined_total, fq, rqkv_ref, 0)

    xt = lambda: xt_v[...].reshape(width, rows)
    pairs = width // 128

    def grad_part(grad, number):
        near, far = number, number + pairs // 2
        columns = lambda pair: slice(pair * 128, pair * 128 + 128)
        terms = (
            lambda: product_nt(xt(), dqt_v[columns(near), :]), lambda: product_nt(xt(), dqt_v[columns(far), :]),
            lambda: product(xt(), dk_v[:, columns(near)]), lambda: product(xt(), dk_v[:, columns(far)]),
            lambda: product(xt(), dv_v[:, columns(near)]), lambda: product(xt(), dv_v[:, columns(far)]),
        )
        for i, term in enumerate(terms):
            grad[:, :, :, columns(i)] = term().astype(BF).reshape(groups, 2, -1, 128)
        joined[number].start()

    def first_part():
        xt_load.wait()
        grad_part(ga_v, 0)

    table = {
        letter + str(i) + str(stage): act
        for letter, group, ends_ in (("d", d, down_end), ("u", u, up_end), ("o", o, out_end))
        for i, (piece, end) in enumerate(zip(group, ends_))
        for stage, act in enumerate((piece.start, piece.one, piece.two, piece.three, piece.four, end))
    }
    for letter, piece in zip("abc", joined):
        for stage, act in enumerate((piece.one, piece.two, piece.three, piece.four)):
            table[letter + str(stage + 1)] = act
    table.update({"a0": first_part, "b0": functools.partial(grad_part, gb_v, 1), "c0": functools.partial(grad_part, gc_v, 2)})
    events = {turn: [table[step] for step in steps] for turn, steps in SUMS.items()}
    length_bias = jnp.where(lax.broadcasted_iota(jnp.int32, (rows, 1), 0) < len_ref[p.c, seq_ref[p.c, p.g]], 0.0, NEGATIVE)
    chunks = rows // BACK_CHUNK

    def attend(step, carry):
        for when_, acts in events.items():
            def act(acts=acts):
                for a in acts:
                    a()
            pl.when(step == when_)(act)
        turn, at_row = step // chunks, step % chunks
        pair = turn % 2 * (pairs // 2) + turn // 2
        columns = [pl.ds(aligned(i * width + pair * 128, 128), 128) for i in range(3)]
        keys, values = qkv_v[:, columns[1]], qkv_v[:, columns[2]]
        keys_t = keys.T
        lane = lax.broadcasted_iota(jnp.int32, (rows, 128), 1)
        short = lax.broadcasted_iota(jnp.int32, (BACK_CHUNK, 128), 1)
        own_rows = pl.ds(aligned(at_row * BACK_CHUNK, BACK_CHUNK), BACK_CHUNK)
        queries = qkv_v[own_rows, columns[0]] * jnp.asarray(0.125, BF)
        back = dctx_v[own_rows, columns[0]]
        back_t = back.T.astype(F32)
        forth_t = ctx_v[pl.ds(aligned(pair * 128, 128), 128), own_rows].astype(F32)
        both = back_t * forth_t
        d_keys = d_values = None
        for h in range(2):
            def own(block, index):
                return jnp.where((index < HEAD) == (h == 0), block, jnp.zeros_like(block))
            delta = jnp.sum(both[h * HEAD:(h + 1) * HEAD], axis=0, keepdims=True)
            scores = product_nt(own(keys, lane), queries) + length_bias
            soft = jnp.exp(scores - lse_v[2 * pair + h, :, own_rows])
            d_probs = product_nt(own(values, lane), back)
            d_scores = (soft * (d_probs - delta)).astype(BF)
            head_rows = pl.ds(aligned(pair * 128 + h * HEAD, HEAD), HEAD)
            dqt_v[head_rows, own_rows] = (product(keys_t[h * HEAD:(h + 1) * HEAD], d_scores) * 0.125).astype(BF)
            to_values = product(soft.astype(BF), own(back, short))
            to_keys = product(d_scores, own(queries, short))
            d_values = to_values if d_values is None else d_values + to_values
            d_keys = to_keys if d_keys is None else d_keys + to_keys

        @pl.when(at_row == 0)
        def _():
            acc_k[...] = d_keys
            acc_v[...] = d_values

        @pl.when(at_row > 0)
        def _():
            acc_k[...] += d_keys
            acc_v[...] += d_values

        @pl.when(at_row == chunks - 1)
        def _():
            dk_v[:, columns[0]] = acc_k[...].astype(BF)
            dv_v[:, columns[0]] = acc_v[...].astype(BF)
        return carry

    lax.fori_loop(0, width // 128 * chunks, attend, 0)
    for made in later:
        made.wait()

    def tok_copy(target):
        return pltpu.make_async_remote_copy(
            src_ref=dxt_v.at[target // n_col, :, pl.ds(aligned((target % n_col) * span, 128), span)],
            dst_ref=trecv.at[p.c * slots + p.g],
            send_sem=tok_send.at[target], recv_sem=tok_recv.at[p.flat],
            device_id=p.of_flat(target), device_id_type=MESH,
        )

    half_groups = groups // 2
    half_width = width // 2

    def tok_batch(part, low, high):
        def one(i, carry):
            target = part * half_groups * n_col + (p.flat + i * 5) % (half_groups * n_col)

            @pl.when(target != p.flat)
            def _():
                tok_copy(target).start()
            return carry

        lax.fori_loop(low, high, one, 0)

    def grad_input(part):
        near = pl.ds(part * half_groups, half_groups)
        w_rows = lambda i: w_v[near, :, :, i * width:(i + 1) * width].reshape(half_width, width)
        total = gm_v[:, part * half_width:(part + 1) * half_width].T
        total = total + product(w_rows(0), dqt_v[...])
        total = total + product_nt(w_rows(1), dk_v[...])
        total = total + product_nt(w_rows(2), dv_v[...])
        dxt_v[near] = total.astype(BF).reshape(half_groups, width // groups, rows)

    count = half_groups * n_col
    table["c0"]()
    grad_input(0)
    made_parts = 1
    for step in PACE:
        if isinstance(step, str):
            table[step]()
            continue
        low, high = step
        if high > count and made_parts == 1:
            grad_input(1)
            made_parts = 2
            own_tok = keep(dxt_v.at[p.g, :, pl.ds(aligned(p.c * span, 128), span)], trecv.at[p.c * slots + p.g])
        for part in range(2):
            first, last = max(low, part * count) - part * count, min(high, part * count + count) - part * count
            if first < last:
                tok_batch(part, first, last)
    for step in LATE:
        table[step]()

    def norm_wait(i, carry):
        source = (p.flat + p.n - i) % p.n
        pltpu.make_async_remote_copy(
            src_ref=nrecv.at[source], dst_ref=nrecv.at[source], send_sem=norm_send.at[i], recv_sem=norm_recv.at[i],
            device_id=p.of_flat(source), device_id_type=MESH,
        ).wait_recv()
        norm_copy(i).wait_send()
        return carry

    lax.fori_loop(1, p.n, norm_wait, 0)
    nsum_ref[...] = jnp.sum(nrecv[...], axis=0)
    joined_end()
    own_tok.wait()

    def tok_wait(i, carry):
        source = (p.flat + p.n - i) % p.n
        landing = trecv.at[(source % n_col) * slots + source // n_col]
        pltpu.make_async_remote_copy(
            src_ref=landing, dst_ref=landing, send_sem=tok_send.at[source], recv_sem=tok_recv.at[source],
            device_id=p.of_flat(source), device_id_type=MESH,
        ).wait_recv()
        tok_copy((p.flat + i) % p.n).wait_send()
        return carry

    lax.fori_loop(1, p.n, tok_wait, 0)
    for m in range(micro):
        for s in range(slots):
            place = jnp.int32(0)
            for j in range(slots):
                place = jnp.where(seq_ref[m, j] == s, jnp.int32(j), place)
            tgrad_ref[m, s] = trecv[m * slots + place]
    for end in ends:
        end()
    lanes.finish()


def backward(dims, seq_order, lengths, qkv, ctx_t, lse, d_context, xt, w_qkv, g_mixed, g_out, g_up, part_x, part_y, n_grads):
    n_dp, n_row, n_col = dims
    groups, n = n_dp * n_row, n_dp * n_row * n_col
    micro, slots = seq_order.shape
    width, rows = ctx_t.shape
    feats, span = width // groups, rows // n_col
    shape = jax.ShapeDtypeStruct
    plan, buffers = [], []
    for name, grad, kind, axes in (
        ("down", part_y, "lanes", DOWN), ("up", g_up, "rows", UP), ("out", g_out, "rows", OUT),
        *((letter, g_out, "rows", axis) for letter, axis in zip("abc", JOINED)),
    ):
        if name == "down":
            lead, each, columns = 2, part_y.shape[1], part_y.shape[2]
        else:
            lead, _, across, columns = grad.shape
            each = across // len(axes)
        for i, axis in enumerate(axes):
            plan.append((name, kind, axis, i * each, each))
            sizes = piece_buffers(kind, axis, lead, each, columns, n_row, groups)
            if name == "down":
                sizes[0] = (16, 128)
            buffers += [pltpu.VMEM(size, BF) for size in sizes]
    outs = (
        shape((micro, slots, feats, span), BF),
        shape((w_qkv.shape[2] * 2, w_qkv.shape[3] // n_col), F32),
        shape((g_out.shape[2] * 2, g_out.shape[3] // n_col), F32),
        shape((g_up.shape[2] * 2, g_up.shape[3] // n_col), F32),
        shape((len(DOWN) * part_y.shape[1], part_y.shape[2] // groups), F32),
        shape((8, 256), F32),
    )
    vm = lambda like, kind=BF: pltpu.VMEM(like.shape, kind)
    temps = [pltpu.VMEM((g.shape[2], g.shape[3] // n_col), F32) for g in (w_qkv, g_out, g_up)]
    carried = [pltpu.VMEM((g.shape[0],) + g.shape[2:], BF) for g in (g_out, g_up)]
    return pl.pallas_call(
        functools.partial(backward_kernel, dims, plan),
        out_shape=outs,
        in_specs=[SM, SM, ANY, ANY, ANY, ANY, ANY, ANY, ANY, ANY, ANY, ANY, ANY, VM],
        out_specs=[VM, VM, VM, VM, VM, VM],
        scratch_shapes=[
            vm(qkv), vm(ctx_t), vm(lse, F32), vm(d_context), vm(xt), vm(w_qkv), vm(g_mixed, F32), *carried, vm(g_out), vm(g_out), vm(g_out),
            pltpu.VMEM((width, rows), BF), pltpu.VMEM((rows, width), BF), pltpu.VMEM((rows, width), BF),
            pltpu.VMEM((rows, 128), F32), pltpu.VMEM((rows, 128), F32),
            pltpu.VMEM((groups, feats, rows), BF), pltpu.VMEM((micro * slots, feats, span), BF),
            pltpu.VMEM((n, 8, 256), F32), *temps,
            DMA((n,)), DMA((n,)), DMA((n,)), DMA((n,)),
            DMA((80,)), DMA((80,)), DMA((16,)), *buffers,
        ],
        compiler_params=pltpu.CompilerParams(
            collective_id=1, has_side_effects=True, vmem_limit_bytes=62 * 2**20
        ),
        name="backward_part",
    )(seq_order, lengths, qkv, ctx_t, lse, d_context, xt, w_qkv, g_mixed, g_out, g_up, part_x, part_y, n_grads)
def layer_norm(values, factor, offset):
    average = jnp.mean(values, axis=-1, keepdims=True)
    centered = values - average
    variance = jnp.mean(centered * centered, axis=-1, keepdims=True)
    return centered * lax.rsqrt(variance + EPSILON) * factor + offset


def gelu_act(values):
    return 0.5 * values * (1.0 + lax.erf(values * ROOT_HALF))


def attention(qkv, length):
    rows, width = qkv.shape[0], qkv.shape[1] // 3
    heads = width // HEAD
    q, k, v = (qkv[:, i * width:(i + 1) * width].reshape(rows, heads, HEAD) for i in range(3))
    scores = jnp.einsum("qhe,khe->hqk", q, k, preferred_element_type=F32) * 0.125
    valid = jnp.arange(rows, dtype=jnp.int32) < length
    scores = jnp.where(valid[None, None, :], scores, NEGATIVE)
    top = jnp.max(scores, axis=-1, keepdims=True)
    exps = jnp.exp(scores - top)
    total = jnp.sum(exps, axis=-1, keepdims=True)
    probs = (exps / total).astype(BF)
    context = jnp.einsum("hqk,khe->qhe", probs, v, preferred_element_type=F32)
    return context.astype(BF).reshape(rows, width), top + jnp.log(total)


def attention_back(qkv, length, stats, d_context):
    rows, width = qkv.shape[0], qkv.shape[1] // 3
    heads = width // HEAD
    q, k, v = (qkv[:, i * width:(i + 1) * width].reshape(rows, heads, HEAD) for i in range(3))
    dc = d_context.reshape(rows, heads, HEAD)
    scores = jnp.einsum("qhe,khe->hqk", q, k, preferred_element_type=F32) * 0.125
    valid = jnp.arange(rows, dtype=jnp.int32) < length
    scores = jnp.where(valid[None, None, :], scores, NEGATIVE)
    soft = jnp.exp(scores - stats)
    d_probs = jnp.einsum("qhe,khe->hqk", dc, v, preferred_element_type=F32)
    delta = jnp.sum(soft * d_probs, axis=-1, keepdims=True)
    d_scores = (soft * (d_probs - delta)).astype(BF)
    dq = jnp.einsum("hqk,khe->qhe", d_scores, k, preferred_element_type=F32) * 0.125
    dk = jnp.einsum("hqk,qhe->khe", d_scores, q, preferred_element_type=F32) * 0.125
    dv = jnp.einsum("hqk,qhe->khe", soft.astype(BF), dc, preferred_element_type=F32)
    return jnp.concatenate([a.astype(BF).reshape(rows, width) for a in (dq, dk, dv)], axis=-1)


def middle(x, context, context_t, cot, w_out, w_up, w_down_t, gain_one, shift_one, gain_two, shift_two):
    mixed = x.astype(F32) + product(context, w_out)
    hidden = layer_norm(mixed, gain_one, shift_one)
    hidden_low = hidden.astype(BF)
    pre_act = product(hidden_low, w_up)
    act_low = gelu_act(pre_act).astype(BF)
    summed = hidden + product_nt(act_low, w_down_t)
    output = layer_norm(summed, gain_two, shift_two).astype(BF)
    _, norm_two_back = jax.vjp(layer_norm, summed, gain_two, shift_two)
    g_summed, g_gain_two, g_shift_two = norm_two_back(cot.astype(F32))
    d_down = g_summed.astype(BF)
    g_down_t = product_tn(d_down, act_low).astype(BF)
    d_act = product(d_down, w_down_t)
    _, gelu_back = jax.vjp(gelu_act, pre_act)
    d_pre = gelu_back(d_act)[0].astype(BF)
    g_up = product_tn(hidden_low, d_pre).astype(BF)
    g_hidden = g_summed + product_nt(d_pre, w_up)
    _, norm_one_back = jax.vjp(layer_norm, mixed, gain_one, shift_one)
    g_mixed, g_gain_one, g_shift_one = norm_one_back(g_hidden)
    d_attn = g_mixed.astype(BF)
    g_out = product(context_t, d_attn).astype(BF)
    d_context = product_nt(d_attn, w_out).astype(BF)
    return output, g_mixed, d_context, g_down_t, g_up, g_out, (g_gain_one, g_shift_one, g_gain_two, g_shift_two)


def take_blocks(blocks, places):
    def body(place_ref, in_ref, out_ref):
        def step(i, carry):
            out_ref[i] = in_ref[place_ref[i]]
            return carry

        lax.fori_loop(0, blocks.shape[0], step, 0)

    return pl.pallas_call(
        body, out_shape=jax.ShapeDtypeStruct(blocks.shape, blocks.dtype), in_specs=[SM, VM], out_specs=VM,
        compiler_params=pltpu.CompilerParams(vmem_limit_bytes=48 * 2**20), name="take_blocks",
    )(places, blocks)


def own_length(lengths, seq_order):
    n_row = lax.axis_size("row")
    slot = lax.axis_index("dp") * n_row + lax.axis_index("row")
    micro = lax.axis_index("col")
    index = jnp.arange(seq_order.shape[1], dtype=jnp.int32)
    order = jnp.sum(jnp.where(jnp.arange(seq_order.shape[0])[:, None] == micro, seq_order, 0), axis=0)
    source = jnp.sum(jnp.where(index == slot, order, 0))
    mine = jnp.sum(jnp.where(jnp.arange(seq_order.shape[0])[:, None] == micro, lengths, 0), axis=0)
    return jnp.sum(jnp.where(index == source, mine, 0))


def local(
    tokens, cotangent, lengths, seq_order, w_qkv, w_out, w_up, w_down, gain_one, shift_one, gain_two, shift_two,
):
    dims = tuple(lax.axis_size(a) for a in ("dp", "row", "col"))
    n_dp, n_row, n_col = dims
    groups = n_dp * n_row
    micro, slots, span, feats = tokens.shape
    width = cotangent.shape[3]
    rows = span * n_col
    direct = n_dp == 2 and n_row == 4 and n_col == 4 and feats % 32 == 0 and w_qkv.shape[0] % 32 == 0
    tok_t = jnp.swapaxes(tokens, 2, 3)
    w_down_t = w_down.T
    norms = jnp.stack([gain_one, shift_one, gain_two, shift_two])
    length = own_length(lengths, seq_order)
    everyone = ("dp", "row", "col")
    if direct:
        each = norms.shape[1]
        place = (lax.axis_index("dp") * n_row + lax.axis_index("row")) * n_col + lax.axis_index("col")
        lane = jnp.arange(256, dtype=jnp.int32)
        here = lane[None, :] == (place * each) % 128 + jnp.arange(each, dtype=jnp.int32)[:, None]
        packed = jnp.sum(jnp.where(here[None], norms[:, :, None].astype(F32), 0.0), axis=1).astype(BF)
        packed = jnp.pad(packed, ((0, 12), (0, 0)))
        xt, w_joined, qkv, context_t, lse, output, g_mixed, d_context, g_out, g_up, part_x, part_y, norm_grads = forward(
            dims, seq_order, lengths, tok_t, cotangent[:, 0], w_qkv, w_out, w_up, w_down_t, packed
        )
    else:
        offset = jnp.arange(micro, dtype=jnp.int32)[:, None] * slots
        sent = take_blocks(tok_t.reshape(micro * slots, feats, span), (seq_order + offset).reshape(-1))
        sent = jnp.swapaxes(sent.reshape(micro, slots, feats, span), 0, 1).reshape(micro * slots, feats, span)
        got = lax.all_to_all(sent, everyone, split_axis=0, concat_axis=0, tiled=True)
        xt = got.reshape(groups, n_col, feats, span).transpose(0, 2, 1, 3).reshape(width, rows)
        cot = lax.all_to_all(cotangent[:, 0], "col", split_axis=0, concat_axis=0, tiled=True).reshape(rows, width)

        def whole(w, row_axes, col_axes):
            w = lax.all_gather(w, col_axes, axis=1, tiled=True)
            return lax.all_gather(w, row_axes, axis=0, tiled=True)

        f_qkv, f_out, f_up = (whole(w, ("dp", "row"), "col") for w in (w_qkv, w_out, w_up))
        f_down_t = whole(w_down_t, "col", ("dp", "row"))
        f_norms = lax.all_gather(norms, everyone, axis=1, tiled=True)
    if direct:
        tgrad, r_qkv, r_out, r_up, r_down_t, n_sum = backward(
            dims, seq_order, lengths, qkv, context_t, lse, d_context, xt, w_joined, g_mixed,
            g_out, g_up, part_x, part_y, norm_grads,
        )
        n_sum = lax.dynamic_slice(n_sum, (0, place * each % 128), (4, each))
    else:
        gains = [f_norms[i].astype(F32) for i in range(4)]
        x = xt.T
        qkv = product(x, f_qkv).astype(BF)
        context, stats = attention(qkv, length)
        output, g_mixed, d_context, g_down_t, g_up, g_out, norm_grads = middle(
            x, context, context.T, cot, f_out, f_up, f_down_t, *gains
        )
        norm_grads = jnp.stack(norm_grads)
        d_qkv = attention_back(qkv, length, stats, d_context)
        g_qkv = product(xt, d_qkv).astype(BF)
        dxt = (g_mixed + product_nt(d_qkv, f_qkv)).astype(BF).T
        n_sum = lax.psum_scatter(norm_grads, everyone, scatter_dimension=1, tiled=True)
        output = lax.all_to_all(output.reshape(n_col, span, width), "col", split_axis=0, concat_axis=0, tiled=True)
        sent = dxt.reshape(groups, feats, n_col, span).transpose(0, 2, 1, 3).reshape(micro * slots, feats, span)
        got = lax.all_to_all(sent, everyone, split_axis=0, concat_axis=0, tiled=True)
        got = jnp.swapaxes(got.reshape(slots, micro, feats, span), 0, 1).reshape(micro * slots, feats, span)
        index = jnp.arange(slots, dtype=jnp.int32)
        inverse = jnp.sum(jnp.where(seq_order[:, :, None] == index, index[None, :, None], 0), axis=1)
        offset = jnp.arange(micro, dtype=jnp.int32)[:, None] * slots
        tgrad = take_blocks(got, (inverse + offset).reshape(-1)).reshape(micro, slots, feats, span)

        def parts(g, row_axes, col_axes):
            g = lax.psum_scatter(g, col_axes, scatter_dimension=1, tiled=True)
            return lax.psum_scatter(g, row_axes, scatter_dimension=0, tiled=True).astype(F32)

        r_qkv, r_out, r_up = (parts(g, ("dp", "row"), "col") for g in (g_qkv, g_out, g_up))
        r_down_t = parts(g_down_t, "col", ("dp", "row"))
    return (
        output[:, None], jnp.swapaxes(tgrad, 2, 3), r_qkv, r_out, r_up, r_down_t.T,
        n_sum[0], n_sum[1], n_sum[2], n_sum[3],
    )


def solution(mesh):
    rows = ("dp", "row")
    every = ("dp", "row", "col")
    in_specs = (
        P(None, None, "col", rows), P(None, rows, "col", None), P(), P(),
        P(rows, "col"), P(rows, "col"), P(rows, "col"), P(rows, "col"),
        P(every), P(every), P(every), P(every),
    )
    out_specs = (
        P(None, rows, "col", None), P(None, None, "col", rows),
        P(rows, "col"), P(rows, "col"), P(rows, "col"), P(rows, "col"),
        P(every), P(every), P(every), P(every),
    )
    return jax.shard_map(local, mesh=mesh, in_specs=in_specs, out_specs=out_specs, check_vma=False)
```

```python
import functools

import jax
import jax.numpy as jnp
from jax import lax
from jax.experimental import pallas as pl
from jax.experimental.pallas import tpu as pltpu
from jax.sharding import PartitionSpec as P

HEAD = 64
NEGATIVE = -1000000000.0
EPSILON = 1e-12
ROOT_HALF = 0.7071067811865476
ROOT_TWO_PI = 0.3989422804014327
MESH = pl.DeviceIdType.MESH
BF = jnp.bfloat16
F32 = jnp.float32
ANY = pl.BlockSpec(memory_space=pl.ANY)
VM = pl.BlockSpec(memory_space=pltpu.VMEM)
SM = pl.BlockSpec(memory_space=pltpu.SMEM)
DMA = pltpu.SemaphoreType.DMA


def aligned(value, step):
    return pl.multiple_of(value, step)


def product(left, right):
    return jnp.dot(left, right, preferred_element_type=F32)


def product_tn(left, right):
    return lax.dot_general(left, right, (((0,), (0,)), ((), ())), preferred_element_type=F32)


def product_nt(left, right):
    return lax.dot_general(left, right, (((1,), (1,)), ((), ())), preferred_element_type=F32)


class Place:
    def __init__(self, n_dp, n_row, n_col):
        self.n_dp, self.n_row, self.n_col = n_dp, n_row, n_col
        self.n = n_dp * n_row * n_col
        self.x = lax.axis_index("dp")
        self.z = lax.axis_index("row")
        self.c = lax.axis_index("col")
        self.y, self.k = self.c // 2, self.c % 2
        self.g = self.x * n_row + self.z
        self.flat = self.g * n_col + self.c

    def of_flat(self, flat):
        group = flat // self.n_col
        return (group // self.n_row, group % self.n_row, flat % self.n_col)

    def dev(self, x=None, z=None, y=None, k=None):
        x = self.x if x is None else x
        z = self.z if z is None else z
        y = self.y if y is None else y
        k = self.k if k is None else k
        return (x, z, y * 2 + k)

    def greet(self):
        sem = pltpu.get_barrier_semaphore()

        def one(i, carry):
            pl.semaphore_signal(
                sem, inc=1, device_id=self.of_flat((self.flat + i) % self.n), device_id_type=MESH
            )
            return carry

        lax.fori_loop(1, self.n, one, 0)

    def met(self):
        pl.semaphore_wait(pltpu.get_barrier_semaphore(), self.n - 1)


class Lanes:
    def __init__(self, send_sems, recv_sems):
        self.send_sems, self.recv_sems, self.sent = send_sems, recv_sems, []
        self.used = [0, 0]

    def take(self, which, count):
        first = self.used[which]
        self.used[which] += count
        return first

    def copy(self, src, dst, device, s, r):
        return pltpu.make_async_remote_copy(
            src_ref=src, dst_ref=dst, send_sem=self.send_sems.at[s],
            recv_sem=self.recv_sems.at[r], device_id=device, device_id_type=MESH,
        )

    def send(self, make):
        self.copy(*make()).start()
        self.sent.append(make)

    def arrived(self, landing, device, r):
        self.copy(landing, landing, device, 0, r).wait_recv()

    def finish(self):
        for make in self.sent:
            self.copy(*make()).wait_send()
        self.sent = []


class Gather:
    def __init__(self, place, lanes, region, first):
        self.p, self.lanes, self.region, self.first = p, lanes, region, first = place, lanes, region, first
        self.to_x, self.to_y, self.to_core = p.dev(x=1 - p.x), p.dev(y=1 - p.y), p.dev(k=1 - p.k)
        self.one, self.two = (self.to_x, self.to_y) if first == "x" else (self.to_y, self.to_x)
        n = p.n_row
        self.s = {name: lanes.take(0, n) for name in ("z", 1, 2, 3, "core")}
        self.r = {name: lanes.take(1, n) for name in ("z", 1, 2, 3, "core")}
        self.far = (p.z + n // 2) % n
        self.near = p.z + 1 - 2 * (p.z % 2)
        self.cross = (self.near + n // 2) % n
        self.to_near = p.dev(z=self.near)

    def side(self, hop):
        p = self.p
        x_side = hop in ((1, 3) if self.first == "x" else (2, 3))
        y_side = hop in ((2, 3) if self.first == "x" else (1, 3))
        return (1 - p.x if x_side else p.x), (1 - p.y if y_side else p.y)

    def at(self, hop, z, k):
        x, y = self.side(hop)
        return self.region(x, z, 1, y, k)

    def line(self, hop, k):
        x, y = self.side(hop)
        return self.region(x, 0, self.p.n_row, y, k)

    def start(self, own):
        p = self.p

        def to(hop, device):
            return lambda: (own, self.at(0, p.z, p.k), device, self.s[hop] + p.z, self.r[hop] + p.z)

        self.lanes.send(to(1, self.one))
        self.lanes.send(to(2, self.two))
        self.own = own

    def z_start(self):
        p, own = self.p, self.own
        self.lanes.send(lambda: (own, self.at(0, p.z, p.k), p.dev(z=self.far), self.s["z"], self.r["z"]))
        self.lanes.send(lambda: (own, self.at(0, p.z, p.k), p.dev(z=self.near), self.s["z"] + 1, self.r["z"] + 1))

    def z_step(self, number):
        p = self.p
        source = (self.far, self.near, self.cross)[number - 1]
        peer = self.far if number == 1 else self.near
        self.lanes.arrived(self.at(0, source, p.k), p.dev(z=peer), self.r["z"] + number - 1)

        def to(device, hop, index):
            def make():
                ref = self.at(0, source, p.k)
                return (ref, ref, device, self.s[hop] + index, self.r[hop] + index)
            return make

        if number == 1:
            self.lanes.send(to(self.to_near, "z", 2))
        self.lanes.send(to(self.one, 1, source))
        self.lanes.send(to(self.two, 2, source))

    def z_steps(self):
        for distance in range(1, self.p.n_row):
            self.z_step(distance)
        self.z_done()

    def z_done(self):
        self.local.wait()
        self.to_other_core(0)

    def to_other_core(self, hop):
        def make():
            line = self.line(hop, self.p.k)
            return (line, line, self.to_core, self.s["core"] + hop, self.r["core"] + hop)
        self.lanes.send(make)

    def first_steps(self):
        p = self.p
        for source in (p.z, self.far, self.near, self.cross):
            self.lanes.arrived(self.at(1, source, p.k), self.one, self.r[1] + source)

            def make(source=source):
                ref = self.at(1, source, p.k)
                return (ref, ref, self.two, self.s[3] + source, self.r[3] + source)

            self.lanes.send(make)
        self.to_other_core(1)

    def second_steps(self, hops=(2, 3)):
        p = self.p
        for hop in hops:
            for i in range(p.n_row):
                self.lanes.arrived(self.at(hop, i, p.k), self.two, self.r[hop] + i)
            self.to_other_core(hop)

    def stage(self, name):
        if name == "z":
            self.z_start()
        elif name == "f":
            self.first_steps()
        elif name == "s":
            self.second_steps((2,))
        elif name == "t":
            self.second_steps((3,))
        else:
            self.z_step(int(name))
            if name == "3":
                self.z_done()

    def end(self):
        for hop in range(4):
            self.lanes.arrived(self.line(hop, 1 - self.p.k), self.to_core, self.r["core"] + hop)


def rows_region(ref, n_row, low=0, high=None):
    width = ref.shape[3] // 2
    high = width if high is None else high

    def region(x, z, nz, y, k):
        columns = pl.ds(aligned(y * width + low, 128), high - low)
        if nz == 1:
            return ref.at[x * n_row + z, k, :, columns]
        return ref.at[pl.ds(x * n_row + z, nz), k, :, columns]

    return region


def lanes_region(ref, n_dp, n_row, low=0, high=None):
    width = ref.shape[3] // (n_dp * n_row)
    high = ref.shape[2] if high is None else high

    def region(x, z, nz, y, k):
        return ref.at[y, k, pl.ds(low, high - low), pl.ds(aligned((x * n_row + z) * width, 128), nz * width)]

    return region


CHUNK = 512
ROWS = 256
BATCH = (6, 6, 6, 6, 7)
FIRST = {"q": "x", "o": "y", "u": "y", "v": "y", "d": "y", "e": "y"}
DOWN, UP, OUT, JOINED = "xyx", "xyx", "y", "xyx"
SCHEDULE = {
    "first": {4: ("oz", "uz",), 5: ("o1", "u1", "vz",)},
    "turn": {0: ("o2", "u2", "v1", "dz",), 2: ("o3", "u3", "v2", "d1",)},
    "project": {0: ("of", "v3", "d2",), 3: ("uf", "d3",), 6: ("vf", "ez",)},
    "attend": {0: ("df", "os", "e1",), 1: ("e2",), 2: ("us", "e3",), 3: ("ot", "ut",), 4: ("ef",), 5: ("vs",), 6: ("vt",), 7: ("c1",), 8: ("c2", "c3",), 9: ("ds",), 11: ("dt",)},
    "mix": {1: ("es",)},
    "rise": {0: ("et",)},
}


def forward_kernel(
    dims, seq_ref, len_ref, tok_ref, cot_ref, qkv_ref, out_ref, up_ref, down_ref, norm_ref,
    xt_out, wqkv_out, qkv_out, ctx_out, lse_out, output_out, gm_out, dctx_out, gout_out, gup_out, part_x_out, part_y_out, nsum_out,
    tsend, half_qkv, half_out, half_up, pair_qkv, pair_out, pair_up,
    xt_v, x_v, w_v, wide_v, ctx_v, lse_v, wout_v, wup_v, wdown_v, norm_v, gains_v, cot_v, act_v, mixed_v, gsum_v, hl_v,
    output_v, down_v, attn_v, dctx_v, turn_v, nsum_v,
    tok_send, tok_recv, norm_send, norm_recv, cot_send, cot_recv, w_send, w_recv, half_send, half_recv, local_sem, out_send, out_recv, r_send, r_recv,
    *pieces,
):
    n_dp, n_row, n_col = dims
    p = Place(n_dp, n_row, n_col)
    micro, slots, _, span = tok_ref.shape
    rows, width = x_v.shape
    qkv_v = wide_v.at[:, pl.ds(0, 3 * width)]
    p.greet()
    for m in range(micro):
        for j in range(slots):
            tsend[m * slots + j] = tok_ref[m, seq_ref[m, j]]
    p.met()
    halves = Lanes(half_send, half_recv)
    lanes = Lanes(w_send, w_recv)
    partner = p.dev(k=1 - p.k)
    for i, (block, landing) in enumerate(((qkv_ref, half_qkv), (out_ref, half_out), (up_ref, half_up))):
        def make(i=i, block=block, landing=landing):
            count = landing.shape[0]
            return (block.at[pl.ds(aligned((1 - p.k) * count, 16), count), :], landing, partner, i, i)
        halves.send(make)

    def join(i, block, landing, pair):
        halves.arrived(landing, partner, i)
        count, across = landing.shape
        mine = block[pl.ds(aligned(p.k * count, 16), count), :]
        theirs = landing[...]
        pair[:, :across] = jnp.where(p.k == 0, mine, theirs)
        pair[:, across:] = jnp.where(p.k == 0, theirs, mine)

    local = []

    def keep(src, dst):
        made = pltpu.make_async_copy(src, dst, local_sem.at[len(local)])
        made.start()
        local.append(made)
        return made

    region_qkv = rows_region(w_v, n_row)
    join(0, qkv_ref, half_qkv, pair_qkv)
    own_w = keep(pair_qkv, region_qkv(p.x, p.z, 1, p.y, p.k))
    g_qkv = Gather(p, lanes, region_qkv, FIRST["q"])
    g_qkv.local = own_w
    g_qkv.start(pair_qkv)
    g_qkv.z_start()

    def tok_copy(i):
        target = (p.flat + i) % p.n
        return pltpu.make_async_remote_copy(
            src_ref=tsend.at[(target % n_col) * slots + target // n_col],
            dst_ref=xt_v.at[p.g, :, pl.ds(aligned(p.c * span, 128), span)],
            send_sem=tok_send.at[i], recv_sem=tok_recv.at[i],
            device_id=p.of_flat(target), device_id_type=MESH,
        )

    def norm_copy(i):
        return pltpu.make_async_remote_copy(
            src_ref=norm_ref, dst_ref=norm_v.at[p.flat],
            send_sem=norm_send.at[i], recv_sem=norm_recv.at[i],
            device_id=p.of_flat((p.flat + i) % p.n), device_id_type=MESH,
        )

    sent = [1]

    def tok_batch(count):
        def one(j, carry):
            tok_copy((j * 13) % p.n).start()
            return carry

        lax.fori_loop(sent[0], min(sent[0] + count, p.n), one, 0)
        sent[0] = min(sent[0] + count, p.n)

    def norm_start(i, carry):
        norm_copy(i).start()
        return carry

    tok_batch(BATCH[0])
    own_tok = keep(tsend.at[p.c * slots + p.g], xt_v.at[p.g, :, pl.ds(aligned(p.c * span, 128), span)])

    waves = []

    def wave(own, region, first):
        gather = Gather(p, lanes, region, first)
        gather.local = keep(own, region(p.x, p.z, 1, p.y, p.k))
        gather.start(own)
        waves.append(gather)

    join(1, out_ref, half_out, pair_out)
    wave(pair_out, rows_region(wout_v, n_row), FIRST["o"])
    join(2, up_ref, half_up, pair_up)
    cut = pair_up.shape[1] // 2
    wave(pair_up.at[:, pl.ds(0, cut)], rows_region(wup_v, n_row, 0, cut), FIRST["u"])
    wave(pair_up.at[:, pl.ds(cut, cut)], rows_region(wup_v, n_row, cut, 2 * cut), FIRST["v"])
    cut = down_ref.shape[0] // 2
    wave(down_ref.at[pl.ds(0, cut), :], lanes_region(wdown_v, n_dp, n_row, 0, cut), FIRST["d"])
    wave(down_ref.at[pl.ds(cut, cut), :], lanes_region(wdown_v, n_dp, n_row, cut, 2 * cut), FIRST["e"])
    lax.fori_loop(1, p.n, norm_start, 0)
    own_norm = keep(norm_ref, norm_v.at[p.flat])

    def cot_copy(i):
        target = (p.c + i) % n_col
        return pltpu.make_async_remote_copy(
            src_ref=cot_ref.at[target], dst_ref=cot_v.at[p.c],
            send_sem=cot_send.at[i], recv_sem=cot_recv.at[i],
            device_id=(p.x, p.z, target), device_id_type=MESH,
        )

    own_cot = keep(cot_ref.at[p.c], cot_v.at[p.c])
    names = dict(zip("ouvde", waves))

    def begin_cot(i):
        cot_copy(i).start()

    def agenda(phase):
        table = {}
        for turn, steps in SCHEDULE.get(phase, {}).items():
            table[turn] = [functools.partial(begin_cot, int(step[1:])) if step[0] == "c" else functools.partial(names[step[0]].stage, step[1:]) for step in steps]
        return table

    first = agenda("first")

    def now(turn):
        for act in first.get(turn, ()):
            act()

    now(0)
    for distance in range(1, n_row):
        g_qkv.z_step(distance)
        tok_batch(BATCH[distance])
        now(distance)
    g_qkv.z_done()
    g_qkv.first_steps()
    tok_batch(BATCH[4])
    now(4)
    g_qkv.second_steps()
    tok_batch(p.n)
    now(5)
    own_tok.wait()

    def tok_wait(i, carry):
        source = (p.flat + p.n - i) % p.n
        landing = xt_v.at[source // n_col, :, pl.ds(aligned((source % n_col) * span, 128), span)]
        pltpu.make_async_remote_copy(
            src_ref=landing, dst_ref=landing, send_sem=tok_send.at[i], recv_sem=tok_recv.at[i],
            device_id=p.of_flat(source), device_id_type=MESH,
        ).wait_recv()
        return carry

    lax.fori_loop(1, p.n, tok_wait, 0)
    keep(xt_v, xt_out)

    def turn(i, carry):
        run_events(i, agenda("turn"))
        at = pl.ds(aligned(i * 256, 256), 256)
        x_v[at, :] = xt_v[:, :, at].reshape(width, 256).T
        return carry

    lax.fori_loop(0, rows // 256, turn, 0)
    g_qkv.end()
    keep(w_v, wqkv_out)

    def project(i, carry):
        run_events(i, agenda("project"))
        at = pl.ds(aligned(i * 256, 256), 256)
        wide_v[:, at] = product(x_v[...], w_v[:, :, :, at].reshape(width, 256)).astype(BF)
        return carry

    lax.fori_loop(0, 3 * width // 256, project, 0)
    kept_qkv = keep(qkv_v, qkv_out)
    out, up_a, up_b, down_a, down_b = waves
    length = len_ref[p.c, seq_ref[p.c, p.g]]
    bias = jnp.where(lax.broadcasted_iota(jnp.int32, (rows, 1), 0) < length, 0.0, NEGATIVE)
    chunks = rows // CHUNK

    def attend(step, carry):
        run_events(step, agenda("attend"))
        pair, at_row = step // chunks, step % chunks
        columns = [pl.ds(aligned(i * width + pair * 128, 128), 128) for i in range(3)]
        keys = wide_v[:, columns[1]]
        values_t = wide_v[:, columns[2]].T
        lane = lax.broadcasted_iota(jnp.int32, (rows, 128), 1)
        own_rows = pl.ds(aligned(at_row * CHUNK, CHUNK), CHUNK)
        queries = wide_v[own_rows, columns[0]] * jnp.asarray(0.125, BF)
        for h in range(2):
            mine = jnp.where((lane < HEAD) == (h == 0), keys, jnp.zeros_like(keys))
            scores = product_nt(mine, queries) + bias
            top = jnp.max(scores, axis=0, keepdims=True)
            exps = jnp.exp(scores - top)
            total = jnp.sum(exps, axis=0, keepdims=True)
            context = product(values_t[h * HEAD:(h + 1) * HEAD], exps.astype(BF))
            head_rows = pl.ds(aligned(pair * 128 + h * HEAD, HEAD), HEAD)
            ctx_v[head_rows, own_rows] = (context * (1.0 / total)).astype(BF)
            lse_v[2 * pair + h, :, own_rows] = top + jnp.log(total)
        return carry

    lax.fori_loop(0, width // 128 * chunks, attend, 0)
    keep(ctx_v, ctx_out)
    keep(lse_v, lse_out)

    own_norm.wait()

    def norm_wait(i, carry):
        source = (p.flat + p.n - i) % p.n
        pltpu.make_async_remote_copy(
            src_ref=norm_ref, dst_ref=norm_v.at[source], send_sem=norm_send.at[i], recv_sem=norm_recv.at[i],
            device_id=p.of_flat(source), device_id_type=MESH,
        ).wait_recv()
        return carry

    lax.fori_loop(1, p.n, norm_wait, 0)
    each = width // p.n
    gains_v[...] = jnp.zeros_like(gains_v)
    for source in range(p.n):
        low = source * each // 128 * 128
        gains_v[:, low:low + 256] += norm_v[source].astype(F32)
    gain_one, shift_one, gain_two, shift_two = (gains_v[i:i + 1, :width] for i in range(4))

    def normal(values):
        centered = values - jnp.mean(values, axis=-1, keepdims=True)
        scale = lax.rsqrt(jnp.mean(centered * centered, axis=-1, keepdims=True) + EPSILON)
        return centered * scale, scale

    def normal_back(grad, unit, scale, gain):
        grad = grad * gain
        return scale * (grad - jnp.mean(grad, axis=-1, keepdims=True) - unit * jnp.mean(grad * unit, axis=-1, keepdims=True))

    nsum_v[...] = jnp.zeros_like(nsum_v)
    whole = lambda ref: ref[...].reshape(width, -1)
    out.end()

    def mix(step, carry):
        run_events(step, agenda("mix"))
        at = pl.ds(aligned(step * ROWS, ROWS), ROWS)
        mixed = x_v[at, :].astype(F32) + product_tn(ctx_v[:, at], whole(wout_v))
        mixed_v[at, :] = mixed
        unit, _ = normal(mixed)
        hl_v[at, :] = (unit * gain_one + shift_one).astype(BF)
        return carry

    lax.fori_loop(0, rows // ROWS, mix, 0)
    up_a.end()
    up_b.end()
    kept_qkv.wait()

    def rise(step, carry):
        run_events(step, agenda("rise"))
        at = pl.ds(aligned(step * 256, 256), 256)
        pre = product(hl_v[...], wup_v[:, :, :, at].reshape(width, 256))
        half = 0.5 * (1.0 + lax.erf(pre * ROOT_HALF))
        act_v[:, at] = (pre * half).astype(BF)
        wide_v[:, at] = (half + pre * jnp.exp(pre * pre * -0.5) * ROOT_TWO_PI).astype(BF)
        return carry

    lax.fori_loop(0, 4 * width // 256, rise, 0)
    down_a.end()
    down_b.end()
    for i in range(1, n_col):
        source = (p.c + n_col - i) % n_col
        pltpu.make_async_remote_copy(
            src_ref=cot_v.at[source], dst_ref=cot_v.at[source],
            send_sem=cot_send.at[i], recv_sem=cot_recv.at[i],
            device_id=(p.x, p.z, source), device_id_type=MESH,
        ).wait_recv()
    own_cot.wait()

    def out_copy(target):
        return pltpu.make_async_remote_copy(
            src_ref=output_v.at[pl.ds(aligned(target * span, 16), span), :], dst_ref=output_out.at[p.c],
            send_sem=out_send.at[target], recv_sem=out_recv.at[p.c],
            device_id=(p.x, p.z, target), device_id_type=MESH,
        )

    def fall(step, carry):
        at = pl.ds(aligned(step * ROWS, ROWS), ROWS)
        unit_one, _ = normal(mixed_v[at, :])
        summed = unit_one * gain_one + shift_one + product_nt(act_v[at, :], whole(wdown_v))
        unit, scale = normal(summed)
        output_v[at, :] = (unit * gain_two + shift_two).astype(BF)
        per = span // ROWS
        cot = cot_v[step // per, pl.ds(aligned(step % per * ROWS, ROWS), ROWS), :].astype(F32)
        nsum_v[2:3, :width] += jnp.sum(cot * unit, axis=0, keepdims=True)
        nsum_v[3:4, :width] += jnp.sum(cot, axis=0, keepdims=True)
        grad = normal_back(cot, unit, scale, gain_two)
        gsum_v[at, :] = grad
        down_v[at, :] = grad.astype(BF)
        turn_v[:, at] = grad.T.astype(BF)
        target = step // per

        @pl.when((step % per == per - 1) & (target != p.c))
        def _():
            out_copy(target).start()
        return carry

    lax.fori_loop(0, rows // ROWS, fall, 0)
    keep(output_v.at[pl.ds(aligned(p.c * span, 16), span), :], output_out.at[p.c])

    def rise_back(step, carry):
        at = pl.ds(aligned(step * 512, 512), 512)
        back = product(down_v[...], wdown_v[:, :, :, at].reshape(width, 512))
        wide_v[:, at] = (back * wide_v[:, at].astype(F32)).astype(BF)
        return carry

    lax.fori_loop(0, 4 * width // 512, rise_back, 0)
    lanes.finish()

    def grad_down(step, carry):
        at = pl.ds(aligned(step * 512, 512), 512)
        wdown_v[:, :, :, at] = product(turn_v[...], act_v[:, at]).astype(BF).reshape(wdown_v.shape[:3] + (512,))
        return carry

    lax.fori_loop(0, 4 * width // 512, grad_down, 0)

    rlanes = Lanes(r_send, r_recv)
    early = []
    piece_rows = wdown_v.shape[2] // len(DOWN)
    for i, axis in enumerate(DOWN):
        at = pl.ds(i * piece_rows, piece_rows)
        piece = Reduce(
            p, rlanes, wdown_v.at[:, 1 - p.k, at], wdown_v.at[:, p.k, at], pieces[2 * i:2 * i + 2] + (None, None, None), "lanes", axis
        )
        piece.start()
        early.append(piece)

    def mix_back(step, carry):
        run_events(step, {1: (early[0].one, early[1].one), 2: (early[2].one,)})
        at = pl.ds(aligned(step * ROWS, ROWS), ROWS)
        grad = gsum_v[at, :] + product_nt(wide_v[at, :], whole(wup_v))
        unit, scale = normal(mixed_v[at, :])
        nsum_v[0:1, :width] += jnp.sum(grad * unit, axis=0, keepdims=True)
        nsum_v[1:2, :width] += jnp.sum(grad, axis=0, keepdims=True)
        grad = normal_back(grad, unit, scale, gain_one)
        gsum_v[at, :] = grad
        low = grad.astype(BF)
        attn_v[at, :] = low
        dctx_v[at, :] = product_nt(low, whole(wout_v)).astype(BF)
        turn_v[:, at] = hl_v[at, :].T
        return carry

    lax.fori_loop(0, rows // ROWS, mix_back, 0)
    keep(gsum_v, gm_out)
    keep(dctx_v, dctx_out)
    keep(nsum_v, nsum_out)

    def grad_up(step, carry):
        at = pl.ds(aligned(step * 512, 512), 512)
        wup_v[:, :, :, at] = product(turn_v[...], wide_v[:, at]).astype(BF).reshape(wup_v.shape[:3] + (512,))
        return carry

    lax.fori_loop(0, 4 * width // 512, grad_up, 0)
    keep(wup_v, gup_out)

    def grad_out(step, carry):
        at = pl.ds(aligned(step * 256, 256), 256)
        wout_v[:, :, :, at] = product(ctx_v[...], attn_v[:, at]).astype(BF).reshape(wout_v.shape[:3] + (256,))
        return carry

    lax.fori_loop(0, width // 256, grad_out, 0)
    keep(wout_v, gout_out)
    outs = {"x": [part_x_out.at[i] for i in range(DOWN.count("x"))], "y": [part_y_out.at[i] for i in range(DOWN.count("y"))]}
    for piece, axis in zip(early, DOWN):
        piece.add_half(1)
        keep(piece.b[1], outs[axis].pop(0))

    def small_wait(i, carry):
        norm_copy(i).wait_send()
        tok_copy(i).wait_send()
        return carry

    lax.fori_loop(1, p.n, small_wait, 0)
    for i in range(1, n_col):
        cot_copy(i).wait_send()
        source = (p.c + n_col - i) % n_col
        pltpu.make_async_remote_copy(
            src_ref=output_out.at[source], dst_ref=output_out.at[source],
            send_sem=out_send.at[source], recv_sem=out_recv.at[source],
            device_id=(p.x, p.z, source), device_id_type=MESH,
        ).wait_recv()
        out_copy((p.c + i) % n_col).wait_send()
    waited = [own_tok, own_norm, own_w, own_cot, kept_qkv] + [gather.local for gather in waves]
    for made in local:
        if not any(made is w for w in waited):
            made.wait()
    halves.finish()
    rlanes.finish()


def run_events(step, events):
    for when_, acts in events.items():
        def act(acts=acts):
            for a in acts:
                a()
        pl.when(step == when_)(act)


def forward(dims, seq_order, lengths, tok_t, cot, w_qkv, w_out, w_up, w_down_t, norms):
    n_dp, n_row, n_col = dims
    groups, n = n_dp * n_row, n_dp * n_row * n_col
    micro, slots, feats, span = tok_t.shape
    rows, width = n_col * span, groups * feats
    heads = width // HEAD
    qr, qc = w_qkv.shape
    orow, oc = w_out.shape
    ur, uc = w_up.shape
    dr, dc = w_down_t.shape
    shape = jax.ShapeDtypeStruct
    joined = (groups, 2, qr // 2, qc * n_col)
    out_all = (groups, 2, orow // 2, oc * n_col)
    up_all = (groups, 2, ur // 2, uc * n_col)
    down_all = (2, 2, dr, dc * groups)
    outs = (
        shape((groups, feats, rows), BF),
        shape(joined, BF),
        shape((rows, 3 * width), BF),
        shape((width, rows), BF),
        shape((heads, 1, rows), F32),
        shape((n_col, span, width), BF),
        shape((rows, width), F32),
        shape((rows, width), BF),
        shape(out_all, BF),
        shape(up_all, BF),
        shape((DOWN.count("x"), 2, dr // len(DOWN), dc * groups // 2), BF),
        shape((DOWN.count("y"), dr // len(DOWN), dc * groups), BF),
        shape((8, width + 256), F32),
    )
    vm = pltpu.VMEM
    early_buffers = [
        vm(size, BF) for axis in DOWN for size in piece_buffers("lanes", axis, 0, dr // len(DOWN), dc * groups, n_row, groups)[:2]
    ]
    return pl.pallas_call(
        functools.partial(forward_kernel, dims),
        out_shape=outs,
        in_specs=[SM, SM, VM, ANY, VM, VM, VM, VM, VM],
        out_specs=[ANY] * len(outs),
        scratch_shapes=[
            vm((micro * slots, feats, span), BF),
            vm((qr // 2, qc), BF), vm((orow // 2, oc), BF), vm((ur // 2, uc), BF),
            vm((qr // 2, qc * 2), BF), vm((orow // 2, oc * 2), BF), vm((ur // 2, uc * 2), BF),
            vm((groups, feats, rows), BF),
            vm((rows, width), BF),
            vm(joined, BF),
            vm((rows, 4 * width), BF),
            vm((width, rows), BF),
            vm((heads, 1, rows), F32),
            vm(out_all, BF), vm(up_all, BF), vm(down_all, BF),
            vm((n,) + norms.shape, BF),
            vm((norms.shape[0], width + 256), F32),
            vm(cot.shape, BF),
            vm((rows, 4 * width), BF),
            vm((rows, width), F32), vm((rows, width), F32),
            vm((rows, width), BF), vm((rows, width), BF), vm((rows, width), BF), vm((rows, width), BF), vm((rows, width), BF),
            vm((width, rows), BF),
            vm((8, width + 256), F32),
            DMA((n,)), DMA((n,)), DMA((n,)), DMA((n,)), DMA((n_col,)), DMA((n_col,)),
            DMA((6 * 5 * n_row,)), DMA((6 * 5 * n_row,)), DMA((3,)), DMA((3,)), DMA((24,)), DMA((n_col,)), DMA((n_col,)),
            DMA((24,)), DMA((24,)), *early_buffers,
        ],
        compiler_params=pltpu.CompilerParams(
            collective_id=0, has_side_effects=True, vmem_limit_bytes=63 * 2**20
        ),
        name="forward_part",
    )(seq_order, lengths, tok_t, cot, w_qkv, w_out, w_up, w_down_t, norms)


BACK_CHUNK = 256
SUMS = {
    0: ("u20", "o00",), 1: ("u01", "u11",), 3: ("u21", "d13",), 4: ("d03",), 6: ("d23", "d14",), 7: ("d04",), 8: ("a0", "u02",), 9: ("o01", "d24", "d15",), 10: ("a1", "d05",),
    12: ("u12", "d25",), 14: ("u22", "u03",), 16: ("b0",), 17: ("u13", "u04",), 18: ("o02", "b1",), 20: ("u14", "u05",), 21: ("a2", "u23",), 22: ("u15",), 23: ("o03",),
}
PACE = ((0, 16), "c0", "c1", "a3", "b2", "u24", "o04", (16, 32), "c2", "a4", "b3", "c3", "b4", "c4")
LATE = ("o05", "u25")


def add_into(target, term):
    shape = target.shape
    if len(shape) == 2:
        target[...] = (target[...].astype(F32) + term[...].astype(F32)).astype(BF)
        return

    def body(i, carry):
        target[i] = (target[i].astype(F32) + term[i].astype(F32)).astype(BF)
        return carry

    lax.fori_loop(0, shape[0], body, 0)


class Reduce:
    def __init__(self, place, lanes, theirs, mine, buffers, kind, first):
        self.p, self.lanes, self.theirs, self.mine, self.b = place, lanes, theirs, mine, buffers
        self.kind, self.axes = kind, ("x", "y") if first == "x" else ("y", "x")
        self.s = [lanes.take(0, 1) for _ in range(3)] + [lanes.take(0, 3)]
        self.r = [lanes.take(1, 1) for _ in range(3)] + [lanes.take(1, 3)]
        n = place.n_row
        self.far = (place.z + n // 2) % n
        self.near = place.z + 1 - 2 * (place.z % 2)
        self.cross = (self.near + n // 2) % n

    def start(self):
        p = self.p
        self.lanes.send(lambda: (self.theirs, self.b[0], p.dev(k=1 - p.k), self.s[0], self.r[0]))

    def half(self, ref, axis, side):
        if self.kind == "lanes" and axis == "y":
            return ref.at[side]
        if self.kind == "rows" and axis == "x":
            count = ref.shape[0] // 2
            return ref.at[pl.ds(side * count, count)]
        width = ref.shape[-1] // 2
        lead = (slice(None),) * (len(ref.shape) - 1)
        return ref.at[lead + (pl.ds(aligned(side * width, 128), width),)]

    def where(self, axis):
        p = self.p
        return (p.x, p.dev(x=1 - p.x)) if axis == "x" else (p.y, p.dev(y=1 - p.y))

    def send_half(self, stage):
        def make():
            side, peer = self.where(self.axes[stage - 1])
            return (self.half(self.b[stage - 1], self.axes[stage - 1], 1 - side), self.b[stage], peer, self.s[stage], self.r[stage])

        self.lanes.send(make)

    def add_half(self, stage):
        side, peer = self.where(self.axes[stage - 1])
        self.lanes.arrived(self.b[stage], peer, self.r[stage])
        add_into(self.b[stage], self.half(self.b[stage - 1], self.axes[stage - 1], side))

    def one(self):
        p = self.p
        self.lanes.arrived(self.b[0], p.dev(k=1 - p.k), self.r[0])
        add_into(self.b[0], self.mine)
        self.send_half(1)

    def two(self):
        self.add_half(1)
        self.send_half(2)

    def part(self, z):
        ref = self.b[2]
        if self.kind == "rows":
            return ref.at[z]
        width = self.b[3].shape[-1]
        return ref.at[:, pl.ds(aligned(z * width, 128), width)]

    def three(self):
        p = self.p
        self.add_half(2)
        for i, target in enumerate((self.cross, self.near)):
            def make(i=i, target=target):
                return (self.part(target), self.b[3].at[1 - i], p.dev(z=self.near), self.s[3] + i, self.r[3] + i)
            self.lanes.send(make)

    def four(self):
        p = self.p
        self.lanes.arrived(self.b[3].at[1], p.dev(z=self.near), self.r[3])
        add_into(self.b[3].at[1], self.part(self.far))
        self.lanes.send(lambda: (self.b[3].at[1], self.b[4], p.dev(z=self.far), self.s[3] + 2, self.r[3] + 2))

    def five(self):
        p = self.p
        self.lanes.arrived(self.b[3].at[0], p.dev(z=self.near), self.r[3] + 1)
        total = self.part(p.z)[...].astype(F32) + self.b[3][0].astype(F32)
        self.lanes.arrived(self.b[4], p.dev(z=self.far), self.r[3] + 2)
        return total + self.b[4][...].astype(F32)


def piece_buffers(kind, first, lead, rows, columns, n_row, groups):
    if kind == "lanes":
        one = (2, rows, columns // 2) if first == "x" else (rows, columns)
        return [(2, rows, columns), one, (rows, columns // 2), (2, rows, columns // groups), (rows, columns // groups)]
    one = (lead // 2, rows, columns) if first == "x" else (lead, rows, columns // 2)
    return [(lead, rows, columns), one, (lead // 2, rows, columns // 2), (2, rows, columns // 2), (rows, columns // 2)]


def backward_kernel(
    dims, plan, seq_ref, len_ref, qkv_ref, ctx_ref, lse_ref, dctx_ref, xt_ref, w_ref, gm_ref, gout_ref, gup_ref, part_x_ref, part_y_ref,
    ngrad_ref, tgrad_ref, rqkv_ref, rout_ref, rup_ref, rdown_ref, nsum_ref, *scratch,
):
    n_dp, n_row, n_col = dims
    p = Place(n_dp, n_row, n_col)
    groups = n_dp * n_row
    (
        qkv_v, ctx_v, lse_v, dctx_v, xt_v, w_v, gm_v, m_out, m_up, ga_v, gb_v, gc_v, dqt_v, dk_v, dv_v, acc_k, acc_v, dxt_v, trecv,
        nrecv, fq, fo, fu, tok_send, tok_recv, norm_send, norm_recv, w_send, w_recv, local_sem,
    ) = scratch[:30]
    pieces = scratch[30:]
    micro, slots, _, span = tgrad_ref.shape
    width, rows = ctx_ref.shape
    p.greet()
    local = []

    def keep(src, dst):
        made = pltpu.make_async_copy(src, dst, local_sem.at[len(local)])
        made.start()
        local.append(made)
        return made

    needed = [keep(qkv_ref, qkv_v), keep(dctx_ref, dctx_v), keep(ctx_ref, ctx_v), keep(lse_ref, lse_v)]
    mine_up = keep(gup_ref.at[:, p.k], m_up)
    mine_out = keep(gout_ref.at[:, p.k], m_out)
    xt_load = keep(xt_ref, xt_v)
    later = [keep(w_ref, w_v), keep(gm_ref, gm_v)]
    p.met()
    lanes = Lanes(w_send, w_recv)
    partner = p.dev(k=1 - p.k)
    waves = {"down": [], "up": [], "out": [], "a": [], "b": [], "c": []}
    parts = []
    made_here = {"a": ga_v, "b": gb_v, "c": gc_v}
    whole = {"up": gup_ref, "out": gout_ref, **made_here}
    carried = {"up": m_up, "out": m_out}
    sources = {"x": [part_x_ref.at[i] for i in range(DOWN.count("x"))], "y": [part_y_ref.at[i] for i in range(DOWN.count("y"))]}
    for index, (name, kind, first, low, count) in enumerate(plan):
        if name == "down":
            piece = Reduce(p, lanes, None, None, pieces[5 * index:5 * index + 5], kind, first)
            parts.append(keep(sources[first].pop(0), piece.b[1]))
            waves["down"].append(piece)
            continue
        at = pl.ds(low, count)
        theirs = whole[name].at[:, 1 - p.k, at]
        mine = made_here[name].at[:, p.k, at] if name in made_here else carried[name].at[:, at]
        waves[name].append(Reduce(p, lanes, theirs, mine, pieces[5 * index:5 * index + 5], kind, first))
    d, u, o = waves["down"], waves["up"], waves["out"]
    joined = [waves[name][0] for name in "abc"]

    def window(device):
        return pl.ds(aligned(device * (width // p.n) // 128 * 128, 128), 256)

    def norm_copy(i):
        target = (p.flat + i) % p.n
        return pltpu.make_async_remote_copy(
            src_ref=ngrad_ref.at[:, window(target)], dst_ref=nrecv.at[p.flat],
            send_sem=norm_send.at[i], recv_sem=norm_recv.at[i],
            device_id=p.of_flat(target), device_id_type=MESH,
        )

    def norm_start(i, carry):
        norm_copy(i).start()
        return carry

    u[0].start()
    u[1].start()
    for made, piece in zip(parts, d):
        made.wait()
        piece.send_half(2)
    lax.fori_loop(1, p.n, norm_start, 0)
    nrecv[p.flat] = ngrad_ref[:, window(p.flat)]
    for made in needed:
        made.wait()
    mine_up.wait()
    mine_out.wait()

    def finish_rows(piece, temp, result, low):
        total = piece()
        count, across = total.shape[0], total.shape[1] // 2
        half_rows = result.shape[0] // 2
        temp[pl.ds(low, count), :] = jnp.where(p.k == 0, total[:, across:], total[:, :across])
        result[pl.ds(aligned(p.k * half_rows + low, 16), count), :] = jnp.where(p.k == 0, total[:, :across], total[:, across:])
        s, r = lanes.take(0, 1), lanes.take(1, 1)
        place = lambda k: result.at[pl.ds(aligned(k * half_rows + low, 16), count), :]
        lanes.send(lambda: (temp.at[pl.ds(low, count), :], place(p.k), partner, s, r))
        ends.append(lambda: lanes.arrived(place(1 - p.k), partner, r))

    ends = []

    def finish_down(piece, low):
        total = piece.five()
        rdown_ref[pl.ds(low, total.shape[0]), :] = total

    lows = {name: [low for other, _, _, low, _ in plan if other == name] for name in waves}
    down_end = [functools.partial(finish_down, piece, low) for piece, low in zip(d, lows["down"])]
    up_end = [functools.partial(finish_rows, piece.five, fu, rup_ref, low) for piece, low in zip(u, lows["up"])]
    out_end = [functools.partial(finish_rows, piece.five, fo, rout_ref, low) for piece, low in zip(o, lows["out"])]

    def joined_total():
        blocks = [[total[:, i * 128:(i + 1) * 128] for i in range(3)] for total in (piece.five() for piece in joined)]
        middle = [piece[1] for piece in blocks]
        queries = [piece[0] for piece in blocks] + middle + [piece[2] for piece in blocks]
        return jnp.concatenate(queries, axis=1)

    def joined_end():
        finish_rows(joined_total, fq, rqkv_ref, 0)

    xt = lambda: xt_v[...].reshape(width, rows)
    pairs = width // 128

    def grad_part(grad, number):
        near, far = number, number + pairs // 2
        columns = lambda pair: slice(pair * 128, pair * 128 + 128)
        terms = (
            lambda: product_nt(xt(), dqt_v[columns(near), :]), lambda: product_nt(xt(), dqt_v[columns(far), :]),
            lambda: product(xt(), dk_v[:, columns(near)]), lambda: product(xt(), dk_v[:, columns(far)]),
            lambda: product(xt(), dv_v[:, columns(near)]), lambda: product(xt(), dv_v[:, columns(far)]),
        )
        for i, term in enumerate(terms):
            grad[:, :, :, columns(i)] = term().astype(BF).reshape(groups, 2, -1, 128)
        joined[number].start()

    def first_part():
        xt_load.wait()
        grad_part(ga_v, 0)

    table = {
        letter + str(i) + str(stage): act
        for letter, group, ends_ in (("d", d, down_end), ("u", u, up_end), ("o", o, out_end))
        for i, (piece, end) in enumerate(zip(group, ends_))
        for stage, act in enumerate((piece.start, piece.one, piece.two, piece.three, piece.four, end))
    }
    for letter, piece in zip("abc", joined):
        for stage, act in enumerate((piece.one, piece.two, piece.three, piece.four)):
            table[letter + str(stage + 1)] = act
    table.update({"a0": first_part, "b0": functools.partial(grad_part, gb_v, 1), "c0": functools.partial(grad_part, gc_v, 2)})
    events = {turn: [table[step] for step in steps] for turn, steps in SUMS.items()}
    length_bias = jnp.where(lax.broadcasted_iota(jnp.int32, (rows, 1), 0) < len_ref[p.c, seq_ref[p.c, p.g]], 0.0, NEGATIVE)
    chunks = rows // BACK_CHUNK

    def attend(step, carry):
        for when_, acts in events.items():
            def act(acts=acts):
                for a in acts:
                    a()
            pl.when(step == when_)(act)
        turn, at_row = step // chunks, step % chunks
        pair = turn % 2 * (pairs // 2) + turn // 2
        columns = [pl.ds(aligned(i * width + pair * 128, 128), 128) for i in range(3)]
        keys, values = qkv_v[:, columns[1]], qkv_v[:, columns[2]]
        keys_t = keys.T
        lane = lax.broadcasted_iota(jnp.int32, (rows, 128), 1)
        short = lax.broadcasted_iota(jnp.int32, (BACK_CHUNK, 128), 1)
        own_rows = pl.ds(aligned(at_row * BACK_CHUNK, BACK_CHUNK), BACK_CHUNK)
        queries = qkv_v[own_rows, columns[0]] * jnp.asarray(0.125, BF)
        back = dctx_v[own_rows, columns[0]]
        back_t = back.T.astype(F32)
        forth_t = ctx_v[pl.ds(aligned(pair * 128, 128), 128), own_rows].astype(F32)
        both = back_t * forth_t
        d_keys = d_values = None
        for h in range(2):
            def own(block, index):
                return jnp.where((index < HEAD) == (h == 0), block, jnp.zeros_like(block))
            delta = jnp.sum(both[h * HEAD:(h + 1) * HEAD], axis=0, keepdims=True)
            scores = product_nt(own(keys, lane), queries) + length_bias
            soft = jnp.exp(scores - lse_v[2 * pair + h, :, own_rows])
            d_probs = product_nt(own(values, lane), back)
            d_scores = (soft * (d_probs - delta)).astype(BF)
            head_rows = pl.ds(aligned(pair * 128 + h * HEAD, HEAD), HEAD)
            dqt_v[head_rows, own_rows] = (product(keys_t[h * HEAD:(h + 1) * HEAD], d_scores) * 0.125).astype(BF)
            to_values = product(soft.astype(BF), own(back, short))
            to_keys = product(d_scores, own(queries, short))
            d_values = to_values if d_values is None else d_values + to_values
            d_keys = to_keys if d_keys is None else d_keys + to_keys

        @pl.when(at_row == 0)
        def _():
            acc_k[...] = d_keys
            acc_v[...] = d_values

        @pl.when(at_row > 0)
        def _():
            acc_k[...] += d_keys
            acc_v[...] += d_values

        @pl.when(at_row == chunks - 1)
        def _():
            dk_v[:, columns[0]] = acc_k[...].astype(BF)
            dv_v[:, columns[0]] = acc_v[...].astype(BF)
        return carry

    lax.fori_loop(0, width // 128 * chunks, attend, 0)
    for made in later:
        made.wait()

    def tok_copy(target):
        return pltpu.make_async_remote_copy(
            src_ref=dxt_v.at[target // n_col, :, pl.ds(aligned((target % n_col) * span, 128), span)],
            dst_ref=trecv.at[p.c * slots + p.g],
            send_sem=tok_send.at[target], recv_sem=tok_recv.at[p.flat],
            device_id=p.of_flat(target), device_id_type=MESH,
        )

    half_groups = groups // 2
    half_width = width // 2

    def tok_batch(part, low, high):
        def one(i, carry):
            target = part * half_groups * n_col + (p.flat + i * 5) % (half_groups * n_col)

            @pl.when(target != p.flat)
            def _():
                tok_copy(target).start()
            return carry

        lax.fori_loop(low, high, one, 0)

    def grad_input(part):
        near = pl.ds(part * half_groups, half_groups)
        w_rows = lambda i: w_v[near, :, :, i * width:(i + 1) * width].reshape(half_width, width)
        total = gm_v[:, part * half_width:(part + 1) * half_width].T
        total = total + product(w_rows(0), dqt_v[...])
        total = total + product_nt(w_rows(1), dk_v[...])
        total = total + product_nt(w_rows(2), dv_v[...])
        dxt_v[near] = total.astype(BF).reshape(half_groups, width // groups, rows)

    count = half_groups * n_col
    grad_input(0)
    made_parts = 1
    for step in PACE:
        if isinstance(step, str):
            table[step]()
            continue
        low, high = step
        if high > count and made_parts == 1:
            grad_input(1)
            made_parts = 2
            own_tok = keep(dxt_v.at[p.g, :, pl.ds(aligned(p.c * span, 128), span)], trecv.at[p.c * slots + p.g])
        for part in range(2):
            first, last = max(low, part * count) - part * count, min(high, part * count + count) - part * count
            if first < last:
                tok_batch(part, first, last)
    for step in LATE:
        table[step]()

    def norm_wait(i, carry):
        source = (p.flat + p.n - i) % p.n
        pltpu.make_async_remote_copy(
            src_ref=nrecv.at[source], dst_ref=nrecv.at[source], send_sem=norm_send.at[i], recv_sem=norm_recv.at[i],
            device_id=p.of_flat(source), device_id_type=MESH,
        ).wait_recv()
        norm_copy(i).wait_send()
        return carry

    lax.fori_loop(1, p.n, norm_wait, 0)
    nsum_ref[...] = jnp.sum(nrecv[...], axis=0)
    joined_end()
    own_tok.wait()

    def tok_wait(i, carry):
        source = (p.flat + p.n - i) % p.n
        landing = trecv.at[(source % n_col) * slots + source // n_col]
        pltpu.make_async_remote_copy(
            src_ref=landing, dst_ref=landing, send_sem=tok_send.at[source], recv_sem=tok_recv.at[source],
            device_id=p.of_flat(source), device_id_type=MESH,
        ).wait_recv()
        tok_copy((p.flat + i) % p.n).wait_send()
        return carry

    lax.fori_loop(1, p.n, tok_wait, 0)
    for m in range(micro):
        for s in range(slots):
            place = jnp.int32(0)
            for j in range(slots):
                place = jnp.where(seq_ref[m, j] == s, jnp.int32(j), place)
            tgrad_ref[m, s] = trecv[m * slots + place]
    for end in ends:
        end()
    lanes.finish()


def backward(dims, seq_order, lengths, qkv, ctx_t, lse, d_context, xt, w_qkv, g_mixed, g_out, g_up, part_x, part_y, n_grads):
    n_dp, n_row, n_col = dims
    groups, n = n_dp * n_row, n_dp * n_row * n_col
    micro, slots = seq_order.shape
    width, rows = ctx_t.shape
    feats, span = width // groups, rows // n_col
    shape = jax.ShapeDtypeStruct
    plan, buffers = [], []
    for name, grad, kind, axes in (
        ("down", part_y, "lanes", DOWN), ("up", g_up, "rows", UP), ("out", g_out, "rows", OUT),
        *((letter, g_out, "rows", axis) for letter, axis in zip("abc", JOINED)),
    ):
        if name == "down":
            lead, each, columns = 2, part_y.shape[1], part_y.shape[2]
        else:
            lead, _, across, columns = grad.shape
            each = across // len(axes)
        for i, axis in enumerate(axes):
            plan.append((name, kind, axis, i * each, each))
            sizes = piece_buffers(kind, axis, lead, each, columns, n_row, groups)
            if name == "down":
                sizes[0] = (16, 128)
            buffers += [pltpu.VMEM(size, BF) for size in sizes]
    outs = (
        shape((micro, slots, feats, span), BF),
        shape((w_qkv.shape[2] * 2, w_qkv.shape[3] // n_col), F32),
        shape((g_out.shape[2] * 2, g_out.shape[3] // n_col), F32),
        shape((g_up.shape[2] * 2, g_up.shape[3] // n_col), F32),
        shape((len(DOWN) * part_y.shape[1], part_y.shape[2] // groups), F32),
        shape((8, 256), F32),
    )
    vm = lambda like, kind=BF: pltpu.VMEM(like.shape, kind)
    temps = [pltpu.VMEM((g.shape[2], g.shape[3] // n_col), F32) for g in (w_qkv, g_out, g_up)]
    carried = [pltpu.VMEM((g.shape[0],) + g.shape[2:], BF) for g in (g_out, g_up)]
    return pl.pallas_call(
        functools.partial(backward_kernel, dims, plan),
        out_shape=outs,
        in_specs=[SM, SM, ANY, ANY, ANY, ANY, ANY, ANY, ANY, ANY, ANY, ANY, ANY, VM],
        out_specs=[VM, VM, VM, VM, VM, VM],
        scratch_shapes=[
            vm(qkv), vm(ctx_t), vm(lse, F32), vm(d_context), vm(xt), vm(w_qkv), vm(g_mixed, F32), *carried, vm(g_out), vm(g_out), vm(g_out),
            pltpu.VMEM((width, rows), BF), pltpu.VMEM((rows, width), BF), pltpu.VMEM((rows, width), BF),
            pltpu.VMEM((rows, 128), F32), pltpu.VMEM((rows, 128), F32),
            pltpu.VMEM((groups, feats, rows), BF), pltpu.VMEM((micro * slots, feats, span), BF),
            pltpu.VMEM((n, 8, 256), F32), *temps,
            DMA((n,)), DMA((n,)), DMA((n,)), DMA((n,)),
            DMA((80,)), DMA((80,)), DMA((16,)), *buffers,
        ],
        compiler_params=pltpu.CompilerParams(
            collective_id=1, has_side_effects=True, vmem_limit_bytes=62 * 2**20
        ),
        name="backward_part",
    )(seq_order, lengths, qkv, ctx_t, lse, d_context, xt, w_qkv, g_mixed, g_out, g_up, part_x, part_y, n_grads)
def layer_norm(values, factor, offset):
    average = jnp.mean(values, axis=-1, keepdims=True)
    centered = values - average
    variance = jnp.mean(centered * centered, axis=-1, keepdims=True)
    return centered * lax.rsqrt(variance + EPSILON) * factor + offset


def gelu_act(values):
    return 0.5 * values * (1.0 + lax.erf(values * ROOT_HALF))


def attention(qkv, length):
    rows, width = qkv.shape[0], qkv.shape[1] // 3
    heads = width // HEAD
    q, k, v = (qkv[:, i * width:(i + 1) * width].reshape(rows, heads, HEAD) for i in range(3))
    scores = jnp.einsum("qhe,khe->hqk", q, k, preferred_element_type=F32) * 0.125
    valid = jnp.arange(rows, dtype=jnp.int32) < length
    scores = jnp.where(valid[None, None, :], scores, NEGATIVE)
    top = jnp.max(scores, axis=-1, keepdims=True)
    exps = jnp.exp(scores - top)
    total = jnp.sum(exps, axis=-1, keepdims=True)
    probs = (exps / total).astype(BF)
    context = jnp.einsum("hqk,khe->qhe", probs, v, preferred_element_type=F32)
    return context.astype(BF).reshape(rows, width), top + jnp.log(total)


def attention_back(qkv, length, stats, d_context):
    rows, width = qkv.shape[0], qkv.shape[1] // 3
    heads = width // HEAD
    q, k, v = (qkv[:, i * width:(i + 1) * width].reshape(rows, heads, HEAD) for i in range(3))
    dc = d_context.reshape(rows, heads, HEAD)
    scores = jnp.einsum("qhe,khe->hqk", q, k, preferred_element_type=F32) * 0.125
    valid = jnp.arange(rows, dtype=jnp.int32) < length
    scores = jnp.where(valid[None, None, :], scores, NEGATIVE)
    soft = jnp.exp(scores - stats)
    d_probs = jnp.einsum("qhe,khe->hqk", dc, v, preferred_element_type=F32)
    delta = jnp.sum(soft * d_probs, axis=-1, keepdims=True)
    d_scores = (soft * (d_probs - delta)).astype(BF)
    dq = jnp.einsum("hqk,khe->qhe", d_scores, k, preferred_element_type=F32) * 0.125
    dk = jnp.einsum("hqk,qhe->khe", d_scores, q, preferred_element_type=F32) * 0.125
    dv = jnp.einsum("hqk,qhe->khe", soft.astype(BF), dc, preferred_element_type=F32)
    return jnp.concatenate([a.astype(BF).reshape(rows, width) for a in (dq, dk, dv)], axis=-1)


def middle(x, context, context_t, cot, w_out, w_up, w_down_t, gain_one, shift_one, gain_two, shift_two):
    mixed = x.astype(F32) + product(context, w_out)
    hidden = layer_norm(mixed, gain_one, shift_one)
    hidden_low = hidden.astype(BF)
    pre_act = product(hidden_low, w_up)
    act_low = gelu_act(pre_act).astype(BF)
    summed = hidden + product_nt(act_low, w_down_t)
    output = layer_norm(summed, gain_two, shift_two).astype(BF)
    _, norm_two_back = jax.vjp(layer_norm, summed, gain_two, shift_two)
    g_summed, g_gain_two, g_shift_two = norm_two_back(cot.astype(F32))
    d_down = g_summed.astype(BF)
    g_down_t = product_tn(d_down, act_low).astype(BF)
    d_act = product(d_down, w_down_t)
    _, gelu_back = jax.vjp(gelu_act, pre_act)
    d_pre = gelu_back(d_act)[0].astype(BF)
    g_up = product_tn(hidden_low, d_pre).astype(BF)
    g_hidden = g_summed + product_nt(d_pre, w_up)
    _, norm_one_back = jax.vjp(layer_norm, mixed, gain_one, shift_one)
    g_mixed, g_gain_one, g_shift_one = norm_one_back(g_hidden)
    d_attn = g_mixed.astype(BF)
    g_out = product(context_t, d_attn).astype(BF)
    d_context = product_nt(d_attn, w_out).astype(BF)
    return output, g_mixed, d_context, g_down_t, g_up, g_out, (g_gain_one, g_shift_one, g_gain_two, g_shift_two)


def take_blocks(blocks, places):
    def body(place_ref, in_ref, out_ref):
        def step(i, carry):
            out_ref[i] = in_ref[place_ref[i]]
            return carry

        lax.fori_loop(0, blocks.shape[0], step, 0)

    return pl.pallas_call(
        body, out_shape=jax.ShapeDtypeStruct(blocks.shape, blocks.dtype), in_specs=[SM, VM], out_specs=VM,
        compiler_params=pltpu.CompilerParams(vmem_limit_bytes=48 * 2**20), name="take_blocks",
    )(places, blocks)


def own_length(lengths, seq_order):
    n_row = lax.axis_size("row")
    slot = lax.axis_index("dp") * n_row + lax.axis_index("row")
    micro = lax.axis_index("col")
    index = jnp.arange(seq_order.shape[1], dtype=jnp.int32)
    order = jnp.sum(jnp.where(jnp.arange(seq_order.shape[0])[:, None] == micro, seq_order, 0), axis=0)
    source = jnp.sum(jnp.where(index == slot, order, 0))
    mine = jnp.sum(jnp.where(jnp.arange(seq_order.shape[0])[:, None] == micro, lengths, 0), axis=0)
    return jnp.sum(jnp.where(index == source, mine, 0))


def local(
    tokens, cotangent, lengths, seq_order, w_qkv, w_out, w_up, w_down, gain_one, shift_one, gain_two, shift_two,
):
    dims = tuple(lax.axis_size(a) for a in ("dp", "row", "col"))
    n_dp, n_row, n_col = dims
    groups = n_dp * n_row
    micro, slots, span, feats = tokens.shape
    width = cotangent.shape[3]
    rows = span * n_col
    direct = n_dp == 2 and n_row == 4 and n_col == 4 and feats % 32 == 0 and w_qkv.shape[0] % 32 == 0
    tok_t = jnp.swapaxes(tokens, 2, 3)
    w_down_t = w_down.T
    norms = jnp.stack([gain_one, shift_one, gain_two, shift_two])
    length = own_length(lengths, seq_order)
    everyone = ("dp", "row", "col")
    if direct:
        each = norms.shape[1]
        place = (lax.axis_index("dp") * n_row + lax.axis_index("row")) * n_col + lax.axis_index("col")
        lane = jnp.arange(256, dtype=jnp.int32)
        here = lane[None, :] == (place * each) % 128 + jnp.arange(each, dtype=jnp.int32)[:, None]
        packed = jnp.sum(jnp.where(here[None], norms[:, :, None].astype(F32), 0.0), axis=1).astype(BF)
        packed = jnp.pad(packed, ((0, 12), (0, 0)))
        xt, w_joined, qkv, context_t, lse, output, g_mixed, d_context, g_out, g_up, part_x, part_y, norm_grads = forward(
            dims, seq_order, lengths, tok_t, cotangent[:, 0], w_qkv, w_out, w_up, w_down_t, packed
        )
    else:
        offset = jnp.arange(micro, dtype=jnp.int32)[:, None] * slots
        sent = take_blocks(tok_t.reshape(micro * slots, feats, span), (seq_order + offset).reshape(-1))
        sent = jnp.swapaxes(sent.reshape(micro, slots, feats, span), 0, 1).reshape(micro * slots, feats, span)
        got = lax.all_to_all(sent, everyone, split_axis=0, concat_axis=0, tiled=True)
        xt = got.reshape(groups, n_col, feats, span).transpose(0, 2, 1, 3).reshape(width, rows)
        cot = lax.all_to_all(cotangent[:, 0], "col", split_axis=0, concat_axis=0, tiled=True).reshape(rows, width)

        def whole(w, row_axes, col_axes):
            w = lax.all_gather(w, col_axes, axis=1, tiled=True)
            return lax.all_gather(w, row_axes, axis=0, tiled=True)

        f_qkv, f_out, f_up = (whole(w, ("dp", "row"), "col") for w in (w_qkv, w_out, w_up))
        f_down_t = whole(w_down_t, "col", ("dp", "row"))
        f_norms = lax.all_gather(norms, everyone, axis=1, tiled=True)
    if direct:
        tgrad, r_qkv, r_out, r_up, r_down_t, n_sum = backward(
            dims, seq_order, lengths, qkv, context_t, lse, d_context, xt, w_joined, g_mixed,
            g_out, g_up, part_x, part_y, norm_grads,
        )
        n_sum = lax.dynamic_slice(n_sum, (0, place * each % 128), (4, each))
    else:
        gains = [f_norms[i].astype(F32) for i in range(4)]
        x = xt.T
        qkv = product(x, f_qkv).astype(BF)
        context, stats = attention(qkv, length)
        output, g_mixed, d_context, g_down_t, g_up, g_out, norm_grads = middle(
            x, context, context.T, cot, f_out, f_up, f_down_t, *gains
        )
        norm_grads = jnp.stack(norm_grads)
        d_qkv = attention_back(qkv, length, stats, d_context)
        g_qkv = product(xt, d_qkv).astype(BF)
        dxt = (g_mixed + product_nt(d_qkv, f_qkv)).astype(BF).T
        n_sum = lax.psum_scatter(norm_grads, everyone, scatter_dimension=1, tiled=True)
        output = lax.all_to_all(output.reshape(n_col, span, width), "col", split_axis=0, concat_axis=0, tiled=True)
        sent = dxt.reshape(groups, feats, n_col, span).transpose(0, 2, 1, 3).reshape(micro * slots, feats, span)
        got = lax.all_to_all(sent, everyone, split_axis=0, concat_axis=0, tiled=True)
        got = jnp.swapaxes(got.reshape(slots, micro, feats, span), 0, 1).reshape(micro * slots, feats, span)
        index = jnp.arange(slots, dtype=jnp.int32)
        inverse = jnp.sum(jnp.where(seq_order[:, :, None] == index, index[None, :, None], 0), axis=1)
        offset = jnp.arange(micro, dtype=jnp.int32)[:, None] * slots
        tgrad = take_blocks(got, (inverse + offset).reshape(-1)).reshape(micro, slots, feats, span)

        def parts(g, row_axes, col_axes):
            g = lax.psum_scatter(g, col_axes, scatter_dimension=1, tiled=True)
            return lax.psum_scatter(g, row_axes, scatter_dimension=0, tiled=True).astype(F32)

        r_qkv, r_out, r_up = (parts(g, ("dp", "row"), "col") for g in (g_qkv, g_out, g_up))
        r_down_t = parts(g_down_t, "col", ("dp", "row"))
    return (
        output[:, None], jnp.swapaxes(tgrad, 2, 3), r_qkv, r_out, r_up, r_down_t.T,
        n_sum[0], n_sum[1], n_sum[2], n_sum[3],
    )


def solution(mesh):
    rows = ("dp", "row")
    every = ("dp", "row", "col")
    in_specs = (
        P(None, None, "col", rows), P(None, rows, "col", None), P(), P(),
        P(rows, "col"), P(rows, "col"), P(rows, "col"), P(rows, "col"),
        P(every), P(every), P(every), P(every),
    )
    out_specs = (
        P(None, rows, "col", None), P(None, None, "col", rows),
        P(rows, "col"), P(rows, "col"), P(rows, "col"), P(rows, "col"),
        P(every), P(every), P(every), P(every),
    )
    return jax.shard_map(local, mesh=mesh, in_specs=in_specs, out_specs=out_specs, check_vma=False)
```

```python
import functools

import jax
import jax.numpy as jnp
from jax import lax
from jax.experimental import pallas as pl
from jax.experimental.pallas import tpu as pltpu
from jax.sharding import PartitionSpec as P

HEAD = 64
NEGATIVE = -1000000000.0
EPSILON = 1e-12
ROOT_HALF = 0.7071067811865476
ROOT_TWO_PI = 0.3989422804014327
MESH = pl.DeviceIdType.MESH
BF = jnp.bfloat16
F32 = jnp.float32
ANY = pl.BlockSpec(memory_space=pl.ANY)
VM = pl.BlockSpec(memory_space=pltpu.VMEM)
SM = pl.BlockSpec(memory_space=pltpu.SMEM)
DMA = pltpu.SemaphoreType.DMA


def aligned(value, step):
    return pl.multiple_of(value, step)


def product(left, right):
    return jnp.dot(left, right, preferred_element_type=F32)


def product_tn(left, right):
    return lax.dot_general(left, right, (((0,), (0,)), ((), ())), preferred_element_type=F32)


def product_nt(left, right):
    return lax.dot_general(left, right, (((1,), (1,)), ((), ())), preferred_element_type=F32)


class Place:
    def __init__(self, n_dp, n_row, n_col):
        self.n_dp, self.n_row, self.n_col = n_dp, n_row, n_col
        self.n = n_dp * n_row * n_col
        self.x = lax.axis_index("dp")
        self.z = lax.axis_index("row")
        self.c = lax.axis_index("col")
        self.y, self.k = self.c // 2, self.c % 2
        self.g = self.x * n_row + self.z
        self.flat = self.g * n_col + self.c

    def of_flat(self, flat):
        group = flat // self.n_col
        return (group // self.n_row, group % self.n_row, flat % self.n_col)

    def dev(self, x=None, z=None, y=None, k=None):
        x = self.x if x is None else x
        z = self.z if z is None else z
        y = self.y if y is None else y
        k = self.k if k is None else k
        return (x, z, y * 2 + k)

    def greet(self):
        sem = pltpu.get_barrier_semaphore()

        def one(i, carry):
            pl.semaphore_signal(
                sem, inc=1, device_id=self.of_flat((self.flat + i) % self.n), device_id_type=MESH
            )
            return carry

        lax.fori_loop(1, self.n, one, 0)

    def met(self):
        pl.semaphore_wait(pltpu.get_barrier_semaphore(), self.n - 1)


class Lanes:
    def __init__(self, send_sems, recv_sems):
        self.send_sems, self.recv_sems, self.sent = send_sems, recv_sems, []
        self.used = [0, 0]

    def take(self, which, count):
        first = self.used[which]
        self.used[which] += count
        return first

    def copy(self, src, dst, device, s, r):
        return pltpu.make_async_remote_copy(
            src_ref=src, dst_ref=dst, send_sem=self.send_sems.at[s],
            recv_sem=self.recv_sems.at[r], device_id=device, device_id_type=MESH,
        )

    def send(self, make):
        self.copy(*make()).start()
        self.sent.append(make)

    def arrived(self, landing, device, r):
        self.copy(landing, landing, device, 0, r).wait_recv()

    def finish(self):
        for make in self.sent:
            self.copy(*make()).wait_send()
        self.sent = []


class Gather:
    def __init__(self, place, lanes, region, first):
        self.p, self.lanes, self.region, self.first = p, lanes, region, first = place, lanes, region, first
        self.to_x, self.to_y, self.to_core = p.dev(x=1 - p.x), p.dev(y=1 - p.y), p.dev(k=1 - p.k)
        self.one, self.two = (self.to_x, self.to_y) if first == "x" else (self.to_y, self.to_x)
        n = p.n_row
        self.s = {name: lanes.take(0, n) for name in ("z", 1, 2, 3, "core")}
        self.r = {name: lanes.take(1, n) for name in ("z", 1, 2, 3, "core")}
        self.far = (p.z + n // 2) % n
        self.near = p.z + 1 - 2 * (p.z % 2)
        self.cross = (self.near + n // 2) % n
        self.to_near = p.dev(z=self.near)

    def side(self, hop):
        p = self.p
        x_side = hop in ((1, 3) if self.first == "x" else (2, 3))
        y_side = hop in ((2, 3) if self.first == "x" else (1, 3))
        return (1 - p.x if x_side else p.x), (1 - p.y if y_side else p.y)

    def at(self, hop, z, k):
        x, y = self.side(hop)
        return self.region(x, z, 1, y, k)

    def line(self, hop, k):
        x, y = self.side(hop)
        return self.region(x, 0, self.p.n_row, y, k)

    def start(self, own):
        p = self.p

        def to(hop, device):
            return lambda: (own, self.at(0, p.z, p.k), device, self.s[hop] + p.z, self.r[hop] + p.z)

        self.lanes.send(to(1, self.one))
        self.lanes.send(to(2, self.two))
        self.own = own

    def z_start(self):
        p, own = self.p, self.own
        self.lanes.send(lambda: (own, self.at(0, p.z, p.k), p.dev(z=self.far), self.s["z"], self.r["z"]))
        self.lanes.send(lambda: (own, self.at(0, p.z, p.k), p.dev(z=self.near), self.s["z"] + 1, self.r["z"] + 1))

    def z_step(self, number):
        p = self.p
        source = (self.far, self.near, self.cross)[number - 1]
        peer = self.far if number == 1 else self.near
        self.lanes.arrived(self.at(0, source, p.k), p.dev(z=peer), self.r["z"] + number - 1)

        def to(device, hop, index):
            def make():
                ref = self.at(0, source, p.k)
                return (ref, ref, device, self.s[hop] + index, self.r[hop] + index)
            return make

        if number == 1:
            self.lanes.send(to(self.to_near, "z", 2))
        self.lanes.send(to(self.one, 1, source))
        self.lanes.send(to(self.two, 2, source))

    def z_steps(self):
        for distance in range(1, self.p.n_row):
            self.z_step(distance)
        self.z_done()

    def z_done(self):
        self.local.wait()
        self.to_other_core(0)

    def to_other_core(self, hop):
        def make():
            line = self.line(hop, self.p.k)
            return (line, line, self.to_core, self.s["core"] + hop, self.r["core"] + hop)
        self.lanes.send(make)

    def first_steps(self):
        p = self.p
        for source in (p.z, self.far, self.near, self.cross):
            self.lanes.arrived(self.at(1, source, p.k), self.one, self.r[1] + source)

            def make(source=source):
                ref = self.at(1, source, p.k)
                return (ref, ref, self.two, self.s[3] + source, self.r[3] + source)

            self.lanes.send(make)
        self.to_other_core(1)

    def second_steps(self, hops=(2, 3)):
        p = self.p
        for hop in hops:
            for i in range(p.n_row):
                self.lanes.arrived(self.at(hop, i, p.k), self.two, self.r[hop] + i)
            self.to_other_core(hop)

    def stage(self, name):
        if name == "z":
            self.z_start()
        elif name == "f":
            self.first_steps()
        elif name == "s":
            self.second_steps((2,))
        elif name == "t":
            self.second_steps((3,))
        else:
            self.z_step(int(name))
            if name == "3":
                self.z_done()

    def end(self):
        for hop in range(4):
            self.lanes.arrived(self.line(hop, 1 - self.p.k), self.to_core, self.r["core"] + hop)


def rows_region(ref, n_row, low=0, high=None):
    width = ref.shape[3] // 2
    high = width if high is None else high

    def region(x, z, nz, y, k):
        columns = pl.ds(aligned(y * width + low, 128), high - low)
        if nz == 1:
            return ref.at[x * n_row + z, k, :, columns]
        return ref.at[pl.ds(x * n_row + z, nz), k, :, columns]

    return region


def lanes_region(ref, n_dp, n_row, low=0, high=None):
    width = ref.shape[3] // (n_dp * n_row)
    high = ref.shape[2] if high is None else high

    def region(x, z, nz, y, k):
        return ref.at[y, k, pl.ds(low, high - low), pl.ds(aligned((x * n_row + z) * width, 128), nz * width)]

    return region


CHUNK = 512
ROWS = 256
BATCH = (6, 6, 6, 6, 7)
FIRST = {"q": "x", "o": "y", "u": "y", "v": "y", "d": "y", "e": "y"}
DOWN, UP, OUT, JOINED = "xyx", "xyx", "y", "xyx"
SCHEDULE = {
    "first": {4: ("oz", "uz",), 5: ("o1", "u1", "vz",)},
    "turn": {0: ("o2", "u2", "v1", "dz",), 2: ("o3", "u3", "v2", "d1",)},
    "project": {0: ("of", "v3", "d2",), 3: ("uf", "d3",), 6: ("vf", "ez",)},
    "attend": {0: ("df", "os", "e1",), 1: ("e2",), 2: ("us", "e3",), 3: ("ot", "ut",), 4: ("ef",), 5: ("vs",), 6: ("vt",), 7: ("c1",), 8: ("c2", "c3",), 9: ("ds",), 11: ("dt",)},
    "mix": {1: ("es",)},
    "rise": {3: ("et",)},
}


def forward_kernel(
    dims, seq_ref, len_ref, tok_ref, cot_ref, qkv_ref, out_ref, up_ref, down_ref, norm_ref,
    xt_out, wqkv_out, qkv_out, ctx_out, lse_out, output_out, gm_out, dctx_out, gout_out, gup_out, part_x_out, part_y_out, nsum_out,
    tsend, half_qkv, half_out, half_up, pair_qkv, pair_out, pair_up,
    xt_v, x_v, w_v, wide_v, ctx_v, lse_v, wout_v, wup_v, wdown_v, norm_v, gains_v, cot_v, act_v, mixed_v, gsum_v, hl_v,
    output_v, down_v, attn_v, dctx_v, turn_v, nsum_v,
    tok_send, tok_recv, norm_send, norm_recv, cot_send, cot_recv, w_send, w_recv, half_send, half_recv, local_sem, out_send, out_recv, r_send, r_recv,
    *pieces,
):
    n_dp, n_row, n_col = dims
    p = Place(n_dp, n_row, n_col)
    micro, slots, _, span = tok_ref.shape
    rows, width = x_v.shape
    qkv_v = wide_v.at[:, pl.ds(0, 3 * width)]
    p.greet()
    for m in range(micro):
        for j in range(slots):
            tsend[m * slots + j] = tok_ref[m, seq_ref[m, j]]
    p.met()
    halves = Lanes(half_send, half_recv)
    lanes = Lanes(w_send, w_recv)
    partner = p.dev(k=1 - p.k)
    for i, (block, landing) in enumerate(((qkv_ref, half_qkv), (out_ref, half_out), (up_ref, half_up))):
        def make(i=i, block=block, landing=landing):
            count = landing.shape[0]
            return (block.at[pl.ds(aligned((1 - p.k) * count, 16), count), :], landing, partner, i, i)
        halves.send(make)

    def join(i, block, landing, pair):
        halves.arrived(landing, partner, i)
        count, across = landing.shape
        mine = block[pl.ds(aligned(p.k * count, 16), count), :]
        theirs = landing[...]
        pair[:, :across] = jnp.where(p.k == 0, mine, theirs)
        pair[:, across:] = jnp.where(p.k == 0, theirs, mine)

    local = []

    def keep(src, dst):
        made = pltpu.make_async_copy(src, dst, local_sem.at[len(local)])
        made.start()
        local.append(made)
        return made

    region_qkv = rows_region(w_v, n_row)
    join(0, qkv_ref, half_qkv, pair_qkv)
    own_w = keep(pair_qkv, region_qkv(p.x, p.z, 1, p.y, p.k))
    g_qkv = Gather(p, lanes, region_qkv, FIRST["q"])
    g_qkv.local = own_w
    g_qkv.start(pair_qkv)
    g_qkv.z_start()

    def tok_copy(i):
        target = (p.flat + i) % p.n
        return pltpu.make_async_remote_copy(
            src_ref=tsend.at[(target % n_col) * slots + target // n_col],
            dst_ref=xt_v.at[p.g, :, pl.ds(aligned(p.c * span, 128), span)],
            send_sem=tok_send.at[i], recv_sem=tok_recv.at[i],
            device_id=p.of_flat(target), device_id_type=MESH,
        )

    def norm_copy(i):
        return pltpu.make_async_remote_copy(
            src_ref=norm_ref, dst_ref=norm_v.at[p.flat],
            send_sem=norm_send.at[i], recv_sem=norm_recv.at[i],
            device_id=p.of_flat((p.flat + i) % p.n), device_id_type=MESH,
        )

    sent = [1]

    def tok_batch(count):
        def one(j, carry):
            tok_copy((j * 13) % p.n).start()
            return carry

        lax.fori_loop(sent[0], min(sent[0] + count, p.n), one, 0)
        sent[0] = min(sent[0] + count, p.n)

    def norm_start(i, carry):
        norm_copy(i).start()
        return carry

    tok_batch(BATCH[0])
    own_tok = keep(tsend.at[p.c * slots + p.g], xt_v.at[p.g, :, pl.ds(aligned(p.c * span, 128), span)])

    waves = []

    def wave(own, region, first):
        gather = Gather(p, lanes, region, first)
        gather.local = keep(own, region(p.x, p.z, 1, p.y, p.k))
        gather.start(own)
        waves.append(gather)

    join(1, out_ref, half_out, pair_out)
    wave(pair_out, rows_region(wout_v, n_row), FIRST["o"])
    join(2, up_ref, half_up, pair_up)
    cut = pair_up.shape[1] // 2
    wave(pair_up.at[:, pl.ds(0, cut)], rows_region(wup_v, n_row, 0, cut), FIRST["u"])
    wave(pair_up.at[:, pl.ds(cut, cut)], rows_region(wup_v, n_row, cut, 2 * cut), FIRST["v"])
    cut = down_ref.shape[0] // 2
    wave(down_ref.at[pl.ds(0, cut), :], lanes_region(wdown_v, n_dp, n_row, 0, cut), FIRST["d"])
    wave(down_ref.at[pl.ds(cut, cut), :], lanes_region(wdown_v, n_dp, n_row, cut, 2 * cut), FIRST["e"])
    lax.fori_loop(1, p.n, norm_start, 0)
    own_norm = keep(norm_ref, norm_v.at[p.flat])

    def cot_copy(i):
        target = (p.c + i) % n_col
        return pltpu.make_async_remote_copy(
            src_ref=cot_ref.at[target], dst_ref=cot_v.at[p.c],
            send_sem=cot_send.at[i], recv_sem=cot_recv.at[i],
            device_id=(p.x, p.z, target), device_id_type=MESH,
        )

    own_cot = keep(cot_ref.at[p.c], cot_v.at[p.c])
    names = dict(zip("ouvde", waves))

    def begin_cot(i):
        cot_copy(i).start()

    def agenda(phase):
        table = {}
        for turn, steps in SCHEDULE.get(phase, {}).items():
            table[turn] = [functools.partial(begin_cot, int(step[1:])) if step[0] == "c" else functools.partial(names[step[0]].stage, step[1:]) for step in steps]
        return table

    first = agenda("first")

    def now(turn):
        for act in first.get(turn, ()):
            act()

    now(0)
    for distance in range(1, n_row):
        g_qkv.z_step(distance)
        tok_batch(BATCH[distance])
        now(distance)
    g_qkv.z_done()
    g_qkv.first_steps()
    tok_batch(BATCH[4])
    now(4)
    g_qkv.second_steps()
    tok_batch(p.n)
    now(5)
    own_tok.wait()

    def tok_wait(i, carry):
        source = (p.flat + p.n - i) % p.n
        landing = xt_v.at[source // n_col, :, pl.ds(aligned((source % n_col) * span, 128), span)]
        pltpu.make_async_remote_copy(
            src_ref=landing, dst_ref=landing, send_sem=tok_send.at[i], recv_sem=tok_recv.at[i],
            device_id=p.of_flat(source), device_id_type=MESH,
        ).wait_recv()
        return carry

    lax.fori_loop(1, p.n, tok_wait, 0)
    keep(xt_v, xt_out)

    def turn(i, carry):
        run_events(i, agenda("turn"))
        at = pl.ds(aligned(i * 256, 256), 256)
        x_v[at, :] = xt_v[:, :, at].reshape(width, 256).T
        return carry

    lax.fori_loop(0, rows // 256, turn, 0)
    g_qkv.end()
    keep(w_v, wqkv_out)

    def project(i, carry):
        run_events(i, agenda("project"))
        at = pl.ds(aligned(i * 256, 256), 256)
        wide_v[:, at] = product(x_v[...], w_v[:, :, :, at].reshape(width, 256)).astype(BF)
        return carry

    lax.fori_loop(0, 3 * width // 256, project, 0)
    kept_qkv = keep(qkv_v, qkv_out)
    out, up_a, up_b, down_a, down_b = waves
    length = len_ref[p.c, seq_ref[p.c, p.g]]
    bias = jnp.where(lax.broadcasted_iota(jnp.int32, (rows, 1), 0) < length, 0.0, NEGATIVE)
    chunks = rows // CHUNK

    def attend(step, carry):
        run_events(step, agenda("attend"))
        pair, at_row = step // chunks, step % chunks
        columns = [pl.ds(aligned(i * width + pair * 128, 128), 128) for i in range(3)]
        keys = wide_v[:, columns[1]]
        values_t = wide_v[:, columns[2]].T
        lane = lax.broadcasted_iota(jnp.int32, (rows, 128), 1)
        own_rows = pl.ds(aligned(at_row * CHUNK, CHUNK), CHUNK)
        queries = wide_v[own_rows, columns[0]] * jnp.asarray(0.125, BF)
        for h in range(2):
            mine = jnp.where((lane < HEAD) == (h == 0), keys, jnp.zeros_like(keys))
            scores = product_nt(mine, queries) + bias
            top = jnp.max(scores, axis=0, keepdims=True)
            exps = jnp.exp(scores - top)
            total = jnp.sum(exps, axis=0, keepdims=True)
            context = product(values_t[h * HEAD:(h + 1) * HEAD], exps.astype(BF))
            head_rows = pl.ds(aligned(pair * 128 + h * HEAD, HEAD), HEAD)
            ctx_v[head_rows, own_rows] = (context * (1.0 / total)).astype(BF)
            lse_v[2 * pair + h, :, own_rows] = top + jnp.log(total)
        return carry

    lax.fori_loop(0, width // 128 * chunks, attend, 0)
    keep(ctx_v, ctx_out)
    keep(lse_v, lse_out)

    own_norm.wait()

    def norm_wait(i, carry):
        source = (p.flat + p.n - i) % p.n
        pltpu.make_async_remote_copy(
            src_ref=norm_ref, dst_ref=norm_v.at[source], send_sem=norm_send.at[i], recv_sem=norm_recv.at[i],
            device_id=p.of_flat(source), device_id_type=MESH,
        ).wait_recv()
        return carry

    lax.fori_loop(1, p.n, norm_wait, 0)
    each = width // p.n
    gains_v[...] = jnp.zeros_like(gains_v)
    for source in range(p.n):
        low = source * each // 128 * 128
        gains_v[:, low:low + 256] += norm_v[source].astype(F32)
    gain_one, shift_one, gain_two, shift_two = (gains_v[i:i + 1, :width] for i in range(4))

    def normal(values):
        centered = values - jnp.mean(values, axis=-1, keepdims=True)
        scale = lax.rsqrt(jnp.mean(centered * centered, axis=-1, keepdims=True) + EPSILON)
        return centered * scale, scale

    def normal_back(grad, unit, scale, gain):
        grad = grad * gain
        return scale * (grad - jnp.mean(grad, axis=-1, keepdims=True) - unit * jnp.mean(grad * unit, axis=-1, keepdims=True))

    nsum_v[...] = jnp.zeros_like(nsum_v)
    whole = lambda ref: ref[...].reshape(width, -1)
    out.end()

    def mix(step, carry):
        run_events(step, agenda("mix"))
        at = pl.ds(aligned(step * ROWS, ROWS), ROWS)
        mixed = x_v[at, :].astype(F32) + product_tn(ctx_v[:, at], whole(wout_v))
        mixed_v[at, :] = mixed
        unit, _ = normal(mixed)
        hl_v[at, :] = (unit * gain_one + shift_one).astype(BF)
        return carry

    lax.fori_loop(0, rows // ROWS, mix, 0)
    up_a.end()
    up_b.end()
    kept_qkv.wait()

    def rise(step, carry):
        run_events(step, agenda("rise"))
        at = pl.ds(aligned(step * 256, 256), 256)
        pre = product(hl_v[...], wup_v[:, :, :, at].reshape(width, 256))
        half = 0.5 * (1.0 + lax.erf(pre * ROOT_HALF))
        act_v[:, at] = (pre * half).astype(BF)
        wide_v[:, at] = (half + pre * jnp.exp(pre * pre * -0.5) * ROOT_TWO_PI).astype(BF)
        return carry

    lax.fori_loop(0, 4 * width // 256, rise, 0)
    down_a.end()
    down_b.end()
    for i in range(1, n_col):
        source = (p.c + n_col - i) % n_col
        pltpu.make_async_remote_copy(
            src_ref=cot_v.at[source], dst_ref=cot_v.at[source],
            send_sem=cot_send.at[i], recv_sem=cot_recv.at[i],
            device_id=(p.x, p.z, source), device_id_type=MESH,
        ).wait_recv()
    own_cot.wait()

    def out_copy(target):
        return pltpu.make_async_remote_copy(
            src_ref=output_v.at[pl.ds(aligned(target * span, 16), span), :], dst_ref=output_out.at[p.c],
            send_sem=out_send.at[target], recv_sem=out_recv.at[p.c],
            device_id=(p.x, p.z, target), device_id_type=MESH,
        )

    def fall(step, carry):
        at = pl.ds(aligned(step * ROWS, ROWS), ROWS)
        unit_one, _ = normal(mixed_v[at, :])
        summed = unit_one * gain_one + shift_one + product_nt(act_v[at, :], whole(wdown_v))
        unit, scale = normal(summed)
        output_v[at, :] = (unit * gain_two + shift_two).astype(BF)
        per = span // ROWS
        cot = cot_v[step // per, pl.ds(aligned(step % per * ROWS, ROWS), ROWS), :].astype(F32)
        nsum_v[2:3, :width] += jnp.sum(cot * unit, axis=0, keepdims=True)
        nsum_v[3:4, :width] += jnp.sum(cot, axis=0, keepdims=True)
        grad = normal_back(cot, unit, scale, gain_two)
        gsum_v[at, :] = grad
        down_v[at, :] = grad.astype(BF)
        turn_v[:, at] = grad.T.astype(BF)
        target = step // per

        @pl.when((step % per == per - 1) & (target != p.c))
        def _():
            out_copy(target).start()
        return carry

    lax.fori_loop(0, rows // ROWS, fall, 0)
    keep(output_v.at[pl.ds(aligned(p.c * span, 16), span), :], output_out.at[p.c])

    def rise_back(step, carry):
        at = pl.ds(aligned(step * 512, 512), 512)
        back = product(down_v[...], wdown_v[:, :, :, at].reshape(width, 512))
        wide_v[:, at] = (back * wide_v[:, at].astype(F32)).astype(BF)
        return carry

    lax.fori_loop(0, 4 * width // 512, rise_back, 0)
    lanes.finish()

    def grad_down(step, carry):
        at = pl.ds(aligned(step * 512, 512), 512)
        wdown_v[:, :, :, at] = product(turn_v[...], act_v[:, at]).astype(BF).reshape(wdown_v.shape[:3] + (512,))
        return carry

    lax.fori_loop(0, 4 * width // 512, grad_down, 0)

    rlanes = Lanes(r_send, r_recv)
    early = []
    piece_rows = wdown_v.shape[2] // len(DOWN)
    for i, axis in enumerate(DOWN):
        at = pl.ds(i * piece_rows, piece_rows)
        piece = Reduce(
            p, rlanes, wdown_v.at[:, 1 - p.k, at], wdown_v.at[:, p.k, at], pieces[2 * i:2 * i + 2] + (None, None, None), "lanes", axis
        )
        piece.start()
        early.append(piece)

    def mix_back(step, carry):
        run_events(step, {1: (early[0].one, early[1].one), 2: (early[2].one,)})
        at = pl.ds(aligned(step * ROWS, ROWS), ROWS)
        grad = gsum_v[at, :] + product_nt(wide_v[at, :], whole(wup_v))
        unit, scale = normal(mixed_v[at, :])
        nsum_v[0:1, :width] += jnp.sum(grad * unit, axis=0, keepdims=True)
        nsum_v[1:2, :width] += jnp.sum(grad, axis=0, keepdims=True)
        grad = normal_back(grad, unit, scale, gain_one)
        gsum_v[at, :] = grad
        low = grad.astype(BF)
        attn_v[at, :] = low
        dctx_v[at, :] = product_nt(low, whole(wout_v)).astype(BF)
        turn_v[:, at] = hl_v[at, :].T
        return carry

    lax.fori_loop(0, rows // ROWS, mix_back, 0)
    keep(gsum_v, gm_out)
    keep(dctx_v, dctx_out)
    keep(nsum_v, nsum_out)

    def grad_up(step, carry):
        at = pl.ds(aligned(step * 512, 512), 512)
        wup_v[:, :, :, at] = product(turn_v[...], wide_v[:, at]).astype(BF).reshape(wup_v.shape[:3] + (512,))
        return carry

    lax.fori_loop(0, 4 * width // 512, grad_up, 0)
    keep(wup_v, gup_out)

    def grad_out(step, carry):
        at = pl.ds(aligned(step * 256, 256), 256)
        wout_v[:, :, :, at] = product(ctx_v[...], attn_v[:, at]).astype(BF).reshape(wout_v.shape[:3] + (256,))
        return carry

    lax.fori_loop(0, width // 256, grad_out, 0)
    keep(wout_v, gout_out)
    outs = {"x": [part_x_out.at[i] for i in range(DOWN.count("x"))], "y": [part_y_out.at[i] for i in range(DOWN.count("y"))]}
    for piece, axis in zip(early, DOWN):
        piece.add_half(1)
        keep(piece.b[1], outs[axis].pop(0))

    def small_wait(i, carry):
        norm_copy(i).wait_send()
        tok_copy(i).wait_send()
        return carry

    lax.fori_loop(1, p.n, small_wait, 0)
    for i in range(1, n_col):
        cot_copy(i).wait_send()
        source = (p.c + n_col - i) % n_col
        pltpu.make_async_remote_copy(
            src_ref=output_out.at[source], dst_ref=output_out.at[source],
            send_sem=out_send.at[source], recv_sem=out_recv.at[source],
            device_id=(p.x, p.z, source), device_id_type=MESH,
        ).wait_recv()
        out_copy((p.c + i) % n_col).wait_send()
    waited = [own_tok, own_norm, own_w, own_cot, kept_qkv] + [gather.local for gather in waves]
    for made in local:
        if not any(made is w for w in waited):
            made.wait()
    halves.finish()
    rlanes.finish()


def run_events(step, events):
    for when_, acts in events.items():
        def act(acts=acts):
            for a in acts:
                a()
        pl.when(step == when_)(act)


def forward(dims, seq_order, lengths, tok_t, cot, w_qkv, w_out, w_up, w_down_t, norms):
    n_dp, n_row, n_col = dims
    groups, n = n_dp * n_row, n_dp * n_row * n_col
    micro, slots, feats, span = tok_t.shape
    rows, width = n_col * span, groups * feats
    heads = width // HEAD
    qr, qc = w_qkv.shape
    orow, oc = w_out.shape
    ur, uc = w_up.shape
    dr, dc = w_down_t.shape
    shape = jax.ShapeDtypeStruct
    joined = (groups, 2, qr // 2, qc * n_col)
    out_all = (groups, 2, orow // 2, oc * n_col)
    up_all = (groups, 2, ur // 2, uc * n_col)
    down_all = (2, 2, dr, dc * groups)
    outs = (
        shape((groups, feats, rows), BF),
        shape(joined, BF),
        shape((rows, 3 * width), BF),
        shape((width, rows), BF),
        shape((heads, 1, rows), F32),
        shape((n_col, span, width), BF),
        shape((rows, width), F32),
        shape((rows, width), BF),
        shape(out_all, BF),
        shape(up_all, BF),
        shape((DOWN.count("x"), 2, dr // len(DOWN), dc * groups // 2), BF),
        shape((DOWN.count("y"), dr // len(DOWN), dc * groups), BF),
        shape((8, width + 256), F32),
    )
    vm = pltpu.VMEM
    early_buffers = [
        vm(size, BF) for axis in DOWN for size in piece_buffers("lanes", axis, 0, dr // len(DOWN), dc * groups, n_row, groups)[:2]
    ]
    return pl.pallas_call(
        functools.partial(forward_kernel, dims),
        out_shape=outs,
        in_specs=[SM, SM, VM, ANY, VM, VM, VM, VM, VM],
        out_specs=[ANY] * len(outs),
        scratch_shapes=[
            vm((micro * slots, feats, span), BF),
            vm((qr // 2, qc), BF), vm((orow // 2, oc), BF), vm((ur // 2, uc), BF),
            vm((qr // 2, qc * 2), BF), vm((orow // 2, oc * 2), BF), vm((ur // 2, uc * 2), BF),
            vm((groups, feats, rows), BF),
            vm((rows, width), BF),
            vm(joined, BF),
            vm((rows, 4 * width), BF),
            vm((width, rows), BF),
            vm((heads, 1, rows), F32),
            vm(out_all, BF), vm(up_all, BF), vm(down_all, BF),
            vm((n,) + norms.shape, BF),
            vm((norms.shape[0], width + 256), F32),
            vm(cot.shape, BF),
            vm((rows, 4 * width), BF),
            vm((rows, width), F32), vm((rows, width), F32),
            vm((rows, width), BF), vm((rows, width), BF), vm((rows, width), BF), vm((rows, width), BF), vm((rows, width), BF),
            vm((width, rows), BF),
            vm((8, width + 256), F32),
            DMA((n,)), DMA((n,)), DMA((n,)), DMA((n,)), DMA((n_col,)), DMA((n_col,)),
            DMA((6 * 5 * n_row,)), DMA((6 * 5 * n_row,)), DMA((3,)), DMA((3,)), DMA((24,)), DMA((n_col,)), DMA((n_col,)),
            DMA((24,)), DMA((24,)), *early_buffers,
        ],
        compiler_params=pltpu.CompilerParams(
            collective_id=0, has_side_effects=True, vmem_limit_bytes=63 * 2**20
        ),
        name="forward_part",
    )(seq_order, lengths, tok_t, cot, w_qkv, w_out, w_up, w_down_t, norms)


BACK_CHUNK = 256
SUMS = {
    0: ("u20", "o00",), 1: ("u01", "u11",), 3: ("u21", "d13",), 4: ("d03",), 6: ("d23", "d14",), 7: ("d04",), 8: ("a0", "u02",), 9: ("o01", "d24", "d15",), 10: ("a1", "d05",),
    12: ("u12", "d25",), 14: ("u22", "u03",), 16: ("b0",), 17: ("u13", "u04",), 18: ("o02", "b1",), 20: ("u14", "u05",), 21: ("a2", "u23",), 22: ("u15",), 23: ("o03",),
}
PACE = ((0, 16), "c0", "c1", "a3", "b2", "u24", "o04", (16, 32), "c2", "a4", "b3", "c3", "b4", "c4")
LATE = ("o05", "u25")


def add_into(target, term):
    shape = target.shape
    if len(shape) == 2:
        target[...] = (target[...].astype(F32) + term[...].astype(F32)).astype(BF)
        return

    def body(i, carry):
        target[i] = (target[i].astype(F32) + term[i].astype(F32)).astype(BF)
        return carry

    lax.fori_loop(0, shape[0], body, 0)


class Reduce:
    def __init__(self, place, lanes, theirs, mine, buffers, kind, first):
        self.p, self.lanes, self.theirs, self.mine, self.b = place, lanes, theirs, mine, buffers
        self.kind, self.axes = kind, ("x", "y") if first == "x" else ("y", "x")
        self.s = [lanes.take(0, 1) for _ in range(3)] + [lanes.take(0, 3)]
        self.r = [lanes.take(1, 1) for _ in range(3)] + [lanes.take(1, 3)]
        n = place.n_row
        self.far = (place.z + n // 2) % n
        self.near = place.z + 1 - 2 * (place.z % 2)
        self.cross = (self.near + n // 2) % n

    def start(self):
        p = self.p
        self.lanes.send(lambda: (self.theirs, self.b[0], p.dev(k=1 - p.k), self.s[0], self.r[0]))

    def half(self, ref, axis, side):
        if self.kind == "lanes" and axis == "y":
            return ref.at[side]
        if self.kind == "rows" and axis == "x":
            count = ref.shape[0] // 2
            return ref.at[pl.ds(side * count, count)]
        width = ref.shape[-1] // 2
        lead = (slice(None),) * (len(ref.shape) - 1)
        return ref.at[lead + (pl.ds(aligned(side * width, 128), width),)]

    def where(self, axis):
        p = self.p
        return (p.x, p.dev(x=1 - p.x)) if axis == "x" else (p.y, p.dev(y=1 - p.y))

    def send_half(self, stage):
        def make():
            side, peer = self.where(self.axes[stage - 1])
            return (self.half(self.b[stage - 1], self.axes[stage - 1], 1 - side), self.b[stage], peer, self.s[stage], self.r[stage])

        self.lanes.send(make)

    def add_half(self, stage):
        side, peer = self.where(self.axes[stage - 1])
        self.lanes.arrived(self.b[stage], peer, self.r[stage])
        add_into(self.b[stage], self.half(self.b[stage - 1], self.axes[stage - 1], side))

    def one(self):
        p = self.p
        self.lanes.arrived(self.b[0], p.dev(k=1 - p.k), self.r[0])
        add_into(self.b[0], self.mine)
        self.send_half(1)

    def two(self):
        self.add_half(1)
        self.send_half(2)

    def part(self, z):
        ref = self.b[2]
        if self.kind == "rows":
            return ref.at[z]
        width = self.b[3].shape[-1]
        return ref.at[:, pl.ds(aligned(z * width, 128), width)]

    def three(self):
        p = self.p
        self.add_half(2)
        for i, target in enumerate((self.cross, self.near)):
            def make(i=i, target=target):
                return (self.part(target), self.b[3].at[1 - i], p.dev(z=self.near), self.s[3] + i, self.r[3] + i)
            self.lanes.send(make)

    def four(self):
        p = self.p
        self.lanes.arrived(self.b[3].at[1], p.dev(z=self.near), self.r[3])
        add_into(self.b[3].at[1], self.part(self.far))
        self.lanes.send(lambda: (self.b[3].at[1], self.b[4], p.dev(z=self.far), self.s[3] + 2, self.r[3] + 2))

    def five(self):
        p = self.p
        self.lanes.arrived(self.b[3].at[0], p.dev(z=self.near), self.r[3] + 1)
        total = self.part(p.z)[...].astype(F32) + self.b[3][0].astype(F32)
        self.lanes.arrived(self.b[4], p.dev(z=self.far), self.r[3] + 2)
        return total + self.b[4][...].astype(F32)


def piece_buffers(kind, first, lead, rows, columns, n_row, groups):
    if kind == "lanes":
        one = (2, rows, columns // 2) if first == "x" else (rows, columns)
        return [(2, rows, columns), one, (rows, columns // 2), (2, rows, columns // groups), (rows, columns // groups)]
    one = (lead // 2, rows, columns) if first == "x" else (lead, rows, columns // 2)
    return [(lead, rows, columns), one, (lead // 2, rows, columns // 2), (2, rows, columns // 2), (rows, columns // 2)]


def backward_kernel(
    dims, plan, seq_ref, len_ref, qkv_ref, ctx_ref, lse_ref, dctx_ref, xt_ref, w_ref, gm_ref, gout_ref, gup_ref, part_x_ref, part_y_ref,
    ngrad_ref, tgrad_ref, rqkv_ref, rout_ref, rup_ref, rdown_ref, nsum_ref, *scratch,
):
    n_dp, n_row, n_col = dims
    p = Place(n_dp, n_row, n_col)
    groups = n_dp * n_row
    (
        qkv_v, ctx_v, lse_v, dctx_v, xt_v, w_v, gm_v, m_out, m_up, ga_v, gb_v, gc_v, dqt_v, dk_v, dv_v, acc_k, acc_v, dxt_v, trecv,
        nrecv, fq, fo, fu, tok_send, tok_recv, norm_send, norm_recv, w_send, w_recv, local_sem,
    ) = scratch[:30]
    pieces = scratch[30:]
    micro, slots, _, span = tgrad_ref.shape
    width, rows = ctx_ref.shape
    p.greet()
    local = []

    def keep(src, dst):
        made = pltpu.make_async_copy(src, dst, local_sem.at[len(local)])
        made.start()
        local.append(made)
        return made

    needed = [keep(qkv_ref, qkv_v), keep(dctx_ref, dctx_v), keep(ctx_ref, ctx_v), keep(lse_ref, lse_v)]
    mine_up = keep(gup_ref.at[:, p.k], m_up)
    mine_out = keep(gout_ref.at[:, p.k], m_out)
    xt_load = keep(xt_ref, xt_v)
    later = [keep(w_ref, w_v), keep(gm_ref, gm_v)]
    p.met()
    lanes = Lanes(w_send, w_recv)
    partner = p.dev(k=1 - p.k)
    waves = {"down": [], "up": [], "out": [], "a": [], "b": [], "c": []}
    parts = []
    made_here = {"a": ga_v, "b": gb_v, "c": gc_v}
    whole = {"up": gup_ref, "out": gout_ref, **made_here}
    carried = {"up": m_up, "out": m_out}
    sources = {"x": [part_x_ref.at[i] for i in range(DOWN.count("x"))], "y": [part_y_ref.at[i] for i in range(DOWN.count("y"))]}
    for index, (name, kind, first, low, count) in enumerate(plan):
        if name == "down":
            piece = Reduce(p, lanes, None, None, pieces[5 * index:5 * index + 5], kind, first)
            parts.append(keep(sources[first].pop(0), piece.b[1]))
            waves["down"].append(piece)
            continue
        at = pl.ds(low, count)
        theirs = whole[name].at[:, 1 - p.k, at]
        mine = made_here[name].at[:, p.k, at] if name in made_here else carried[name].at[:, at]
        waves[name].append(Reduce(p, lanes, theirs, mine, pieces[5 * index:5 * index + 5], kind, first))
    d, u, o = waves["down"], waves["up"], waves["out"]
    joined = [waves[name][0] for name in "abc"]

    def window(device):
        return pl.ds(aligned(device * (width // p.n) // 128 * 128, 128), 256)

    def norm_copy(i):
        target = (p.flat + i) % p.n
        return pltpu.make_async_remote_copy(
            src_ref=ngrad_ref.at[:, window(target)], dst_ref=nrecv.at[p.flat],
            send_sem=norm_send.at[i], recv_sem=norm_recv.at[i],
            device_id=p.of_flat(target), device_id_type=MESH,
        )

    def norm_start(i, carry):
        norm_copy(i).start()
        return carry

    u[0].start()
    u[1].start()
    for made, piece in zip(parts, d):
        made.wait()
        piece.send_half(2)
    lax.fori_loop(1, p.n, norm_start, 0)
    nrecv[p.flat] = ngrad_ref[:, window(p.flat)]
    for made in needed:
        made.wait()
    mine_up.wait()
    mine_out.wait()

    def finish_rows(piece, temp, result, low):
        total = piece()
        count, across = total.shape[0], total.shape[1] // 2
        half_rows = result.shape[0] // 2
        temp[pl.ds(low, count), :] = jnp.where(p.k == 0, total[:, across:], total[:, :across])
        result[pl.ds(aligned(p.k * half_rows + low, 16), count), :] = jnp.where(p.k == 0, total[:, :across], total[:, across:])
        s, r = lanes.take(0, 1), lanes.take(1, 1)
        place = lambda k: result.at[pl.ds(aligned(k * half_rows + low, 16), count), :]
        lanes.send(lambda: (temp.at[pl.ds(low, count), :], place(p.k), partner, s, r))
        ends.append(lambda: lanes.arrived(place(1 - p.k), partner, r))

    ends = []

    def finish_down(piece, low):
        total = piece.five()
        rdown_ref[pl.ds(low, total.shape[0]), :] = total

    lows = {name: [low for other, _, _, low, _ in plan if other == name] for name in waves}
    down_end = [functools.partial(finish_down, piece, low) for piece, low in zip(d, lows["down"])]
    up_end = [functools.partial(finish_rows, piece.five, fu, rup_ref, low) for piece, low in zip(u, lows["up"])]
    out_end = [functools.partial(finish_rows, piece.five, fo, rout_ref, low) for piece, low in zip(o, lows["out"])]

    def joined_total():
        blocks = [[total[:, i * 128:(i + 1) * 128] for i in range(3)] for total in (piece.five() for piece in joined)]
        middle = [piece[1] for piece in blocks]
        queries = [piece[0] for piece in blocks] + middle + [piece[2] for piece in blocks]
        return jnp.concatenate(queries, axis=1)

    def joined_end():
        finish_rows(joined_total, fq, rqkv_ref, 0)

    xt = lambda: xt_v[...].reshape(width, rows)
    pairs = width // 128

    def grad_part(grad, number):
        near, far = number, number + pairs // 2
        columns = lambda pair: slice(pair * 128, pair * 128 + 128)
        terms = (
            lambda: product_nt(xt(), dqt_v[columns(near), :]), lambda: product_nt(xt(), dqt_v[columns(far), :]),
            lambda: product(xt(), dk_v[:, columns(near)]), lambda: product(xt(), dk_v[:, columns(far)]),
            lambda: product(xt(), dv_v[:, columns(near)]), lambda: product(xt(), dv_v[:, columns(far)]),
        )
        for i, term in enumerate(terms):
            grad[:, :, :, columns(i)] = term().astype(BF).reshape(groups, 2, -1, 128)
        joined[number].start()

    def first_part():
        xt_load.wait()
        grad_part(ga_v, 0)

    table = {
        letter + str(i) + str(stage): act
        for letter, group, ends_ in (("d", d, down_end), ("u", u, up_end), ("o", o, out_end))
        for i, (piece, end) in enumerate(zip(group, ends_))
        for stage, act in enumerate((piece.start, piece.one, piece.two, piece.three, piece.four, end))
    }
    for letter, piece in zip("abc", joined):
        for stage, act in enumerate((piece.one, piece.two, piece.three, piece.four)):
            table[letter + str(stage + 1)] = act
    table.update({"a0": first_part, "b0": functools.partial(grad_part, gb_v, 1), "c0": functools.partial(grad_part, gc_v, 2)})
    events = {turn: [table[step] for step in steps] for turn, steps in SUMS.items()}
    length_bias = jnp.where(lax.broadcasted_iota(jnp.int32, (rows, 1), 0) < len_ref[p.c, seq_ref[p.c, p.g]], 0.0, NEGATIVE)
    chunks = rows // BACK_CHUNK

    def attend(step, carry):
        for when_, acts in events.items():
            def act(acts=acts):
                for a in acts:
                    a()
            pl.when(step == when_)(act)
        turn, at_row = step // chunks, step % chunks
        pair = turn % 2 * (pairs // 2) + turn // 2
        columns = [pl.ds(aligned(i * width + pair * 128, 128), 128) for i in range(3)]
        keys, values = qkv_v[:, columns[1]], qkv_v[:, columns[2]]
        keys_t = keys.T
        lane = lax.broadcasted_iota(jnp.int32, (rows, 128), 1)
        short = lax.broadcasted_iota(jnp.int32, (BACK_CHUNK, 128), 1)
        own_rows = pl.ds(aligned(at_row * BACK_CHUNK, BACK_CHUNK), BACK_CHUNK)
        queries = qkv_v[own_rows, columns[0]] * jnp.asarray(0.125, BF)
        back = dctx_v[own_rows, columns[0]]
        back_t = back.T.astype(F32)
        forth_t = ctx_v[pl.ds(aligned(pair * 128, 128), 128), own_rows].astype(F32)
        both = back_t * forth_t
        d_keys = d_values = None
        for h in range(2):
            def own(block, index):
                return jnp.where((index < HEAD) == (h == 0), block, jnp.zeros_like(block))
            delta = jnp.sum(both[h * HEAD:(h + 1) * HEAD], axis=0, keepdims=True)
            scores = product_nt(own(keys, lane), queries) + length_bias
            soft = jnp.exp(scores - lse_v[2 * pair + h, :, own_rows])
            d_probs = product_nt(own(values, lane), back)
            d_scores = (soft * (d_probs - delta)).astype(BF)
            head_rows = pl.ds(aligned(pair * 128 + h * HEAD, HEAD), HEAD)
            dqt_v[head_rows, own_rows] = (product(keys_t[h * HEAD:(h + 1) * HEAD], d_scores) * 0.125).astype(BF)
            to_values = product(soft.astype(BF), own(back, short))
            to_keys = product(d_scores, own(queries, short))
            d_values = to_values if d_values is None else d_values + to_values
            d_keys = to_keys if d_keys is None else d_keys + to_keys

        @pl.when(at_row == 0)
        def _():
            acc_k[...] = d_keys
            acc_v[...] = d_values

        @pl.when(at_row > 0)
        def _():
            acc_k[...] += d_keys
            acc_v[...] += d_values

        @pl.when(at_row == chunks - 1)
        def _():
            dk_v[:, columns[0]] = acc_k[...].astype(BF)
            dv_v[:, columns[0]] = acc_v[...].astype(BF)
        return carry

    lax.fori_loop(0, width // 128 * chunks, attend, 0)
    for made in later:
        made.wait()

    def tok_copy(target):
        return pltpu.make_async_remote_copy(
            src_ref=dxt_v.at[target // n_col, :, pl.ds(aligned((target % n_col) * span, 128), span)],
            dst_ref=trecv.at[p.c * slots + p.g],
            send_sem=tok_send.at[target], recv_sem=tok_recv.at[p.flat],
            device_id=p.of_flat(target), device_id_type=MESH,
        )

    half_groups = groups // 2
    half_width = width // 2

    def tok_batch(part, low, high):
        def one(i, carry):
            target = part * half_groups * n_col + (p.flat + i * 5) % (half_groups * n_col)

            @pl.when(target != p.flat)
            def _():
                tok_copy(target).start()
            return carry

        lax.fori_loop(low, high, one, 0)

    def grad_input(part):
        near = pl.ds(part * half_groups, half_groups)
        w_rows = lambda i: w_v[near, :, :, i * width:(i + 1) * width].reshape(half_width, width)
        total = gm_v[:, part * half_width:(part + 1) * half_width].T
        total = total + product(w_rows(0), dqt_v[...])
        total = total + product_nt(w_rows(1), dk_v[...])
        total = total + product_nt(w_rows(2), dv_v[...])
        dxt_v[near] = total.astype(BF).reshape(half_groups, width // groups, rows)

    count = half_groups * n_col
    grad_input(0)
    made_parts = 1
    for step in PACE:
        if isinstance(step, str):
            table[step]()
            continue
        low, high = step
        if high > count and made_parts == 1:
            grad_input(1)
            made_parts = 2
            own_tok = keep(dxt_v.at[p.g, :, pl.ds(aligned(p.c * span, 128), span)], trecv.at[p.c * slots + p.g])
        for part in range(2):
            first, last = max(low, part * count) - part * count, min(high, part * count + count) - part * count
            if first < last:
                tok_batch(part, first, last)
    for step in LATE:
        table[step]()

    def norm_wait(i, carry):
        source = (p.flat + p.n - i) % p.n
        pltpu.make_async_remote_copy(
            src_ref=nrecv.at[source], dst_ref=nrecv.at[source], send_sem=norm_send.at[i], recv_sem=norm_recv.at[i],
            device_id=p.of_flat(source), device_id_type=MESH,
        ).wait_recv()
        norm_copy(i).wait_send()
        return carry

    lax.fori_loop(1, p.n, norm_wait, 0)
    nsum_ref[...] = jnp.sum(nrecv[...], axis=0)
    joined_end()
    own_tok.wait()

    def tok_wait(i, carry):
        source = (p.flat + p.n - i) % p.n
        landing = trecv.at[(source % n_col) * slots + source // n_col]
        pltpu.make_async_remote_copy(
            src_ref=landing, dst_ref=landing, send_sem=tok_send.at[source], recv_sem=tok_recv.at[source],
            device_id=p.of_flat(source), device_id_type=MESH,
        ).wait_recv()
        tok_copy((p.flat + i) % p.n).wait_send()
        return carry

    lax.fori_loop(1, p.n, tok_wait, 0)
    for m in range(micro):
        for s in range(slots):
            place = jnp.int32(0)
            for j in range(slots):
                place = jnp.where(seq_ref[m, j] == s, jnp.int32(j), place)
            tgrad_ref[m, s] = trecv[m * slots + place]
    for end in ends:
        end()
    lanes.finish()


def backward(dims, seq_order, lengths, qkv, ctx_t, lse, d_context, xt, w_qkv, g_mixed, g_out, g_up, part_x, part_y, n_grads):
    n_dp, n_row, n_col = dims
    groups, n = n_dp * n_row, n_dp * n_row * n_col
    micro, slots = seq_order.shape
    width, rows = ctx_t.shape
    feats, span = width // groups, rows // n_col
    shape = jax.ShapeDtypeStruct
    plan, buffers = [], []
    for name, grad, kind, axes in (
        ("down", part_y, "lanes", DOWN), ("up", g_up, "rows", UP), ("out", g_out, "rows", OUT),
        *((letter, g_out, "rows", axis) for letter, axis in zip("abc", JOINED)),
    ):
        if name == "down":
            lead, each, columns = 2, part_y.shape[1], part_y.shape[2]
        else:
            lead, _, across, columns = grad.shape
            each = across // len(axes)
        for i, axis in enumerate(axes):
            plan.append((name, kind, axis, i * each, each))
            sizes = piece_buffers(kind, axis, lead, each, columns, n_row, groups)
            if name == "down":
                sizes[0] = (16, 128)
            buffers += [pltpu.VMEM(size, BF) for size in sizes]
    outs = (
        shape((micro, slots, feats, span), BF),
        shape((w_qkv.shape[2] * 2, w_qkv.shape[3] // n_col), F32),
        shape((g_out.shape[2] * 2, g_out.shape[3] // n_col), F32),
        shape((g_up.shape[2] * 2, g_up.shape[3] // n_col), F32),
        shape((len(DOWN) * part_y.shape[1], part_y.shape[2] // groups), F32),
        shape((8, 256), F32),
    )
    vm = lambda like, kind=BF: pltpu.VMEM(like.shape, kind)
    temps = [pltpu.VMEM((g.shape[2], g.shape[3] // n_col), F32) for g in (w_qkv, g_out, g_up)]
    carried = [pltpu.VMEM((g.shape[0],) + g.shape[2:], BF) for g in (g_out, g_up)]
    return pl.pallas_call(
        functools.partial(backward_kernel, dims, plan),
        out_shape=outs,
        in_specs=[SM, SM, ANY, ANY, ANY, ANY, ANY, ANY, ANY, ANY, ANY, ANY, ANY, VM],
        out_specs=[VM, VM, VM, VM, VM, VM],
        scratch_shapes=[
            vm(qkv), vm(ctx_t), vm(lse, F32), vm(d_context), vm(xt), vm(w_qkv), vm(g_mixed, F32), *carried, vm(g_out), vm(g_out), vm(g_out),
            pltpu.VMEM((width, rows), BF), pltpu.VMEM((rows, width), BF), pltpu.VMEM((rows, width), BF),
            pltpu.VMEM((rows, 128), F32), pltpu.VMEM((rows, 128), F32),
            pltpu.VMEM((groups, feats, rows), BF), pltpu.VMEM((micro * slots, feats, span), BF),
            pltpu.VMEM((n, 8, 256), F32), *temps,
            DMA((n,)), DMA((n,)), DMA((n,)), DMA((n,)),
            DMA((80,)), DMA((80,)), DMA((16,)), *buffers,
        ],
        compiler_params=pltpu.CompilerParams(
            collective_id=1, has_side_effects=True, vmem_limit_bytes=62 * 2**20
        ),
        name="backward_part",
    )(seq_order, lengths, qkv, ctx_t, lse, d_context, xt, w_qkv, g_mixed, g_out, g_up, part_x, part_y, n_grads)
def layer_norm(values, factor, offset):
    average = jnp.mean(values, axis=-1, keepdims=True)
    centered = values - average
    variance = jnp.mean(centered * centered, axis=-1, keepdims=True)
    return centered * lax.rsqrt(variance + EPSILON) * factor + offset


def gelu_act(values):
    return 0.5 * values * (1.0 + lax.erf(values * ROOT_HALF))


def attention(qkv, length):
    rows, width = qkv.shape[0], qkv.shape[1] // 3
    heads = width // HEAD
    q, k, v = (qkv[:, i * width:(i + 1) * width].reshape(rows, heads, HEAD) for i in range(3))
    scores = jnp.einsum("qhe,khe->hqk", q, k, preferred_element_type=F32) * 0.125
    valid = jnp.arange(rows, dtype=jnp.int32) < length
    scores = jnp.where(valid[None, None, :], scores, NEGATIVE)
    top = jnp.max(scores, axis=-1, keepdims=True)
    exps = jnp.exp(scores - top)
    total = jnp.sum(exps, axis=-1, keepdims=True)
    probs = (exps / total).astype(BF)
    context = jnp.einsum("hqk,khe->qhe", probs, v, preferred_element_type=F32)
    return context.astype(BF).reshape(rows, width), top + jnp.log(total)


def attention_back(qkv, length, stats, d_context):
    rows, width = qkv.shape[0], qkv.shape[1] // 3
    heads = width // HEAD
    q, k, v = (qkv[:, i * width:(i + 1) * width].reshape(rows, heads, HEAD) for i in range(3))
    dc = d_context.reshape(rows, heads, HEAD)
    scores = jnp.einsum("qhe,khe->hqk", q, k, preferred_element_type=F32) * 0.125
    valid = jnp.arange(rows, dtype=jnp.int32) < length
    scores = jnp.where(valid[None, None, :], scores, NEGATIVE)
    soft = jnp.exp(scores - stats)
    d_probs = jnp.einsum("qhe,khe->hqk", dc, v, preferred_element_type=F32)
    delta = jnp.sum(soft * d_probs, axis=-1, keepdims=True)
    d_scores = (soft * (d_probs - delta)).astype(BF)
    dq = jnp.einsum("hqk,khe->qhe", d_scores, k, preferred_element_type=F32) * 0.125
    dk = jnp.einsum("hqk,qhe->khe", d_scores, q, preferred_element_type=F32) * 0.125
    dv = jnp.einsum("hqk,qhe->khe", soft.astype(BF), dc, preferred_element_type=F32)
    return jnp.concatenate([a.astype(BF).reshape(rows, width) for a in (dq, dk, dv)], axis=-1)


def middle(x, context, context_t, cot, w_out, w_up, w_down_t, gain_one, shift_one, gain_two, shift_two):
    mixed = x.astype(F32) + product(context, w_out)
    hidden = layer_norm(mixed, gain_one, shift_one)
    hidden_low = hidden.astype(BF)
    pre_act = product(hidden_low, w_up)
    act_low = gelu_act(pre_act).astype(BF)
    summed = hidden + product_nt(act_low, w_down_t)
    output = layer_norm(summed, gain_two, shift_two).astype(BF)
    _, norm_two_back = jax.vjp(layer_norm, summed, gain_two, shift_two)
    g_summed, g_gain_two, g_shift_two = norm_two_back(cot.astype(F32))
    d_down = g_summed.astype(BF)
    g_down_t = product_tn(d_down, act_low).astype(BF)
    d_act = product(d_down, w_down_t)
    _, gelu_back = jax.vjp(gelu_act, pre_act)
    d_pre = gelu_back(d_act)[0].astype(BF)
    g_up = product_tn(hidden_low, d_pre).astype(BF)
    g_hidden = g_summed + product_nt(d_pre, w_up)
    _, norm_one_back = jax.vjp(layer_norm, mixed, gain_one, shift_one)
    g_mixed, g_gain_one, g_shift_one = norm_one_back(g_hidden)
    d_attn = g_mixed.astype(BF)
    g_out = product(context_t, d_attn).astype(BF)
    d_context = product_nt(d_attn, w_out).astype(BF)
    return output, g_mixed, d_context, g_down_t, g_up, g_out, (g_gain_one, g_shift_one, g_gain_two, g_shift_two)


def take_blocks(blocks, places):
    def body(place_ref, in_ref, out_ref):
        def step(i, carry):
            out_ref[i] = in_ref[place_ref[i]]
            return carry

        lax.fori_loop(0, blocks.shape[0], step, 0)

    return pl.pallas_call(
        body, out_shape=jax.ShapeDtypeStruct(blocks.shape, blocks.dtype), in_specs=[SM, VM], out_specs=VM,
        compiler_params=pltpu.CompilerParams(vmem_limit_bytes=48 * 2**20), name="take_blocks",
    )(places, blocks)


def own_length(lengths, seq_order):
    n_row = lax.axis_size("row")
    slot = lax.axis_index("dp") * n_row + lax.axis_index("row")
    micro = lax.axis_index("col")
    index = jnp.arange(seq_order.shape[1], dtype=jnp.int32)
    order = jnp.sum(jnp.where(jnp.arange(seq_order.shape[0])[:, None] == micro, seq_order, 0), axis=0)
    source = jnp.sum(jnp.where(index == slot, order, 0))
    mine = jnp.sum(jnp.where(jnp.arange(seq_order.shape[0])[:, None] == micro, lengths, 0), axis=0)
    return jnp.sum(jnp.where(index == source, mine, 0))


def local(
    tokens, cotangent, lengths, seq_order, w_qkv, w_out, w_up, w_down, gain_one, shift_one, gain_two, shift_two,
):
    dims = tuple(lax.axis_size(a) for a in ("dp", "row", "col"))
    n_dp, n_row, n_col = dims
    groups = n_dp * n_row
    micro, slots, span, feats = tokens.shape
    width = cotangent.shape[3]
    rows = span * n_col
    direct = n_dp == 2 and n_row == 4 and n_col == 4 and feats % 32 == 0 and w_qkv.shape[0] % 32 == 0
    tok_t = jnp.swapaxes(tokens, 2, 3)
    w_down_t = w_down.T
    norms = jnp.stack([gain_one, shift_one, gain_two, shift_two])
    length = own_length(lengths, seq_order)
    everyone = ("dp", "row", "col")
    if direct:
        each = norms.shape[1]
        place = (lax.axis_index("dp") * n_row + lax.axis_index("row")) * n_col + lax.axis_index("col")
        lane = jnp.arange(256, dtype=jnp.int32)
        here = lane[None, :] == (place * each) % 128 + jnp.arange(each, dtype=jnp.int32)[:, None]
        packed = jnp.sum(jnp.where(here[None], norms[:, :, None].astype(F32), 0.0), axis=1).astype(BF)
        packed = jnp.pad(packed, ((0, 12), (0, 0)))
        xt, w_joined, qkv, context_t, lse, output, g_mixed, d_context, g_out, g_up, part_x, part_y, norm_grads = forward(
            dims, seq_order, lengths, tok_t, cotangent[:, 0], w_qkv, w_out, w_up, w_down_t, packed
        )
    else:
        offset = jnp.arange(micro, dtype=jnp.int32)[:, None] * slots
        sent = take_blocks(tok_t.reshape(micro * slots, feats, span), (seq_order + offset).reshape(-1))
        sent = jnp.swapaxes(sent.reshape(micro, slots, feats, span), 0, 1).reshape(micro * slots, feats, span)
        got = lax.all_to_all(sent, everyone, split_axis=0, concat_axis=0, tiled=True)
        xt = got.reshape(groups, n_col, feats, span).transpose(0, 2, 1, 3).reshape(width, rows)
        cot = lax.all_to_all(cotangent[:, 0], "col", split_axis=0, concat_axis=0, tiled=True).reshape(rows, width)

        def whole(w, row_axes, col_axes):
            w = lax.all_gather(w, col_axes, axis=1, tiled=True)
            return lax.all_gather(w, row_axes, axis=0, tiled=True)

        f_qkv, f_out, f_up = (whole(w, ("dp", "row"), "col") for w in (w_qkv, w_out, w_up))
        f_down_t = whole(w_down_t, "col", ("dp", "row"))
        f_norms = lax.all_gather(norms, everyone, axis=1, tiled=True)
    if direct:
        tgrad, r_qkv, r_out, r_up, r_down_t, n_sum = backward(
            dims, seq_order, lengths, qkv, context_t, lse, d_context, xt, w_joined, g_mixed,
            g_out, g_up, part_x, part_y, norm_grads,
        )
        n_sum = lax.dynamic_slice(n_sum, (0, place * each % 128), (4, each))
    else:
        gains = [f_norms[i].astype(F32) for i in range(4)]
        x = xt.T
        qkv = product(x, f_qkv).astype(BF)
        context, stats = attention(qkv, length)
        output, g_mixed, d_context, g_down_t, g_up, g_out, norm_grads = middle(
            x, context, context.T, cot, f_out, f_up, f_down_t, *gains
        )
        norm_grads = jnp.stack(norm_grads)
        d_qkv = attention_back(qkv, length, stats, d_context)
        g_qkv = product(xt, d_qkv).astype(BF)
        dxt = (g_mixed + product_nt(d_qkv, f_qkv)).astype(BF).T
        n_sum = lax.psum_scatter(norm_grads, everyone, scatter_dimension=1, tiled=True)
        output = lax.all_to_all(output.reshape(n_col, span, width), "col", split_axis=0, concat_axis=0, tiled=True)
        sent = dxt.reshape(groups, feats, n_col, span).transpose(0, 2, 1, 3).reshape(micro * slots, feats, span)
        got = lax.all_to_all(sent, everyone, split_axis=0, concat_axis=0, tiled=True)
        got = jnp.swapaxes(got.reshape(slots, micro, feats, span), 0, 1).reshape(micro * slots, feats, span)
        index = jnp.arange(slots, dtype=jnp.int32)
        inverse = jnp.sum(jnp.where(seq_order[:, :, None] == index, index[None, :, None], 0), axis=1)
        offset = jnp.arange(micro, dtype=jnp.int32)[:, None] * slots
        tgrad = take_blocks(got, (inverse + offset).reshape(-1)).reshape(micro, slots, feats, span)

        def parts(g, row_axes, col_axes):
            g = lax.psum_scatter(g, col_axes, scatter_dimension=1, tiled=True)
            return lax.psum_scatter(g, row_axes, scatter_dimension=0, tiled=True).astype(F32)

        r_qkv, r_out, r_up = (parts(g, ("dp", "row"), "col") for g in (g_qkv, g_out, g_up))
        r_down_t = parts(g_down_t, "col", ("dp", "row"))
    return (
        output[:, None], jnp.swapaxes(tgrad, 2, 3), r_qkv, r_out, r_up, r_down_t.T,
        n_sum[0], n_sum[1], n_sum[2], n_sum[3],
    )


def solution(mesh):
    rows = ("dp", "row")
    every = ("dp", "row", "col")
    in_specs = (
        P(None, None, "col", rows), P(None, rows, "col", None), P(), P(),
        P(rows, "col"), P(rows, "col"), P(rows, "col"), P(rows, "col"),
        P(every), P(every), P(every), P(every),
    )
    out_specs = (
        P(None, rows, "col", None), P(None, None, "col", rows),
        P(rows, "col"), P(rows, "col"), P(rows, "col"), P(rows, "col"),
        P(every), P(every), P(every), P(every),
    )
    return jax.shard_map(local, mesh=mesh, in_specs=in_specs, out_specs=out_specs, check_vma=False)
```
